512 devices in a mesh: lat: 32 (over z, core), dep: 16 (over y, x).
Axes of the slice: x: 4, y: 4, z: 16, core: 2. Of those that a mesh axis runs over, the one named last changes fastest.
Arguments:
- pressure_prev: float32 [128, 2048, 512], P('dep', 'lat'), may hold values from -6 to 6
- pressure_now: float32 [128, 2048, 512], P('dep', 'lat'), may hold values from -6 to 6
- materials: int32 [128, 2048, 512], P('dep', 'lat'), may hold values from 0 to 15
- courant_table: float32 [16], replicated, may hold values from 0.1 to 0.45
- tf_weights: float32 [4, 8], replicated, may hold values from 0.05 to 1.5
- source_cell: int32 [3], replicated, may hold values from 0 to 2047, as said below
- start_step: int32 [1], replicated, may hold values from 0 to 23
Outputs:
- pressure: float32 [128, 2048, 512], P('dep', 'lat')
- image: float32 [4, 2048, 512], P(None, 'lat', 'dep')
The draws below stay inside these ranges and needn't reach their ends.
Inputs may be any that keep to these rules, and one draw needn't show every extreme that they name: source_cell holds a depth index below 128, an x index below 2048 and a y index below 512; along the dimension with the most cells (depth first on ties, then x) the index is that dimension's last cell.
All inputs are finite; a program needn't handle non-finite values.
Results may differ from the reference program's by a relative error of at most 0.000051.
Values sent between devices are 32-bit elements; how exact they have to be, the bound alone decides.
No kernel may reach another device: no remote copies, remote signals or barrier semaphores. Data moves between devices by JAX's collectives and lax.ppermute only.
A program may use at most 64 MiB of HBM per device.

```python
import math
import jax
import jax.numpy as jnp

NY = 512
STEPS = 3
MATS = 16
BUMPS = 8
NX = 2048
NZ = 128


def draw_source_cell(key, part):
    key = jax.random.fold_in(key, 5)
    keys = jax.random.split(key, 3)
    depth_index = jax.random.randint(keys[0], (1,), 0, NZ)
    lateral_x = jax.random.randint(keys[1], (1,), 0, NX)
    lateral_y = jax.random.randint(keys[2], (1,), 0, NY)
    longest = max(max(NZ, NX), NY)
    if NZ == longest:
        depth_index = jnp.full((1,), NZ - 1, jnp.int32)
    elif NX == longest:
        lateral_x = jnp.full((1,), NX - 1, jnp.int32)
    else:
        lateral_y = jnp.full((1,), NY - 1, jnp.int32)
    return jnp.concatenate([depth_index, lateral_x, lateral_y]).astype(jnp.int32)


def set_ends(array, stream_key, least, top_value):
    spot = [jax.random.randint(jax.random.fold_in(stream_key, axis), (), 0, length) for axis, length in enumerate(array.shape)]
    widest = array.shape.index(max(array.shape))
    neighbour = spot[:widest] + [(spot[widest] + 1) % array.shape[widest]] + spot[widest + 1:]
    return array.at[tuple(spot)].set(least).at[tuple(neighbour)].set(top_value)


def shard_levels(key, shape, shards, low, largest):
    level, own = 1.0, jax.random.fold_in(key, 6)
    for dim, shards_of in shards:
        draws = jnp.exp(jax.random.uniform(jax.random.fold_in(own, dim), (shards_of,), jnp.float32, low / len(shards), largest / len(shards)))
        level = level * jnp.repeat(draws, shape[dim] // shards_of).reshape([-1 if axis == dim else 1 for axis in range(len(shape))])
    return level


def scatter_about(own_key, dims, scale, bound, cuts=(), dtype=jnp.bfloat16):
    values = jax.random.normal(own_key, dims, jnp.float32) * scale
    if len(cuts) > 0:
        values = shard_levels(own_key, dims, cuts, -0.22, 0.18) * values
    return jnp.clip(values, min=-bound, max=bound).astype(dtype)


def setup_inputs(seed: int = 0) -> dict:
    splits = jax.random.split(jax.random.key(seed), 8)
    pressure_prev = scatter_about(splits[0], (NZ, NX, NY), 1.0, 6.0, ((0, 16), (1, 32)), jnp.float32)
    pressure_now = scatter_about(splits[1], (NZ, NX, NY), 1.0, 6.0, ((0, 16), (1, 32)), jnp.float32)
    materials = set_ends(jax.random.randint(splits[2], (NZ, NX, NY), 0, MATS), jax.random.fold_in(splits[2], 1), 0, MATS - 1).astype(jnp.int32)
    courant_table = jnp.clip(jax.random.uniform(splits[3], (MATS,), jnp.float32, 0.1, 0.45), 0.1, 0.45)
    tf_weights = jnp.clip(jnp.exp(jax.random.uniform(splits[4], (4, BUMPS), jnp.float32, math.log(0.05), math.log(1.5))), 0.05, 1.5)
    source_cell = draw_source_cell(jax.random.fold_in(splits[7], 71), 0)
    start_step = jax.random.randint(splits[6], (1,), 0, 24).astype(jnp.int32)
    return {"pressure_prev": pressure_prev, "pressure_now": pressure_now, "materials": materials, "courant_table": courant_table, "tf_weights": tf_weights, "source_cell": source_cell, "start_step": start_step}


def laplace_inner(extended):
    core = extended[2:-2, 2:-2, :]
    ypadded = jnp.pad(core, ((0, 0), (0, 0), (2, 2)))
    total = (3.0 * -2.5) * core
    total = total + (4.0 / 3.0) * (extended[3:-1, 2:-2, :] + extended[1:-3, 2:-2, :])
    total = total - (1.0 / 12.0) * (extended[4:, 2:-2, :] + extended[:-4, 2:-2, :])
    total = total + (4.0 / 3.0) * (extended[2:-2, 3:-1, :] + extended[2:-2, 1:-3, :])
    total = total - (1.0 / 12.0) * (extended[2:-2, 4:, :] + extended[2:-2, :-4, :])
    total = total + (4.0 / 3.0) * (ypadded[:, :, 3:-1] + ypadded[:, :, 1:-3])
    total = total - (1.0 / 12.0) * (ypadded[:, :, 4:] + ypadded[:, :, :-4])
    return total


def wavelet(level):
    shifted = 0.3 * (level.astype(jnp.float32) - 10.0)
    return 4.0 * (1.0 - 2.0 * shifted * shifted) * jnp.exp(-shifted * shifted)


def render_terms(field, tf_weights):
    colours = [jnp.zeros_like(field) for channel in range(3)]
    extinct = jnp.zeros_like(field)
    for bump_index in range(BUMPS):
        centre = -3.0 + 6.0 * bump_index / (BUMPS - 1)
        scaled = (field - centre) / 0.8
        bump = jnp.exp(-scaled * scaled)
        colours = [colours[channel] + tf_weights[channel, bump_index] * bump for channel in range(3)]
        extinct = extinct + tf_weights[3, bump_index] * bump
    return colours, extinct


def reference(pressure_prev, pressure_now, materials, courant_table, tf_weights, source_cell, start_step):
    stiffness = jnp.take(courant_table, materials)
    stiffness = stiffness * stiffness
    previous, current = pressure_prev, pressure_now
    for sweep_index in range(STEPS):
        extended = jnp.pad(current, ((2, 2), (2, 2), (0, 0)))
        advanced = 2.0 * current - previous + stiffness * laplace_inner(extended)
        amplitude = wavelet(start_step[0] + sweep_index)
        advanced = advanced.at[source_cell[0], source_cell[1], source_cell[2]].add(amplitude)
        previous, current = current, advanced
    colours, extinct = render_terms(current, tf_weights)
    sigma = extinct * (1.5 / NZ)
    prefix = jnp.cumsum(sigma, axis=0) - sigma
    weight = jnp.exp(-prefix) * (1.0 - jnp.exp(-sigma))
    image = jnp.stack([jnp.sum(weight * colours[0], axis=0), jnp.sum(weight * colours[1], axis=0),
                       jnp.sum(weight * colours[2], axis=0), 1.0 - jnp.exp(-jnp.sum(sigma, axis=0))])
    return current, image
```

```python
import functools
import math

import jax
import jax.numpy as jnp
from jax import lax
from jax.experimental import pallas as pl
from jax.experimental.pallas import tpu as pltpu
from jax.sharding import PartitionSpec as P

BUMPS = 8
Z, X, T = 8, 64, 4
ROWS = X + 32
CORE = 16
VMEM = pl.BlockSpec(memory_space=pltpu.VMEM)
SMEM = pl.BlockSpec(memory_space=pltpu.SMEM)
UP1, RIGHT1, SRC_Z, SRC_X, SRC_Y = range(5)


def lane_masks():
    lane = lax.broadcasted_iota(jnp.int32, (8, 128), 1)
    return lane < 1, lane < 2, lane >= 127, lane >= 126


def columns_sum(c, masks):
    zero = jnp.zeros((8, 128), jnp.float32)
    low1, low2, high1, high2 = masks
    a1 = [pltpu.roll(v, 1, 1) for v in c]
    a2 = [pltpu.roll(v, 2, 1) for v in c]
    b1 = [pltpu.roll(v, 127, 1) for v in c]
    b2 = [pltpu.roll(v, 126, 1) for v in c]
    out = []
    for i in range(T):
        first, last = i == 0, i == T - 1
        near = jnp.where(low1, zero if first else a1[i - 1], a1[i]) + jnp.where(
            high1, zero if last else b1[i + 1], b1[i]
        )
        far = jnp.where(low2, zero if first else a2[i - 1], a2[i]) + jnp.where(
            high2, zero if last else b2[i + 1], b2[i]
        )
        out.append((near, far))
    return out


def plane_terms(ref, k, row, masks):
    c = [ref[k, i, pl.ds(row, 8), :] for i in range(T)]
    sums = columns_sum(c, masks)
    out = []
    for i in range(T):
        near = sums[i][0] + (ref[k, i, pl.ds(row - 1, 8), :] + ref[k, i, pl.ds(row + 1, 8), :])
        far = sums[i][1] + (ref[k, i, pl.ds(row - 2, 8), :] + ref[k, i, pl.ds(row + 2, 8), :])
        out.append((c[i], near, far))
    return out


def full_terms(ref, k, row, masks):
    out = []
    for i, (c, near, far) in enumerate(plane_terms(ref, k, row, masks)):
        rows = pl.ds(row, 8)
        near = near + (ref[k - 1, i, rows, :] + ref[k + 1, i, rows, :])
        far = far + (ref[k - 2, i, rows, :] + ref[k + 2, i, rows, :])
        out.append((c, 16.0 * near - far - 90.0 * c))
    return out


def strike(ref, ints, amplitude, layers, rows_low, rows_high):
    z, x, y = ints[SRC_Z], ints[SRC_X], ints[SRC_Y]
    row = x + CORE
    here = (z >= 0) & (z < layers) & (row >= rows_low) & (row < rows_high)

    @pl.when(here)
    def _():
        tile, lane = y // 128, y % 128
        old = ref[z + 2, tile, pl.ds(row, 1), :]
        ids = lax.broadcasted_iota(jnp.int32, (1, 128), 1)
        ref[z + 2, tile, pl.ds(row, 1), :] = old + jnp.where(ids == lane, amplitude, 0.0)


def stiffness(table, materials):
    return jnp.take_along_axis(table, materials, axis=1, mode="promise_in_bounds")


def pack_depth(flags, now_a, now_b, mat_a, mat_b, table_ref, out_a, out_b):
    table = table_ref[...]
    for now, mat, out in ((now_a, mat_a, out_a), (now_b, mat_b, out_b)):
        for k in range(2):
            for i in range(T):
                lanes = slice(128 * i, 128 * i + 128)
                out[k, i] = now[k, :, lanes]
                for t in range(X // 8):
                    rows = slice(8 * t, 8 * t + 8)
                    out[2 + k, i, rows, :] = stiffness(table, mat[k, rows, lanes])


def pack_lateral(flags, now_a, now_b, prev_a, prev_b, mat_a, mat_b, table_ref, out_a, out_b):
    table = table_ref[...]
    upper_half = lax.broadcasted_iota(jnp.int32, (8, 128), 0) >= 4
    right1 = flags[RIGHT1] == 1
    for slot, (now, prev, mat, out) in enumerate(((now_a, prev_a, mat_a, out_a), (now_b, prev_b, mat_b, out_b))):
        keep = upper_half == (right1 if slot == 0 else jnp.logical_not(right1))

        def layer(k, carry, now=now, prev=prev, mat=mat, out=out, keep=keep):
            for i in range(T):
                lanes = slice(128 * i, 128 * i + 128)
                out[k, i, 0:8, :] = now[k, :, lanes]
                moved = pltpu.roll(stiffness(table, mat[k, :, lanes]), 4, 0)
                out[k, i, 8:16, :] = jnp.where(keep, prev[k, :, lanes], moved)
            return carry

        lax.fori_loop(0, Z, layer, 0)


def advance_alone(
    ints, amplitudes, now_ref, prev_ref, mat_ref, table_ref, lat_a, lat_b, now_out, stiff_out, one_out, out_a, out_b,
    now, prev, one, two,
):
    table = table_ref[...]
    masks = lane_masks()
    right1 = ints[RIGHT1] == 1
    zeros = jnp.zeros((T, ROWS, 128), jnp.float32)
    for k in (0, 1, Z + 2, Z + 3):
        now[k] = zeros
        one[k] = zeros

    def fill(k, carry):
        for i in range(T):
            lanes = slice(128 * i, 128 * i + 128)
            now[k + 2, i, CORE : CORE + X, :] = now_ref[k, :, lanes]
            prev[k, i, CORE : CORE + X, :] = prev_ref[k, :, lanes]
            now_out[k, i, CORE : CORE + X, :] = now_ref[k, :, lanes]
            for t in range(X // 8):
                stiff_out[k, i, CORE + 8 * t : CORE + 8 * t + 8, :] = stiffness(
                    table, mat_ref[k, 8 * t : 8 * t + 8, lanes]
                )
            for half, row in ((0, CORE + X), (1, CORE - 8)):
                wanted = right1 if half == 0 else jnp.logical_not(right1)
                got = jnp.where(wanted, lat_a[k, i], lat_b[k, i])
                now[k + 2, i, row : row + 8, :] = got[0:8]
                now_out[k, i, row : row + 8, :] = got[0:8]
                prev[k, i, row : row + 8, :] = got[8:16]
                stiff_out[k, i, row : row + 8, :] = pltpu.roll(got[8:16], 4, 0)
        return carry

    lax.fori_loop(0, Z, fill, 0)

    def first(k, carry):
        for row in range(CORE - 8, CORE + X + 8, 8):
            rows = pl.ds(row, 8)
            for i, (c, lap) in enumerate(full_terms(now, k + 2, row, masks)):
                one[k + 2, i, rows, :] = 2.0 * c - prev[k, i, rows, :] + stiff_out[k, i, rows, :] * lap
        return carry

    lax.fori_loop(0, Z, first, 0)
    strike(one, ints, amplitudes[0], Z, CORE - 8, CORE + X + 8)

    def second(n, carry):
        k = jnp.where(n < 2, n, n + 4)
        for row in range(CORE, CORE + X, 8):
            rows = pl.ds(row, 8)
            for i, (c, lap) in enumerate(full_terms(one, k + 2, row, masks)):
                two[k + 2, i, rows, :] = 2.0 * c - now[k + 2, i, rows, :] + stiff_out[k, i, rows, :] * lap
        return carry

    lax.fori_loop(0, 4, second, 0)
    strike(two, ints, amplitudes[1], Z, CORE, CORE + X)

    def keep(k, carry):
        one_out[k] = one[k + 2]
        return carry

    lax.fori_loop(0, Z, keep, 0)

    sub = lax.broadcasted_iota(jnp.int32, (8, 128), 0)
    left, right = slice(CORE - 8, CORE), slice(CORE + X, CORE + X + 8)

    def message(z, out):
        for k in range(2):
            for i in range(T):
                out[k, i, 0:X, :] = one[z + k + 2, i, CORE : CORE + X, :]
                out[2 + k, i, 0:X, :] = two[z + k + 2, i, CORE : CORE + X, :]
                out[k, i, X : X + 8, :] = jnp.where(sub >= 4, now[z + k + 2, i, left, :], now[z + k + 2, i, right, :])
                ones = jnp.where(sub >= 4, one[z + k + 2, i, left, :], one[z + k + 2, i, right, :])
                stiff = jnp.where(sub >= 4, stiff_out[z + k, i, left, :], stiff_out[z + k, i, right, :])
                outer = (sub < 2) | (sub >= 6)
                out[2 + k, i, X : X + 8, :] = jnp.where(outer, ones, pltpu.roll(stiff, 4, 0))

    up1 = ints[UP1] == 1

    @pl.when(up1)
    def _():
        message(Z - 2, out_a)
        message(0, out_b)

    @pl.when(jnp.logical_not(up1))
    def _():
        message(0, out_a)
        message(Z - 2, out_b)


def clamp_for_bumps(p):
    return jnp.minimum(jnp.maximum(p, -7.4), 7.4)


def finish(
    ints, amplitudes, weights, now, stiff, one_in, early_a, early_b, late_a, late_b, pressure, partial,
    one, two, delta, halo_stiff, halo_two,
):
    masks = lane_masks()
    up1 = ints[UP1] == 1
    core = slice(CORE, CORE + X)
    left, right = slice(CORE - 8, CORE), slice(CORE + X, CORE + X + 8)

    def copy(k, carry):
        one[k + 2] = one_in[k]
        return carry

    lax.fori_loop(0, Z, copy, 0)

    for high in (False, True):
        use_a = up1 if high else jnp.logical_not(up1)
        base = 2 if high else 0
        edge = Z - 2 if high else 0

        def rows_of(k, i, t, early_a=early_a, early_b=early_b, use_a=use_a):
            rows = slice(8 * t, 8 * t + 8)
            return jnp.where(use_a, early_a[k, i, rows, :], early_b[k, i, rows, :])

        def late_of(k, i, t, use_a=use_a):
            rows = slice(8 * t, 8 * t + 8)
            return jnp.where(use_a, late_a[k, i, rows, :], late_b[k, i, rows, :])

        near, far = (0, 1) if high else (1, 0)
        n_in, n_next = (Z - 1, Z - 2) if high else (0, 1)
        for i in range(T):
            for t in range(-1, X // 8 + 1):
                row = CORE + 8 * t
                rows = slice(row, row + 8)
                inside = 0 <= t < X // 8
                if inside:
                    zero_h = [rows_of(k, i, t) for k in range(2)]
                    st_h = [rows_of(2 + k, i, t) for k in range(2)]
                    one_h = [late_of(k, i, t) for k in range(2)]
                    for k in range(2):
                        halo_two[base + k, i, 8 * t : 8 * t + 8, :] = late_of(2 + k, i, t)
                else:
                    zero_h = [late_of(k, i, X // 8) for k in range(2)]
                    one_h = [late_of(2 + k, i, X // 8) for k in range(2)]
                    st_h = [pltpu.roll(v, 4, 0) for v in one_h]
                one[n_in + 2, i, rows, :] += stiff[n_in, i, rows, :] * (16.0 * zero_h[near] - zero_h[far])
                one[n_next + 2, i, rows, :] -= stiff[n_next, i, rows, :] * zero_h[near]
                d_near = st_h[near] * (16.0 * now[n_in, i, rows, :] - now[n_next, i, rows, :])
                d_far = -st_h[far] * now[n_in, i, rows, :]
                zi = Z + 2 if high else 0
                one[zi + near, i, rows, :] = one_h[near] + d_near
                one[zi + far, i, rows, :] = one_h[far] + d_far
                delta[base + near, i, rows, :] = d_near
                delta[base + far, i, rows, :] = d_far
                if inside:
                    halo_stiff[base + near, i, 8 * t : 8 * t + 8, :] = st_h[near]
                    halo_stiff[base + far, i, 8 * t : 8 * t + 8, :] = st_h[far]

    def second(k, carry):
        for row in range(CORE - 8, CORE + X + 8, 8):
            rows = pl.ds(row, 8)
            for i, (c, lap) in enumerate(full_terms(one, k + 2, row, masks)):
                two[k + 2, i, rows, :] = 2.0 * c - now[k, i, rows, :] + stiff[k, i, rows, :] * lap
        return carry

    lax.fori_loop(0, Z, second, 0)
    strike(two, ints, amplitudes[1], Z, CORE - 8, CORE + X + 8)

    for high in (False, True):
        base = 2 if high else 0
        zi = Z + 2 if high else 0
        near, far = (0, 1) if high else (1, 0)
        n_in, n_next = (Z + 1, Z) if high else (2, 3)

        def tile(t, carry, base=base, zi=zi, near=near, far=far, n_in=n_in, n_next=n_next):
            row = pl.multiple_of(CORE + 8 * t, 8)
            rows, own = pl.ds(row, 8), pl.ds(pl.multiple_of(8 * t, 8), 8)
            terms = {k: plane_terms(delta, base + k, row, masks) for k in range(2)}
            for i in range(T):
                for k in range(2):
                    c, near_sum, far_sum = terms[k][i]
                    near_sum = near_sum + terms[1 - k][i][0]
                    if k == near:
                        near_sum = near_sum + one[n_in, i, rows, :]
                        far_sum = far_sum + one[n_next, i, rows, :]
                    else:
                        far_sum = far_sum + one[n_in, i, rows, :]
                    lap = 16.0 * near_sum - far_sum - 90.0 * c
                    two[zi + k, i, rows, :] = (
                        halo_two[base + k, i, own, :] + 2.0 * c + halo_stiff[base + k, i, own, :] * lap
                    )
            return carry

        lax.fori_loop(0, X // 8, tile, 0)

    def third(k, carry):
        for row in range(CORE, CORE + X, 8):
            rows = pl.ds(row, 8)
            for i, (c, lap) in enumerate(full_terms(two, k + 2, row, masks)):
                one[k + 2, i, rows, :] = 2.0 * c - one[k + 2, i, rows, :] + stiff[k, i, rows, :] * lap
        return carry

    lax.fori_loop(0, Z, third, 0)
    strike(one, ints, amplitudes[2], Z, CORE, CORE + X)

    group = lax.broadcasted_iota(jnp.int32, (8, 128), 1) // 32
    step = 6.0 / (BUMPS - 1)
    half_rate = step / (0.8 * 0.8)
    half = BUMPS // 2

    def render(t, carry):
        rows = pl.ds(pl.multiple_of(CORE + 8 * t, 8), 8)
        own = pl.ds(pl.multiple_of(8 * t, 8), 8)
        for i in range(T):
            colour = [jnp.zeros((8, 128), jnp.float32) for _ in range(3)]
            through = jnp.ones((8, 128), jnp.float32)
            depth = jnp.zeros((8, 128), jnp.float32)
            for k in range(Z):
                p = one[k + 2, i, rows, :]
                pressure[k, own, 128 * i : 128 * i + 128] = p
                p = clamp_for_bumps(p)
                gauss = jnp.exp(p * p * (-1.0 / 0.64))
                rise = jnp.exp(p * half_rate)
                fall = jnp.exp(p * -half_rate)
                up, down = rise * rise, fall * fall
                above, below = gauss * rise, gauss * fall
                value = []
                for n in range(4):
                    a = weights[n, BUMPS - 1] * up + weights[n, BUMPS - 2]
                    b = weights[n, 0] * down + weights[n, 1]
                    for j in range(2, half):
                        a = a * up + weights[n, BUMPS - 1 - j]
                        b = b * down + weights[n, j]
                    value.append(a * above + b * below)
                sigma = value[3]
                stay = jnp.exp(-sigma)
                weight = through * (1.0 - stay)
                through = through * stay
                depth = depth + sigma
                colour = [colour[n] + weight * value[n] for n in range(3)]
            parts = colour + [depth]
            for q in range(4):
                packed = None
                for n in range(4):
                    shift = (32 * (n - q)) % 128
                    moved = parts[n] if shift == 0 else pltpu.roll(parts[n], shift, 1)
                    packed = moved if packed is None else jnp.where(group == n, moved, packed)
                partial[4 * i + q, own, :] = packed
        return carry

    lax.fori_loop(0, X // 8, render, 0)


def composite(parts, image):
    group = lax.broadcasted_iota(jnp.int32, (8, 128), 1) // 32

    def tile(t, carry):
        rows = pl.ds(pl.multiple_of(8 * t, 8), 8)
        before = jnp.zeros((8, 128), jnp.float32)
        total = jnp.zeros((8, 128), jnp.float32)
        for d in range(parts.shape[0]):
            v = parts[d, rows, :]
            total = total + jnp.exp(-before) * v
            depth = v
            for n in range(3):
                depth = jnp.where(group == n, pltpu.roll(v, 32 * (n + 1), 1), depth)
            before = before + depth
        total = jnp.where(group == 3, 1.0 - jnp.exp(-before), total)
        for n in range(4):
            moved = total if n == 0 else pltpu.roll(total, 128 - 32 * n, 1)
            image[n, rows, :] = moved[:, 0:32]
        return carry

    lax.fori_loop(0, X // 8, tile, 0)


def wavelet(level):
    shifted = 0.3 * (level.astype(jnp.float32) - 10.0)
    return 4.0 * (1.0 - 2.0 * shifted * shifted) * jnp.exp(-shifted * shifted)


def swaps(n_lat, n_dep, kind):
    out = []
    for lat in range(n_lat):
        for dep in range(n_dep):
            other_lat, other_dep = lat, dep
            if kind in ("d1", "d2"):
                up = ((lat % 2 == 0) == (dep % 2 == 0)) == (kind == "d1")
                other_dep = dep + 1 if up else dep - 1
            else:
                right = (lat % 2 == 0) == (kind == "l1")
                other_lat = lat + 1 if right else lat - 1
            if 0 <= other_lat < n_lat and 0 <= other_dep < n_dep:
                out.append((lat * n_dep + dep, other_lat * n_dep + other_dep))
    return out


def on_device(n_lat, n_dep, pressure_prev, pressure_now, materials, courant_table, tf_weights, source_cell, start_step):
    f32 = jnp.float32
    lat, dep = lax.axis_index("lat"), lax.axis_index("dep")
    up1 = ((lat % 2 == 0) == (dep % 2 == 0)).astype(jnp.int32)
    right1 = (lat % 2 == 0).astype(jnp.int32)
    ints = jnp.stack([up1, right1, source_cell[0] - dep * Z, source_cell[1] - lat * X, source_cell[2]])
    amplitudes = wavelet(start_step[0] + jnp.arange(3))
    table = jnp.broadcast_to(jnp.pad(courant_table * courant_table * (1.0 / 12.0), (0, 112))[None], (8, 128))
    centres = [(-3.0 + 6.0 * j / (BUMPS - 1)) / 0.8 for j in range(BUMPS)]
    scale = jnp.asarray([math.exp(-c * c) for c in centres], f32)
    rows = jnp.asarray([1.0, 1.0, 1.0, 1.5 / (Z * n_dep)], f32)
    weights = tf_weights * scale[None] * rows[:, None]

    def swap(v, kind):
        return lax.ppermute(v, ("lat", "dep"), swaps(n_lat, n_dep, kind))

    def shape(*dims):
        return jax.ShapeDtypeStruct(dims, f32)

    params = pltpu.CompilerParams(vmem_limit_bytes=48 * 1024 * 1024)

    def layers(slot):
        place = (lambda g, f: (3 * f[UP1], 0, 0)) if slot == 0 else (lambda g, f: (3 - 3 * f[UP1], 0, 0))
        return pl.BlockSpec((2, X, 512), place)

    def edge(slot):
        last = X // 8 - 1
        place = (lambda g, f: (0, last * f[RIGHT1], 0)) if slot == 0 else (lambda g, f: (0, last - last * f[RIGHT1], 0))
        return pl.BlockSpec((Z, 8, 512), place)

    def whole(*dims):
        return pl.BlockSpec(dims, lambda g, f: (0,) * len(dims))

    early = pl.pallas_call(
        pack_depth,
        grid_spec=pltpu.PrefetchScalarGridSpec(
            num_scalar_prefetch=1,
            grid=(1,),
            in_specs=[layers(0), layers(1), layers(0), layers(1), whole(8, 128)],
            out_specs=[whole(4, T, X, 128)] * 2,
        ),
        out_shape=[shape(4, T, X, 128)] * 2,
        compiler_params=params,
        name="pack_depth",
    )(ints, pressure_now, pressure_now, materials, materials, table)
    side = pl.pallas_call(
        pack_lateral,
        grid_spec=pltpu.PrefetchScalarGridSpec(
            num_scalar_prefetch=1,
            grid=(1,),
            in_specs=[edge(0), edge(1)] * 3 + [whole(8, 128)],
            out_specs=[whole(Z, T, 16, 128)] * 2,
        ),
        out_shape=[shape(Z, T, 16, 128)] * 2,
        compiler_params=params,
        name="pack_lateral",
    )(ints, pressure_now, pressure_now, pressure_prev, pressure_prev, materials, materials, table)
    early_a = swap(early[0], "d1")
    side_a = swap(side[0], "l1")
    side_b = swap(side[1], "l2")
    early_b = swap(early[1], "d2")

    padded = pltpu.VMEM((Z + 4, T, ROWS, 128), f32)
    now, stiff, one, late_1, late_2 = pl.pallas_call(
        advance_alone,
        in_specs=[SMEM, SMEM] + [VMEM] * 6,
        out_specs=[VMEM] * 5,
        out_shape=[shape(Z, T, ROWS, 128)] * 3 + [shape(4, T, X + 8, 128)] * 2,
        scratch_shapes=[padded, pltpu.VMEM((Z, T, ROWS, 128), f32), padded, padded],
        compiler_params=params,
        name="advance_alone",
    )(ints, amplitudes, pressure_now, pressure_prev, materials, table, side_a, side_b)
    late_a = swap(late_1, "d1")
    late_b = swap(late_2, "d2")

    pressure, partial = pl.pallas_call(
        finish,
        in_specs=[SMEM, SMEM, SMEM] + [VMEM] * 7,
        out_specs=[VMEM] * 2,
        out_shape=[shape(Z, X, 512), shape(n_dep, X, 128)],
        scratch_shapes=[
            padded,
            padded,
            pltpu.VMEM((4, T, ROWS, 128), f32),
            pltpu.VMEM((4, T, X, 128), f32),
            pltpu.VMEM((4, T, X, 128), f32),
        ],
        compiler_params=params,
        name="finish",
    )(ints, amplitudes, weights, now, stiff, one, early_a, early_b, late_a, late_b)
    parts = lax.all_to_all(partial, "dep", 0, 0, tiled=True)
    image = pl.pallas_call(
        composite,
        in_specs=[VMEM],
        out_specs=VMEM,
        out_shape=shape(4, X, 512 // n_dep),
        compiler_params=params,
        name="composite",
    )(parts)
    return pressure, image


def solution(mesh):
    block = P("dep", "lat", None)
    return jax.shard_map(
        functools.partial(on_device, mesh.shape["lat"], mesh.shape["dep"]),
        mesh=mesh,
        in_specs=(block, block, block, P(), P(), P(), P()),
        out_specs=(block, P(None, "lat", "dep")),
        check_vma=False,
    )
```

```python
import functools
import math

import jax
import jax.numpy as jnp
from jax import lax
from jax.experimental import pallas as pl
from jax.experimental.pallas import tpu as pltpu
from jax.sharding import PartitionSpec as P

BUMPS = 8
Z, X, T = 8, 64, 4
ROWS = X + 32
CORE = 16
VMEM = pl.BlockSpec(memory_space=pltpu.VMEM)
SMEM = pl.BlockSpec(memory_space=pltpu.SMEM)
HBM = pl.BlockSpec(memory_space=pltpu.HBM)


def lane_masks():
    lane = lax.broadcasted_iota(jnp.int32, (8, 128), 1)
    return lane < 1, lane < 2, lane >= 127, lane >= 126


def columns_sum(c, masks):
    zero = jnp.zeros((8, 128), jnp.float32)
    low1, low2, high1, high2 = masks
    a1 = [pltpu.roll(v, 1, 1) for v in c]
    a2 = [pltpu.roll(v, 2, 1) for v in c]
    b1 = [pltpu.roll(v, 127, 1) for v in c]
    b2 = [pltpu.roll(v, 126, 1) for v in c]
    out = []
    for i in range(T):
        first, last = i == 0, i == T - 1
        near = jnp.where(low1, zero if first else a1[i - 1], a1[i]) + jnp.where(
            high1, zero if last else b1[i + 1], b1[i]
        )
        far = jnp.where(low2, zero if first else a2[i - 1], a2[i]) + jnp.where(
            high2, zero if last else b2[i + 1], b2[i]
        )
        out.append((near, far))
    return out


def plane_terms(ref, k, row, masks):
    c = [ref[k, i, pl.ds(row, 8), :] for i in range(T)]
    sums = columns_sum(c, masks)
    out = []
    for i in range(T):
        near = sums[i][0] + (ref[k, i, pl.ds(row - 1, 8), :] + ref[k, i, pl.ds(row + 1, 8), :])
        far = sums[i][1] + (ref[k, i, pl.ds(row - 2, 8), :] + ref[k, i, pl.ds(row + 2, 8), :])
        out.append((c[i], near, far))
    return out


def full_terms(ref, k, row, masks):
    out = []
    for i, (c, near, far) in enumerate(plane_terms(ref, k, row, masks)):
        rows = pl.ds(row, 8)
        near = near + (ref[k - 1, i, rows, :] + ref[k + 1, i, rows, :])
        far = far + (ref[k - 2, i, rows, :] + ref[k + 2, i, rows, :])
        out.append((c, 16.0 * near - far - 90.0 * c))
    return out


def strike(ref, outer, place, amplitude, layers, rows_low, rows_high):
    z, x, y = place
    row = x + CORE
    here = (z >= 0) & (z < layers) & (row >= rows_low) & (row < rows_high)

    @pl.when(here)
    def _():
        tile, lane = y // 128, y % 128
        old = ref[z + outer, tile, pl.ds(row, 1), :]
        ids = lax.broadcasted_iota(jnp.int32, (1, 128), 1)
        ref[z + outer, tile, pl.ds(row, 1), :] = old + jnp.where(ids == lane, amplitude, 0.0)


def stiffness(table, materials):
    return jnp.take_along_axis(table, materials, axis=1, mode="promise_in_bounds")


def ways():
    lat, dep = lax.axis_index("lat"), lax.axis_index("dep")
    return (lat + dep + 1) % 2, (lat + 1) % 2


def source_place(cell):
    return cell[0] - lax.axis_index("dep") * Z, cell[1] - lax.axis_index("lat") * X, cell[2]


def wavelet(start, step):
    level = jnp.full((1, 128), start[0] + step, jnp.int32).astype(jnp.float32)
    shifted = 0.3 * (level - 10.0)
    return 4.0 * (1.0 - 2.0 * shifted * shifted) * jnp.exp(-shifted * shifted)


def stiffness_table(courant):
    lane = lax.broadcasted_iota(jnp.int32, (8, 128), 1)
    table = jnp.zeros((8, 128), jnp.float32)
    for m in range(16):
        table = jnp.where(lane == m, courant[m], table)
    return table * table * (1.0 / 12.0)


def pack(
    courant, now, prev, mat, early_1, early_2, side_1, side_2,
    now_z, mat_z, now_x, prev_x, mat_x, depth_sems, side_sems,
):
    up1, right1 = ways()
    waits = []
    for slot in range(2):
        first = 6 * up1 if slot == 0 else 6 - 6 * up1
        for n, (src, dst) in enumerate(((now, now_z), (mat, mat_z))):
            waits.append(
                pltpu.make_async_copy(src.at[pl.ds(first, 2)], dst.at[slot], depth_sems.at[2 * slot + n])
            )
    for slot in range(2):
        row = pl.multiple_of((X - 8) * right1 if slot == 0 else (X - 8) - (X - 8) * right1, 8)
        for n, (src, dst) in enumerate(((now, now_x), (prev, prev_x), (mat, mat_x))):
            waits.append(
                pltpu.make_async_copy(src.at[:, pl.ds(row, 8), :], dst.at[slot], side_sems.at[3 * slot + n])
            )
    for copy in waits:
        copy.start()
    table = stiffness_table(courant)
    upper_half = (lax.broadcasted_iota(jnp.int32, (8, 128), 0) >= 4).astype(jnp.int32)
    for slot, out in enumerate((early_1, early_2)):
        waits[2 * slot].wait()
        waits[2 * slot + 1].wait()
        for k in range(2):
            for i in range(T):
                lanes = slice(128 * i, 128 * i + 128)
                out[k, i] = now_z[slot, k, :, lanes]
                for t in range(X // 8):
                    rows = slice(8 * t, 8 * t + 8)
                    out[2 + k, i, rows, :] = stiffness(table, mat_z[slot, k, rows, lanes])
    for slot, out in enumerate((side_1, side_2)):
        for n in range(3):
            waits[4 + 3 * slot + n].wait()
        keep = upper_half == (right1 if slot == 0 else 1 - right1)

        def layer(k, carry, slot=slot, out=out, keep=keep):
            for i in range(T):
                lanes = slice(128 * i, 128 * i + 128)
                out[k, i, 0:8, :] = now_x[slot, k, :, lanes]
                moved = pltpu.roll(stiffness(table, mat_x[slot, k, :, lanes]), 4, 0)
                out[k, i, 8:16, :] = jnp.where(keep, prev_x[slot, k, :, lanes], moved)
            return carry

        lax.fori_loop(0, Z, layer, 0)


def advance_alone(
    cell, start, courant, now_ref, prev_ref, mat_ref, lat_a, lat_b, now_out, stiff_out, one_out, two_out,
    now, prev, one,
):
    table = stiffness_table(courant)
    masks = lane_masks()
    place = source_place(cell)
    right1 = ways()[1] == 1
    zeros = jnp.zeros((T, ROWS, 128), jnp.float32)
    for k in (0, 1, Z + 2, Z + 3):
        now[k] = zeros
        one[k] = zeros

    def fill(k, carry):
        for i in range(T):
            lanes = slice(128 * i, 128 * i + 128)
            now[k + 2, i, CORE : CORE + X, :] = now_ref[k, :, lanes]
            prev[k, i, CORE : CORE + X, :] = prev_ref[k, :, lanes]
            now_out[k, i, CORE : CORE + X, :] = now_ref[k, :, lanes]
            for t in range(X // 8):
                stiff_out[k, i, CORE + 8 * t : CORE + 8 * t + 8, :] = stiffness(
                    table, mat_ref[k, 8 * t : 8 * t + 8, lanes]
                )
            for half, row in ((0, CORE + X), (1, CORE - 8)):
                wanted = right1 if half == 0 else jnp.logical_not(right1)
                got = jnp.where(wanted, lat_a[k, i], lat_b[k, i])
                now[k + 2, i, row : row + 8, :] = got[0:8]
                now_out[k, i, row : row + 8, :] = got[0:8]
                prev[k, i, row : row + 8, :] = got[8:16]
                stiff_out[k, i, row : row + 8, :] = pltpu.roll(got[8:16], 4, 0)
        return carry

    lax.fori_loop(0, Z, fill, 0)

    def first(k, carry):
        for row in range(CORE - 8, CORE + X + 8, 8):
            rows = pl.ds(row, 8)
            for i, (c, lap) in enumerate(full_terms(now, k + 2, row, masks)):
                one[k + 2, i, rows, :] = 2.0 * c - prev[k, i, rows, :] + stiff_out[k, i, rows, :] * lap
        return carry

    lax.fori_loop(0, Z, first, 0)
    strike(one, 2, place, wavelet(start, 0), Z, CORE - 8, CORE + X + 8)

    def second(n, carry):
        k = jnp.where(n < 2, n, n + 4)
        for row in range(CORE, CORE + X, 8):
            rows = pl.ds(row, 8)
            for i, (c, lap) in enumerate(full_terms(one, k + 2, row, masks)):
                two_out[n, i, rows, :] = 2.0 * c - now[k + 2, i, rows, :] + stiff_out[k, i, rows, :] * lap
        return carry

    lax.fori_loop(0, 4, second, 0)
    z = place[0]
    inner = (z >= 2) & (z < Z - 2)
    strike(two_out, 0, (jnp.where(inner, -1, jnp.where(z < 2, z, z - 4)),) + place[1:], wavelet(start, 1), 4, CORE, CORE + X)

    def keep(k, carry):
        one_out[k] = one[k + 2]
        return carry

    lax.fori_loop(0, Z, keep, 0)


def pack_late(now, stiff, one, two, early_a, early_b, out_a, out_b):
    sub = lax.broadcasted_iota(jnp.int32, (8, 128), 0)
    left, right = slice(CORE - 8, CORE), slice(CORE + X, CORE + X + 8)
    up1 = ways()[0]
    for slot, out in ((0, out_a), (1, out_b)):
        high = up1 if slot == 0 else 1 - up1
        for k in range(2):
            z = (Z - 2) * high + k
            for i in range(T):
                out[k, i, 0:X, :] = one[z, i, CORE : CORE + X, :]
                out[2 + k, i, 0:X, :] = two[2 * high + k, i, CORE : CORE + X, :]
                out[k, i, X : X + 8, :] = jnp.where(sub >= 4, now[z, i, left, :], now[z, i, right, :])
                ones = jnp.where(sub >= 4, one[z, i, left, :], one[z, i, right, :])
                side = jnp.where(sub >= 4, stiff[z, i, left, :], stiff[z, i, right, :])
                outer = (sub < 2) | (sub >= 6)
                out[2 + k, i, X : X + 8, :] = jnp.where(outer, ones, pltpu.roll(side, 4, 0))


def clamp_for_bumps(p):
    return jnp.minimum(jnp.maximum(p, -7.4), 7.4)


def finish(
    n_dep, cell, start, transfer, now, stiff, one_in, early_a, early_b, late_a, late_b, pressure, partial,
    one, two, delta, halo_stiff, halo_two, weights,
):
    masks = lane_masks()
    place = source_place(cell)
    up1 = ways()[0] == 1
    for n in range(4):
        for j in range(BUMPS):
            centre = (-3.0 + 6.0 * j / (BUMPS - 1)) / 0.8
            weights[n, j] = transfer[n, j] * (math.exp(-centre * centre) * (1.5 / (Z * n_dep) if n == 3 else 1.0))
    core = slice(CORE, CORE + X)
    left, right = slice(CORE - 8, CORE), slice(CORE + X, CORE + X + 8)

    def copy(k, carry):
        one[k + 2] = one_in[k]
        return carry

    lax.fori_loop(0, Z, copy, 0)

    for high in (False, True):
        use_a = up1 if high else jnp.logical_not(up1)
        base = 2 if high else 0
        edge = Z - 2 if high else 0

        def rows_of(k, i, t, early_a=early_a, early_b=early_b, use_a=use_a):
            rows = slice(8 * t, 8 * t + 8)
            return jnp.where(use_a, early_a[k, i, rows, :], early_b[k, i, rows, :])

        def late_of(k, i, t, use_a=use_a):
            rows = slice(8 * t, 8 * t + 8)
            return jnp.where(use_a, late_a[k, i, rows, :], late_b[k, i, rows, :])

        near, far = (0, 1) if high else (1, 0)
        n_in, n_next = (Z - 1, Z - 2) if high else (0, 1)
        for i in range(T):
            for t in range(-1, X // 8 + 1):
                row = CORE + 8 * t
                rows = slice(row, row + 8)
                inside = 0 <= t < X // 8
                if inside:
                    zero_h = [rows_of(k, i, t) for k in range(2)]
                    st_h = [rows_of(2 + k, i, t) for k in range(2)]
                    one_h = [late_of(k, i, t) for k in range(2)]
                    for k in range(2):
                        halo_two[base + k, i, 8 * t : 8 * t + 8, :] = late_of(2 + k, i, t)
                else:
                    zero_h = [late_of(k, i, X // 8) for k in range(2)]
                    one_h = [late_of(2 + k, i, X // 8) for k in range(2)]
                    st_h = [pltpu.roll(v, 4, 0) for v in one_h]
                one[n_in + 2, i, rows, :] += stiff[n_in, i, rows, :] * (16.0 * zero_h[near] - zero_h[far])
                one[n_next + 2, i, rows, :] -= stiff[n_next, i, rows, :] * zero_h[near]
                d_near = st_h[near] * (16.0 * now[n_in, i, rows, :] - now[n_next, i, rows, :])
                d_far = -st_h[far] * now[n_in, i, rows, :]
                zi = Z + 2 if high else 0
                one[zi + near, i, rows, :] = one_h[near] + d_near
                one[zi + far, i, rows, :] = one_h[far] + d_far
                delta[base + near, i, rows, :] = d_near
                delta[base + far, i, rows, :] = d_far
                if inside:
                    halo_stiff[base + near, i, 8 * t : 8 * t + 8, :] = st_h[near]
                    halo_stiff[base + far, i, 8 * t : 8 * t + 8, :] = st_h[far]

    def second(k, carry):
        for row in range(CORE - 8, CORE + X + 8, 8):
            rows = pl.ds(row, 8)
            for i, (c, lap) in enumerate(full_terms(one, k + 2, row, masks)):
                two[k + 2, i, rows, :] = 2.0 * c - now[k, i, rows, :] + stiff[k, i, rows, :] * lap
        return carry

    lax.fori_loop(0, Z, second, 0)
    strike(two, 2, place, wavelet(start, 1), Z, CORE - 8, CORE + X + 8)

    for high in (False, True):
        base = 2 if high else 0
        zi = Z + 2 if high else 0
        near, far = (0, 1) if high else (1, 0)
        n_in, n_next = (Z + 1, Z) if high else (2, 3)

        def tile(t, carry, base=base, zi=zi, near=near, far=far, n_in=n_in, n_next=n_next):
            row = pl.multiple_of(CORE + 8 * t, 8)
            rows, own = pl.ds(row, 8), pl.ds(pl.multiple_of(8 * t, 8), 8)
            terms = {k: plane_terms(delta, base + k, row, masks) for k in range(2)}
            for i in range(T):
                for k in range(2):
                    c, near_sum, far_sum = terms[k][i]
                    near_sum = near_sum + terms[1 - k][i][0]
                    if k == near:
                        near_sum = near_sum + one[n_in, i, rows, :]
                        far_sum = far_sum + one[n_next, i, rows, :]
                    else:
                        far_sum = far_sum + one[n_in, i, rows, :]
                    lap = 16.0 * near_sum - far_sum - 90.0 * c
                    two[zi + k, i, rows, :] = (
                        halo_two[base + k, i, own, :] + 2.0 * c + halo_stiff[base + k, i, own, :] * lap
                    )
            return carry

        lax.fori_loop(0, X // 8, tile, 0)

    def third(k, carry):
        for row in range(CORE, CORE + X, 8):
            rows = pl.ds(row, 8)
            for i, (c, lap) in enumerate(full_terms(two, k + 2, row, masks)):
                one[k + 2, i, rows, :] = 2.0 * c - one[k + 2, i, rows, :] + stiff[k, i, rows, :] * lap
        return carry

    lax.fori_loop(0, Z, third, 0)
    strike(one, 2, place, wavelet(start, 2), Z, CORE, CORE + X)

    group = lax.broadcasted_iota(jnp.int32, (8, 128), 1) // 32
    step = 6.0 / (BUMPS - 1)
    half_rate = step / (0.8 * 0.8)
    half = BUMPS // 2

    def render(t, carry):
        rows = pl.ds(pl.multiple_of(CORE + 8 * t, 8), 8)
        own = pl.ds(pl.multiple_of(8 * t, 8), 8)
        for i in range(T):
            colour = [jnp.zeros((8, 128), jnp.float32) for _ in range(3)]
            through = jnp.ones((8, 128), jnp.float32)
            depth = jnp.zeros((8, 128), jnp.float32)
            for k in range(Z):
                p = one[k + 2, i, rows, :]
                pressure[k, own, 128 * i : 128 * i + 128] = p
                p = clamp_for_bumps(p)
                gauss = jnp.exp(p * p * (-1.0 / 0.64))
                rise = jnp.exp(p * half_rate)
                fall = jnp.exp(p * -half_rate)
                up, down = rise * rise, fall * fall
                above, below = gauss * rise, gauss * fall
                value = []
                for n in range(4):
                    a = weights[n, BUMPS - 1] * up + weights[n, BUMPS - 2]
                    b = weights[n, 0] * down + weights[n, 1]
                    for j in range(2, half):
                        a = a * up + weights[n, BUMPS - 1 - j]
                        b = b * down + weights[n, j]
                    value.append(a * above + b * below)
                sigma = value[3]
                stay = jnp.exp(-sigma)
                weight = through * (1.0 - stay)
                through = through * stay
                depth = depth + sigma
                colour = [colour[n] + weight * value[n] for n in range(3)]
            parts = colour + [depth]
            for q in range(4):
                packed = None
                for n in range(4):
                    shift = (32 * (n - q)) % 128
                    moved = parts[n] if shift == 0 else pltpu.roll(parts[n], shift, 1)
                    packed = moved if packed is None else jnp.where(group == n, moved, packed)
                partial[4 * i + q, own, :] = packed
        return carry

    lax.fori_loop(0, X // 8, render, 0)


def composite(parts, image):
    group = lax.broadcasted_iota(jnp.int32, (X, 128), 1) // 32
    before = jnp.zeros((X, 128), jnp.float32)
    total = jnp.zeros((X, 128), jnp.float32)
    for d in range(parts.shape[0]):
        v = parts[d]
        total = total + jnp.exp(-before) * v
        depth = v
        for n in range(3):
            depth = jnp.where(group == n, pltpu.roll(v, 32 * (n + 1), 1), depth)
        before = before + depth
    image[...] = jnp.where(group == 3, 1.0 - jnp.exp(-before), total).T


def swaps(n_lat, n_dep, kind):
    out = []
    for lat in range(n_lat):
        for dep in range(n_dep):
            other_lat, other_dep = lat, dep
            if kind in ("d1", "d2"):
                up = ((lat % 2 == 0) == (dep % 2 == 0)) == (kind == "d1")
                other_dep = dep + 1 if up else dep - 1
            else:
                right = (lat % 2 == 0) == (kind == "l1")
                other_lat = lat + 1 if right else lat - 1
            if 0 <= other_lat < n_lat and 0 <= other_dep < n_dep:
                out.append((lat * n_dep + dep, other_lat * n_dep + other_dep))
    return out


def on_device(n_lat, n_dep, pressure_prev, pressure_now, materials, courant_table, tf_weights, source_cell, start_step):
    f32 = jnp.float32

    def swap(v, kind):
        return lax.ppermute(v, ("lat", "dep"), swaps(n_lat, n_dep, kind))

    def shape(*dims):
        return jax.ShapeDtypeStruct(dims, f32)

    params = pltpu.CompilerParams(vmem_limit_bytes=24 * 1024 * 1024)
    i32 = jnp.int32
    early_1, early_2, side_1, side_2 = pl.pallas_call(
        pack,
        in_specs=[SMEM] + [HBM] * 3,
        out_specs=[VMEM] * 4,
        out_shape=[shape(4, T, X, 128)] * 2 + [shape(Z, T, 16, 128)] * 2,
        scratch_shapes=[
            pltpu.VMEM((2, 2, X, 512), f32),
            pltpu.VMEM((2, 2, X, 512), i32),
            pltpu.VMEM((2, Z, 8, 512), f32),
            pltpu.VMEM((2, Z, 8, 512), f32),
            pltpu.VMEM((2, Z, 8, 512), i32),
            pltpu.SemaphoreType.DMA((4,)),
            pltpu.SemaphoreType.DMA((6,)),
        ],
        compiler_params=params,
        name="pack",
    )(courant_table, pressure_now, pressure_prev, materials)
    early_a = swap(early_1, "d1")
    side_a = swap(side_1, "l1")
    side_b = swap(side_2, "l2")
    early_b = swap(early_2, "d2")

    padded = pltpu.VMEM((Z + 4, T, ROWS, 128), f32)
    now, stiff, one, two = pl.pallas_call(
        advance_alone,
        in_specs=[SMEM] * 3 + [VMEM] * 5,
        out_specs=[VMEM] * 4,
        out_shape=[shape(Z, T, ROWS, 128)] * 3 + [shape(4, T, ROWS, 128)],
        scratch_shapes=[padded, pltpu.VMEM((Z, T, ROWS, 128), f32), padded],
        compiler_params=params,
        name="advance_alone",
    )(source_cell, start_step, courant_table, pressure_now, pressure_prev, materials, side_a, side_b)
    late_1, late_2 = pl.pallas_call(
        pack_late,
        in_specs=[VMEM] * 4 + [pl.BlockSpec(memory_space=pl.ANY)] * 2,
        out_specs=[VMEM] * 2,
        out_shape=[shape(4, T, X + 8, 128)] * 2,
        compiler_params=params,
        name="pack_late",
    )(now, stiff, one, two, early_a, early_b)
    late_a = swap(late_1, "d1")
    late_b = swap(late_2, "d2")

    pressure, partial = pl.pallas_call(
        functools.partial(finish, n_dep),
        in_specs=[SMEM] * 3 + [VMEM] * 7,
        out_specs=[VMEM] * 2,
        out_shape=[shape(Z, X, 512), shape(n_dep, X, 128)],
        scratch_shapes=[
            padded,
            padded,
            pltpu.VMEM((4, T, ROWS, 128), f32),
            pltpu.VMEM((4, T, X, 128), f32),
            pltpu.VMEM((4, T, X, 128), f32),
            pltpu.SMEM((4, BUMPS), f32),
        ],
        compiler_params=params,
        name="finish",
    )(source_cell, start_step, tf_weights, now, stiff, one, early_a, early_b, late_a, late_b)
    parts = lax.all_to_all(partial, "dep", 0, 0, tiled=True)
    image = pl.pallas_call(
        composite,
        in_specs=[VMEM],
        out_specs=VMEM,
        out_shape=shape(128, X),
        compiler_params=params,
        name="composite",
    )(parts)
    return pressure, jnp.swapaxes(image.reshape(4, 512 // n_dep, X), 1, 2)


def solution(mesh):
    block = P("dep", "lat", None)
    return jax.shard_map(
        functools.partial(on_device, mesh.shape["lat"], mesh.shape["dep"]),
        mesh=mesh,
        in_specs=(block, block, block, P(), P(), P(), P()),
        out_specs=(block, P(None, "lat", "dep")),
        check_vma=False,
    )
```

```python
import functools
import math

import jax
import jax.numpy as jnp
from jax import lax
from jax.experimental import pallas as pl
from jax.experimental.pallas import tpu as pltpu
from jax.sharding import PartitionSpec as P

BUMPS = 8
Z, X, T = 8, 64, 4
ROWS = X + 32
CORE = 16
INNER_LIMIT = 44 * 1024 * 1024
VMEM = pl.BlockSpec(memory_space=pltpu.VMEM)
SMEM = pl.BlockSpec(memory_space=pltpu.SMEM)
HBM = pl.BlockSpec(memory_space=pltpu.HBM)


def lane_masks():
    lane = lax.broadcasted_iota(jnp.int32, (8, 128), 1)
    return lane < 1, lane < 2, lane >= 127, lane >= 126


def columns_sum(c, masks):
    zero = jnp.zeros((8, 128), jnp.float32)
    low1, low2, high1, high2 = masks
    a1 = [pltpu.roll(v, 1, 1) for v in c]
    a2 = [pltpu.roll(v, 2, 1) for v in c]
    b1 = [pltpu.roll(v, 127, 1) for v in c]
    b2 = [pltpu.roll(v, 126, 1) for v in c]
    out = []
    for i in range(T):
        first, last = i == 0, i == T - 1
        near = jnp.where(low1, zero if first else a1[i - 1], a1[i]) + jnp.where(
            high1, zero if last else b1[i + 1], b1[i]
        )
        far = jnp.where(low2, zero if first else a2[i - 1], a2[i]) + jnp.where(
            high2, zero if last else b2[i + 1], b2[i]
        )
        out.append((near, far))
    return out


def plane_terms(ref, k, row, masks):
    c = [ref[k, i, pl.ds(row, 8), :] for i in range(T)]
    sums = columns_sum(c, masks)
    out = []
    for i in range(T):
        near = sums[i][0] + (ref[k, i, pl.ds(row - 1, 8), :] + ref[k, i, pl.ds(row + 1, 8), :])
        far = sums[i][1] + (ref[k, i, pl.ds(row - 2, 8), :] + ref[k, i, pl.ds(row + 2, 8), :])
        out.append((c[i], near, far))
    return out


def full_terms(ref, k, row, masks):
    out = []
    for i, (c, near, far) in enumerate(plane_terms(ref, k, row, masks)):
        rows = pl.ds(row, 8)
        near = near + (ref[k - 1, i, rows, :] + ref[k + 1, i, rows, :])
        far = far + (ref[k - 2, i, rows, :] + ref[k + 2, i, rows, :])
        out.append((c, 16.0 * near - far - 90.0 * c))
    return out


def strike(ref, outer, place, amplitude, layers, rows_low, rows_high):
    z, x, y = place
    row = x + CORE
    here = (z >= 0) & (z < layers) & (row >= rows_low) & (row < rows_high)

    @pl.when(here)
    def _():
        tile, lane = y // 128, y % 128
        old = ref[z + outer, tile, pl.ds(row, 1), :]
        ids = lax.broadcasted_iota(jnp.int32, (1, 128), 1)
        ref[z + outer, tile, pl.ds(row, 1), :] = old + jnp.where(ids == lane, amplitude, 0.0)


def stiffness(table, materials):
    return jnp.take_along_axis(table, materials, axis=1, mode="promise_in_bounds")


def ways():
    lat, dep = lax.axis_index("lat"), lax.axis_index("dep")
    return (lat + dep + 1) % 2, (lat + 1) % 2


def source_place(cell):
    return cell[0] - lax.axis_index("dep") * Z, cell[1] - lax.axis_index("lat") * X, cell[2]


def wavelet(start, step):
    level = jnp.full((1, 128), start[0] + step, jnp.int32).astype(jnp.float32)
    shifted = 0.3 * (level - 10.0)
    return 4.0 * (1.0 - 2.0 * shifted * shifted) * jnp.exp(-shifted * shifted)


def stiffness_table(courant):
    lane = lax.broadcasted_iota(jnp.int32, (8, 128), 1)
    table = jnp.zeros((8, 128), jnp.float32)
    for m in range(16):
        table = jnp.where(lane == m, courant[m], table)
    return table * table * (1.0 / 12.0)


def pack(
    courant, now, prev, mat, early_1, early_2, side_1, side_2,
    now_z, mat_z, now_x, prev_x, mat_x, depth_sems, side_sems,
):
    up1, right1 = ways()
    waits = []
    for slot in range(2):
        first = 6 * up1 if slot == 0 else 6 - 6 * up1
        for n, (src, dst) in enumerate(((now, now_z), (mat, mat_z))):
            waits.append(
                pltpu.make_async_copy(src.at[pl.ds(first, 2)], dst.at[slot], depth_sems.at[2 * slot + n])
            )
    for slot in range(2):
        row = pl.multiple_of((X - 8) * right1 if slot == 0 else (X - 8) - (X - 8) * right1, 8)
        for n, (src, dst) in enumerate(((now, now_x), (prev, prev_x), (mat, mat_x))):
            waits.append(
                pltpu.make_async_copy(src.at[:, pl.ds(row, 8), :], dst.at[slot], side_sems.at[3 * slot + n])
            )
    for copy in waits:
        copy.start()
    table = stiffness_table(courant)
    upper_half = (lax.broadcasted_iota(jnp.int32, (8, 128), 0) >= 4).astype(jnp.int32)
    for slot, out in enumerate((early_1, early_2)):
        waits[2 * slot].wait()
        waits[2 * slot + 1].wait()
        for k in range(2):
            for i in range(T):
                lanes = slice(128 * i, 128 * i + 128)
                out[k, i] = now_z[slot, k, :, lanes]
                for t in range(X // 8):
                    rows = slice(8 * t, 8 * t + 8)
                    out[2 + k, i, rows, :] = stiffness(table, mat_z[slot, k, rows, lanes])
    for slot, out in enumerate((side_1, side_2)):
        for n in range(3):
            waits[4 + 3 * slot + n].wait()
        keep = upper_half == (right1 if slot == 0 else 1 - right1)

        def layer(k, carry, slot=slot, out=out, keep=keep):
            for i in range(T):
                lanes = slice(128 * i, 128 * i + 128)
                out[k, i, 0:8, :] = now_x[slot, k, :, lanes]
                moved = pltpu.roll(stiffness(table, mat_x[slot, k, :, lanes]), 4, 0)
                out[k, i, 8:16, :] = jnp.where(keep, prev_x[slot, k, :, lanes], moved)
            return carry

        lax.fori_loop(0, Z, layer, 0)


INNER = range(CORE + 8, CORE + X - 8, 8)
OUTER = (CORE - 8, CORE, CORE + X - 8, CORE + X)


def advance_inner(courant, now_in, prev_in, mat_in, now_out, stiff_out, one_out, prev_out, now, prev, mat, sems):
    copies = [
        pltpu.make_async_copy(src, dst, sems.at[n]) for n, (src, dst) in enumerate(((now_in, now), (mat_in, mat), (prev_in, prev)))
    ]
    for copy in copies:
        copy.start()
    table = stiffness_table(courant)
    masks = lane_masks()
    zeros = jnp.zeros((T, X, 128), jnp.float32)
    for k in (0, 1, Z + 2, Z + 3):
        now_out[k] = zeros
    copies[0].wait()

    def fill(k, carry):
        for i in range(T):
            now_out[k + 2, i] = now[k, :, 128 * i : 128 * i + 128]
        return carry

    lax.fori_loop(0, Z, fill, 0)
    copies[1].wait()
    copies[2].wait()

    def first(k, carry):
        for i in range(T):
            lanes = slice(128 * i, 128 * i + 128)
            prev_out[k, i, 0:8, :] = prev[k, 0:8, lanes]
            prev_out[k, i, 8:16, :] = prev[k, X - 8 : X, lanes]
            for t in range(X // 8):
                rows = slice(8 * t, 8 * t + 8)
                stiff_out[k, i, rows, :] = stiffness(table, mat[k, rows, lanes])
        for row in range(8, X - 8, 8):
            rows = slice(row, row + 8)
            for i, (c, lap) in enumerate(full_terms(now_out, k + 2, row, masks)):
                before = prev[k, rows, 128 * i : 128 * i + 128]
                one_out[k, i, rows, :] = 2.0 * c - before + stiff_out[k, i, rows, :] * lap
        return carry

    lax.fori_loop(0, Z, first, 0)


def advance_outer(
    cell, start, now_in, stiff_in, one_in, prev_in, lat_a, lat_b, now_side, stiff_side, one_out, two_out,
    now, prev_side, one,
):
    masks = lane_masks()
    place = source_place(cell)
    right1 = ways()[1] == 1
    core = slice(CORE, CORE + X)
    zeros = jnp.zeros((T, ROWS, 128), jnp.float32)
    for k in (0, 1, Z + 2, Z + 3):
        now[k] = zeros
        one[k] = zeros

    def fill(k, carry):
        for i in range(T):
            now[k + 2, i, core, :] = now_in[k + 2, i]
            one[k + 2, i, CORE + 8 : CORE + X - 8, :] = one_in[k, i, 8 : X - 8, :]
            for left in (False, True):
                wanted = jnp.logical_not(right1) if left else right1
                got = jnp.where(wanted, lat_a[k, i], lat_b[k, i])
                row = CORE - 8 if left else CORE + X
                half = slice(0, 8) if left else slice(8, 16)
                now[k + 2, i, row : row + 8, :] = got[0:8]
                now_side[k, i, half, :] = got[0:8]
                prev_side[k, i, half, :] = got[8:16]
                stiff_side[k, i, half, :] = pltpu.roll(got[8:16], 4, 0)
        return carry

    lax.fori_loop(0, Z, fill, 0)

    def first(k, carry):
        for row in OUTER:
            rows = slice(row, row + 8)
            for i, (c, lap) in enumerate(full_terms(now, k + 2, row, masks)):
                if row < CORE or row == CORE + X:
                    half = slice(0, 8) if row < CORE else slice(8, 16)
                    before, stiff = prev_side[k, i, half, :], stiff_side[k, i, half, :]
                else:
                    half = slice(0, 8) if row == CORE else slice(8, 16)
                    before, stiff = prev_in[k, i, half, :], stiff_in[k, i, row - CORE : row - CORE + 8, :]
                one[k + 2, i, rows, :] = 2.0 * c - before + stiff * lap
        return carry

    lax.fori_loop(0, Z, first, 0)
    strike(one, 2, place, wavelet(start, 0), Z, CORE - 8, CORE + X + 8)

    def second(n, carry):
        k = jnp.where(n < 2, n, n + 4)
        for row in range(CORE, CORE + X, 8):
            rows = slice(row, row + 8)
            for i, (c, lap) in enumerate(full_terms(one, k + 2, row, masks)):
                stiff = stiff_in[k, i, row - CORE : row - CORE + 8, :]
                two_out[n, i, rows, :] = 2.0 * c - now[k + 2, i, rows, :] + stiff * lap
        return carry

    lax.fori_loop(0, 4, second, 0)
    z = place[0]
    inner = (z >= 2) & (z < Z - 2)
    strike(two_out, 0, (jnp.where(inner, -1, jnp.where(z < 2, z, z - 4)),) + place[1:], wavelet(start, 1), 4, CORE, CORE + X)

    def keep(k, carry):
        one_out[k] = one[k + 2]
        return carry

    lax.fori_loop(0, Z, keep, 0)


def pack_late(now_side, stiff_side, one, two, early_a, early_b, out_a, out_b):
    sub = lax.broadcasted_iota(jnp.int32, (8, 128), 0)
    left, right = slice(CORE - 8, CORE), slice(CORE + X, CORE + X + 8)
    up1 = ways()[0]
    for slot, out in ((0, out_a), (1, out_b)):
        high = up1 if slot == 0 else 1 - up1
        for k in range(2):
            z = (Z - 2) * high + k
            for i in range(T):
                out[k, i, 0:X, :] = one[z, i, CORE : CORE + X, :]
                out[2 + k, i, 0:X, :] = two[2 * high + k, i, CORE : CORE + X, :]
                out[k, i, X : X + 8, :] = jnp.where(sub >= 4, now_side[z, i, 0:8, :], now_side[z, i, 8:16, :])
                ones = jnp.where(sub >= 4, one[z, i, left, :], one[z, i, right, :])
                side = jnp.where(sub >= 4, stiff_side[z, i, 0:8, :], stiff_side[z, i, 8:16, :])
                outer = (sub < 2) | (sub >= 6)
                out[2 + k, i, X : X + 8, :] = jnp.where(outer, ones, pltpu.roll(side, 4, 0))


def clamp_for_bumps(p):
    return jnp.minimum(jnp.maximum(p, -7.4), 7.4)


SIDES = ((False, 0, 1, 0, 0, 1, 0), (True, 2, 0, 1, Z - 1, Z - 2, Z + 2))


def halo_step(delta, one, halo_stiff, base, near, n_in, n_next, row, masks):
    rows, own = pl.ds(row, 8), pl.ds(row - CORE, 8)
    terms = {k: plane_terms(delta, base + k, row, masks) for k in range(2)}
    out = {}
    for i in range(T):
        for k in range(2):
            c, near_sum, far_sum = terms[k][i]
            near_sum = near_sum + terms[1 - k][i][0]
            if k == near:
                near_sum = near_sum + one[n_in + 2, i, rows, :]
                far_sum = far_sum + one[n_next + 2, i, rows, :]
            else:
                far_sum = far_sum + one[n_in + 2, i, rows, :]
            lap = 16.0 * near_sum - far_sum - 90.0 * c
            out[k, i] = 2.0 * c + halo_stiff[base + k, i, own, :] * lap
    return out


def couple(now, stiff, one_in, early_a, early_b, one, two, delta, halo_stiff, halo_two):
    masks = lane_masks()
    up1 = ways()[0] == 1

    def copy(k, carry):
        one[k + 2] = one_in[k]
        return carry

    lax.fori_loop(0, Z, copy, 0)
    for high, base, near, far, n_in, n_next, zi in SIDES:
        use_a = up1 if high else jnp.logical_not(up1)

        def tile(t, carry, use_a=use_a, base=base, near=near, far=far, n_in=n_in, n_next=n_next, zi=zi):
            own, rows = pl.ds(pl.multiple_of(8 * t, 8), 8), pl.ds(pl.multiple_of(CORE + 8 * t, 8), 8)
            for i in range(T):
                zero_h = [jnp.where(use_a, early_a[k, i, own, :], early_b[k, i, own, :]) for k in range(2)]
                st_h = [jnp.where(use_a, early_a[2 + k, i, own, :], early_b[2 + k, i, own, :]) for k in range(2)]
                one[n_in + 2, i, rows, :] += stiff[n_in, i, own, :] * (16.0 * zero_h[near] - zero_h[far])
                one[n_next + 2, i, rows, :] -= stiff[n_next, i, own, :] * zero_h[near]
                d_near = st_h[near] * (16.0 * now[n_in + 2, i, own, :] - now[n_next + 2, i, own, :])
                d_far = -st_h[far] * now[n_in + 2, i, own, :]
                for place, d, st in ((near, d_near, st_h[near]), (far, d_far, st_h[far])):
                    one[zi + place, i, rows, :] = d
                    delta[base + place, i, rows, :] = d
                    halo_stiff[base + place, i, own, :] = st
            return carry

        lax.fori_loop(0, X // 8, tile, 0)

    def second(k, carry):
        for row in INNER:
            rows = slice(row, row + 8)
            for i, (c, lap) in enumerate(full_terms(one, k + 2, row, masks)):
                own = slice(row - CORE, row - CORE + 8)
                two[k + 2, i, rows, :] = 2.0 * c - now[k + 2, i, own, :] + stiff[k, i, own, :] * lap
        return carry

    lax.fori_loop(0, Z, second, 0)
    for high, base, near, far, n_in, n_next, zi in SIDES:

        def beyond(t, carry, base=base, near=near, n_in=n_in, n_next=n_next):
            row = pl.multiple_of(CORE + 8 * t, 8)
            for (k, i), v in halo_step(delta, one, halo_stiff, base, near, n_in, n_next, row, masks).items():
                halo_two[base + k, i, pl.ds(pl.multiple_of(8 * t, 8), 8), :] = v
            return carry

        lax.fori_loop(1, X // 8 - 1, beyond, 0)


def finish(
    n_dep, cell, start, transfer, now, stiff, now_side, stiff_side, one_in, two_in, delta_in, halo_stiff, halo_two,
    late_a, late_b, pressure, partial, one, two, delta, weights,
):
    masks = lane_masks()
    place = source_place(cell)
    up1 = ways()[0] == 1
    for n in range(4):
        for j in range(BUMPS):
            centre = (-3.0 + 6.0 * j / (BUMPS - 1)) / 0.8
            weights[n, j] = transfer[n, j] * (math.exp(-centre * centre) * (1.5 / (Z * n_dep) if n == 3 else 1.0))

    def copy(k, carry):
        one[k] = one_in[k]
        two[k, :, CORE + 8 : CORE + X - 8, :] = two_in[k, :, CORE + 8 : CORE + X - 8, :]
        return carry

    lax.fori_loop(0, Z + 4, copy, 0)
    for k in range(4):
        delta[k] = delta_in[k]

    for high, base, near, far, n_in, n_next, zi in SIDES:
        use_a = up1 if high else jnp.logical_not(up1)

        def late_of(k, i, row, use_a=use_a):
            rows = pl.ds(row - CORE, 8)
            return jnp.where(use_a, late_a[k, i, rows, :], late_b[k, i, rows, :])

        for row in (CORE - 8, CORE + X):
            rows, half = slice(row, row + 8), slice(0, 8) if row < CORE else slice(8, 16)
            for i in range(T):
                zero_h = [late_of(k, i, CORE + X) for k in range(2)]
                one_h = [late_of(2 + k, i, CORE + X) for k in range(2)]
                st_h = [pltpu.roll(v, 4, 0) for v in one_h]
                one[n_in + 2, i, rows, :] += stiff_side[n_in, i, half, :] * (16.0 * zero_h[near] - zero_h[far])
                one[n_next + 2, i, rows, :] -= stiff_side[n_next, i, half, :] * zero_h[near]
                d_near = st_h[near] * (16.0 * now_side[n_in, i, half, :] - now_side[n_next, i, half, :])
                d_far = -st_h[far] * now_side[n_in, i, half, :]
                for at, d in ((near, d_near), (far, d_far)):
                    one[zi + at, i, rows, :] = one_h[at] + d
                    delta[base + at, i, rows, :] = d

        def inner(t, carry, base=base, near=near, far=far, n_in=n_in, n_next=n_next, zi=zi, late_of=late_of):
            row = pl.multiple_of(CORE + 8 * t, 8)
            rows, own = pl.ds(row, 8), pl.ds(pl.multiple_of(8 * t, 8), 8)
            for i in range(T):
                one_h = [late_of(k, i, row) for k in range(2)]
                for k in range(2):
                    one[zi + k, i, rows, :] += one_h[k]
                    two[zi + k, i, rows, :] = late_of(2 + k, i, row) + halo_two[base + k, i, own, :]
                two[n_in + 2, i, rows, :] += stiff[n_in, i, own, :] * (16.0 * one_h[near] - one_h[far])
                two[n_next + 2, i, rows, :] -= stiff[n_next, i, own, :] * one_h[near]
            return carry

        lax.fori_loop(0, X // 8, inner, 0)
        for row in (CORE, CORE + X - 8):
            for (k, i), v in halo_step(delta, one, halo_stiff, base, near, n_in, n_next, row, masks).items():
                two[zi + k, i, row : row + 8, :] = late_of(2 + k, i, row) + v

    def second(k, carry):
        for row in OUTER:
            rows = slice(row, row + 8)
            for i, (c, lap) in enumerate(full_terms(one, k + 2, row, masks)):
                if CORE <= row < CORE + X:
                    own = slice(row - CORE, row - CORE + 8)
                    before, st = now[k + 2, i, own, :], stiff[k, i, own, :]
                else:
                    half = slice(0, 8) if row < CORE else slice(8, 16)
                    before, st = now_side[k, i, half, :], stiff_side[k, i, half, :]
                two[k + 2, i, rows, :] = 2.0 * c - before + st * lap
        return carry

    lax.fori_loop(0, Z, second, 0)
    strike(two, 2, place, wavelet(start, 1), Z, CORE - 8, CORE + X + 8)

    def third(k, carry):
        for row in range(CORE, CORE + X, 8):
            rows = pl.ds(row, 8)
            for i, (c, lap) in enumerate(full_terms(two, k + 2, row, masks)):
                own = pl.ds(row - CORE, 8)
                one[k + 2, i, rows, :] = 2.0 * c - one[k + 2, i, rows, :] + stiff[k, i, own, :] * lap
        return carry

    lax.fori_loop(0, Z, third, 0)
    strike(one, 2, place, wavelet(start, 2), Z, CORE, CORE + X)

    group = lax.broadcasted_iota(jnp.int32, (8, 128), 1) // 32
    step = 6.0 / (BUMPS - 1)
    half_rate = step / (0.8 * 0.8)
    half = BUMPS // 2

    def render(t, carry):
        rows = pl.ds(pl.multiple_of(CORE + 8 * t, 8), 8)
        own = pl.ds(pl.multiple_of(8 * t, 8), 8)
        for i in range(T):
            colour = [jnp.zeros((8, 128), jnp.float32) for _ in range(3)]
            through = jnp.ones((8, 128), jnp.float32)
            depth = jnp.zeros((8, 128), jnp.float32)
            for k in range(Z):
                p = one[k + 2, i, rows, :]
                pressure[k, own, 128 * i : 128 * i + 128] = p
                p = clamp_for_bumps(p)
                gauss = jnp.exp(p * p * (-1.0 / 0.64))
                rise = jnp.exp(p * half_rate)
                fall = jnp.exp(p * -half_rate)
                up, down = rise * rise, fall * fall
                above, below = gauss * rise, gauss * fall
                value = []
                for n in range(4):
                    a = weights[n, BUMPS - 1] * up + weights[n, BUMPS - 2]
                    b = weights[n, 0] * down + weights[n, 1]
                    for j in range(2, half):
                        a = a * up + weights[n, BUMPS - 1 - j]
                        b = b * down + weights[n, j]
                    value.append(a * above + b * below)
                sigma = value[3]
                stay = jnp.exp(-sigma)
                weight = through * (1.0 - stay)
                through = through * stay
                depth = depth + sigma
                colour = [colour[n] + weight * value[n] for n in range(3)]
            parts = colour + [depth]
            for q in range(4):
                packed = None
                for n in range(4):
                    shift = (32 * (n - q)) % 128
                    moved = parts[n] if shift == 0 else pltpu.roll(parts[n], shift, 1)
                    packed = moved if packed is None else jnp.where(group == n, moved, packed)
                partial[4 * i + q, own, :] = packed
        return carry

    lax.fori_loop(0, X // 8, render, 0)


def composite(parts, image):
    group = lax.broadcasted_iota(jnp.int32, (X, 128), 1) // 32
    before = jnp.zeros((X, 128), jnp.float32)
    total = jnp.zeros((X, 128), jnp.float32)
    for d in range(parts.shape[0]):
        v = parts[d]
        total = total + jnp.exp(-before) * v
        depth = v
        for n in range(3):
            depth = jnp.where(group == n, pltpu.roll(v, 32 * (n + 1), 1), depth)
        before = before + depth
    image[...] = jnp.where(group == 3, 1.0 - jnp.exp(-before), total).T


def swaps(n_lat, n_dep, kind):
    out = []
    for lat in range(n_lat):
        for dep in range(n_dep):
            other_lat, other_dep = lat, dep
            if kind in ("d1", "d2"):
                up = ((lat % 2 == 0) == (dep % 2 == 0)) == (kind == "d1")
                other_dep = dep + 1 if up else dep - 1
            else:
                right = (lat % 2 == 0) == (kind == "l1")
                other_lat = lat + 1 if right else lat - 1
            if 0 <= other_lat < n_lat and 0 <= other_dep < n_dep:
                out.append((lat * n_dep + dep, other_lat * n_dep + other_dep))
    return out


def on_device(n_lat, n_dep, pressure_prev, pressure_now, materials, courant_table, tf_weights, source_cell, start_step):
    f32 = jnp.float32

    def swap(v, kind):
        return lax.ppermute(v, ("lat", "dep"), swaps(n_lat, n_dep, kind))

    def busy(microseconds):
        return pl.CostEstimate(
            flops=int(microseconds * 1.0e9), bytes_accessed=int(microseconds * 3.0e6), transcendentals=0
        )

    def shape(*dims):
        return jax.ShapeDtypeStruct(dims, f32)

    params = pltpu.CompilerParams(vmem_limit_bytes=24 * 1024 * 1024)
    i32 = jnp.int32
    early_1, early_2, side_1, side_2 = pl.pallas_call(
        pack,
        in_specs=[SMEM] + [HBM] * 3,
        out_specs=[VMEM] * 4,
        out_shape=[shape(4, T, X, 128)] * 2 + [shape(Z, T, 16, 128)] * 2,
        scratch_shapes=[
            pltpu.VMEM((2, 2, X, 512), f32),
            pltpu.VMEM((2, 2, X, 512), i32),
            pltpu.VMEM((2, Z, 8, 512), f32),
            pltpu.VMEM((2, Z, 8, 512), f32),
            pltpu.VMEM((2, Z, 8, 512), i32),
            pltpu.SemaphoreType.DMA((4,)),
            pltpu.SemaphoreType.DMA((6,)),
        ],
        compiler_params=pltpu.CompilerParams(vmem_limit_bytes=62 * 1024 * 1024),
        name="pack",
    )(courant_table, pressure_now, pressure_prev, materials)
    early_a = swap(early_1, "d1")
    side_a = swap(side_1, "l1")
    side_b = swap(side_2, "l2")
    early_b = swap(early_2, "d2")

    padded = (Z + 4, T, ROWS, 128)
    block, side = (Z, T, X, 128), (Z, T, 16, 128)
    now, stiff, one, prev = pl.pallas_call(
        advance_inner,
        in_specs=[SMEM] + [HBM] * 3,
        out_specs=[VMEM] * 4,
        out_shape=[shape(Z + 4, T, X, 128), shape(*block), shape(*block), shape(*side)],
        scratch_shapes=[pltpu.VMEM((Z, X, 512), d) for d in (f32, f32, i32)] + [pltpu.SemaphoreType.DMA((3,))],
        compiler_params=pltpu.CompilerParams(vmem_limit_bytes=INNER_LIMIT),
        cost_estimate=busy(3.0),
        name="advance_inner",
    )(courant_table, pressure_now, pressure_prev, materials)
    now_side, stiff_side, one, two = pl.pallas_call(
        advance_outer,
        in_specs=[SMEM] * 2 + [VMEM] * 6,
        out_specs=[VMEM] * 4,
        out_shape=[shape(*side)] * 2 + [shape(Z, T, ROWS, 128), shape(4, T, ROWS, 128)],
        scratch_shapes=[pltpu.VMEM(padded, f32), pltpu.VMEM(side, f32), pltpu.VMEM(padded, f32)],
        compiler_params=params,
        cost_estimate=busy(5.0),
        name="advance_outer",
    )(source_cell, start_step, now, stiff, one, prev, side_a, side_b)
    late_1, late_2 = pl.pallas_call(
        pack_late,
        in_specs=[VMEM] * 4 + [pl.BlockSpec(memory_space=pl.ANY)] * 2,
        out_specs=[VMEM] * 2,
        out_shape=[shape(4, T, X + 8, 128)] * 2,
        compiler_params=params,
        name="pack_late",
    )(now_side, stiff_side, one, two, early_a, early_b)
    late_a = swap(late_1, "d1")
    late_b = swap(late_2, "d2")
    one, two, delta, halo_stiff, halo_two = pl.pallas_call(
        couple,
        in_specs=[VMEM] * 5,
        out_specs=[VMEM] * 5,
        out_shape=[shape(*padded)] * 2 + [shape(4, T, ROWS, 128)] + [shape(4, T, X, 128)] * 2,
        compiler_params=params,
        cost_estimate=busy(4.0),
        name="couple",
    )(now, stiff, one, early_a, early_b)
    pressure, partial = pl.pallas_call(
        functools.partial(finish, n_dep),
        in_specs=[SMEM] * 3 + [VMEM] * 11,
        out_specs=[VMEM] * 2,
        out_shape=[shape(Z, X, 512), shape(n_dep, X, 128)],
        scratch_shapes=[
            pltpu.VMEM(padded, f32),
            pltpu.VMEM(padded, f32),
            pltpu.VMEM((4, T, ROWS, 128), f32),
            pltpu.SMEM((4, BUMPS), f32),
        ],
        compiler_params=params,
        name="finish",
    )(
        source_cell, start_step, tf_weights, now, stiff, now_side, stiff_side, one, two, delta, halo_stiff, halo_two,
        late_a, late_b,
    )
    parts = lax.all_to_all(partial, "dep", 0, 0, tiled=True)
    image = pl.pallas_call(
        composite,
        in_specs=[VMEM],
        out_specs=VMEM,
        out_shape=shape(128, X),
        compiler_params=params,
        name="composite",
    )(parts)
    return pressure, jnp.swapaxes(image.reshape(4, 512 // n_dep, X), 1, 2)


def solution(mesh):
    block = P("dep", "lat", None)
    return jax.shard_map(
        functools.partial(on_device, mesh.shape["lat"], mesh.shape["dep"]),
        mesh=mesh,
        in_specs=(block, block, block, P(), P(), P(), P()),
        out_specs=(block, P(None, "lat", "dep")),
        check_vma=False,
    )
```

```python
import functools
import math

import jax
import jax.numpy as jnp
from jax import lax
from jax.experimental import pallas as pl
from jax.experimental.pallas import tpu as pltpu
from jax.sharding import PartitionSpec as P

BUMPS = 8
Z, X, T = 8, 64, 4
ROWS = X + 32
CORE = 16
VMEM = pl.BlockSpec(memory_space=pltpu.VMEM)
SMEM = pl.BlockSpec(memory_space=pltpu.SMEM)
HBM = pl.BlockSpec(memory_space=pltpu.HBM)


def lane_masks():
    lane = lax.broadcasted_iota(jnp.int32, (8, 128), 1)
    return lane < 1, lane < 2, lane >= 127, lane >= 126


def columns_sum(c, masks):
    zero = jnp.zeros((8, 128), jnp.float32)
    low1, low2, high1, high2 = masks
    a1 = [pltpu.roll(v, 1, 1) for v in c]
    a2 = [pltpu.roll(v, 2, 1) for v in c]
    b1 = [pltpu.roll(v, 127, 1) for v in c]
    b2 = [pltpu.roll(v, 126, 1) for v in c]
    out = []
    for i in range(T):
        first, last = i == 0, i == T - 1
        near = jnp.where(low1, zero if first else a1[i - 1], a1[i]) + jnp.where(
            high1, zero if last else b1[i + 1], b1[i]
        )
        far = jnp.where(low2, zero if first else a2[i - 1], a2[i]) + jnp.where(
            high2, zero if last else b2[i + 1], b2[i]
        )
        out.append((near, far))
    return out


def plane_terms(ref, k, row, masks):
    c = [ref[k, i, pl.ds(row, 8), :] for i in range(T)]
    sums = columns_sum(c, masks)
    out = []
    for i in range(T):
        near = sums[i][0] + (ref[k, i, pl.ds(row - 1, 8), :] + ref[k, i, pl.ds(row + 1, 8), :])
        far = sums[i][1] + (ref[k, i, pl.ds(row - 2, 8), :] + ref[k, i, pl.ds(row + 2, 8), :])
        out.append((c[i], near, far))
    return out


def full_terms(ref, k, row, masks):
    out = []
    for i, (c, near, far) in enumerate(plane_terms(ref, k, row, masks)):
        rows = pl.ds(row, 8)
        near = near + (ref[k - 1, i, rows, :] + ref[k + 1, i, rows, :])
        far = far + (ref[k - 2, i, rows, :] + ref[k + 2, i, rows, :])
        out.append((c, 16.0 * near - far - 90.0 * c))
    return out


def strike(ref, outer, place, amplitude, layers, rows_low, rows_high):
    z, x, y = place
    row = x + CORE
    here = (z >= 0) & (z < layers) & (row >= rows_low) & (row < rows_high)

    @pl.when(here)
    def _():
        tile, lane = y // 128, y % 128
        old = ref[z + outer, tile, pl.ds(row, 1), :]
        ids = lax.broadcasted_iota(jnp.int32, (1, 128), 1)
        ref[z + outer, tile, pl.ds(row, 1), :] = old + jnp.where(ids == lane, amplitude, 0.0)


def stiffness(table, materials):
    return jnp.take_along_axis(table, materials, axis=1, mode="promise_in_bounds")


def ways():
    lat, dep = lax.axis_index("lat"), lax.axis_index("dep")
    return (lat + dep + 1) % 2, (lat + 1) % 2


def source_place(cell):
    return cell[0] - lax.axis_index("dep") * Z, cell[1] - lax.axis_index("lat") * X, cell[2]


def wavelet(start, step):
    level = jnp.full((1, 128), start[0] + step, jnp.int32).astype(jnp.float32)
    shifted = 0.3 * (level - 10.0)
    return 4.0 * (1.0 - 2.0 * shifted * shifted) * jnp.exp(-shifted * shifted)


def stiffness_table(courant):
    lane = lax.broadcasted_iota(jnp.int32, (8, 128), 1)
    table = jnp.zeros((8, 128), jnp.float32)
    for m in range(16):
        table = jnp.where(lane == m, courant[m], table)
    return table * table * (1.0 / 12.0)


def pack(
    courant, now, prev, mat, early_1, early_2, side_1, side_2,
    now_z, mat_z, now_x, prev_x, mat_x, depth_sems, side_sems,
):
    up1, right1 = ways()
    waits = []
    depth_waits, side_waits = [], []
    for slot in range(2):
        row = pl.multiple_of((X - 8) * right1 if slot == 0 else (X - 8) - (X - 8) * right1, 8)
        for n, (src, dst) in enumerate(((now, now_x), (prev, prev_x), (mat, mat_x))):
            side_waits.append(
                pltpu.make_async_copy(src.at[:, pl.ds(row, 8), :], dst.at[slot], side_sems.at[3 * slot + n])
            )
    for slot in range(2):
        first = 6 * up1 if slot == 0 else 6 - 6 * up1
        for n, (src, dst) in enumerate(((now, now_z), (mat, mat_z))):
            depth_waits.append(
                pltpu.make_async_copy(src.at[pl.ds(first, 2)], dst.at[slot], depth_sems.at[2 * slot + n])
            )
    for copy in side_waits + depth_waits:
        copy.start()
    table = stiffness_table(courant)
    upper_half = (lax.broadcasted_iota(jnp.int32, (8, 128), 0) >= 4).astype(jnp.int32)
    for slot, out in enumerate((side_1, side_2)):
        for n in range(3):
            side_waits[3 * slot + n].wait()
        keep = upper_half == (right1 if slot == 0 else 1 - right1)
        for k in range(Z):
            for i in range(T):
                lanes = slice(128 * i, 128 * i + 128)
                out[k, i, 0:8, :] = now_x[slot, k, :, lanes]
                moved = pltpu.roll(stiffness(table, mat_x[slot, k, :, lanes]), 4, 0)
                out[k, i, 8:16, :] = jnp.where(keep, prev_x[slot, k, :, lanes], moved)
    for slot, out in enumerate((early_1, early_2)):
        depth_waits[2 * slot].wait()
        depth_waits[2 * slot + 1].wait()
        for k in range(2):
            for i in range(T):
                lanes = slice(128 * i, 128 * i + 128)
                out[k, i] = now_z[slot, k, :, lanes]
                for t in range(X // 8):
                    rows = slice(8 * t, 8 * t + 8)
                    out[2 + k, i, rows, :] = stiffness(table, mat_z[slot, k, rows, lanes])


INNER = range(CORE + 8, CORE + X - 8, 8)
OUTER = (CORE - 8, CORE, CORE + X - 8, CORE + X)


def advance_inner(courant, now_in, prev_in, mat_in, now_out, stiff_out, one_out, prev_out, now, prev, mat, sems):
    copies = [
        pltpu.make_async_copy(src, dst, sems.at[n]) for n, (src, dst) in enumerate(((now_in, now), (mat_in, mat), (prev_in, prev)))
    ]
    for copy in copies:
        copy.start()
    table = stiffness_table(courant)
    masks = lane_masks()
    zeros = jnp.zeros((T, ROWS, 128), jnp.float32)
    for k in (0, 1, Z + 2, Z + 3):
        now_out[k] = zeros
        one_out[k] = zeros
    copies[0].wait()

    def fill(k, carry):
        for i in range(T):
            now_out[k + 2, i, CORE : CORE + X, :] = now[k, :, 128 * i : 128 * i + 128]
        return carry

    lax.fori_loop(0, Z, fill, 0)
    copies[1].wait()
    copies[2].wait()

    def first(k, carry):
        for i in range(T):
            lanes = slice(128 * i, 128 * i + 128)
            prev_out[k, i, 0:8, :] = prev[k, 0:8, lanes]
            prev_out[k, i, 8:16, :] = prev[k, X - 8 : X, lanes]
            for t in range(X // 8):
                rows = slice(8 * t, 8 * t + 8)
                stiff_out[k, i, rows, :] = stiffness(table, mat[k, rows, lanes])
        for row in INNER:
            own = slice(row - CORE, row - CORE + 8)
            for i, (c, lap) in enumerate(full_terms(now_out, k + 2, row, masks)):
                before = prev[k, own, 128 * i : 128 * i + 128]
                one_out[k + 2, i, row : row + 8, :] = 2.0 * c - before + stiff_out[k, i, own, :] * lap
        return carry

    lax.fori_loop(0, Z, first, 0)


def advance_outer(
    cell, start, now_in, stiff_in, one_in, prev_in, lat_a, lat_b, now, one, now_side, stiff_side, two_out,
    prev_side,
):
    del now_in, one_in
    masks = lane_masks()
    right1 = ways()[1] == 1

    def fill(k, carry):
        for i in range(T):
            for left in (False, True):
                wanted = jnp.logical_not(right1) if left else right1
                got = jnp.where(wanted, lat_a[k, i], lat_b[k, i])
                row = CORE - 8 if left else CORE + X
                half = slice(0, 8) if left else slice(8, 16)
                now[k + 2, i, row : row + 8, :] = got[0:8]
                now_side[k, i, half, :] = got[0:8]
                prev_side[k, i, half, :] = got[8:16]
                stiff_side[k, i, half, :] = pltpu.roll(got[8:16], 4, 0)
        return carry

    lax.fori_loop(0, Z, fill, 0)

    def first(k, carry):
        for row in OUTER:
            rows = slice(row, row + 8)
            for i, (c, lap) in enumerate(full_terms(now, k + 2, row, masks)):
                if row < CORE or row == CORE + X:
                    half = slice(0, 8) if row < CORE else slice(8, 16)
                    before, stiff = prev_side[k, i, half, :], stiff_side[k, i, half, :]
                else:
                    half = slice(0, 8) if row == CORE else slice(8, 16)
                    before, stiff = prev_in[k, i, half, :], stiff_in[k, i, row - CORE : row - CORE + 8, :]
                one[k + 2, i, rows, :] = 2.0 * c - before + stiff * lap
        return carry

    lax.fori_loop(0, Z, first, 0)
    place = source_place(cell)
    strike(one, 2, place, wavelet(start, 0), Z, CORE - 8, CORE + X + 8)

    def second(n, carry):
        k = jnp.where(n < 2, n, n + 4)
        for row in range(CORE, CORE + X, 8):
            rows = slice(row, row + 8)
            for i, (c, lap) in enumerate(full_terms(one, k + 2, row, masks)):
                stiff = stiff_in[k, i, row - CORE : row - CORE + 8, :]
                two_out[n, i, rows, :] = 2.0 * c - now[k + 2, i, rows, :] + stiff * lap
        return carry

    lax.fori_loop(0, 4, second, 0)
    z = place[0]
    inner = (z >= 2) & (z < Z - 2)
    strike(two_out, 0, (jnp.where(inner, -1, jnp.where(z < 2, z, z - 4)),) + place[1:], wavelet(start, 1), 4, CORE, CORE + X)


def pack_late(now_side, stiff_side, one, two, early_a, early_b, out_a, out_b):
    sub = lax.broadcasted_iota(jnp.int32, (8, 128), 0)
    left, right = slice(CORE - 8, CORE), slice(CORE + X, CORE + X + 8)
    up1 = ways()[0]
    for slot, out in ((0, out_a), (1, out_b)):
        high = up1 if slot == 0 else 1 - up1
        for k in range(2):
            z = (Z - 2) * high + k
            for i in range(T):
                out[k, i, 0:X, :] = one[z + 2, i, CORE : CORE + X, :]
                out[2 + k, i, 0:X, :] = two[2 * high + k, i, CORE : CORE + X, :]
                out[k, i, X : X + 8, :] = jnp.where(sub >= 4, now_side[z, i, 0:8, :], now_side[z, i, 8:16, :])
                ones = jnp.where(sub >= 4, one[z + 2, i, left, :], one[z + 2, i, right, :])
                side = jnp.where(sub >= 4, stiff_side[z, i, 0:8, :], stiff_side[z, i, 8:16, :])
                outer = (sub < 2) | (sub >= 6)
                out[2 + k, i, X : X + 8, :] = jnp.where(outer, ones, pltpu.roll(side, 4, 0))


def clamp_for_bumps(p):
    return jnp.minimum(jnp.maximum(p, -7.4), 7.4)


SIDES = ((False, 0, 1, 0, 0, 1, 0), (True, 2, 0, 1, Z - 1, Z - 2, Z + 2))


def halo_step(delta, one, halo_stiff, base, near, n_in, n_next, row, masks):
    rows, own = pl.ds(row, 8), pl.ds(row - CORE, 8)
    terms = {k: plane_terms(delta, base + k, row, masks) for k in range(2)}
    out = {}
    for i in range(T):
        for k in range(2):
            c, near_sum, far_sum = terms[k][i]
            near_sum = near_sum + terms[1 - k][i][0]
            if k == near:
                near_sum = near_sum + one[n_in + 2, i, rows, :]
                far_sum = far_sum + one[n_next + 2, i, rows, :]
            else:
                far_sum = far_sum + one[n_in + 2, i, rows, :]
            lap = 16.0 * near_sum - far_sum - 90.0 * c
            out[k, i] = 2.0 * c + halo_stiff[base + k, i, own, :] * lap
    return out


def couple(now, stiff, one_in, early_a, early_b, sent, one, two, delta, halo_stiff, halo_two):
    del one_in, sent
    masks = lane_masks()
    up1 = ways()[0] == 1
    for high, base, near, far, n_in, n_next, zi in SIDES:
        use_a = up1 if high else jnp.logical_not(up1)

        def tile(t, carry, use_a=use_a, base=base, near=near, far=far, n_in=n_in, n_next=n_next, zi=zi):
            own, rows = pl.ds(pl.multiple_of(8 * t, 8), 8), pl.ds(pl.multiple_of(CORE + 8 * t, 8), 8)
            for i in range(T):
                zero_h = [jnp.where(use_a, early_a[k, i, own, :], early_b[k, i, own, :]) for k in range(2)]
                st_h = [jnp.where(use_a, early_a[2 + k, i, own, :], early_b[2 + k, i, own, :]) for k in range(2)]
                one[n_in + 2, i, rows, :] += stiff[n_in, i, own, :] * (16.0 * zero_h[near] - zero_h[far])
                one[n_next + 2, i, rows, :] -= stiff[n_next, i, own, :] * zero_h[near]
                d_near = st_h[near] * (16.0 * now[n_in + 2, i, rows, :] - now[n_next + 2, i, rows, :])
                d_far = -st_h[far] * now[n_in + 2, i, rows, :]
                for place, d, st in ((near, d_near, st_h[near]), (far, d_far, st_h[far])):
                    one[zi + place, i, rows, :] = d
                    delta[base + place, i, rows, :] = d
                    halo_stiff[base + place, i, own, :] = st
            return carry

        lax.fori_loop(0, X // 8, tile, 0)

    def second(k, carry):
        for row in INNER:
            rows = slice(row, row + 8)
            for i, (c, lap) in enumerate(full_terms(one, k + 2, row, masks)):
                own = slice(row - CORE, row - CORE + 8)
                two[k + 2, i, rows, :] = 2.0 * c - now[k + 2, i, rows, :] + stiff[k, i, own, :] * lap
        return carry

    lax.fori_loop(0, Z, second, 0)
    for high, base, near, far, n_in, n_next, zi in SIDES:

        def beyond(t, carry, base=base, near=near, n_in=n_in, n_next=n_next):
            row = pl.multiple_of(CORE + 8 * t, 8)
            for (k, i), v in halo_step(delta, one, halo_stiff, base, near, n_in, n_next, row, masks).items():
                halo_two[base + k, i, pl.ds(pl.multiple_of(8 * t, 8), 8), :] = v
            return carry

        lax.fori_loop(1, X // 8 - 1, beyond, 0)


def finish(
    n_dep, cell, start, transfer, now, stiff, now_side, stiff_side, one_in, two_in, delta_in, halo_stiff, halo_two,
    late_a, late_b, pressure, partial, one, two, delta, weights,
):
    del one_in, two_in, delta_in
    masks = lane_masks()
    up1 = ways()[0] == 1
    for n in range(4):
        for j in range(BUMPS):
            centre = (-3.0 + 6.0 * j / (BUMPS - 1)) / 0.8
            weights[n, j] = transfer[n, j] * (math.exp(-centre * centre) * (1.5 / (Z * n_dep) if n == 3 else 1.0))

    for high, base, near, far, n_in, n_next, zi in SIDES:
        use_a = up1 if high else jnp.logical_not(up1)

        def late_of(k, i, row, use_a=use_a):
            rows = pl.ds(row - CORE, 8)
            return jnp.where(use_a, late_a[k, i, rows, :], late_b[k, i, rows, :])

        for row in (CORE - 8, CORE + X):
            rows, half = slice(row, row + 8), slice(0, 8) if row < CORE else slice(8, 16)
            for i in range(T):
                zero_h = [late_of(k, i, CORE + X) for k in range(2)]
                one_h = [late_of(2 + k, i, CORE + X) for k in range(2)]
                st_h = [pltpu.roll(v, 4, 0) for v in one_h]
                one[n_in + 2, i, rows, :] += stiff_side[n_in, i, half, :] * (16.0 * zero_h[near] - zero_h[far])
                one[n_next + 2, i, rows, :] -= stiff_side[n_next, i, half, :] * zero_h[near]
                d_near = st_h[near] * (16.0 * now_side[n_in, i, half, :] - now_side[n_next, i, half, :])
                d_far = -st_h[far] * now_side[n_in, i, half, :]
                for at, d in ((near, d_near), (far, d_far)):
                    one[zi + at, i, rows, :] = one_h[at] + d
                    delta[base + at, i, rows, :] = d

        def inner(t, carry, base=base, near=near, far=far, n_in=n_in, n_next=n_next, zi=zi, late_of=late_of):
            row = pl.multiple_of(CORE + 8 * t, 8)
            rows, own = pl.ds(row, 8), pl.ds(pl.multiple_of(8 * t, 8), 8)
            for i in range(T):
                one_h = [late_of(k, i, row) for k in range(2)]
                for k in range(2):
                    one[zi + k, i, rows, :] += one_h[k]
                    two[zi + k, i, rows, :] = late_of(2 + k, i, row) + halo_two[base + k, i, own, :]
                two[n_in + 2, i, rows, :] += stiff[n_in, i, own, :] * (16.0 * one_h[near] - one_h[far])
                two[n_next + 2, i, rows, :] -= stiff[n_next, i, own, :] * one_h[near]
            return carry

        lax.fori_loop(0, X // 8, inner, 0)
        for row in (CORE, CORE + X - 8):
            for (k, i), v in halo_step(delta, one, halo_stiff, base, near, n_in, n_next, row, masks).items():
                two[zi + k, i, row : row + 8, :] = late_of(2 + k, i, row) + v

    def second(k, carry):
        for row in OUTER:
            rows = slice(row, row + 8)
            for i, (c, lap) in enumerate(full_terms(one, k + 2, row, masks)):
                if CORE <= row < CORE + X:
                    st = stiff[k, i, row - CORE : row - CORE + 8, :]
                else:
                    st = stiff_side[k, i, 0:8, :] if row < CORE else stiff_side[k, i, 8:16, :]
                two[k + 2, i, rows, :] = 2.0 * c - now[k + 2, i, rows, :] + st * lap
        return carry

    lax.fori_loop(0, Z, second, 0)
    place = source_place(cell)
    strike(two, 2, place, wavelet(start, 1), Z, CORE - 8, CORE + X + 8)

    def third(k, carry):
        for row in range(CORE, CORE + X, 8):
            rows = pl.ds(row, 8)
            for i, (c, lap) in enumerate(full_terms(two, k + 2, row, masks)):
                own = pl.ds(row - CORE, 8)
                one[k + 2, i, rows, :] = 2.0 * c - one[k + 2, i, rows, :] + stiff[k, i, own, :] * lap
        return carry

    lax.fori_loop(0, Z, third, 0)
    strike(one, 2, place, wavelet(start, 2), Z, CORE, CORE + X)

    group = lax.broadcasted_iota(jnp.int32, (8, 128), 1) // 32
    step = 6.0 / (BUMPS - 1)
    half_rate = step / (0.8 * 0.8)
    half = BUMPS // 2

    def render(t, carry):
        rows = pl.ds(pl.multiple_of(CORE + 8 * t, 8), 8)
        own = pl.ds(pl.multiple_of(8 * t, 8), 8)
        for i in range(T):
            colour = [jnp.zeros((8, 128), jnp.float32) for _ in range(3)]
            through = jnp.ones((8, 128), jnp.float32)
            depth = jnp.zeros((8, 128), jnp.float32)
            for k in range(Z):
                p = one[k + 2, i, rows, :]
                pressure[k, own, 128 * i : 128 * i + 128] = p
                p = clamp_for_bumps(p)
                gauss = jnp.exp(p * p * (-1.0 / 0.64))
                rise = jnp.exp(p * half_rate)
                fall = jnp.exp(p * -half_rate)
                up, down = rise * rise, fall * fall
                above, below = gauss * rise, gauss * fall
                value = []
                for n in range(4):
                    a = weights[n, BUMPS - 1] * up + weights[n, BUMPS - 2]
                    b = weights[n, 0] * down + weights[n, 1]
                    for j in range(2, half):
                        a = a * up + weights[n, BUMPS - 1 - j]
                        b = b * down + weights[n, j]
                    value.append(a * above + b * below)
                sigma = value[3]
                stay = jnp.exp(-sigma)
                weight = through * (1.0 - stay)
                through = through * stay
                depth = depth + sigma
                colour = [colour[n] + weight * value[n] for n in range(3)]
            parts = colour + [depth]
            for q in range(4):
                packed = None
                for n in range(4):
                    shift = (32 * (n - q)) % 128
                    moved = parts[n] if shift == 0 else pltpu.roll(parts[n], shift, 1)
                    packed = moved if packed is None else jnp.where(group == n, moved, packed)
                partial[4 * i + q, own, :] = packed
        return carry

    lax.fori_loop(0, X // 8, render, 0)


def composite(parts, image):
    group = lax.broadcasted_iota(jnp.int32, (X, 128), 1) // 32
    before = jnp.zeros((X, 128), jnp.float32)
    total = jnp.zeros((X, 128), jnp.float32)
    for d in range(parts.shape[0]):
        v = parts[d]
        total = total + jnp.exp(-before) * v
        depth = v
        for n in range(3):
            depth = jnp.where(group == n, pltpu.roll(v, 32 * (n + 1), 1), depth)
        before = before + depth
    image[...] = jnp.where(group == 3, 1.0 - jnp.exp(-before), total).T


def swaps(n_lat, n_dep, kind):
    out = []
    for lat in range(n_lat):
        for dep in range(n_dep):
            other_lat, other_dep = lat, dep
            if kind in ("d1", "d2"):
                up = ((lat % 2 == 0) == (dep % 2 == 0)) == (kind == "d1")
                other_dep = dep + 1 if up else dep - 1
            else:
                right = (lat % 2 == 0) == (kind == "l1")
                other_lat = lat + 1 if right else lat - 1
            if 0 <= other_lat < n_lat and 0 <= other_dep < n_dep:
                out.append((lat * n_dep + dep, other_lat * n_dep + other_dep))
    return out


def on_device(n_lat, n_dep, pressure_prev, pressure_now, materials, courant_table, tf_weights, source_cell, start_step):
    f32 = jnp.float32

    def swap(v, kind):
        return lax.ppermute(v, ("lat", "dep"), swaps(n_lat, n_dep, kind))

    def busy(microseconds):
        return pl.CostEstimate(
            flops=int(microseconds * 1.0e9), bytes_accessed=int(microseconds * 3.0e6), transcendentals=0
        )

    def shape(*dims):
        return jax.ShapeDtypeStruct(dims, f32)

    def kept(*dims):
        return pltpu.VMEM(dims, f32)

    def in_hbm(v):
        return pltpu.with_memory_space_constraint(v, pltpu.HBM)

    params = pltpu.CompilerParams(vmem_limit_bytes=24 * 1024 * 1024)
    i32 = jnp.int32
    inputs = [in_hbm(v) for v in (pressure_now, pressure_prev, materials)]
    early_1, early_2, side_1, side_2 = pl.pallas_call(
        pack,
        in_specs=[SMEM] + [HBM] * 3,
        out_specs=[VMEM] * 4,
        out_shape=[kept(4, T, X, 128)] * 2 + [kept(Z, T, 16, 128)] * 2,
        scratch_shapes=[
            pltpu.VMEM((2, 2, X, 512), f32),
            pltpu.VMEM((2, 2, X, 512), i32),
            pltpu.VMEM((2, Z, 8, 512), f32),
            pltpu.VMEM((2, Z, 8, 512), f32),
            pltpu.VMEM((2, Z, 8, 512), i32),
            pltpu.SemaphoreType.DMA((4,)),
            pltpu.SemaphoreType.DMA((6,)),
        ],
        compiler_params=params,
        name="pack",
    )(courant_table, *inputs)
    side_a = swap(side_1, "l1")
    side_b = swap(side_2, "l2")
    early_a = swap(early_1, "d1")
    early_b = swap(early_2, "d2")

    padded = (Z + 4, T, ROWS, 128)
    block, side = (Z, T, X, 128), (Z, T, 16, 128)
    now, stiff, one, prev = pl.pallas_call(
        advance_inner,
        in_specs=[SMEM] + [HBM] * 3,
        out_specs=[VMEM] * 4,
        out_shape=[kept(*padded), kept(*block), kept(*padded), kept(*side)],
        scratch_shapes=[pltpu.VMEM((Z, X, 512), d) for d in (f32, f32, i32)] + [pltpu.SemaphoreType.DMA((3,))],
        compiler_params=params,
        cost_estimate=busy(3.0),
        name="advance_inner",
    )(courant_table, *inputs)
    now, one, now_side, stiff_side, two = pl.pallas_call(
        advance_outer,
        in_specs=[SMEM] * 2 + [VMEM] * 6,
        out_specs=[VMEM] * 5,
        out_shape=[kept(*padded)] * 2 + [kept(*side)] * 2 + [kept(4, T, ROWS, 128)],
        scratch_shapes=[pltpu.VMEM(side, f32)],
        input_output_aliases={2: 0, 4: 1},
        compiler_params=params,
        cost_estimate=busy(5.0),
        name="advance_outer",
    )(source_cell, start_step, now, stiff, one, prev, side_a, side_b)
    late_1, late_2 = pl.pallas_call(
        pack_late,
        in_specs=[VMEM] * 4 + [pl.BlockSpec(memory_space=pl.ANY)] * 2,
        out_specs=[VMEM] * 2,
        out_shape=[kept(4, T, X + 8, 128)] * 2,
        compiler_params=params,
        name="pack_late",
    )(now_side, stiff_side, one, two, early_a, early_b)
    late_a = swap(late_1, "d1")
    late_b = swap(late_2, "d2")
    one, two, delta, halo_stiff, halo_two = pl.pallas_call(
        couple,
        in_specs=[VMEM] * 5 + [pl.BlockSpec(memory_space=pl.ANY)],
        out_specs=[VMEM] * 5,
        out_shape=[kept(*padded)] * 2 + [kept(4, T, ROWS, 128)] + [kept(4, T, X, 128)] * 2,
        input_output_aliases={2: 0},
        compiler_params=params,
        cost_estimate=busy(4.0),
        name="couple",
    )(now, stiff, one, early_a, early_b, late_1)
    pressure, partial, _, _, _ = pl.pallas_call(
        functools.partial(finish, n_dep),
        in_specs=[SMEM] * 3 + [VMEM] * 11,
        out_specs=[VMEM] * 5,
        out_shape=[shape(Z, X, 512), shape(n_dep, X, 128)] + [kept(*padded)] * 2 + [kept(4, T, ROWS, 128)],
        scratch_shapes=[pltpu.SMEM((4, BUMPS), f32)],
        input_output_aliases={7: 2, 8: 3, 9: 4},
        compiler_params=params,
        name="finish",
    )(
        source_cell, start_step, tf_weights, now, stiff, now_side, stiff_side, one, two, delta, halo_stiff,
        halo_two, late_a, late_b,
    )
    parts = lax.all_to_all(partial, "dep", 0, 0, tiled=True)
    image = pl.pallas_call(
        composite,
        in_specs=[VMEM],
        out_specs=VMEM,
        out_shape=shape(128, X),
        compiler_params=params,
        name="composite",
    )(parts)
    return pressure, jnp.swapaxes(image.reshape(4, 512 // n_dep, X), 1, 2)


def solution(mesh):
    block = P("dep", "lat", None)
    return jax.shard_map(
        functools.partial(on_device, mesh.shape["lat"], mesh.shape["dep"]),
        mesh=mesh,
        in_specs=(block, block, block, P(), P(), P(), P()),
        out_specs=(block, P(None, "lat", "dep")),
        check_vma=False,
    )
```

```python
import functools
import math

import jax
import jax.numpy as jnp
from jax import lax
from jax.experimental import pallas as pl
from jax.experimental.pallas import tpu as pltpu
from jax.sharding import PartitionSpec as P

BUMPS = 8
LOG2E = math.log2(math.e)
Z, X, T = 8, 64, 4
ROWS = X + 32
CORE = 16
VMEM = pl.BlockSpec(memory_space=pltpu.VMEM)
SMEM = pl.BlockSpec(memory_space=pltpu.SMEM)
HBM = pl.BlockSpec(memory_space=pltpu.HBM)


def lane_masks():
    lane = lax.broadcasted_iota(jnp.int32, (8, 128), 1)
    return lane < 1, lane < 2, lane >= 127, lane >= 126


def columns_sum(c, masks):
    zero = jnp.zeros((8, 128), jnp.float32)
    low1, low2, high1, high2 = masks
    a1 = [pltpu.roll(v, 1, 1) for v in c]
    a2 = [pltpu.roll(v, 2, 1) for v in c]
    b1 = [pltpu.roll(v, 127, 1) for v in c]
    b2 = [pltpu.roll(v, 126, 1) for v in c]
    out = []
    for i in range(T):
        first, last = i == 0, i == T - 1
        near = jnp.where(low1, zero if first else a1[i - 1], a1[i]) + jnp.where(
            high1, zero if last else b1[i + 1], b1[i]
        )
        far = jnp.where(low2, zero if first else a2[i - 1], a2[i]) + jnp.where(
            high2, zero if last else b2[i + 1], b2[i]
        )
        out.append((near, far))
    return out


def plane_terms(ref, k, row, masks):
    c = [ref[k, i, pl.ds(row, 8), :] for i in range(T)]
    sums = columns_sum(c, masks)
    out = []
    for i in range(T):
        near = sums[i][0] + (ref[k, i, pl.ds(row - 1, 8), :] + ref[k, i, pl.ds(row + 1, 8), :])
        far = sums[i][1] + (ref[k, i, pl.ds(row - 2, 8), :] + ref[k, i, pl.ds(row + 2, 8), :])
        out.append((c[i], near, far))
    return out


def full_terms(ref, k, row, masks):
    out = []
    for i, (c, near, far) in enumerate(plane_terms(ref, k, row, masks)):
        rows = pl.ds(row, 8)
        near = near + (ref[k - 1, i, rows, :] + ref[k + 1, i, rows, :])
        far = far + (ref[k - 2, i, rows, :] + ref[k + 2, i, rows, :])
        out.append((c, 16.0 * near - far - 90.0 * c))
    return out


def strike(ref, outer, place, amplitude, layers, rows_low, rows_high):
    z, x, y = place
    row = x + CORE
    here = (z >= 0) & (z < layers) & (row >= rows_low) & (row < rows_high)

    @pl.when(here)
    def _():
        tile, lane = y // 128, y % 128
        old = ref[z + outer, tile, pl.ds(row, 1), :]
        ids = lax.broadcasted_iota(jnp.int32, (1, 128), 1)
        ref[z + outer, tile, pl.ds(row, 1), :] = old + jnp.where(ids == lane, amplitude, 0.0)


def stiffness(table, materials):
    return jnp.take_along_axis(table, materials, axis=1, mode="promise_in_bounds")


def ways():
    lat, dep = lax.axis_index("lat"), lax.axis_index("dep")
    return (lat + dep + 1) % 2, (lat + 1) % 2


def source_place(cell):
    return cell[0] - lax.axis_index("dep") * Z, cell[1] - lax.axis_index("lat") * X, cell[2]


def wavelet(start, step):
    level = jnp.full((1, 128), start[0] + step, jnp.int32).astype(jnp.float32)
    shifted = 0.3 * (level - 10.0)
    return 4.0 * (1.0 - 2.0 * shifted * shifted) * jnp.exp(-shifted * shifted)


def stiffness_table(courant):
    lane = lax.broadcasted_iota(jnp.int32, (8, 128), 1)
    table = jnp.zeros((8, 128), jnp.float32)
    for m in range(16):
        table = jnp.where(lane == m, courant[m], table)
    return table * table * (1.0 / 12.0)


def pack(
    courant_in, now_in, prev_in, mat_in, early_1, early_2, side_1, side_2, now, prev, mat, courant, sems,
):
    up1, right1 = ways()
    copies = [
        pltpu.make_async_copy(src, dst, sems.at[n])
        for n, (src, dst) in enumerate(((courant_in, courant), (mat_in, mat), (now_in, now), (prev_in, prev)))
    ]
    for copy in copies:
        copy.start()
    upper_half = (lax.broadcasted_iota(jnp.int32, (8, 128), 0) >= 4).astype(jnp.int32)
    copies[0].wait()
    table = stiffness_table(courant)
    copies[1].wait()
    copies[2].wait()
    for slot, out in enumerate((early_1, early_2)):
        first = 6 * up1 if slot == 0 else 6 - 6 * up1
        for k in range(2):
            for i in range(T):
                lanes = slice(128 * i, 128 * i + 128)
                out[k, i] = now[first + k, :, lanes]
                for t in range(X // 8):
                    rows = slice(8 * t, 8 * t + 8)
                    out[2 + k, i, rows, :] = stiffness(table, mat[first + k, rows, lanes])
    copies[3].wait()
    for slot, out in enumerate((side_1, side_2)):
        right = right1 if slot == 0 else 1 - right1
        rows = pl.ds(pl.multiple_of((X - 8) * right, 8), 8)
        keep = upper_half == right
        for k in range(Z):
            for i in range(T):
                lanes = slice(128 * i, 128 * i + 128)
                out[k, i, 0:8, :] = now[k, rows, lanes]
                moved = pltpu.roll(stiffness(table, mat[k, rows, lanes]), 4, 0)
                out[k, i, 8:16, :] = jnp.where(keep, prev[k, rows, lanes], moved)


INNER = range(CORE + 8, CORE + X - 8, 8)
OUTER = (CORE - 8, CORE, CORE + X - 8, CORE + X)


def advance_inner(courant, now, prev, mat, now_out, stiff_out, one_out, prev_out):
    table = stiffness_table(courant)
    masks = lane_masks()
    zeros = jnp.zeros((T, ROWS, 128), jnp.float32)
    for k in (0, 1, Z + 2, Z + 3):
        now_out[k] = zeros
        one_out[k] = zeros

    def fill(k, carry):
        for i in range(T):
            now_out[k + 2, i, CORE : CORE + X, :] = now[k, :, 128 * i : 128 * i + 128]
        return carry

    lax.fori_loop(0, Z, fill, 0)

    def first(k, carry):
        for i in range(T):
            lanes = slice(128 * i, 128 * i + 128)
            prev_out[k, i, 0:8, :] = prev[k, 0:8, lanes]
            prev_out[k, i, 8:16, :] = prev[k, X - 8 : X, lanes]
            for t in range(X // 8):
                rows = slice(8 * t, 8 * t + 8)
                stiff_out[k, i, rows, :] = stiffness(table, mat[k, rows, lanes])
        for row in INNER:
            own = slice(row - CORE, row - CORE + 8)
            for i, (c, lap) in enumerate(full_terms(now_out, k + 2, row, masks)):
                before = prev[k, own, 128 * i : 128 * i + 128]
                one_out[k + 2, i, row : row + 8, :] = 2.0 * c - before + stiff_out[k, i, own, :] * lap
        return carry

    lax.fori_loop(0, Z, first, 0)


def advance_outer(
    cell, start, now_in, stiff_in, one_in, prev_in, lat_a, lat_b, now, one, now_side, stiff_side, two_out,
    prev_side,
):
    del now_in, one_in
    masks = lane_masks()
    right1 = ways()[1] == 1

    def fill(k, carry):
        for i in range(T):
            for left in (False, True):
                wanted = jnp.logical_not(right1) if left else right1
                got = jnp.where(wanted, lat_a[k, i], lat_b[k, i])
                row = CORE - 8 if left else CORE + X
                half = slice(0, 8) if left else slice(8, 16)
                now[k + 2, i, row : row + 8, :] = got[0:8]
                now_side[k, i, half, :] = got[0:8]
                prev_side[k, i, half, :] = got[8:16]
                stiff_side[k, i, half, :] = pltpu.roll(got[8:16], 4, 0)
        return carry

    lax.fori_loop(0, Z, fill, 0)

    def first(k, carry):
        for row in OUTER:
            rows = slice(row, row + 8)
            for i, (c, lap) in enumerate(full_terms(now, k + 2, row, masks)):
                if row < CORE or row == CORE + X:
                    half = slice(0, 8) if row < CORE else slice(8, 16)
                    before, stiff = prev_side[k, i, half, :], stiff_side[k, i, half, :]
                else:
                    half = slice(0, 8) if row == CORE else slice(8, 16)
                    before, stiff = prev_in[k, i, half, :], stiff_in[k, i, row - CORE : row - CORE + 8, :]
                one[k + 2, i, rows, :] = 2.0 * c - before + stiff * lap
        return carry

    lax.fori_loop(0, Z, first, 0)
    place = source_place(cell)
    strike(one, 2, place, wavelet(start, 0), Z, CORE - 8, CORE + X + 8)

    def second(n, carry):
        k = jnp.where(n < 2, n, n + 4)
        for row in range(CORE, CORE + X, 8):
            rows = slice(row, row + 8)
            for i, (c, lap) in enumerate(full_terms(one, k + 2, row, masks)):
                stiff = stiff_in[k, i, row - CORE : row - CORE + 8, :]
                two_out[n, i, rows, :] = 2.0 * c - now[k + 2, i, rows, :] + stiff * lap
        return carry

    lax.fori_loop(0, 4, second, 0)
    z = place[0]
    inner = (z >= 2) & (z < Z - 2)
    strike(two_out, 0, (jnp.where(inner, -1, jnp.where(z < 2, z, z - 4)),) + place[1:], wavelet(start, 1), 4, CORE, CORE + X)


def pack_late(now_side, stiff_side, one, two, out_a, out_b):
    sub = lax.broadcasted_iota(jnp.int32, (8, 128), 0)
    left, right = slice(CORE - 8, CORE), slice(CORE + X, CORE + X + 8)
    up1 = ways()[0]
    for slot, out in ((0, out_a), (1, out_b)):
        high = up1 if slot == 0 else 1 - up1
        for k in range(2):
            z = (Z - 2) * high + k
            for i in range(T):
                out[k, i, 0:X, :] = one[z + 2, i, CORE : CORE + X, :]
                out[2 + k, i, 0:X, :] = two[2 * high + k, i, CORE : CORE + X, :]
                out[k, i, X : X + 8, :] = jnp.where(sub >= 4, now_side[z, i, 0:8, :], now_side[z, i, 8:16, :])
                ones = jnp.where(sub >= 4, one[z + 2, i, left, :], one[z + 2, i, right, :])
                side = jnp.where(sub >= 4, stiff_side[z, i, 0:8, :], stiff_side[z, i, 8:16, :])
                outer = (sub < 2) | (sub >= 6)
                out[2 + k, i, X : X + 8, :] = jnp.where(outer, ones, pltpu.roll(side, 4, 0))


def clamp_for_bumps(p):
    return jnp.minimum(jnp.maximum(p, -7.4), 7.4)


SIDES = ((False, 0, 1, 0, 0, 1, 0), (True, 2, 0, 1, Z - 1, Z - 2, Z + 2))


def halo_step(delta, one, halo_stiff, base, near, n_in, n_next, row, masks):
    rows, own = pl.ds(row, 8), pl.ds(row - CORE, 8)
    terms = {k: plane_terms(delta, base + k, row, masks) for k in range(2)}
    out = {}
    for i in range(T):
        for k in range(2):
            c, near_sum, far_sum = terms[k][i]
            near_sum = near_sum + terms[1 - k][i][0]
            if k == near:
                near_sum = near_sum + one[n_in + 2, i, rows, :]
                far_sum = far_sum + one[n_next + 2, i, rows, :]
            else:
                far_sum = far_sum + one[n_in + 2, i, rows, :]
            lap = 16.0 * near_sum - far_sum - 90.0 * c
            out[k, i] = 2.0 * c + halo_stiff[base + k, i, own, :] * lap
    return out


def couple(now, stiff, one_in, early_a, early_b, sent, one, two, delta, halo_stiff, halo_two):
    del one_in, sent
    masks = lane_masks()
    up1 = ways()[0] == 1
    for high, base, near, far, n_in, n_next, zi in SIDES:
        use_a = up1 if high else jnp.logical_not(up1)

        def tile(t, carry, use_a=use_a, base=base, near=near, far=far, n_in=n_in, n_next=n_next, zi=zi):
            own, rows = pl.ds(pl.multiple_of(8 * t, 8), 8), pl.ds(pl.multiple_of(CORE + 8 * t, 8), 8)
            for i in range(T):
                zero_h = [jnp.where(use_a, early_a[k, i, own, :], early_b[k, i, own, :]) for k in range(2)]
                st_h = [jnp.where(use_a, early_a[2 + k, i, own, :], early_b[2 + k, i, own, :]) for k in range(2)]
                one[n_in + 2, i, rows, :] += stiff[n_in, i, own, :] * (16.0 * zero_h[near] - zero_h[far])
                one[n_next + 2, i, rows, :] -= stiff[n_next, i, own, :] * zero_h[near]
                d_near = st_h[near] * (16.0 * now[n_in + 2, i, rows, :] - now[n_next + 2, i, rows, :])
                d_far = -st_h[far] * now[n_in + 2, i, rows, :]
                for place, d, st in ((near, d_near, st_h[near]), (far, d_far, st_h[far])):
                    one[zi + place, i, rows, :] = d
                    delta[base + place, i, rows, :] = d
                    halo_stiff[base + place, i, own, :] = st
            return carry

        lax.fori_loop(0, X // 8, tile, 0)

    def second(k, carry):
        for row in INNER:
            rows = slice(row, row + 8)
            for i, (c, lap) in enumerate(full_terms(one, k + 2, row, masks)):
                own = slice(row - CORE, row - CORE + 8)
                two[k + 2, i, rows, :] = 2.0 * c - now[k + 2, i, rows, :] + stiff[k, i, own, :] * lap
        return carry

    lax.fori_loop(0, Z, second, 0)
    for high, base, near, far, n_in, n_next, zi in SIDES:

        def beyond(t, carry, base=base, near=near, n_in=n_in, n_next=n_next):
            row = pl.multiple_of(CORE + 8 * t, 8)
            for (k, i), v in halo_step(delta, one, halo_stiff, base, near, n_in, n_next, row, masks).items():
                halo_two[base + k, i, pl.ds(pl.multiple_of(8 * t, 8), 8), :] = v
            return carry

        lax.fori_loop(1, X // 8 - 1, beyond, 0)


def finish(
    n_dep, cell, start, transfer, now, stiff, now_side, stiff_side, one_in, two_in, delta_in, halo_stiff, halo_two,
    late_a, late_b, pressure, partial, one, two, delta, weights,
):
    del one_in, two_in, delta_in
    masks = lane_masks()
    up1 = ways()[0] == 1
    for n in range(4):
        for j in range(BUMPS):
            centre = (-3.0 + 6.0 * j / (BUMPS - 1)) / 0.8
            weights[n, j] = transfer[n, j] * (math.exp(-centre * centre) * (-LOG2E * 1.5 / (Z * n_dep) if n == 3 else 1.0))

    for high, base, near, far, n_in, n_next, zi in SIDES:
        use_a = up1 if high else jnp.logical_not(up1)

        def late_of(k, i, row, use_a=use_a):
            rows = pl.ds(row - CORE, 8)
            return jnp.where(use_a, late_a[k, i, rows, :], late_b[k, i, rows, :])

        for row in (CORE - 8, CORE + X):
            rows, half = slice(row, row + 8), slice(0, 8) if row < CORE else slice(8, 16)
            for i in range(T):
                zero_h = [late_of(k, i, CORE + X) for k in range(2)]
                one_h = [late_of(2 + k, i, CORE + X) for k in range(2)]
                st_h = [pltpu.roll(v, 4, 0) for v in one_h]
                one[n_in + 2, i, rows, :] += stiff_side[n_in, i, half, :] * (16.0 * zero_h[near] - zero_h[far])
                one[n_next + 2, i, rows, :] -= stiff_side[n_next, i, half, :] * zero_h[near]
                d_near = st_h[near] * (16.0 * now_side[n_in, i, half, :] - now_side[n_next, i, half, :])
                d_far = -st_h[far] * now_side[n_in, i, half, :]
                for at, d in ((near, d_near), (far, d_far)):
                    one[zi + at, i, rows, :] = one_h[at] + d
                    delta[base + at, i, rows, :] = d

        def inner(t, carry, base=base, near=near, far=far, n_in=n_in, n_next=n_next, zi=zi, late_of=late_of):
            row = pl.multiple_of(CORE + 8 * t, 8)
            rows, own = pl.ds(row, 8), pl.ds(pl.multiple_of(8 * t, 8), 8)
            for i in range(T):
                one_h = [late_of(k, i, row) for k in range(2)]
                for k in range(2):
                    one[zi + k, i, rows, :] += one_h[k]
                    two[zi + k, i, rows, :] = late_of(2 + k, i, row) + halo_two[base + k, i, own, :]
                two[n_in + 2, i, rows, :] += stiff[n_in, i, own, :] * (16.0 * one_h[near] - one_h[far])
                two[n_next + 2, i, rows, :] -= stiff[n_next, i, own, :] * one_h[near]
            return carry

        lax.fori_loop(0, X // 8, inner, 0)
        for row in (CORE, CORE + X - 8):
            for (k, i), v in halo_step(delta, one, halo_stiff, base, near, n_in, n_next, row, masks).items():
                two[zi + k, i, row : row + 8, :] = late_of(2 + k, i, row) + v

    def second(k, carry):
        for row in OUTER:
            rows = slice(row, row + 8)
            for i, (c, lap) in enumerate(full_terms(one, k + 2, row, masks)):
                if CORE <= row < CORE + X:
                    st = stiff[k, i, row - CORE : row - CORE + 8, :]
                else:
                    st = stiff_side[k, i, 0:8, :] if row < CORE else stiff_side[k, i, 8:16, :]
                two[k + 2, i, rows, :] = 2.0 * c - now[k + 2, i, rows, :] + st * lap
        return carry

    lax.fori_loop(0, Z, second, 0)
    place = source_place(cell)
    strike(two, 2, place, wavelet(start, 1), Z, CORE - 8, CORE + X + 8)

    def third(k, carry):
        for row in range(CORE, CORE + X, 8):
            rows = pl.ds(row, 8)
            for i, (c, lap) in enumerate(full_terms(two, k + 2, row, masks)):
                own = pl.ds(row - CORE, 8)
                one[k + 2, i, rows, :] = 2.0 * c - one[k + 2, i, rows, :] + stiff[k, i, own, :] * lap
        return carry

    lax.fori_loop(0, Z, third, 0)
    strike(one, 2, place, wavelet(start, 2), Z, CORE, CORE + X)

    group = lax.broadcasted_iota(jnp.int32, (8, 128), 1) // 32
    half = BUMPS // 2
    rate = 6.0 / (BUMPS - 1) / (0.8 * 0.8) * LOG2E

    def render(t, carry):
        rows = pl.ds(pl.multiple_of(CORE + 8 * t, 8), 8)
        own = pl.ds(pl.multiple_of(8 * t, 8), 8)
        for i in range(T):
            zero = jnp.zeros((8, 128), jnp.float32)
            seen = [zero] * BUMPS
            through = jnp.ones((8, 128), jnp.float32)
            depth = zero
            for k in range(Z):
                p = one[k + 2, i, rows, :]
                pressure[k, own, 128 * i : 128 * i + 128] = p
                p = clamp_for_bumps(p)
                gauss = jnp.exp2(p * p * (-LOG2E / 0.64))
                rise = jnp.exp2(p * rate)
                fall = jnp.exp2(p * -rate)
                up, down = rise * rise, fall * fall
                above, below = gauss * rise, gauss * fall
                a = weights[3, BUMPS - 1] * up + weights[3, BUMPS - 2]
                b = weights[3, 0] * down + weights[3, 1]
                for j in range(2, half):
                    a = a * up + weights[3, BUMPS - 1 - j]
                    b = b * down + weights[3, j]
                power = a * above + b * below
                stay = jnp.exp2(power)
                weight = through * (1.0 - stay)
                through = through * stay
                depth = depth + power
                above, below = weight * above, weight * below
                for j in range(half):
                    seen[half + j] = seen[half + j] + above
                    seen[half - 1 - j] = seen[half - 1 - j] + below
                    if j < half - 1:
                        above, below = above * up, below * down
            parts = []
            for n in range(3):
                colour = weights[n, 0] * seen[0]
                for j in range(1, BUMPS):
                    colour = colour + weights[n, j] * seen[j]
                parts.append(colour)
            parts.append(depth * (-1.0 / LOG2E))
            for q in range(4):
                packed = None
                for n in range(4):
                    shift = (32 * (n - q)) % 128
                    moved = parts[n] if shift == 0 else pltpu.roll(parts[n], shift, 1)
                    packed = moved if packed is None else jnp.where(group == n, moved, packed)
                partial[4 * i + q, own, :] = packed
        return carry

    lax.fori_loop(0, X // 8, render, 0)


def composite(parts, image):
    group = lax.broadcasted_iota(jnp.int32, (X, 128), 1) // 32
    before = jnp.zeros((X, 128), jnp.float32)
    total = jnp.zeros((X, 128), jnp.float32)
    for d in range(parts.shape[0]):
        v = parts[d]
        total = total + jnp.exp(-before) * v
        depth = v
        for n in range(3):
            depth = jnp.where(group == n, pltpu.roll(v, 32 * (n + 1), 1), depth)
        before = before + depth
    image[...] = jnp.where(group == 3, 1.0 - jnp.exp(-before), total).T


def swaps(n_lat, n_dep, kind):
    out = []
    for lat in range(n_lat):
        for dep in range(n_dep):
            other_lat, other_dep = lat, dep
            if kind in ("d1", "d2"):
                up = ((lat % 2 == 0) == (dep % 2 == 0)) == (kind == "d1")
                other_dep = dep + 1 if up else dep - 1
            else:
                right = (lat % 2 == 0) == (kind == "l1")
                other_lat = lat + 1 if right else lat - 1
            if 0 <= other_lat < n_lat and 0 <= other_dep < n_dep:
                out.append((lat * n_dep + dep, other_lat * n_dep + other_dep))
    return out


def on_device(n_lat, n_dep, pressure_prev, pressure_now, materials, courant_table, tf_weights, source_cell, start_step):
    f32 = jnp.float32

    def swap(v, kind):
        return lax.ppermute(v, ("lat", "dep"), swaps(n_lat, n_dep, kind))

    def busy(microseconds):
        return pl.CostEstimate(
            flops=int(microseconds * 1.0e9), bytes_accessed=int(microseconds * 3.0e6), transcendentals=0
        )

    def shape(*dims):
        return jax.ShapeDtypeStruct(dims, f32)

    def kept(*dims):
        return pltpu.VMEM(dims, f32)

    def in_hbm(v):
        return pltpu.with_memory_space_constraint(v, pltpu.HBM)

    params = pltpu.CompilerParams(vmem_limit_bytes=24 * 1024 * 1024)
    i32 = jnp.int32
    blocks = [pltpu.VMEM((Z, X, 512), d) for d in (f32, f32, i32)]
    early_1, early_2, side_1, side_2, *inputs = pl.pallas_call(
        pack,
        in_specs=[HBM] * 4,
        out_specs=[VMEM] * 7,
        out_shape=[kept(4, T, X, 128)] * 2 + [kept(Z, T, 16, 128)] * 2 + blocks,
        scratch_shapes=[pltpu.SMEM((16,), f32), pltpu.SemaphoreType.DMA((4,))],
        compiler_params=params,
        name="pack",
    )(*(in_hbm(v) for v in (courant_table, pressure_now, pressure_prev, materials)))
    side_a = swap(side_1, "l1")
    side_b = swap(side_2, "l2")
    early_a = swap(early_1, "d1")
    early_b = swap(early_2, "d2")

    padded = (Z + 4, T, ROWS, 128)
    block, side = (Z, T, X, 128), (Z, T, 16, 128)
    now, stiff, one, prev = pl.pallas_call(
        advance_inner,
        in_specs=[SMEM] + [VMEM] * 3,
        out_specs=[VMEM] * 4,
        out_shape=[kept(*padded), kept(*block), kept(*padded), kept(*side)],
        compiler_params=params,
        cost_estimate=busy(3.0),
        name="advance_inner",
    )(courant_table, *inputs)
    now, one, now_side, stiff_side, two = pl.pallas_call(
        advance_outer,
        in_specs=[SMEM] * 2 + [VMEM] * 6,
        out_specs=[VMEM] * 5,
        out_shape=[kept(*padded)] * 2 + [kept(*side)] * 2 + [kept(4, T, ROWS, 128)],
        scratch_shapes=[pltpu.VMEM(side, f32)],
        input_output_aliases={2: 0, 4: 1},
        compiler_params=params,
        cost_estimate=busy(5.0),
        name="advance_outer",
    )(source_cell, start_step, now, stiff, one, prev, side_a, side_b)
    late_1, late_2 = pl.pallas_call(
        pack_late,
        in_specs=[VMEM] * 4,
        out_specs=[VMEM] * 2,
        out_shape=[kept(4, T, X + 8, 128)] * 2,
        compiler_params=params,
        name="pack_late",
    )(now_side, stiff_side, one, two)
    late_a = swap(late_1, "d1")
    late_b = swap(late_2, "d2")
    one, two, delta, halo_stiff, halo_two = pl.pallas_call(
        couple,
        in_specs=[VMEM] * 5 + [pl.BlockSpec(memory_space=pl.ANY)],
        out_specs=[VMEM] * 5,
        out_shape=[kept(*padded)] * 2 + [kept(4, T, ROWS, 128)] + [kept(4, T, X, 128)] * 2,
        input_output_aliases={2: 0},
        compiler_params=params,
        cost_estimate=busy(4.0),
        name="couple",
    )(now, stiff, one, early_a, early_b, late_1)
    pressure, partial, _, _, _ = pl.pallas_call(
        functools.partial(finish, n_dep),
        in_specs=[SMEM] * 3 + [VMEM] * 11,
        out_specs=[VMEM] * 5,
        out_shape=[shape(Z, X, 512), shape(n_dep, X, 128)] + [kept(*padded)] * 2 + [kept(4, T, ROWS, 128)],
        scratch_shapes=[pltpu.SMEM((4, BUMPS), f32)],
        input_output_aliases={7: 2, 8: 3, 9: 4},
        compiler_params=params,
        name="finish",
    )(
        source_cell, start_step, tf_weights, now, stiff, now_side, stiff_side, one, two, delta, halo_stiff,
        halo_two, late_a, late_b,
    )
    parts = lax.all_to_all(partial, "dep", 0, 0, tiled=True)
    image = pl.pallas_call(
        composite,
        in_specs=[VMEM],
        out_specs=VMEM,
        out_shape=shape(128, X),
        compiler_params=params,
        name="composite",
    )(parts)
    return pressure, jnp.swapaxes(image.reshape(4, 512 // n_dep, X), 1, 2)


def solution(mesh):
    block = P("dep", "lat", None)
    return jax.shard_map(
        functools.partial(on_device, mesh.shape["lat"], mesh.shape["dep"]),
        mesh=mesh,
        in_specs=(block, block, block, P(), P(), P(), P()),
        out_specs=(block, P(None, "lat", "dep")),
        check_vma=False,
    )
```

```python
import functools
import math

import jax
import jax.numpy as jnp
from jax import lax
from jax.experimental import pallas as pl
from jax.experimental.pallas import tpu as pltpu
from jax.sharding import PartitionSpec as P

BUMPS = 8
LOG2E = math.log2(math.e)
Z, X, T = 8, 64, 4
ROWS = X + 32
CORE = 16
VMEM = pl.BlockSpec(memory_space=pltpu.VMEM)
SMEM = pl.BlockSpec(memory_space=pltpu.SMEM)
HBM = pl.BlockSpec(memory_space=pltpu.HBM)


def lane_masks():
    lane = lax.broadcasted_iota(jnp.int32, (8, 128), 1)
    return lane < 1, lane < 2, lane >= 127, lane >= 126


def columns_sum(c, masks):
    zero = jnp.zeros((8, 128), jnp.float32)
    low1, low2, high1, high2 = masks
    a1 = [pltpu.roll(v, 1, 1) for v in c]
    a2 = [pltpu.roll(v, 2, 1) for v in c]
    b1 = [pltpu.roll(v, 127, 1) for v in c]
    b2 = [pltpu.roll(v, 126, 1) for v in c]
    out = []
    for i in range(T):
        first, last = i == 0, i == T - 1
        near = jnp.where(low1, zero if first else a1[i - 1], a1[i]) + jnp.where(
            high1, zero if last else b1[i + 1], b1[i]
        )
        far = jnp.where(low2, zero if first else a2[i - 1], a2[i]) + jnp.where(
            high2, zero if last else b2[i + 1], b2[i]
        )
        out.append((near, far))
    return out


def plane_terms(ref, k, row, masks):
    c = [ref[k, i, pl.ds(row, 8), :] for i in range(T)]
    sums = columns_sum(c, masks)
    out = []
    for i in range(T):
        near = sums[i][0] + (ref[k, i, pl.ds(row - 1, 8), :] + ref[k, i, pl.ds(row + 1, 8), :])
        far = sums[i][1] + (ref[k, i, pl.ds(row - 2, 8), :] + ref[k, i, pl.ds(row + 2, 8), :])
        out.append((c[i], near, far))
    return out


def band():
    shape = (512, 256)
    d = jnp.abs(lax.broadcasted_iota(jnp.int32, shape, 0) % 256 - lax.broadcasted_iota(jnp.int32, shape, 1))
    return jnp.where(d == 0, -90.0, jnp.where(d == 1, 16.0, jnp.where(d == 2, -1.0, 0.0))).astype(jnp.bfloat16)


def full_rows(ref, k, first, count, bands):
    rows = slice(first, first + count)
    factors = []
    for h in range(2):
        v = jnp.concatenate([ref[k, 2 * h, rows, :], ref[k, 2 * h + 1, rows, :]], axis=1)
        high = v.astype(jnp.bfloat16)
        low = (v - high.astype(jnp.float32)).astype(jnp.bfloat16)
        factors.append(jnp.concatenate([high, low], axis=1))
    product = jnp.dot(jnp.concatenate(factors, axis=0), bands, preferred_element_type=jnp.float32)
    low1, low2, high1, high2 = lane_masks()
    for r in range(0, count, 8):
        row = first + r
        here = slice(row, row + 8)
        for i in range(T):
            c = ref[k, i, here, :]
            inside = product[count * (i // 2) + r : count * (i // 2) + r + 8, 128 * (i % 2) : 128 * (i % 2) + 128]
            near = ref[k, i, row - 1 : row + 7, :] + ref[k, i, row + 1 : row + 9, :]
            far = ref[k, i, row - 2 : row + 6, :] + ref[k, i, row + 2 : row + 10, :]
            near = near + (ref[k - 1, i, here, :] + ref[k + 1, i, here, :])
            far = far + (ref[k - 2, i, here, :] + ref[k + 2, i, here, :])
            if i == 1:
                v = ref[k, 2, here, :]
                near = near + jnp.where(high1, pltpu.roll(v, 127, 1), 0.0)
                far = far + jnp.where(high2, pltpu.roll(v, 126, 1), 0.0)
            if i == 2:
                v = ref[k, 1, here, :]
                near = near + jnp.where(low1, pltpu.roll(v, 1, 1), 0.0)
                far = far + jnp.where(low2, pltpu.roll(v, 2, 1), 0.0)
            yield row, i, c, inside + (16.0 * near - far)


def strike(ref, outer, place, amplitude, layers, rows_low, rows_high):
    z, x, y = place
    row = x + CORE
    here = (z >= 0) & (z < layers) & (row >= rows_low) & (row < rows_high)

    @pl.when(here)
    def _():
        tile, lane = y // 128, y % 128
        old = ref[z + outer, tile, pl.ds(row, 1), :]
        ids = lax.broadcasted_iota(jnp.int32, (1, 128), 1)
        ref[z + outer, tile, pl.ds(row, 1), :] = old + jnp.where(ids == lane, amplitude, 0.0)


def stiffness(table, materials):
    return jnp.take_along_axis(table, materials, axis=1, mode="promise_in_bounds")


def ways():
    lat, dep = lax.axis_index("lat"), lax.axis_index("dep")
    return (lat + dep + 1) % 2, (lat + 1) % 2


def source_place(cell):
    return cell[0] - lax.axis_index("dep") * Z, cell[1] - lax.axis_index("lat") * X, cell[2]


def wavelet(start, step):
    level = jnp.full((1, 128), start[0] + step, jnp.int32).astype(jnp.float32)
    shifted = 0.3 * (level - 10.0)
    return 4.0 * (1.0 - 2.0 * shifted * shifted) * jnp.exp(-shifted * shifted)


def stiffness_table(courant):
    lane = lax.broadcasted_iota(jnp.int32, (8, 128), 1)
    table = jnp.zeros((8, 128), jnp.float32)
    for m in range(16):
        table = jnp.where(lane == m, courant[m], table)
    return table * table * (1.0 / 12.0)


def pack(
    courant_in, now_in, prev_in, mat_in, early_1, early_2, side_1, side_2, now, prev, mat, courant, sems,
):
    up1, right1 = ways()
    copies = [
        pltpu.make_async_copy(src, dst, sems.at[n])
        for n, (src, dst) in enumerate(((courant_in, courant), (mat_in, mat), (now_in, now), (prev_in, prev)))
    ]
    for copy in copies:
        copy.start()
    upper_half = (lax.broadcasted_iota(jnp.int32, (8, 128), 0) >= 4).astype(jnp.int32)
    copies[0].wait()
    table = stiffness_table(courant)
    copies[1].wait()
    copies[2].wait()
    for slot, out in enumerate((early_1, early_2)):
        first = 6 * up1 if slot == 0 else 6 - 6 * up1
        for k in range(2):
            for i in range(T):
                lanes = slice(128 * i, 128 * i + 128)
                out[k, i] = now[first + k, :, lanes]
                for t in range(X // 8):
                    rows = slice(8 * t, 8 * t + 8)
                    out[2 + k, i, rows, :] = stiffness(table, mat[first + k, rows, lanes])
    copies[3].wait()
    for slot, out in enumerate((side_1, side_2)):
        right = right1 if slot == 0 else 1 - right1
        rows = pl.ds(pl.multiple_of((X - 8) * right, 8), 8)
        keep = upper_half == right
        for k in range(Z):
            for i in range(T):
                lanes = slice(128 * i, 128 * i + 128)
                out[k, i, 0:8, :] = now[k, rows, lanes]
                moved = pltpu.roll(stiffness(table, mat[k, rows, lanes]), 4, 0)
                out[k, i, 8:16, :] = jnp.where(keep, prev[k, rows, lanes], moved)


INNER = CORE + 8, X - 16
OUTER = ((CORE - 8, 16), (CORE + X - 8, 16))


def advance_inner(courant, now, prev, mat, now_out, stiff_out, one_out, prev_out, bands):
    table = stiffness_table(courant)
    bands[...] = band()
    zeros = jnp.zeros((T, ROWS, 128), jnp.float32)
    for k in (0, 1, Z + 2, Z + 3):
        now_out[k] = zeros
        one_out[k] = zeros

    def fill(k, carry):
        for i in range(T):
            now_out[k + 2, i, CORE : CORE + X, :] = now[k, :, 128 * i : 128 * i + 128]
        return carry

    lax.fori_loop(0, Z, fill, 0)

    def first(k, carry):
        for i in range(T):
            lanes = slice(128 * i, 128 * i + 128)
            prev_out[k, i, 0:8, :] = prev[k, 0:8, lanes]
            prev_out[k, i, 8:16, :] = prev[k, X - 8 : X, lanes]
            for t in range(X // 8):
                rows = slice(8 * t, 8 * t + 8)
                stiff_out[k, i, rows, :] = stiffness(table, mat[k, rows, lanes])
        for row, i, c, lap in full_rows(now_out, k + 2, *INNER, bands[...]):
            own = slice(row - CORE, row - CORE + 8)
            before = prev[k, own, 128 * i : 128 * i + 128]
            one_out[k + 2, i, row : row + 8, :] = 2.0 * c - before + stiff_out[k, i, own, :] * lap
        return carry

    lax.fori_loop(0, Z, first, 0, unroll=2)


def advance_outer(
    cell, start, bands, now_in, stiff_in, one_in, prev_in, lat_a, lat_b, now, one, now_side, stiff_side, two_out,
    prev_side,
):
    del now_in, one_in
    right1 = ways()[1] == 1

    def fill(k, carry):
        for i in range(T):
            for left in (False, True):
                wanted = jnp.logical_not(right1) if left else right1
                got = jnp.where(wanted, lat_a[k, i], lat_b[k, i])
                row = CORE - 8 if left else CORE + X
                half = slice(0, 8) if left else slice(8, 16)
                now[k + 2, i, row : row + 8, :] = got[0:8]
                now_side[k, i, half, :] = got[0:8]
                prev_side[k, i, half, :] = got[8:16]
                stiff_side[k, i, half, :] = pltpu.roll(got[8:16], 4, 0)
        return carry

    lax.fori_loop(0, Z, fill, 0)

    def first(k, carry):
        for part in OUTER:
            for row, i, c, lap in full_rows(now, k + 2, *part, bands[...]):
                if row < CORE or row == CORE + X:
                    half = slice(0, 8) if row < CORE else slice(8, 16)
                    before, stiff = prev_side[k, i, half, :], stiff_side[k, i, half, :]
                else:
                    half = slice(0, 8) if row == CORE else slice(8, 16)
                    before, stiff = prev_in[k, i, half, :], stiff_in[k, i, row - CORE : row - CORE + 8, :]
                one[k + 2, i, row : row + 8, :] = 2.0 * c - before + stiff * lap
        return carry

    lax.fori_loop(0, Z, first, 0, unroll=2)
    place = source_place(cell)
    strike(one, 2, place, wavelet(start, 0), Z, CORE - 8, CORE + X + 8)

    def second(n, carry):
        k = jnp.where(n < 2, n, n + 4)
        for row, i, c, lap in full_rows(one, k + 2, CORE, X, bands[...]):
            rows = slice(row, row + 8)
            stiff = stiff_in[k, i, row - CORE : row - CORE + 8, :]
            two_out[n, i, rows, :] = 2.0 * c - now[k + 2, i, rows, :] + stiff * lap
        return carry

    lax.fori_loop(0, 4, second, 0, unroll=2)
    z = place[0]
    inner = (z >= 2) & (z < Z - 2)
    strike(two_out, 0, (jnp.where(inner, -1, jnp.where(z < 2, z, z - 4)),) + place[1:], wavelet(start, 1), 4, CORE, CORE + X)


def pack_late(now_side, stiff_side, one, two, out_a, out_b):
    sub = lax.broadcasted_iota(jnp.int32, (8, 128), 0)
    left, right = slice(CORE - 8, CORE), slice(CORE + X, CORE + X + 8)
    up1 = ways()[0]
    for slot, out in ((0, out_a), (1, out_b)):
        high = up1 if slot == 0 else 1 - up1
        for k in range(2):
            z = (Z - 2) * high + k
            for i in range(T):
                out[k, i, 0:X, :] = one[z + 2, i, CORE : CORE + X, :]
                out[2 + k, i, 0:X, :] = two[2 * high + k, i, CORE : CORE + X, :]
                out[k, i, X : X + 8, :] = jnp.where(sub >= 4, now_side[z, i, 0:8, :], now_side[z, i, 8:16, :])
                ones = jnp.where(sub >= 4, one[z + 2, i, left, :], one[z + 2, i, right, :])
                side = jnp.where(sub >= 4, stiff_side[z, i, 0:8, :], stiff_side[z, i, 8:16, :])
                outer = (sub < 2) | (sub >= 6)
                out[2 + k, i, X : X + 8, :] = jnp.where(outer, ones, pltpu.roll(side, 4, 0))


def clamp_for_bumps(p):
    return jnp.minimum(jnp.maximum(p, -7.4), 7.4)


SIDES = ((False, 0, 1, 0, 0, 1, 0), (True, 2, 0, 1, Z - 1, Z - 2, Z + 2))


def halo_step(delta, one, halo_stiff, base, near, n_in, n_next, row, masks):
    rows, own = pl.ds(row, 8), pl.ds(row - CORE, 8)
    terms = {k: plane_terms(delta, base + k, row, masks) for k in range(2)}
    out = {}
    for i in range(T):
        for k in range(2):
            c, near_sum, far_sum = terms[k][i]
            near_sum = near_sum + terms[1 - k][i][0]
            if k == near:
                near_sum = near_sum + one[n_in + 2, i, rows, :]
                far_sum = far_sum + one[n_next + 2, i, rows, :]
            else:
                far_sum = far_sum + one[n_in + 2, i, rows, :]
            lap = 16.0 * near_sum - far_sum - 90.0 * c
            out[k, i] = 2.0 * c + halo_stiff[base + k, i, own, :] * lap
    return out


def couple(bands, now, stiff, one_in, early_a, early_b, sent, one, two, delta, halo_stiff, halo_two):
    del one_in, sent
    masks = lane_masks()
    up1 = ways()[0] == 1
    for high, base, near, far, n_in, n_next, zi in SIDES:
        use_a = up1 if high else jnp.logical_not(up1)

        def tile(t, carry, use_a=use_a, base=base, near=near, far=far, n_in=n_in, n_next=n_next, zi=zi):
            own, rows = pl.ds(pl.multiple_of(8 * t, 8), 8), pl.ds(pl.multiple_of(CORE + 8 * t, 8), 8)
            for i in range(T):
                zero_h = [jnp.where(use_a, early_a[k, i, own, :], early_b[k, i, own, :]) for k in range(2)]
                st_h = [jnp.where(use_a, early_a[2 + k, i, own, :], early_b[2 + k, i, own, :]) for k in range(2)]
                one[n_in + 2, i, rows, :] += stiff[n_in, i, own, :] * (16.0 * zero_h[near] - zero_h[far])
                one[n_next + 2, i, rows, :] -= stiff[n_next, i, own, :] * zero_h[near]
                d_near = st_h[near] * (16.0 * now[n_in + 2, i, rows, :] - now[n_next + 2, i, rows, :])
                d_far = -st_h[far] * now[n_in + 2, i, rows, :]
                for place, d, st in ((near, d_near, st_h[near]), (far, d_far, st_h[far])):
                    one[zi + place, i, rows, :] = d
                    delta[base + place, i, rows, :] = d
                    halo_stiff[base + place, i, own, :] = st
            return carry

        lax.fori_loop(0, X // 8, tile, 0)

    def second(k, carry):
        for row, i, c, lap in full_rows(one, k + 2, *INNER, bands[...]):
            rows, own = slice(row, row + 8), slice(row - CORE, row - CORE + 8)
            two[k + 2, i, rows, :] = 2.0 * c - now[k + 2, i, rows, :] + stiff[k, i, own, :] * lap
        return carry

    lax.fori_loop(0, Z, second, 0, unroll=2)
    for high, base, near, far, n_in, n_next, zi in SIDES:

        def beyond(t, carry, base=base, near=near, n_in=n_in, n_next=n_next):
            row = pl.multiple_of(CORE + 8 * t, 8)
            for (k, i), v in halo_step(delta, one, halo_stiff, base, near, n_in, n_next, row, masks).items():
                halo_two[base + k, i, pl.ds(pl.multiple_of(8 * t, 8), 8), :] = v
            return carry

        lax.fori_loop(1, X // 8 - 1, beyond, 0)


def finish(
    n_dep, cell, start, transfer, bands, now, stiff, now_side, stiff_side, one_in, two_in, delta_in, halo_stiff, halo_two,
    late_a, late_b, pressure, partial, one, two, delta, weights,
):
    del one_in, two_in, delta_in
    masks = lane_masks()
    up1 = ways()[0] == 1
    for n in range(4):
        for j in range(BUMPS):
            centre = (-3.0 + 6.0 * j / (BUMPS - 1)) / 0.8
            weights[n, j] = transfer[n, j] * (math.exp(-centre * centre) * (-LOG2E * 1.5 / (Z * n_dep) if n == 3 else 1.0))

    for high, base, near, far, n_in, n_next, zi in SIDES:
        use_a = up1 if high else jnp.logical_not(up1)

        def late_of(k, i, row, use_a=use_a):
            rows = pl.ds(row - CORE, 8)
            return jnp.where(use_a, late_a[k, i, rows, :], late_b[k, i, rows, :])

        for row in (CORE - 8, CORE + X):
            rows, half = slice(row, row + 8), slice(0, 8) if row < CORE else slice(8, 16)
            for i in range(T):
                zero_h = [late_of(k, i, CORE + X) for k in range(2)]
                one_h = [late_of(2 + k, i, CORE + X) for k in range(2)]
                st_h = [pltpu.roll(v, 4, 0) for v in one_h]
                one[n_in + 2, i, rows, :] += stiff_side[n_in, i, half, :] * (16.0 * zero_h[near] - zero_h[far])
                one[n_next + 2, i, rows, :] -= stiff_side[n_next, i, half, :] * zero_h[near]
                d_near = st_h[near] * (16.0 * now_side[n_in, i, half, :] - now_side[n_next, i, half, :])
                d_far = -st_h[far] * now_side[n_in, i, half, :]
                for at, d in ((near, d_near), (far, d_far)):
                    one[zi + at, i, rows, :] = one_h[at] + d
                    delta[base + at, i, rows, :] = d

        def inner(t, carry, base=base, near=near, far=far, n_in=n_in, n_next=n_next, zi=zi, late_of=late_of):
            row = pl.multiple_of(CORE + 8 * t, 8)
            rows, own = pl.ds(row, 8), pl.ds(pl.multiple_of(8 * t, 8), 8)
            for i in range(T):
                one_h = [late_of(k, i, row) for k in range(2)]
                for k in range(2):
                    one[zi + k, i, rows, :] += one_h[k]
                    two[zi + k, i, rows, :] = late_of(2 + k, i, row) + halo_two[base + k, i, own, :]
                two[n_in + 2, i, rows, :] += stiff[n_in, i, own, :] * (16.0 * one_h[near] - one_h[far])
                two[n_next + 2, i, rows, :] -= stiff[n_next, i, own, :] * one_h[near]
            return carry

        lax.fori_loop(0, X // 8, inner, 0)
        for row in (CORE, CORE + X - 8):
            for (k, i), v in halo_step(delta, one, halo_stiff, base, near, n_in, n_next, row, masks).items():
                two[zi + k, i, row : row + 8, :] = late_of(2 + k, i, row) + v

    def second(k, carry):
        for part in OUTER:
            for row, i, c, lap in full_rows(one, k + 2, *part, bands[...]):
                rows = slice(row, row + 8)
                if CORE <= row < CORE + X:
                    st = stiff[k, i, row - CORE : row - CORE + 8, :]
                else:
                    st = stiff_side[k, i, 0:8, :] if row < CORE else stiff_side[k, i, 8:16, :]
                two[k + 2, i, rows, :] = 2.0 * c - now[k + 2, i, rows, :] + st * lap
        return carry

    lax.fori_loop(0, Z, second, 0, unroll=2)
    place = source_place(cell)
    strike(two, 2, place, wavelet(start, 1), Z, CORE - 8, CORE + X + 8)

    def third(k, carry):
        for row, i, c, lap in full_rows(two, k + 2, CORE, X, bands[...]):
            rows, own = slice(row, row + 8), slice(row - CORE, row - CORE + 8)
            three = 2.0 * c - one[k + 2, i, rows, :] + stiff[k, i, own, :] * lap
            one[k + 2, i, rows, :] = three
        return carry

    lax.fori_loop(0, Z, third, 0, unroll=2)
    strike(one, 2, place, wavelet(start, 2), Z, CORE, CORE + X)

    group = lax.broadcasted_iota(jnp.int32, (8, 128), 1) // 32
    half = BUMPS // 2
    rate = 6.0 / (BUMPS - 1) / (0.8 * 0.8) * LOG2E

    def render(t, carry):
        rows = pl.ds(pl.multiple_of(CORE + 8 * t, 8), 8)
        own = pl.ds(pl.multiple_of(8 * t, 8), 8)
        for i in range(T):
            zero = jnp.zeros((8, 128), jnp.float32)
            seen = [zero] * BUMPS
            through = jnp.ones((8, 128), jnp.float32)
            depth = zero
            for k in range(Z):
                p = one[k + 2, i, rows, :]
                pressure[k, own, 128 * i : 128 * i + 128] = p
                p = clamp_for_bumps(p)
                gauss = jnp.exp2(p * p * (-LOG2E / 0.64))
                rise = jnp.exp2(p * rate)
                fall = jnp.exp2(p * -rate)
                up, down = rise * rise, fall * fall
                above, below = gauss * rise, gauss * fall
                a = weights[3, BUMPS - 1] * up + weights[3, BUMPS - 2]
                b = weights[3, 0] * down + weights[3, 1]
                for j in range(2, half):
                    a = a * up + weights[3, BUMPS - 1 - j]
                    b = b * down + weights[3, j]
                power = a * above + b * below
                stay = jnp.exp2(power)
                weight = through * (1.0 - stay)
                through = through * stay
                depth = depth + power
                above, below = weight * above, weight * below
                for j in range(half):
                    seen[half + j] = seen[half + j] + above
                    seen[half - 1 - j] = seen[half - 1 - j] + below
                    if j < half - 1:
                        above, below = above * up, below * down
            parts = []
            for n in range(3):
                colour = weights[n, 0] * seen[0]
                for j in range(1, BUMPS):
                    colour = colour + weights[n, j] * seen[j]
                parts.append(colour)
            parts.append(depth * (-1.0 / LOG2E))
            for q in range(4):
                packed = None
                for n in range(4):
                    shift = (32 * (n - q)) % 128
                    moved = parts[n] if shift == 0 else pltpu.roll(parts[n], shift, 1)
                    packed = moved if packed is None else jnp.where(group == n, moved, packed)
                partial[4 * i + q, own, :] = packed
        return carry

    lax.fori_loop(0, X // 8, render, 0)


def composite(parts, image):
    group = lax.broadcasted_iota(jnp.int32, (X, 128), 1) // 32
    before = jnp.zeros((X, 128), jnp.float32)
    total = jnp.zeros((X, 128), jnp.float32)
    for d in range(parts.shape[0]):
        v = parts[d]
        total = total + jnp.exp(-before) * v
        depth = v
        for n in range(3):
            depth = jnp.where(group == n, pltpu.roll(v, 32 * (n + 1), 1), depth)
        before = before + depth
    image[...] = jnp.where(group == 3, 1.0 - jnp.exp(-before), total).T


def swaps(n_lat, n_dep, kind):
    out = []
    for lat in range(n_lat):
        for dep in range(n_dep):
            other_lat, other_dep = lat, dep
            if kind in ("d1", "d2"):
                up = ((lat % 2 == 0) == (dep % 2 == 0)) == (kind == "d1")
                other_dep = dep + 1 if up else dep - 1
            else:
                right = (lat % 2 == 0) == (kind == "l1")
                other_lat = lat + 1 if right else lat - 1
            if 0 <= other_lat < n_lat and 0 <= other_dep < n_dep:
                out.append((lat * n_dep + dep, other_lat * n_dep + other_dep))
    return out


def on_device(n_lat, n_dep, pressure_prev, pressure_now, materials, courant_table, tf_weights, source_cell, start_step):
    f32 = jnp.float32

    def swap(v, kind):
        return lax.ppermute(v, ("lat", "dep"), swaps(n_lat, n_dep, kind))

    def busy(microseconds):
        return pl.CostEstimate(
            flops=int(microseconds * 1.0e9), bytes_accessed=int(microseconds * 3.0e6), transcendentals=0
        )

    def shape(*dims):
        return jax.ShapeDtypeStruct(dims, f32)

    def kept(*dims):
        return pltpu.VMEM(dims, f32)

    def in_hbm(v):
        return pltpu.with_memory_space_constraint(v, pltpu.HBM)

    params = pltpu.CompilerParams(vmem_limit_bytes=24 * 1024 * 1024)
    i32 = jnp.int32
    blocks = [pltpu.VMEM((Z, X, 512), d) for d in (f32, f32, i32)]
    early_1, early_2, side_1, side_2, *inputs = pl.pallas_call(
        pack,
        in_specs=[HBM] * 4,
        out_specs=[VMEM] * 7,
        out_shape=[kept(4, T, X, 128)] * 2 + [kept(Z, T, 16, 128)] * 2 + blocks,
        scratch_shapes=[pltpu.SMEM((16,), f32), pltpu.SemaphoreType.DMA((4,))],
        compiler_params=params,
        name="pack",
    )(*(in_hbm(v) for v in (courant_table, pressure_now, pressure_prev, materials)))
    side_a = swap(side_1, "l1")
    side_b = swap(side_2, "l2")
    early_a = swap(early_1, "d1")
    early_b = swap(early_2, "d2")

    padded = (Z + 4, T, ROWS, 128)
    bands = pltpu.VMEM((512, 256), jnp.bfloat16)
    block, side = (Z, T, X, 128), (Z, T, 16, 128)
    now, stiff, one, prev, bands_made = pl.pallas_call(
        advance_inner,
        in_specs=[SMEM] + [VMEM] * 3,
        out_specs=[VMEM] * 5,
        out_shape=[kept(*padded), kept(*block), kept(*padded), kept(*side), bands],
        compiler_params=params,
        cost_estimate=busy(3.0),
        name="advance_inner",
    )(courant_table, *inputs)
    now, one, now_side, stiff_side, two = pl.pallas_call(
        advance_outer,
        in_specs=[SMEM] * 2 + [VMEM] * 7,
        out_specs=[VMEM] * 5,
        out_shape=[kept(*padded)] * 2 + [kept(*side)] * 2 + [kept(4, T, ROWS, 128)],
        scratch_shapes=[pltpu.VMEM(side, f32)],
        input_output_aliases={3: 0, 5: 1},
        compiler_params=params,
        cost_estimate=busy(5.0),
        name="advance_outer",
    )(source_cell, start_step, bands_made, now, stiff, one, prev, side_a, side_b)
    late_1, late_2 = pl.pallas_call(
        pack_late,
        in_specs=[VMEM] * 4,
        out_specs=[VMEM] * 2,
        out_shape=[kept(4, T, X + 8, 128)] * 2,
        compiler_params=params,
        name="pack_late",
    )(now_side, stiff_side, one, two)
    late_a = swap(late_1, "d1")
    late_b = swap(late_2, "d2")
    one, two, delta, halo_stiff, halo_two = pl.pallas_call(
        couple,
        in_specs=[VMEM] * 6 + [pl.BlockSpec(memory_space=pl.ANY)],
        out_specs=[VMEM] * 5,
        out_shape=[kept(*padded)] * 2 + [kept(4, T, ROWS, 128)] + [kept(4, T, X, 128)] * 2,
        input_output_aliases={3: 0},
        compiler_params=params,
        cost_estimate=busy(4.0),
        name="couple",
    )(bands_made, now, stiff, one, early_a, early_b, late_1)
    pressure, partial, _, _, _ = pl.pallas_call(
        functools.partial(finish, n_dep),
        in_specs=[SMEM] * 3 + [VMEM] * 12,
        out_specs=[VMEM] * 5,
        out_shape=[shape(Z, X, 512), shape(n_dep, X, 128)] + [kept(*padded)] * 2 + [kept(4, T, ROWS, 128)],
        scratch_shapes=[pltpu.SMEM((4, BUMPS), f32)],
        input_output_aliases={8: 2, 9: 3, 10: 4},
        compiler_params=params,
        name="finish",
    )(
        source_cell, start_step, tf_weights, bands_made, now, stiff, now_side, stiff_side, one, two, delta, halo_stiff,
        halo_two, late_a, late_b,
    )
    parts = lax.all_to_all(partial, "dep", 0, 0, tiled=True)
    image = pl.pallas_call(
        composite,
        in_specs=[VMEM],
        out_specs=VMEM,
        out_shape=shape(128, X),
        compiler_params=params,
        name="composite",
    )(parts)
    return pressure, jnp.swapaxes(image.reshape(4, 512 // n_dep, X), 1, 2)


def solution(mesh):
    block = P("dep", "lat", None)
    return jax.shard_map(
        functools.partial(on_device, mesh.shape["lat"], mesh.shape["dep"]),
        mesh=mesh,
        in_specs=(block, block, block, P(), P(), P(), P()),
        out_specs=(block, P(None, "lat", "dep")),
        check_vma=False,
    )
```

```python
import functools
import math

import jax
import jax.numpy as jnp
from jax import lax
from jax.experimental import pallas as pl
from jax.experimental.pallas import tpu as pltpu
from jax.sharding import PartitionSpec as P

BUMPS = 8
LOG2E = math.log2(math.e)
Z, X, T = 8, 64, 4
ROWS = X + 32
CORE = 16
VMEM = pl.BlockSpec(memory_space=pltpu.VMEM)
SMEM = pl.BlockSpec(memory_space=pltpu.SMEM)
HBM = pl.BlockSpec(memory_space=pltpu.HBM)


def lane_masks():
    lane = lax.broadcasted_iota(jnp.int32, (8, 128), 1)
    return lane < 1, lane < 2, lane >= 127, lane >= 126


def columns_sum(c, masks):
    zero = jnp.zeros((8, 128), jnp.float32)
    low1, low2, high1, high2 = masks
    a1 = [pltpu.roll(v, 1, 1) for v in c]
    a2 = [pltpu.roll(v, 2, 1) for v in c]
    b1 = [pltpu.roll(v, 127, 1) for v in c]
    b2 = [pltpu.roll(v, 126, 1) for v in c]
    out = []
    for i in range(T):
        first, last = i == 0, i == T - 1
        near = jnp.where(low1, zero if first else a1[i - 1], a1[i]) + jnp.where(
            high1, zero if last else b1[i + 1], b1[i]
        )
        far = jnp.where(low2, zero if first else a2[i - 1], a2[i]) + jnp.where(
            high2, zero if last else b2[i + 1], b2[i]
        )
        out.append((near, far))
    return out


def plane_terms(ref, k, row, masks):
    c = [ref[k, i, pl.ds(row, 8), :] for i in range(T)]
    sums = columns_sum(c, masks)
    out = []
    for i in range(T):
        near = sums[i][0] + (ref[k, i, pl.ds(row - 1, 8), :] + ref[k, i, pl.ds(row + 1, 8), :])
        far = sums[i][1] + (ref[k, i, pl.ds(row - 2, 8), :] + ref[k, i, pl.ds(row + 2, 8), :])
        out.append((c[i], near, far))
    return out


def band():
    shape = (512, 256)
    d = jnp.abs(lax.broadcasted_iota(jnp.int32, shape, 0) % 256 - lax.broadcasted_iota(jnp.int32, shape, 1))
    return jnp.where(d == 0, -90.0, jnp.where(d == 1, 16.0, jnp.where(d == 2, -1.0, 0.0))).astype(jnp.bfloat16)


def full_rows(ref, k, first, count, bands):
    rows = slice(first, first + count)
    factors = []
    for h in range(2):
        v = jnp.concatenate([ref[k, 2 * h, rows, :], ref[k, 2 * h + 1, rows, :]], axis=1)
        high = v.astype(jnp.bfloat16)
        low = (v - high.astype(jnp.float32)).astype(jnp.bfloat16)
        factors.append(jnp.concatenate([high, low], axis=1))
    product = jnp.dot(jnp.concatenate(factors, axis=0), bands, preferred_element_type=jnp.float32)
    low1, low2, high1, high2 = lane_masks()
    for r in range(0, count, 8):
        row = first + r
        here = slice(row, row + 8)
        for i in range(T):
            c = ref[k, i, here, :]
            inside = product[count * (i // 2) + r : count * (i // 2) + r + 8, 128 * (i % 2) : 128 * (i % 2) + 128]
            near = ref[k, i, row - 1 : row + 7, :] + ref[k, i, row + 1 : row + 9, :]
            far = ref[k, i, row - 2 : row + 6, :] + ref[k, i, row + 2 : row + 10, :]
            near = near + (ref[k - 1, i, here, :] + ref[k + 1, i, here, :])
            far = far + (ref[k - 2, i, here, :] + ref[k + 2, i, here, :])
            if i == 1:
                v = ref[k, 2, here, :]
                near = near + jnp.where(high1, pltpu.roll(v, 127, 1), 0.0)
                far = far + jnp.where(high2, pltpu.roll(v, 126, 1), 0.0)
            if i == 2:
                v = ref[k, 1, here, :]
                near = near + jnp.where(low1, pltpu.roll(v, 1, 1), 0.0)
                far = far + jnp.where(low2, pltpu.roll(v, 2, 1), 0.0)
            yield row, i, c, inside + (16.0 * near - far)


def strike(ref, outer, place, amplitude, layers, rows):
    z, x, y = place
    row = x + CORE
    inside = functools.reduce(jnp.logical_or, [(row >= first) & (row < end) for first, end in rows])

    @pl.when((z >= layers[0]) & (z < layers[1]) & inside)
    def _():
        tile, lane = y // 128, y % 128
        old = ref[z + outer, tile, pl.ds(row, 1), :]
        ids = lax.broadcasted_iota(jnp.int32, (1, 128), 1)
        ref[z + outer, tile, pl.ds(row, 1), :] = old + jnp.where(ids == lane, amplitude, 0.0)


def stiffness(table, materials):
    return jnp.take_along_axis(table, materials, axis=1, mode="promise_in_bounds")


def ways():
    return (lax.axis_index("dep") + 1) % 2, (lax.axis_index("lat") + 1) % 2


def source_place(cell):
    return cell[0] - lax.axis_index("dep") * Z, cell[1] - lax.axis_index("lat") * X, cell[2]


def wavelet(start, step):
    level = jnp.full((1, 128), start[0] + step, jnp.int32).astype(jnp.float32)
    shifted = 0.3 * (level - 10.0)
    return 4.0 * (1.0 - 2.0 * shifted * shifted) * jnp.exp(-shifted * shifted)


def stiffness_table(courant):
    lane = lax.broadcasted_iota(jnp.int32, (8, 128), 1)
    table = jnp.zeros((8, 128), jnp.float32)
    for m in range(16):
        table = jnp.where(lane == m, courant[m], table)
    return table * table * (1.0 / 12.0)


def pack(
    courant_in, now_in, prev_in, mat_in, early_1, early_2, side_1, side_2, now, prev, mat, courant, sems,
):
    up1, right1 = ways()
    copies = [
        pltpu.make_async_copy(src, dst, sems.at[n])
        for n, (src, dst) in enumerate(((courant_in, courant), (mat_in, mat), (now_in, now), (prev_in, prev)))
    ]
    for copy in copies:
        copy.start()
    upper_half = (lax.broadcasted_iota(jnp.int32, (8, 128), 0) >= 4).astype(jnp.int32)
    copies[0].wait()
    table = stiffness_table(courant)
    copies[1].wait()
    copies[2].wait()
    for slot, out in enumerate((early_1, early_2)):
        first = 6 * up1 if slot == 0 else 6 - 6 * up1
        for k in range(2):
            for i in range(T):
                lanes = slice(128 * i, 128 * i + 128)
                out[k, i] = now[first + k, :, lanes]
                for t in range(X // 8):
                    rows = slice(8 * t, 8 * t + 8)
                    out[2 + k, i, rows, :] = stiffness(table, mat[first + k, rows, lanes])
    copies[3].wait()
    for slot, out in enumerate((side_1, side_2)):
        right = right1 if slot == 0 else 1 - right1
        rows = pl.ds(pl.multiple_of((X - 8) * right, 8), 8)
        keep = upper_half == right
        for k in range(Z):
            for i in range(T):
                lanes = slice(128 * i, 128 * i + 128)
                out[k, i, 0:8, :] = now[k, rows, lanes]
                moved = pltpu.roll(stiffness(table, mat[k, rows, lanes]), 4, 0)
                out[k, i, 8:16, :] = jnp.where(keep, prev[k, rows, lanes], moved)


INNER = CORE + 8, X - 16
OUTER = ((CORE - 8, 16), (CORE + X - 8, 16))


def advance_inner(courant, now, prev, mat, now_out, stiff_out, one_out, prev_out, bands):
    table = stiffness_table(courant)
    bands[...] = band()
    zeros = jnp.zeros((T, ROWS, 128), jnp.float32)
    for k in (0, 1, Z + 2, Z + 3):
        now_out[k] = zeros
        one_out[k] = zeros

    def fill(k, carry):
        for i in range(T):
            now_out[k + 2, i, CORE : CORE + X, :] = now[k, :, 128 * i : 128 * i + 128]
        return carry

    lax.fori_loop(0, Z, fill, 0)

    def first(k, carry):
        for i in range(T):
            lanes = slice(128 * i, 128 * i + 128)
            prev_out[k, i, 0:8, :] = prev[k, 0:8, lanes]
            prev_out[k, i, 8:16, :] = prev[k, X - 8 : X, lanes]
            for t in range(X // 8):
                rows = slice(8 * t, 8 * t + 8)
                stiff_out[k, i, rows, :] = stiffness(table, mat[k, rows, lanes])
        for row, i, c, lap in full_rows(now_out, k + 2, *INNER, bands[...]):
            own = slice(row - CORE, row - CORE + 8)
            before = prev[k, own, 128 * i : 128 * i + 128]
            one_out[k + 2, i, row : row + 8, :] = 2.0 * c - before + stiff_out[k, i, own, :] * lap
        return carry

    lax.fori_loop(0, Z, first, 0, unroll=2)


def advance_outer(
    cell, start, bands, now_in, stiff_in, one_in, prev_in, lat_a, lat_b, now, one, now_side, stiff_side, two_out,
    prev_side,
):
    del now_in, one_in
    right1 = ways()[1] == 1

    def fill(k, carry):
        for i in range(T):
            for left in (False, True):
                wanted = jnp.logical_not(right1) if left else right1
                got = jnp.where(wanted, lat_a[k, i], lat_b[k, i])
                row = CORE - 8 if left else CORE + X
                half = slice(0, 8) if left else slice(8, 16)
                now[k + 2, i, row : row + 8, :] = got[0:8]
                now_side[k, i, half, :] = got[0:8]
                prev_side[k, i, half, :] = got[8:16]
                stiff_side[k, i, half, :] = pltpu.roll(got[8:16], 4, 0)
        return carry

    lax.fori_loop(0, Z, fill, 0)

    def first(k, carry):
        for part in OUTER:
            for row, i, c, lap in full_rows(now, k + 2, *part, bands[...]):
                if row < CORE or row == CORE + X:
                    half = slice(0, 8) if row < CORE else slice(8, 16)
                    before, stiff = prev_side[k, i, half, :], stiff_side[k, i, half, :]
                else:
                    half = slice(0, 8) if row == CORE else slice(8, 16)
                    before, stiff = prev_in[k, i, half, :], stiff_in[k, i, row - CORE : row - CORE + 8, :]
                one[k + 2, i, row : row + 8, :] = 2.0 * c - before + stiff * lap
        return carry

    lax.fori_loop(0, Z, first, 0, unroll=2)
    place = source_place(cell)
    strike(one, 2, place, wavelet(start, 0), (0, Z), [(CORE - 8, CORE + X + 8)])

    def second(n, carry):
        k = jnp.where(n < 2, n, n + 4)
        for row, i, c, lap in full_rows(one, k + 2, CORE, X, bands[...]):
            rows = slice(row, row + 8)
            stiff = stiff_in[k, i, row - CORE : row - CORE + 8, :]
            two_out[n, i, rows, :] = 2.0 * c - now[k + 2, i, rows, :] + stiff * lap
        return carry

    lax.fori_loop(0, 4, second, 0, unroll=2)
    z = place[0]
    inner = (z >= 2) & (z < Z - 2)
    place = (jnp.where(inner, -1, jnp.where(z < 2, z, z - 4)),) + place[1:]
    strike(two_out, 0, place, wavelet(start, 1), (0, 4), [(CORE, CORE + X)])


def pack_late(now_side, stiff_side, one, two, out_a, out_b):
    sub = lax.broadcasted_iota(jnp.int32, (8, 128), 0)
    left, right = slice(CORE - 8, CORE), slice(CORE + X, CORE + X + 8)
    up1 = ways()[0]
    for slot, out in ((0, out_a), (1, out_b)):
        high = up1 if slot == 0 else 1 - up1
        for k in range(2):
            z = (Z - 2) * high + k
            for i in range(T):
                out[k, i, 0:X, :] = one[z + 2, i, CORE : CORE + X, :]
                out[2 + k, i, 0:X, :] = two[2 * high + k, i, CORE : CORE + X, :]
                out[k, i, X : X + 8, :] = jnp.where(sub >= 4, now_side[z, i, 0:8, :], now_side[z, i, 8:16, :])
                ones = jnp.where(sub >= 4, one[z + 2, i, left, :], one[z + 2, i, right, :])
                side = jnp.where(sub >= 4, stiff_side[z, i, 0:8, :], stiff_side[z, i, 8:16, :])
                outer = (sub < 2) | (sub >= 6)
                out[2 + k, i, X : X + 8, :] = jnp.where(outer, ones, pltpu.roll(side, 4, 0))


def clamp_for_bumps(p):
    return jnp.minimum(jnp.maximum(p, -7.4), 7.4)


SIDES = ((False, 0, 1, 0, 0, 1, 0), (True, 2, 0, 1, Z - 1, Z - 2, Z + 2))


def halo_step(delta, one, halo_stiff, base, near, far, n_in, n_next, row, masks):
    rows, own = pl.ds(row, 8), pl.ds(row - CORE, 8)
    close, distant = plane_terms(delta, base + near, row, masks), plane_terms(delta, base + far, row, masks)
    for i in range(T):
        inner, following = one[n_in + 2, i, rows, :], one[n_next + 2, i, rows, :]
        for place, (c, near_sum, far_sum), (other, _, _), first, second in (
            (near, close[i], distant[i], inner, following),
            (far, distant[i], close[i], None, inner),
        ):
            near_sum = near_sum + other
            if first is not None:
                near_sum = near_sum + first
            lap = 16.0 * near_sum - (far_sum + second) - 90.0 * c
            yield place, i, 2.0 * c + halo_stiff[base + place, i, own, :] * lap


def couple(cell, start, bands, now, stiff, one_in, early_a, early_b, sent, one, two, delta, halo_stiff, halo_two):
    del one_in, sent
    masks = lane_masks()
    up1 = ways()[0] == 1
    for high, base, near, far, n_in, n_next, zi in SIDES:
        use_a = up1 if high else jnp.logical_not(up1)

        def tile(t, carry, use_a=use_a, base=base, near=near, far=far, n_in=n_in, n_next=n_next, zi=zi):
            own, rows = pl.ds(pl.multiple_of(8 * t, 8), 8), pl.ds(pl.multiple_of(CORE + 8 * t, 8), 8)
            for i in range(T):
                zero_h = [jnp.where(use_a, early_a[k, i, own, :], early_b[k, i, own, :]) for k in range(2)]
                st_h = [jnp.where(use_a, early_a[2 + k, i, own, :], early_b[2 + k, i, own, :]) for k in range(2)]
                one[n_in + 2, i, rows, :] += stiff[n_in, i, own, :] * (16.0 * zero_h[near] - zero_h[far])
                one[n_next + 2, i, rows, :] -= stiff[n_next, i, own, :] * zero_h[near]
                d_near = st_h[near] * (16.0 * now[n_in + 2, i, rows, :] - now[n_next + 2, i, rows, :])
                d_far = -st_h[far] * now[n_in + 2, i, rows, :]
                for place, d, st in ((near, d_near, st_h[near]), (far, d_far, st_h[far])):
                    one[zi + place, i, rows, :] = d
                    delta[base + place, i, rows, :] = d
                    halo_stiff[base + place, i, own, :] = st
            return carry

        lax.fori_loop(0, X // 8, tile, 0)

    def second(k, carry):
        for row, i, c, lap in full_rows(one, k + 2, *INNER, bands[...]):
            rows, own = slice(row, row + 8), slice(row - CORE, row - CORE + 8)
            two[k + 2, i, rows, :] = 2.0 * c - now[k + 2, i, rows, :] + stiff[k, i, own, :] * lap
        return carry

    lax.fori_loop(0, Z, second, 0, unroll=2)
    strike(two, 2, source_place(cell), wavelet(start, 1), (0, Z), [(CORE + 8, CORE + X - 8)])
    for high, base, near, far, n_in, n_next, zi in SIDES:

        def beyond(t, carry, base=base, near=near, far=far, n_in=n_in, n_next=n_next):
            row = pl.multiple_of(CORE + 8 * t, 8)
            for k, i, v in halo_step(delta, one, halo_stiff, base, near, far, n_in, n_next, row, masks):
                halo_two[base + k, i, pl.ds(pl.multiple_of(8 * t, 8), 8), :] = v
            return carry

        lax.fori_loop(1, X // 8 - 1, beyond, 0)


def complete(second_half, cell, start, bands, stiff, now, now_side, stiff_side, one, two, delta, halo_stiff, halo_two, late, three):
    masks = lane_masks()
    place = source_place(cell)
    high = 1 - ways()[0] if second_half else ways()[0]
    base, near, far, n_in, n_next, zi = 2 * high, 1 - high, high, (Z - 1) * high, 1 + (Z - 3) * high, (Z + 2) * high

    extra = slice(X, X + 8)
    for row in (CORE - 8, CORE + X):
        rows, half = slice(row, row + 8), slice(0, 8) if row < CORE else slice(8, 16)
        for i in range(T):
            zero_near, zero_far = late[near, i, extra, :], late[far, i, extra, :]
            one[n_in + 2, i, rows, :] += stiff_side[n_in, i, half, :] * (16.0 * zero_near - zero_far)
            one[n_next + 2, i, rows, :] -= stiff_side[n_next, i, half, :] * zero_near
            first, second = now_side[n_in, i, half, :], now_side[n_next, i, half, :]
            for at, term in ((near, 16.0 * first - second), (far, -first)):
                v = late[2 + at, i, extra, :]
                d = pltpu.roll(v, 4, 0) * term
                one[zi + at, i, rows, :] = v + d
                delta[base + at, i, rows, :] = d

    def inner(t, carry):
        row = pl.multiple_of(CORE + 8 * t, 8)
        rows, own = pl.ds(row, 8), pl.ds(pl.multiple_of(8 * t, 8), 8)
        for i in range(T):
            one_near, one_far = late[near, i, own, :], late[far, i, own, :]
            one[zi + near, i, rows, :] += one_near
            one[zi + far, i, rows, :] += one_far
            for k in range(2):
                two[zi + k, i, rows, :] = late[2 + k, i, own, :] + halo_two[base + k, i, own, :]
            two[n_in + 2, i, rows, :] += stiff[n_in, i, own, :] * (16.0 * one_near - one_far)
            two[n_next + 2, i, rows, :] -= stiff[n_next, i, own, :] * one_near
        return carry

    lax.fori_loop(0, X // 8, inner, 0)
    for row in (CORE, CORE + X - 8):
        for k, i, v in halo_step(delta, one, halo_stiff, base, near, far, n_in, n_next, row, masks):
            two[zi + k, i, row : row + 8, :] = late[2 + k, i, row - CORE : row - CORE + 8, :] + v

    count = 4 if second_half else 6
    lowest = (Z - count) * high

    def second(n, carry):
        k = lowest + n
        for part in OUTER:
            for row, i, c, lap in full_rows(one, k + 2, *part, bands[...]):
                rows = slice(row, row + 8)
                if CORE <= row < CORE + X:
                    st = stiff[k, i, row - CORE : row - CORE + 8, :]
                else:
                    st = stiff_side[k, i, 0:8, :] if row < CORE else stiff_side[k, i, 8:16, :]
                two[k + 2, i, rows, :] = 2.0 * c - now[k + 2, i, rows, :] + st * lap
        return carry

    lax.fori_loop(0, count, second, 0, unroll=2)
    outer = [(CORE - 8, CORE + 8), (CORE + X - 8, CORE + X + 8)]
    strike(two, 2, place, wavelet(start, 1), (lowest, lowest + count), outer)

    def third(n, carry):
        k = 4 * high + n
        for row, i, c, lap in full_rows(two, k + 2, CORE, X, bands[...]):
            own = slice(row - CORE, row - CORE + 8)
            before = one[k + 2, i, row : row + 8, :]
            three[n, own, 128 * i : 128 * i + 128] = 2.0 * c - before + stiff[k, i, own, :] * lap
        return carry

    lax.fori_loop(0, 4, third, 0, unroll=2)
    z, x, y = place
    n = z - 4 * high

    @pl.when((n >= 0) & (n < 4) & (x >= 0) & (x < X))
    def _():
        ids = lax.broadcasted_iota(jnp.int32, (1, 512), 1)
        amplitude = jnp.concatenate([wavelet(start, 2)] * T, axis=1)
        three[n, pl.ds(x, 1), :] = three[n, pl.ds(x, 1), :] + jnp.where(ids == y, amplitude, 0.0)


def weigh(n_dep, transfer, weights):
    for n in range(4):
        for j in range(BUMPS):
            centre = (-3.0 + 6.0 * j / (BUMPS - 1)) / 0.8
            weights[n, j] = transfer[n, j] * (math.exp(-centre * centre) * (-LOG2E * 1.5 / (Z * n_dep) if n == 3 else 1.0))


def look(weights, three, i, own):
    half = BUMPS // 2
    rate = 6.0 / (BUMPS - 1) / (0.8 * 0.8) * LOG2E
    zero = jnp.zeros((8, 128), jnp.float32)
    seen = [zero] * BUMPS
    through = jnp.ones((8, 128), jnp.float32)
    depth = zero
    for n in range(4):
        p = clamp_for_bumps(three[n, own, 128 * i : 128 * i + 128])
        gauss = jnp.exp2(p * p * (-LOG2E / 0.64))
        rise = jnp.exp2(p * rate)
        fall = jnp.exp2(p * -rate)
        up, down = rise * rise, fall * fall
        above, below = gauss * rise, gauss * fall
        a = weights[3, BUMPS - 1] * up + weights[3, BUMPS - 2]
        b = weights[3, 0] * down + weights[3, 1]
        for j in range(2, half):
            a = a * up + weights[3, BUMPS - 1 - j]
            b = b * down + weights[3, j]
        power = a * above + b * below
        stay = jnp.exp2(power)
        weight = through * (1.0 - stay)
        through = through * stay
        depth = depth + power
        above, below = weight * above, weight * below
        for j in range(half):
            seen[half + j] = seen[half + j] + above
            seen[half - 1 - j] = seen[half - 1 - j] + below
            if j < half - 1:
                above, below = above * up, below * down
    return seen, through, depth


def finish_first(
    n_dep, cell, start, transfer, bands, now, stiff, now_side, stiff_side, one_in, two_in, delta_in, halo_stiff, halo_two,
    late, three, looked, one, two, delta, weights,
):
    del one_in, two_in, delta_in
    weigh(n_dep, transfer, weights)
    complete(False, cell, start, bands, stiff, now, now_side, stiff_side, one, two, delta, halo_stiff, halo_two, late, three)

    def render(t, carry):
        own = pl.ds(pl.multiple_of(8 * t, 8), 8)
        for i in range(T):
            seen, through, depth = look(weights, three, i, own)
            for j, v in enumerate(seen + [through, depth]):
                looked[j, i, own, :] = v
        return carry

    lax.fori_loop(0, X // 8, render, 0)


def finish_second(
    n_dep, cell, start, transfer, bands, now, stiff, now_side, stiff_side, one_in, two_in, delta_in, halo_stiff, halo_two,
    late, other, looked, pressure, partial, one, two, delta, weights, three, sems,
):
    del one_in, two_in, delta_in
    high = 1 - ways()[0]
    copies = [
        pltpu.make_async_copy(other, pressure.at[pl.ds(4 - 4 * high, 4)], sems.at[0]),
        pltpu.make_async_copy(three, pressure.at[pl.ds(4 * high, 4)], sems.at[1]),
    ]
    copies[0].start()
    weigh(n_dep, transfer, weights)
    complete(True, cell, start, bands, stiff, now, now_side, stiff_side, one, two, delta, halo_stiff, halo_two, late, three)
    copies[1].start()
    group = lax.broadcasted_iota(jnp.int32, (8, 128), 1) // 32
    behind = high == 1

    def render(t, carry):
        own = pl.ds(pl.multiple_of(8 * t, 8), 8)
        for i in range(T):
            seen, through, depth = look(weights, three, i, own)
            mine = jnp.where(behind, looked[BUMPS, i, own, :], 1.0)
            others = jnp.where(behind, 1.0, through)
            seen = [mine * seen[j] + others * looked[j, i, own, :] for j in range(BUMPS)]
            depth = depth + looked[BUMPS + 1, i, own, :]
            parts = []
            for n in range(3):
                colour = weights[n, 0] * seen[0]
                for j in range(1, BUMPS):
                    colour = colour + weights[n, j] * seen[j]
                parts.append(colour)
            parts.append(depth * (-1.0 / LOG2E))
            for q in range(4):
                packed = None
                for n in range(4):
                    shift = (32 * (n - q)) % 128
                    moved = parts[n] if shift == 0 else pltpu.roll(parts[n], shift, 1)
                    packed = moved if packed is None else jnp.where(group == n, moved, packed)
                partial[4 * i + q, own, :] = packed
        return carry

    lax.fori_loop(0, X // 8, render, 0)
    for copy in copies:
        copy.wait()


def composite(parts, image):
    group = lax.broadcasted_iota(jnp.int32, (X, 128), 1) // 32
    before = jnp.zeros((X, 128), jnp.float32)
    total = jnp.zeros((X, 128), jnp.float32)
    for d in range(parts.shape[0]):
        v = parts[d]
        total = total + jnp.exp(-before) * v
        depth = v
        for n in range(3):
            depth = jnp.where(group == n, pltpu.roll(v, 32 * (n + 1), 1), depth)
        before = before + depth
    image[...] = jnp.where(group == 3, 1.0 - jnp.exp(-before), total).T


def swaps(n_lat, n_dep, kind):
    out = []
    for lat in range(n_lat):
        for dep in range(n_dep):
            other_lat, other_dep = lat, dep
            if kind in ("d1", "d2"):
                up = (dep % 2 == 0) == (kind == "d1")
                other_dep = dep + 1 if up else dep - 1
            else:
                right = (lat % 2 == 0) == (kind == "l1")
                other_lat = lat + 1 if right else lat - 1
            if 0 <= other_lat < n_lat and 0 <= other_dep < n_dep:
                out.append((lat * n_dep + dep, other_lat * n_dep + other_dep))
    return out


def on_device(n_lat, n_dep, pressure_prev, pressure_now, materials, courant_table, tf_weights, source_cell, start_step):
    f32 = jnp.float32

    def swap(v, kind):
        return lax.ppermute(v, ("lat", "dep"), swaps(n_lat, n_dep, kind))

    def busy(microseconds):
        return pl.CostEstimate(
            flops=int(microseconds * 1.0e9), bytes_accessed=int(microseconds * 3.0e6), transcendentals=0
        )

    def shape(*dims):
        return jax.ShapeDtypeStruct(dims, f32)

    def kept(*dims):
        return pltpu.VMEM(dims, f32)

    def in_hbm(v):
        return pltpu.with_memory_space_constraint(v, pltpu.HBM)

    params = pltpu.CompilerParams(vmem_limit_bytes=24 * 1024 * 1024)
    i32 = jnp.int32
    blocks = [pltpu.VMEM((Z, X, 512), d) for d in (f32, f32, i32)]
    early_1, early_2, side_1, side_2, *inputs = pl.pallas_call(
        pack,
        in_specs=[HBM] * 4,
        out_specs=[VMEM] * 7,
        out_shape=[kept(4, T, X, 128)] * 2 + [kept(Z, T, 16, 128)] * 2 + blocks,
        scratch_shapes=[pltpu.SMEM((16,), f32), pltpu.SemaphoreType.DMA((4,))],
        compiler_params=params,
        name="pack",
    )(*(in_hbm(v) for v in (courant_table, pressure_now, pressure_prev, materials)))
    side_a = swap(side_1, "l1")
    side_b = swap(side_2, "l2")
    early_a = swap(early_1, "d1")
    early_b = swap(early_2, "d2")

    padded = (Z + 4, T, ROWS, 128)
    bands = pltpu.VMEM((512, 256), jnp.bfloat16)
    block, side = (Z, T, X, 128), (Z, T, 16, 128)
    now, stiff, one, prev, bands_made = pl.pallas_call(
        advance_inner,
        in_specs=[SMEM] + [VMEM] * 3,
        out_specs=[VMEM] * 5,
        out_shape=[kept(*padded), kept(*block), kept(*padded), kept(*side), bands],
        compiler_params=params,
        cost_estimate=busy(3.0),
        name="advance_inner",
    )(courant_table, *inputs)
    now, one, now_side, stiff_side, two = pl.pallas_call(
        advance_outer,
        in_specs=[SMEM] * 2 + [VMEM] * 7,
        out_specs=[VMEM] * 5,
        out_shape=[kept(*padded)] * 2 + [kept(*side)] * 2 + [kept(4, T, ROWS, 128)],
        scratch_shapes=[pltpu.VMEM(side, f32)],
        input_output_aliases={3: 0, 5: 1},
        compiler_params=params,
        cost_estimate=busy(5.0),
        name="advance_outer",
    )(source_cell, start_step, bands_made, now, stiff, one, prev, side_a, side_b)
    late_1, late_2 = pl.pallas_call(
        pack_late,
        in_specs=[VMEM] * 4,
        out_specs=[VMEM] * 2,
        out_shape=[kept(4, T, X + 8, 128)] * 2,
        compiler_params=params,
        name="pack_late",
    )(now_side, stiff_side, one, two)
    late_a = swap(late_1, "d1")
    late_b = swap(late_2, "d2")
    one, two, delta, halo_stiff, halo_two = pl.pallas_call(
        couple,
        in_specs=[SMEM] * 2 + [VMEM] * 6 + [pl.BlockSpec(memory_space=pl.ANY)],
        out_specs=[VMEM] * 5,
        out_shape=[kept(*padded)] * 2 + [kept(4, T, ROWS, 128)] + [kept(4, T, X, 128)] * 2,
        input_output_aliases={5: 0},
        compiler_params=params,
        cost_estimate=busy(4.0),
        name="couple",
    )(source_cell, start_step, bands_made, now, stiff, one, early_a, early_b, late_1)
    changed = [kept(*padded)] * 2 + [kept(4, T, ROWS, 128)]
    scalars, held = (source_cell, start_step, tf_weights), (bands_made, now, stiff, now_side, stiff_side)
    three, looked, one, two, delta = pl.pallas_call(
        functools.partial(finish_first, n_dep),
        in_specs=[SMEM] * 3 + [VMEM] * 11,
        out_specs=[VMEM] * 5,
        out_shape=[kept(4, X, 512), kept(BUMPS + 2, T, X, 128)] + changed,
        scratch_shapes=[pltpu.SMEM((4, BUMPS), f32)],
        input_output_aliases={8: 2, 9: 3, 10: 4},
        compiler_params=params,
        cost_estimate=busy(4.0),
        name="finish_first",
    )(*scalars, *held, one, two, delta, halo_stiff, halo_two, late_a)
    pressure, partial, _, _, _ = pl.pallas_call(
        functools.partial(finish_second, n_dep),
        in_specs=[SMEM] * 3 + [VMEM] * 13,
        out_specs=[HBM] + [VMEM] * 4,
        out_shape=[pltpu.HBM((Z, X, 512), f32), kept(n_dep, X, 128)] + changed,
        scratch_shapes=[pltpu.SMEM((4, BUMPS), f32), pltpu.VMEM((4, X, 512), f32), pltpu.SemaphoreType.DMA((2,))],
        input_output_aliases={8: 2, 9: 3, 10: 4},
        compiler_params=params,
        cost_estimate=busy(4.0),
        name="finish_second",
    )(*scalars, *held, one, two, delta, halo_stiff, halo_two, late_b, three, looked)
    parts = lax.all_to_all(partial, "dep", 0, 0, tiled=True)
    image = pl.pallas_call(
        composite,
        in_specs=[VMEM],
        out_specs=VMEM,
        out_shape=shape(128, X),
        compiler_params=params,
        name="composite",
    )(parts)
    return pressure, jnp.swapaxes(image.reshape(4, 512 // n_dep, X), 1, 2)


def solution(mesh):
    block = P("dep", "lat", None)
    return jax.shard_map(
        functools.partial(on_device, mesh.shape["lat"], mesh.shape["dep"]),
        mesh=mesh,
        in_specs=(block, block, block, P(), P(), P(), P()),
        out_specs=(block, P(None, "lat", "dep")),
        check_vma=False,
    )
```

```python
import functools
import math

import jax
import jax.numpy as jnp
from jax import lax
from jax.experimental import pallas as pl
from jax.experimental.pallas import tpu as pltpu
from jax.sharding import PartitionSpec as P

BUMPS = 8
LOG2E = math.log2(math.e)
Z, X, T = 8, 64, 4
ROWS = X + 32
CORE = 16
VMEM = pl.BlockSpec(memory_space=pltpu.VMEM)
SMEM = pl.BlockSpec(memory_space=pltpu.SMEM)
HBM = pl.BlockSpec(memory_space=pltpu.HBM)


def lane_masks():
    lane = lax.broadcasted_iota(jnp.int32, (8, 128), 1)
    return lane < 1, lane < 2, lane >= 127, lane >= 126


def columns_sum(c, masks):
    zero = jnp.zeros((8, 128), jnp.float32)
    low1, low2, high1, high2 = masks
    a1 = [pltpu.roll(v, 1, 1) for v in c]
    a2 = [pltpu.roll(v, 2, 1) for v in c]
    b1 = [pltpu.roll(v, 127, 1) for v in c]
    b2 = [pltpu.roll(v, 126, 1) for v in c]
    out = []
    for i in range(T):
        first, last = i == 0, i == T - 1
        near = jnp.where(low1, zero if first else a1[i - 1], a1[i]) + jnp.where(
            high1, zero if last else b1[i + 1], b1[i]
        )
        far = jnp.where(low2, zero if first else a2[i - 1], a2[i]) + jnp.where(
            high2, zero if last else b2[i + 1], b2[i]
        )
        out.append((near, far))
    return out


def plane_terms(ref, k, row, masks):
    c = [ref[k, i, pl.ds(row, 8), :] for i in range(T)]
    sums = columns_sum(c, masks)
    out = []
    for i in range(T):
        near = sums[i][0] + (ref[k, i, pl.ds(row - 1, 8), :] + ref[k, i, pl.ds(row + 1, 8), :])
        far = sums[i][1] + (ref[k, i, pl.ds(row - 2, 8), :] + ref[k, i, pl.ds(row + 2, 8), :])
        out.append((c[i], near, far))
    return out


def band():
    shape = (512, 256)
    d = jnp.abs(lax.broadcasted_iota(jnp.int32, shape, 0) % 256 - lax.broadcasted_iota(jnp.int32, shape, 1))
    return jnp.where(d == 0, -90.0, jnp.where(d == 1, 16.0, jnp.where(d == 2, -1.0, 0.0))).astype(jnp.bfloat16)


def full_rows(ref, k, first, count, bands):
    rows = slice(first, first + count)
    factors = []
    for h in range(2):
        v = jnp.concatenate([ref[k, 2 * h, rows, :], ref[k, 2 * h + 1, rows, :]], axis=1)
        high = v.astype(jnp.bfloat16)
        low = (v - high.astype(jnp.float32)).astype(jnp.bfloat16)
        factors.append(jnp.concatenate([high, low], axis=1))
    product = jnp.dot(jnp.concatenate(factors, axis=0), bands, preferred_element_type=jnp.float32)
    low1, low2, high1, high2 = lane_masks()
    for r in range(0, count, 8):
        row = first + r
        here = slice(row, row + 8)
        for i in range(T):
            c = ref[k, i, here, :]
            inside = product[count * (i // 2) + r : count * (i // 2) + r + 8, 128 * (i % 2) : 128 * (i % 2) + 128]
            near = ref[k, i, row - 1 : row + 7, :] + ref[k, i, row + 1 : row + 9, :]
            far = ref[k, i, row - 2 : row + 6, :] + ref[k, i, row + 2 : row + 10, :]
            near = near + (ref[k - 1, i, here, :] + ref[k + 1, i, here, :])
            far = far + (ref[k - 2, i, here, :] + ref[k + 2, i, here, :])
            if i == 1:
                v = ref[k, 2, here, :]
                near = near + jnp.where(high1, pltpu.roll(v, 127, 1), 0.0)
                far = far + jnp.where(high2, pltpu.roll(v, 126, 1), 0.0)
            if i == 2:
                v = ref[k, 1, here, :]
                near = near + jnp.where(low1, pltpu.roll(v, 1, 1), 0.0)
                far = far + jnp.where(low2, pltpu.roll(v, 2, 1), 0.0)
            yield row, i, c, inside + (16.0 * near - far)


def strike(ref, outer, place, amplitude, layers, rows):
    z, x, y = place
    row = x + CORE
    inside = functools.reduce(jnp.logical_or, [(row >= first) & (row < end) for first, end in rows])

    @pl.when((z >= layers[0]) & (z < layers[1]) & inside)
    def _():
        tile, lane = y // 128, y % 128
        old = ref[z + outer, tile, pl.ds(row, 1), :]
        ids = lax.broadcasted_iota(jnp.int32, (1, 128), 1)
        ref[z + outer, tile, pl.ds(row, 1), :] = old + jnp.where(ids == lane, amplitude, 0.0)


def stiffness(table, materials):
    return jnp.take_along_axis(table, materials, axis=1, mode="promise_in_bounds")


def ways():
    return (lax.axis_index("dep") + 1) % 2, (lax.axis_index("lat") + 1) % 2


def source_place(cell):
    return cell[0] - lax.axis_index("dep") * Z, cell[1] - lax.axis_index("lat") * X, cell[2]


def wavelets(start):
    level = (lax.broadcasted_iota(jnp.int32, (8, 128), 0) + start[0]).astype(jnp.float32)
    shifted = 0.3 * (level - 10.0)
    return 4.0 * (1.0 - 2.0 * shifted * shifted) * jnp.exp(-shifted * shifted)


def stiffness_table(courant):
    lane = lax.broadcasted_iota(jnp.int32, (8, 128), 1)
    table = jnp.zeros((8, 128), jnp.float32)
    for m in range(16):
        table = jnp.where(lane == m, courant[m], table)
    return table * table * (1.0 / 12.0)


def pack(
    courant_in, now_in, prev_in, mat_in, early_1, early_2, side_1, side_2, now, prev, mat, courant, sems,
):
    up1, right1 = ways()
    scalars = pltpu.make_async_copy(courant_in, courant, sems.at[0])
    scalars.start()
    copies = {}
    for n, pair in enumerate((0, 3, 1, 2)):
        for m, (src, dst) in enumerate(((mat_in, mat), (now_in, now), (prev_in, prev))):
            layers = pl.ds(2 * pair, 2)
            copies[n, m] = pltpu.make_async_copy(src.at[layers], dst.at[layers], sems.at[1 + 3 * n + m])
    order = [(0, 0), (1, 0), (0, 1), (1, 1), (2, 0), (3, 0), (2, 1), (3, 1), (0, 2), (1, 2), (2, 2), (3, 2)]
    for key in order:
        copies[key].start()
    upper_half = (lax.broadcasted_iota(jnp.int32, (8, 128), 0) >= 4).astype(jnp.int32)
    scalars.wait()
    table = stiffness_table(courant)
    for key in order[:4]:
        copies[key].wait()
    for slot, out in enumerate((early_1, early_2)):
        first = 6 * up1 if slot == 0 else 6 - 6 * up1
        for k in range(2):
            for i in range(T):
                lanes = slice(128 * i, 128 * i + 128)
                out[k, i] = now[first + k, :, lanes]
                for t in range(X // 8):
                    rows = slice(8 * t, 8 * t + 8)
                    out[2 + k, i, rows, :] = stiffness(table, mat[first + k, rows, lanes])
    for key in order[4:]:
        copies[key].wait()
    for slot, out in enumerate((side_1, side_2)):
        right = right1 if slot == 0 else 1 - right1
        rows = pl.ds(pl.multiple_of((X - 8) * right, 8), 8)
        keep = upper_half == right
        for k in range(Z):
            for i in range(T):
                lanes = slice(128 * i, 128 * i + 128)
                out[k, i, 0:8, :] = now[k, rows, lanes]
                moved = pltpu.roll(stiffness(table, mat[k, rows, lanes]), 4, 0)
                out[k, i, 8:16, :] = jnp.where(keep, prev[k, rows, lanes], moved)


INNER = CORE + 8, X - 16
OUTER = ((CORE - 8, 16), (CORE + X - 8, 16))


def advance_inner(courant, start, now, prev, mat, now_out, stiff_out, one_out, prev_out, bands, amplitudes):
    table = stiffness_table(courant)
    bands[...] = band()
    amplitudes[...] = wavelets(start)
    zeros = jnp.zeros((T, ROWS, 128), jnp.float32)
    for k in (0, 1, Z + 2, Z + 3):
        now_out[k] = zeros
        one_out[k] = zeros

    def fill(k, carry):
        for i in range(T):
            now_out[k + 2, i, CORE : CORE + X, :] = now[k, :, 128 * i : 128 * i + 128]
        return carry

    lax.fori_loop(0, Z, fill, 0)

    def first(k, carry):
        for i in range(T):
            lanes = slice(128 * i, 128 * i + 128)
            prev_out[k, i, 0:8, :] = prev[k, 0:8, lanes]
            prev_out[k, i, 8:16, :] = prev[k, X - 8 : X, lanes]
            for t in range(X // 8):
                rows = slice(8 * t, 8 * t + 8)
                stiff_out[k, i, rows, :] = stiffness(table, mat[k, rows, lanes])
        for row, i, c, lap in full_rows(now_out, k + 2, *INNER, bands[...]):
            own = slice(row - CORE, row - CORE + 8)
            before = prev[k, own, 128 * i : 128 * i + 128]
            one_out[k + 2, i, row : row + 8, :] = 2.0 * c - before + stiff_out[k, i, own, :] * lap
        return carry

    lax.fori_loop(0, Z, first, 0, unroll=2)


def advance_outer(
    cell, amplitudes, bands, now_in, stiff_in, one_in, prev_in, lat_a, lat_b, now, one, now_side, stiff_side, two_out,
    prev_side,
):
    del now_in, one_in
    right1 = ways()[1] == 1

    def fill(k, carry):
        for i in range(T):
            for left in (False, True):
                wanted = jnp.logical_not(right1) if left else right1
                got = jnp.where(wanted, lat_a[k, i], lat_b[k, i])
                row = CORE - 8 if left else CORE + X
                half = slice(0, 8) if left else slice(8, 16)
                now[k + 2, i, row : row + 8, :] = got[0:8]
                now_side[k, i, half, :] = got[0:8]
                prev_side[k, i, half, :] = got[8:16]
                stiff_side[k, i, half, :] = pltpu.roll(got[8:16], 4, 0)
        return carry

    lax.fori_loop(0, Z, fill, 0)

    def first(k, carry):
        for part in OUTER:
            for row, i, c, lap in full_rows(now, k + 2, *part, bands[...]):
                if row < CORE or row == CORE + X:
                    half = slice(0, 8) if row < CORE else slice(8, 16)
                    before, stiff = prev_side[k, i, half, :], stiff_side[k, i, half, :]
                else:
                    half = slice(0, 8) if row == CORE else slice(8, 16)
                    before, stiff = prev_in[k, i, half, :], stiff_in[k, i, row - CORE : row - CORE + 8, :]
                one[k + 2, i, row : row + 8, :] = 2.0 * c - before + stiff * lap
        return carry

    lax.fori_loop(0, Z, first, 0, unroll=2)
    place = source_place(cell)
    strike(one, 2, place, amplitudes[0:1, :], (0, Z), [(CORE - 8, CORE + X + 8)])

    def second(n, carry):
        k = jnp.where(n < 2, n, n + 4)
        for row, i, c, lap in full_rows(one, k + 2, CORE, X, bands[...]):
            rows = slice(row, row + 8)
            stiff = stiff_in[k, i, row - CORE : row - CORE + 8, :]
            two_out[n, i, rows, :] = 2.0 * c - now[k + 2, i, rows, :] + stiff * lap
        return carry

    lax.fori_loop(0, 4, second, 0, unroll=2)
    z = place[0]
    inner = (z >= 2) & (z < Z - 2)
    place = (jnp.where(inner, -1, jnp.where(z < 2, z, z - 4)),) + place[1:]
    strike(two_out, 0, place, amplitudes[1:2, :], (0, 4), [(CORE, CORE + X)])


def pack_late(now_side, stiff_side, one, two, out_a, out_b):
    sub = lax.broadcasted_iota(jnp.int32, (8, 128), 0)
    left, right = slice(CORE - 8, CORE), slice(CORE + X, CORE + X + 8)
    up1 = ways()[0]
    for slot, out in ((0, out_a), (1, out_b)):
        high = up1 if slot == 0 else 1 - up1
        for k in range(2):
            z = (Z - 2) * high + k
            for i in range(T):
                out[k, i, 0:X, :] = one[z + 2, i, CORE : CORE + X, :]
                out[2 + k, i, 0:X, :] = two[2 * high + k, i, CORE : CORE + X, :]
                out[k, i, X : X + 8, :] = jnp.where(sub >= 4, now_side[z, i, 0:8, :], now_side[z, i, 8:16, :])
                ones = jnp.where(sub >= 4, one[z + 2, i, left, :], one[z + 2, i, right, :])
                side = jnp.where(sub >= 4, stiff_side[z, i, 0:8, :], stiff_side[z, i, 8:16, :])
                outer = (sub < 2) | (sub >= 6)
                out[2 + k, i, X : X + 8, :] = jnp.where(outer, ones, pltpu.roll(side, 4, 0))


def clamp_for_bumps(p):
    return jnp.minimum(jnp.maximum(p, -7.4), 7.4)


SIDES = ((False, 0, 1, 0, 0, 1, 0), (True, 2, 0, 1, Z - 1, Z - 2, Z + 2))


def halo_step(delta, one, halo_stiff, base, near, far, n_in, n_next, row, masks):
    rows, own = pl.ds(row, 8), pl.ds(row - CORE, 8)
    close, distant = plane_terms(delta, base + near, row, masks), plane_terms(delta, base + far, row, masks)
    for i in range(T):
        inner, following = one[n_in + 2, i, rows, :], one[n_next + 2, i, rows, :]
        for place, (c, near_sum, far_sum), (other, _, _), first, second in (
            (near, close[i], distant[i], inner, following),
            (far, distant[i], close[i], None, inner),
        ):
            near_sum = near_sum + other
            if first is not None:
                near_sum = near_sum + first
            lap = 16.0 * near_sum - (far_sum + second) - 90.0 * c
            yield place, i, 2.0 * c + halo_stiff[base + place, i, own, :] * lap


def outer_second(k, bands, now, stiff, stiff_side, one, two):
    for part in OUTER:
        for row, i, c, lap in full_rows(one, k + 2, *part, bands[...]):
            if CORE <= row < CORE + X:
                st = stiff[k, i, row - CORE : row - CORE + 8, :]
            else:
                st = stiff_side[k, i, 0:8, :] if row < CORE else stiff_side[k, i, 8:16, :]
            rows = slice(row, row + 8)
            two[k + 2, i, rows, :] = 2.0 * c - now[k + 2, i, rows, :] + st * lap


def couple(
    cell, amplitudes, bands, now, stiff, now_side, stiff_side, one_in, early_a, early_b, sent, one, two, delta, halo_stiff,
    halo_two,
):
    del one_in, sent
    masks = lane_masks()
    up1 = ways()[0] == 1
    for high, base, near, far, n_in, n_next, zi in SIDES:
        use_a = up1 if high else jnp.logical_not(up1)

        def tile(t, carry, use_a=use_a, base=base, near=near, far=far, n_in=n_in, n_next=n_next, zi=zi):
            own, rows = pl.ds(pl.multiple_of(8 * t, 8), 8), pl.ds(pl.multiple_of(CORE + 8 * t, 8), 8)
            for i in range(T):
                zero_h = [jnp.where(use_a, early_a[k, i, own, :], early_b[k, i, own, :]) for k in range(2)]
                st_h = [jnp.where(use_a, early_a[2 + k, i, own, :], early_b[2 + k, i, own, :]) for k in range(2)]
                one[n_in + 2, i, rows, :] += stiff[n_in, i, own, :] * (16.0 * zero_h[near] - zero_h[far])
                one[n_next + 2, i, rows, :] -= stiff[n_next, i, own, :] * zero_h[near]
                d_near = st_h[near] * (16.0 * now[n_in + 2, i, rows, :] - now[n_next + 2, i, rows, :])
                d_far = -st_h[far] * now[n_in + 2, i, rows, :]
                for place, d, st in ((near, d_near, st_h[near]), (far, d_far, st_h[far])):
                    one[zi + place, i, rows, :] = d
                    delta[base + place, i, rows, :] = d
                    halo_stiff[base + place, i, own, :] = st
            return carry

        lax.fori_loop(0, X // 8, tile, 0)

    def second(k, carry):
        for row, i, c, lap in full_rows(one, k + 2, *INNER, bands[...]):
            rows, own = slice(row, row + 8), slice(row - CORE, row - CORE + 8)
            two[k + 2, i, rows, :] = 2.0 * c - now[k + 2, i, rows, :] + stiff[k, i, own, :] * lap
        return carry

    lax.fori_loop(0, Z, second, 0, unroll=2)

    def middle(n, carry):
        outer_second(n + 2, bands, now, stiff, stiff_side, one, two)
        return carry

    lax.fori_loop(0, 4, middle, 0, unroll=2)
    place = source_place(cell)
    strike(two, 2, place, amplitudes[1:2, :], (0, Z), [(CORE + 8, CORE + X - 8)])
    strike(two, 2, place, amplitudes[1:2, :], (2, Z - 2), [(CORE - 8, CORE + 8), (CORE + X - 8, CORE + X + 8)])
    for high, base, near, far, n_in, n_next, zi in SIDES:

        def beyond(t, carry, base=base, near=near, far=far, n_in=n_in, n_next=n_next):
            row = pl.multiple_of(CORE + 8 * t, 8)
            for k, i, v in halo_step(delta, one, halo_stiff, base, near, far, n_in, n_next, row, masks):
                halo_two[base + k, i, pl.ds(pl.multiple_of(8 * t, 8), 8), :] = v
            return carry

        lax.fori_loop(1, X // 8 - 1, beyond, 0)


def complete(
    second_half, cell, amplitudes, bands, stiff, now, now_side, stiff_side, one, two, delta, halo_stiff, halo_two, late, three
):
    masks = lane_masks()
    place = source_place(cell)
    high = 1 - ways()[0] if second_half else ways()[0]
    base, near, far, n_in, n_next, zi = 2 * high, 1 - high, high, (Z - 1) * high, 1 + (Z - 3) * high, (Z + 2) * high

    extra = slice(X, X + 8)
    n_third, n_fourth = 2 + (Z - 5) * high, 3 + (Z - 7) * high
    for row in (CORE - 8, CORE + X):
        rows, half = slice(row, row + 8), slice(0, 8) if row < CORE else slice(8, 16)
        for i in range(T):
            zero_near, zero_far = late[near, i, extra, :], late[far, i, extra, :]
            more_in = stiff_side[n_in, i, half, :] * (16.0 * zero_near - zero_far)
            less_next = stiff_side[n_next, i, half, :] * zero_near
            one[n_in + 2, i, rows, :] += more_in
            one[n_next + 2, i, rows, :] -= less_next
            two[n_third + 2, i, rows, :] -= stiff_side[n_third, i, half, :] * (16.0 * less_next + more_in)
            two[n_fourth + 2, i, rows, :] += stiff_side[n_fourth, i, half, :] * less_next
            first, second = now_side[n_in, i, half, :], now_side[n_next, i, half, :]
            for at, term in ((near, 16.0 * first - second), (far, -first)):
                v = late[2 + at, i, extra, :]
                d = pltpu.roll(v, 4, 0) * term
                one[zi + at, i, rows, :] = v + d
                delta[base + at, i, rows, :] = d

    def inner(t, carry):
        row = pl.multiple_of(CORE + 8 * t, 8)
        rows, own = pl.ds(row, 8), pl.ds(pl.multiple_of(8 * t, 8), 8)
        for i in range(T):
            one_near, one_far = late[near, i, own, :], late[far, i, own, :]
            one[zi + near, i, rows, :] += one_near
            one[zi + far, i, rows, :] += one_far
            for k in range(2):
                two[zi + k, i, rows, :] = late[2 + k, i, own, :] + halo_two[base + k, i, own, :]
            two[n_in + 2, i, rows, :] += stiff[n_in, i, own, :] * (16.0 * one_near - one_far)
            two[n_next + 2, i, rows, :] -= stiff[n_next, i, own, :] * one_near
        return carry

    lax.fori_loop(0, X // 8, inner, 0)
    for row in (CORE, CORE + X - 8):
        for k, i, v in halo_step(delta, one, halo_stiff, base, near, far, n_in, n_next, row, masks):
            two[zi + k, i, row : row + 8, :] = late[2 + k, i, row - CORE : row - CORE + 8, :] + v

    lowest = (Z - 2) * high

    def second(n, carry):
        outer_second(lowest + n, bands, now, stiff, stiff_side, one, two)
        return carry

    lax.fori_loop(0, 2, second, 0, unroll=2)
    outer = [(CORE - 8, CORE + 8), (CORE + X - 8, CORE + X + 8)]
    strike(two, 2, place, amplitudes[1:2, :], (lowest, lowest + 2), outer)

    def third(n, carry):
        k = 4 * high + n
        for row, i, c, lap in full_rows(two, k + 2, CORE, X, bands[...]):
            own = slice(row - CORE, row - CORE + 8)
            before = one[k + 2, i, row : row + 8, :]
            three[n, own, 128 * i : 128 * i + 128] = 2.0 * c - before + stiff[k, i, own, :] * lap
        return carry

    lax.fori_loop(0, 4, third, 0, unroll=2)
    z, x, y = place
    n = z - 4 * high

    @pl.when((n >= 0) & (n < 4) & (x >= 0) & (x < X))
    def _():
        ids = lax.broadcasted_iota(jnp.int32, (1, 512), 1)
        amplitude = jnp.concatenate([amplitudes[2:3, :]] * T, axis=1)
        three[n, pl.ds(x, 1), :] = three[n, pl.ds(x, 1), :] + jnp.where(ids == y, amplitude, 0.0)


def weigh(n_dep, transfer, weights):
    for n in range(4):
        for j in range(BUMPS):
            centre = (-3.0 + 6.0 * j / (BUMPS - 1)) / 0.8
            weights[n, j] = transfer[n, j] * (math.exp(-centre * centre) * (-LOG2E * 1.5 / (Z * n_dep) if n == 3 else 1.0))


def look(weights, three, i, own):
    half = BUMPS // 2
    rate = 6.0 / (BUMPS - 1) / (0.8 * 0.8) * LOG2E
    zero = jnp.zeros((8, 128), jnp.float32)
    seen = [zero] * BUMPS
    through = jnp.ones((8, 128), jnp.float32)
    depth = zero
    for n in range(4):
        p = clamp_for_bumps(three[n, own, 128 * i : 128 * i + 128])
        gauss = jnp.exp2(p * p * (-LOG2E / 0.64))
        rise = jnp.exp2(p * rate)
        fall = jnp.exp2(p * -rate)
        up, down = rise * rise, fall * fall
        above, below = gauss * rise, gauss * fall
        a = weights[3, BUMPS - 1] * up + weights[3, BUMPS - 2]
        b = weights[3, 0] * down + weights[3, 1]
        for j in range(2, half):
            a = a * up + weights[3, BUMPS - 1 - j]
            b = b * down + weights[3, j]
        power = a * above + b * below
        stay = jnp.exp2(power)
        weight = through * (1.0 - stay)
        through = through * stay
        depth = depth + power
        above, below = weight * above, weight * below
        for j in range(half):
            seen[half + j] = seen[half + j] + above
            seen[half - 1 - j] = seen[half - 1 - j] + below
            if j < half - 1:
                above, below = above * up, below * down
    return seen, through, depth


def finish_first(
    n_dep, cell, amplitudes, transfer, bands, now, stiff, now_side, stiff_side, one_in, two_in, delta_in, halo_stiff, halo_two,
    late, three, looked, one, two, delta, weights,
):
    del one_in, two_in, delta_in
    weigh(n_dep, transfer, weights)
    complete(False, cell, amplitudes, bands, stiff, now, now_side, stiff_side, one, two, delta, halo_stiff, halo_two, late, three)

    def render(t, carry):
        own = pl.ds(pl.multiple_of(8 * t, 8), 8)
        for i in range(T):
            seen, through, depth = look(weights, three, i, own)
            for j, v in enumerate(seen + [through, depth]):
                looked[j, i, own, :] = v
        return carry

    lax.fori_loop(0, X // 8, render, 0)


def finish_second(
    n_dep, cell, amplitudes, transfer, bands, now, stiff, now_side, stiff_side, one_in, two_in, delta_in, halo_stiff, halo_two,
    late, other, looked, pressure, partial, one, two, delta, weights, three, sems,
):
    del one_in, two_in, delta_in
    high = 1 - ways()[0]
    copies = [
        pltpu.make_async_copy(other, pressure.at[pl.ds(4 - 4 * high, 4)], sems.at[0]),
        pltpu.make_async_copy(three, pressure.at[pl.ds(4 * high, 4)], sems.at[1]),
    ]
    copies[0].start()
    weigh(n_dep, transfer, weights)
    complete(True, cell, amplitudes, bands, stiff, now, now_side, stiff_side, one, two, delta, halo_stiff, halo_two, late, three)
    copies[1].start()
    group = lax.broadcasted_iota(jnp.int32, (8, 128), 1) // 32
    behind = high == 1

    def render(t, carry):
        own = pl.ds(pl.multiple_of(8 * t, 8), 8)
        for i in range(T):
            seen, through, depth = look(weights, three, i, own)
            mine = jnp.where(behind, looked[BUMPS, i, own, :], 1.0)
            others = jnp.where(behind, 1.0, through)
            seen = [mine * seen[j] + others * looked[j, i, own, :] for j in range(BUMPS)]
            depth = depth + looked[BUMPS + 1, i, own, :]
            parts = []
            for n in range(3):
                colour = weights[n, 0] * seen[0]
                for j in range(1, BUMPS):
                    colour = colour + weights[n, j] * seen[j]
                parts.append(colour)
            parts.append(depth * (-1.0 / LOG2E))
            turned = [parts[0]] + [pltpu.roll(parts[n], 32 * n, 1) for n in range(1, 4)]
            for q in range(4):
                packed = turned[0]
                for n in range(1, 4):
                    packed = jnp.where(group == (n + q) % 4, turned[n], packed)
                partial[4 * i + q, own, :] = packed
        return carry

    lax.fori_loop(0, X // 8, render, 0)
    for copy in copies:
        copy.wait()


def composite(parts, image):
    q = lax.axis_index("dep") % 4
    group = lax.broadcasted_iota(jnp.int32, (X, 128), 1) // 32
    last = group == (q + 3) % 4
    before = jnp.zeros((X, 128), jnp.float32)
    total = jnp.zeros((X, 128), jnp.float32)
    for d in range(parts.shape[0]):
        v = parts[d]
        total = total + jnp.exp(-before) * v
        depth = jnp.where(last, v, 0.0)
        depth = depth + pltpu.roll(depth, 32, 1)
        before = before + (depth + pltpu.roll(depth, 64, 1))
    view = jnp.where(last, 1.0 - jnp.exp(-before), total).T
    for g in range(4):
        image[pl.ds(pl.multiple_of(32 * ((g + 4 - q) % 4), 32), 32), :] = view[32 * g : 32 * g + 32, :]


def swaps(n_lat, n_dep, kind):
    out = []
    for lat in range(n_lat):
        for dep in range(n_dep):
            other_lat, other_dep = lat, dep
            if kind in ("d1", "d2"):
                up = (dep % 2 == 0) == (kind == "d1")
                other_dep = dep + 1 if up else dep - 1
            else:
                right = (lat % 2 == 0) == (kind == "l1")
                other_lat = lat + 1 if right else lat - 1
            if 0 <= other_lat < n_lat and 0 <= other_dep < n_dep:
                out.append((lat * n_dep + dep, other_lat * n_dep + other_dep))
    return out


def on_device(n_lat, n_dep, pressure_prev, pressure_now, materials, courant_table, tf_weights, source_cell, start_step):
    f32 = jnp.float32

    def swap(v, kind):
        return lax.ppermute(v, ("lat", "dep"), swaps(n_lat, n_dep, kind))

    def busy(microseconds):
        return pl.CostEstimate(
            flops=int(microseconds * 1.0e9), bytes_accessed=int(microseconds * 3.0e6), transcendentals=0
        )

    def shape(*dims):
        return jax.ShapeDtypeStruct(dims, f32)

    def kept(*dims):
        return pltpu.VMEM(dims, f32)

    def in_hbm(v):
        return pltpu.with_memory_space_constraint(v, pltpu.HBM)

    params = pltpu.CompilerParams(vmem_limit_bytes=24 * 1024 * 1024)
    i32 = jnp.int32
    blocks = [pltpu.VMEM((Z, X, 512), d) for d in (f32, f32, i32)]
    early_1, early_2, side_1, side_2, *inputs = pl.pallas_call(
        pack,
        in_specs=[HBM] * 4,
        out_specs=[VMEM] * 7,
        out_shape=[kept(4, T, X, 128)] * 2 + [kept(Z, T, 16, 128)] * 2 + blocks,
        scratch_shapes=[pltpu.SMEM((16,), f32), pltpu.SemaphoreType.DMA((13,))],
        compiler_params=params,
        name="pack",
    )(*(in_hbm(v) for v in (courant_table, pressure_now, pressure_prev, materials)))
    side_a = swap(side_1, "l1")
    side_b = swap(side_2, "l2")
    early_a = swap(early_1, "d1")
    early_b = swap(early_2, "d2")

    padded = (Z + 4, T, ROWS, 128)
    bands = pltpu.VMEM((512, 256), jnp.bfloat16)
    block, side = (Z, T, X, 128), (Z, T, 16, 128)
    now, stiff, one, prev, bands_made, amplitudes = pl.pallas_call(
        advance_inner,
        in_specs=[SMEM] * 2 + [VMEM] * 3,
        out_specs=[VMEM] * 6,
        out_shape=[kept(*padded), kept(*block), kept(*padded), kept(*side), bands, kept(8, 128)],
        compiler_params=params,
        cost_estimate=busy(3.0),
        name="advance_inner",
    )(courant_table, start_step, *inputs)
    now, one, now_side, stiff_side, two = pl.pallas_call(
        advance_outer,
        in_specs=[SMEM] + [VMEM] * 8,
        out_specs=[VMEM] * 5,
        out_shape=[kept(*padded)] * 2 + [kept(*side)] * 2 + [kept(4, T, ROWS, 128)],
        scratch_shapes=[pltpu.VMEM(side, f32)],
        input_output_aliases={3: 0, 5: 1},
        compiler_params=params,
        cost_estimate=busy(5.0),
        name="advance_outer",
    )(source_cell, amplitudes, bands_made, now, stiff, one, prev, side_a, side_b)
    late_1, late_2 = pl.pallas_call(
        pack_late,
        in_specs=[VMEM] * 4,
        out_specs=[VMEM] * 2,
        out_shape=[kept(4, T, X + 8, 128)] * 2,
        compiler_params=params,
        name="pack_late",
    )(now_side, stiff_side, one, two)
    late_a = swap(late_1, "d1")
    late_b = swap(late_2, "d2")
    one, two, delta, halo_stiff, halo_two = pl.pallas_call(
        couple,
        in_specs=[SMEM] + [VMEM] * 9 + [pl.BlockSpec(memory_space=pl.ANY)],
        out_specs=[VMEM] * 5,
        out_shape=[kept(*padded)] * 2 + [kept(4, T, ROWS, 128)] + [kept(4, T, X, 128)] * 2,
        input_output_aliases={7: 0},
        compiler_params=params,
        cost_estimate=busy(4.0),
        name="couple",
    )(source_cell, amplitudes, bands_made, now, stiff, now_side, stiff_side, one, early_a, early_b, late_1)
    changed = [kept(*padded)] * 2 + [kept(4, T, ROWS, 128)]
    scalars, held = (source_cell, amplitudes, tf_weights), (bands_made, now, stiff, now_side, stiff_side)
    three, looked, one, two, delta = pl.pallas_call(
        functools.partial(finish_first, n_dep),
        in_specs=[SMEM, VMEM, SMEM] + [VMEM] * 11,
        out_specs=[VMEM] * 5,
        out_shape=[kept(4, X, 512), kept(BUMPS + 2, T, X, 128)] + changed,
        scratch_shapes=[pltpu.SMEM((4, BUMPS), f32)],
        input_output_aliases={8: 2, 9: 3, 10: 4},
        compiler_params=params,
        cost_estimate=busy(4.0),
        name="finish_first",
    )(*scalars, *held, one, two, delta, halo_stiff, halo_two, late_a)
    pressure, partial, _, _, _ = pl.pallas_call(
        functools.partial(finish_second, n_dep),
        in_specs=[SMEM, VMEM, SMEM] + [VMEM] * 13,
        out_specs=[HBM] + [VMEM] * 4,
        out_shape=[pltpu.HBM((Z, X, 512), f32), kept(n_dep, X, 128)] + changed,
        scratch_shapes=[pltpu.SMEM((4, BUMPS), f32), pltpu.VMEM((4, X, 512), f32), pltpu.SemaphoreType.DMA((2,))],
        input_output_aliases={8: 2, 9: 3, 10: 4},
        compiler_params=params,
        cost_estimate=busy(4.0),
        name="finish_second",
    )(*scalars, *held, one, two, delta, halo_stiff, halo_two, late_b, three, looked)
    parts = lax.all_to_all(partial, "dep", 0, 0, tiled=True)
    image = pl.pallas_call(
        composite,
        in_specs=[VMEM],
        out_specs=VMEM,
        out_shape=shape(128, X),
        compiler_params=params,
        name="composite",
    )(parts)
    return pressure, jnp.swapaxes(image.reshape(4, 512 // n_dep, X), 1, 2)


def solution(mesh):
    block = P("dep", "lat", None)
    return jax.shard_map(
        functools.partial(on_device, mesh.shape["lat"], mesh.shape["dep"]),
        mesh=mesh,
        in_specs=(block, block, block, P(), P(), P(), P()),
        out_specs=(block, P(None, "lat", "dep")),
        check_vma=False,
    )
```

```python
import functools
import math

import jax
import jax.numpy as jnp
import numpy as np
from jax import lax
from jax.experimental import pallas as pl
from jax.experimental.pallas import tpu as pltpu
from jax.sharding import PartitionSpec as P

BUMPS = 8
LOG2E = math.log2(math.e)
Z, X, T = 8, 64, 4
ROWS = X + 32
CORE = 16
VMEM = pl.BlockSpec(memory_space=pltpu.VMEM)
SMEM = pl.BlockSpec(memory_space=pltpu.SMEM)
HBM = pl.BlockSpec(memory_space=pltpu.HBM)


def lane_masks():
    lane = lax.broadcasted_iota(jnp.int32, (8, 128), 1)
    return lane < 1, lane < 2, lane >= 127, lane >= 126


def columns_sum(c, masks):
    zero = jnp.zeros((8, 128), jnp.float32)
    low1, low2, high1, high2 = masks
    a1 = [pltpu.roll(v, 1, 1) for v in c]
    a2 = [pltpu.roll(v, 2, 1) for v in c]
    b1 = [pltpu.roll(v, 127, 1) for v in c]
    b2 = [pltpu.roll(v, 126, 1) for v in c]
    out = []
    for i in range(T):
        first, last = i == 0, i == T - 1
        near = jnp.where(low1, zero if first else a1[i - 1], a1[i]) + jnp.where(
            high1, zero if last else b1[i + 1], b1[i]
        )
        far = jnp.where(low2, zero if first else a2[i - 1], a2[i]) + jnp.where(
            high2, zero if last else b2[i + 1], b2[i]
        )
        out.append((near, far))
    return out


def plane_terms(ref, k, row, masks):
    c = [ref[k, i, pl.ds(row, 8), :] for i in range(T)]
    sums = columns_sum(c, masks)
    out = []
    for i in range(T):
        near = sums[i][0] + (ref[k, i, pl.ds(row - 1, 8), :] + ref[k, i, pl.ds(row + 1, 8), :])
        far = sums[i][1] + (ref[k, i, pl.ds(row - 2, 8), :] + ref[k, i, pl.ds(row + 2, 8), :])
        out.append((c[i], near, far))
    return out


def band():
    d = np.abs(np.arange(512)[:, None] % 256 - np.arange(256)[None])
    return np.where(d == 0, -90.0, np.where(d == 1, 16.0, np.where(d == 2, -1.0, 0.0)))


def full_rows(ref, k, first, count, bands):
    rows = slice(first, first + count)
    factors = []
    for h in range(2):
        v = jnp.concatenate([ref[k, 2 * h, rows, :], ref[k, 2 * h + 1, rows, :]], axis=1)
        high = v.astype(jnp.bfloat16)
        low = (v - high.astype(jnp.float32)).astype(jnp.bfloat16)
        factors.append(jnp.concatenate([high, low], axis=1))
    product = jnp.dot(jnp.concatenate(factors, axis=0), bands, preferred_element_type=jnp.float32)
    low1, low2, high1, high2 = lane_masks()
    for r in range(0, count, 8):
        row = first + r
        here = slice(row, row + 8)
        for i in range(T):
            c = ref[k, i, here, :]
            inside = product[count * (i // 2) + r : count * (i // 2) + r + 8, 128 * (i % 2) : 128 * (i % 2) + 128]
            near = ref[k, i, row - 1 : row + 7, :] + ref[k, i, row + 1 : row + 9, :]
            far = ref[k, i, row - 2 : row + 6, :] + ref[k, i, row + 2 : row + 10, :]
            near = near + (ref[k - 1, i, here, :] + ref[k + 1, i, here, :])
            far = far + (ref[k - 2, i, here, :] + ref[k + 2, i, here, :])
            if i == 1:
                v = ref[k, 2, here, :]
                near = near + jnp.where(high1, pltpu.roll(v, 127, 1), 0.0)
                far = far + jnp.where(high2, pltpu.roll(v, 126, 1), 0.0)
            if i == 2:
                v = ref[k, 1, here, :]
                near = near + jnp.where(low1, pltpu.roll(v, 1, 1), 0.0)
                far = far + jnp.where(low2, pltpu.roll(v, 2, 1), 0.0)
            yield row, i, c, inside + (16.0 * near - far)


def strike(ref, outer, place, amplitude, layers, rows):
    z, x, y = place
    row = x + CORE
    inside = functools.reduce(jnp.logical_or, [(row >= first) & (row < end) for first, end in rows])

    @pl.when((z >= layers[0]) & (z < layers[1]) & inside)
    def _():
        tile, lane = y // 128, y % 128
        old = ref[z + outer, tile, pl.ds(row, 1), :]
        ids = lax.broadcasted_iota(jnp.int32, (1, 128), 1)
        ref[z + outer, tile, pl.ds(row, 1), :] = old + jnp.where(ids == lane, amplitude, 0.0)


def stiffness(table, materials):
    return jnp.take_along_axis(table, materials, axis=1, mode="promise_in_bounds")


def ways():
    return lax.axis_index("dep") % 2, (lax.axis_index("lat") + 1) % 2


def source_place(cell):
    return cell[0] - lax.axis_index("dep") * Z, cell[1] - lax.axis_index("lat") * X, cell[2]


def wavelets(start):
    level = (lax.broadcasted_iota(jnp.int32, (8, 128), 0) + start[0]).astype(jnp.float32)
    shifted = 0.3 * (level - 10.0)
    return 4.0 * (1.0 - 2.0 * shifted * shifted) * jnp.exp(-shifted * shifted)


def stiffness_table(courant):
    lane = lax.broadcasted_iota(jnp.int32, (8, 128), 1)
    table = jnp.zeros((8, 128), jnp.float32)
    for m in range(16):
        table = jnp.where(lane == m, courant[m], table)
    return table * table * (1.0 / 12.0)


def pack(
    courant_in, now_in, prev_in, mat_in, early_1, early_2, side_1, side_2, now, prev, mat, courant, sems,
):
    up1, right1 = ways()
    scalars = pltpu.make_async_copy(courant_in, courant, sems.at[0])
    scalars.start()
    copies = {}
    for n, pair in enumerate((0, 3, 1, 2)):
        for m, (src, dst) in enumerate(((mat_in, mat), (now_in, now), (prev_in, prev))):
            layers = pl.ds(2 * pair, 2)
            copies[n, m] = pltpu.make_async_copy(src.at[layers], dst.at[layers], sems.at[1 + 3 * n + m])
    order = [(0, 0), (1, 0), (0, 1), (1, 1), (2, 0), (3, 0), (2, 1), (3, 1), (0, 2), (1, 2), (2, 2), (3, 2)]
    for key in order:
        copies[key].start()
    upper_half = (lax.broadcasted_iota(jnp.int32, (8, 128), 0) >= 4).astype(jnp.int32)
    scalars.wait()
    table = stiffness_table(courant)
    for key in order[:4]:
        copies[key].wait()
    for slot, out in enumerate((early_1, early_2)):
        first = 6 * up1 if slot == 0 else 6 - 6 * up1
        for k in range(2):
            for i in range(T):
                lanes = slice(128 * i, 128 * i + 128)
                out[k, i] = now[first + k, :, lanes]
                for t in range(X // 8):
                    rows = slice(8 * t, 8 * t + 8)
                    out[2 + k, i, rows, :] = stiffness(table, mat[first + k, rows, lanes])
    for key in order[4:]:
        copies[key].wait()
    for slot, out in enumerate((side_1, side_2)):
        right = right1 if slot == 0 else 1 - right1
        rows = pl.ds(pl.multiple_of((X - 8) * right, 8), 8)
        keep = upper_half == right
        for k in range(Z):
            for i in range(T):
                lanes = slice(128 * i, 128 * i + 128)
                out[k, i, 0:8, :] = now[k, rows, lanes]
                moved = pltpu.roll(stiffness(table, mat[k, rows, lanes]), 4, 0)
                out[k, i, 8:16, :] = jnp.where(keep, prev[k, rows, lanes], moved)


INNER = CORE + 8, X - 16
OUTER = ((CORE - 8, 16), (CORE + X - 8, 16))


def advance_inner(
    courant, start, bands_in, now, prev, mat, now_out, stiff_out, one_out, prev_out, bands, amplitudes, sem,
):
    table = stiffness_table(courant)
    copy = pltpu.make_async_copy(bands_in, bands, sem)
    copy.start()
    amplitudes[...] = wavelets(start)
    zeros = jnp.zeros((T, ROWS, 128), jnp.float32)
    for k in (0, 1, Z + 2, Z + 3):
        now_out[k] = zeros
        one_out[k] = zeros

    def fill(k, carry):
        for i in range(T):
            now_out[k + 2, i, CORE : CORE + X, :] = now[k, :, 128 * i : 128 * i + 128]
        return carry

    lax.fori_loop(0, Z, fill, 0)
    copy.wait()

    def first(k, carry):
        for i in range(T):
            lanes = slice(128 * i, 128 * i + 128)
            prev_out[k, i, 0:8, :] = prev[k, 0:8, lanes]
            prev_out[k, i, 8:16, :] = prev[k, X - 8 : X, lanes]
            for t in range(X // 8):
                rows = slice(8 * t, 8 * t + 8)
                stiff_out[k, i, rows, :] = stiffness(table, mat[k, rows, lanes])
        for row, i, c, lap in full_rows(now_out, k + 2, *INNER, bands[...]):
            own = slice(row - CORE, row - CORE + 8)
            before = prev[k, own, 128 * i : 128 * i + 128]
            one_out[k + 2, i, row : row + 8, :] = 2.0 * c - before + stiff_out[k, i, own, :] * lap
        return carry

    lax.fori_loop(0, Z, first, 0, unroll=2)


def advance_outer(
    cell, amplitudes, bands, now_in, stiff_in, one_in, prev_in, lat_a, lat_b, now, one, now_side, stiff_side, two_out,
    prev_side,
):
    del now_in, one_in
    right1 = ways()[1] == 1

    def fill(k, carry):
        for i in range(T):
            for left in (False, True):
                wanted = jnp.logical_not(right1) if left else right1
                got = jnp.where(wanted, lat_a[k, i], lat_b[k, i])
                row = CORE - 8 if left else CORE + X
                half = slice(0, 8) if left else slice(8, 16)
                now[k + 2, i, row : row + 8, :] = got[0:8]
                now_side[k, i, half, :] = got[0:8]
                prev_side[k, i, half, :] = got[8:16]
                stiff_side[k, i, half, :] = pltpu.roll(got[8:16], 4, 0)
        return carry

    lax.fori_loop(0, Z, fill, 0)

    def first(k, carry):
        for part in OUTER:
            for row, i, c, lap in full_rows(now, k + 2, *part, bands[...]):
                if row < CORE or row == CORE + X:
                    half = slice(0, 8) if row < CORE else slice(8, 16)
                    before, stiff = prev_side[k, i, half, :], stiff_side[k, i, half, :]
                else:
                    half = slice(0, 8) if row == CORE else slice(8, 16)
                    before, stiff = prev_in[k, i, half, :], stiff_in[k, i, row - CORE : row - CORE + 8, :]
                one[k + 2, i, row : row + 8, :] = 2.0 * c - before + stiff * lap
        return carry

    lax.fori_loop(0, Z, first, 0, unroll=2)
    place = source_place(cell)
    strike(one, 2, place, amplitudes[0:1, :], (0, Z), [(CORE - 8, CORE + X + 8)])

    def second(n, carry):
        k = jnp.where(n < 2, n, n + 4)
        for row, i, c, lap in full_rows(one, k + 2, CORE, X, bands[...]):
            rows = slice(row, row + 8)
            stiff = stiff_in[k, i, row - CORE : row - CORE + 8, :]
            two_out[n, i, rows, :] = 2.0 * c - now[k + 2, i, rows, :] + stiff * lap
        return carry

    lax.fori_loop(0, 4, second, 0, unroll=2)
    z = place[0]
    inner = (z >= 2) & (z < Z - 2)
    place = (jnp.where(inner, -1, jnp.where(z < 2, z, z - 4)),) + place[1:]
    strike(two_out, 0, place, amplitudes[1:2, :], (0, 4), [(CORE, CORE + X)])


def pack_late(now_side, stiff_side, one, two, out_a, out_b):
    sub = lax.broadcasted_iota(jnp.int32, (8, 128), 0)
    left, right = slice(CORE - 8, CORE), slice(CORE + X, CORE + X + 8)
    up1 = ways()[0]
    for slot, out in ((0, out_a), (1, out_b)):
        high = up1 if slot == 0 else 1 - up1
        for k in range(2):
            z = (Z - 2) * high + k
            for i in range(T):
                out[k, i, 0:X, :] = one[z + 2, i, CORE : CORE + X, :]
                out[2 + k, i, 0:X, :] = two[2 * high + k, i, CORE : CORE + X, :]
                out[k, i, X : X + 8, :] = jnp.where(sub >= 4, now_side[z, i, 0:8, :], now_side[z, i, 8:16, :])
                ones = jnp.where(sub >= 4, one[z + 2, i, left, :], one[z + 2, i, right, :])
                side = jnp.where(sub >= 4, stiff_side[z, i, 0:8, :], stiff_side[z, i, 8:16, :])
                outer = (sub < 2) | (sub >= 6)
                out[2 + k, i, X : X + 8, :] = jnp.where(outer, ones, pltpu.roll(side, 4, 0))


def clamp_for_bumps(p):
    return jnp.minimum(jnp.maximum(p, -7.4), 7.4)


SIDES = ((False, 0, 1, 0, 0, 1, 0), (True, 2, 0, 1, Z - 1, Z - 2, Z + 2))


def halo_step(delta, one, halo_stiff, base, near, far, n_in, n_next, row, masks):
    rows, own = pl.ds(row, 8), pl.ds(row - CORE, 8)
    close, distant = plane_terms(delta, base + near, row, masks), plane_terms(delta, base + far, row, masks)
    for i in range(T):
        inner, following = one[n_in + 2, i, rows, :], one[n_next + 2, i, rows, :]
        for place, (c, near_sum, far_sum), (other, _, _), first, second in (
            (near, close[i], distant[i], inner, following),
            (far, distant[i], close[i], None, inner),
        ):
            near_sum = near_sum + other
            if first is not None:
                near_sum = near_sum + first
            lap = 16.0 * near_sum - (far_sum + second) - 90.0 * c
            yield place, i, 2.0 * c + halo_stiff[base + place, i, own, :] * lap


def outer_second(k, bands, now, stiff, stiff_side, one, two):
    for part in OUTER:
        for row, i, c, lap in full_rows(one, k + 2, *part, bands[...]):
            if CORE <= row < CORE + X:
                st = stiff[k, i, row - CORE : row - CORE + 8, :]
            else:
                st = stiff_side[k, i, 0:8, :] if row < CORE else stiff_side[k, i, 8:16, :]
            rows = slice(row, row + 8)
            two[k + 2, i, rows, :] = 2.0 * c - now[k + 2, i, rows, :] + st * lap


def couple(
    cell, amplitudes, bands, now, stiff, now_side, stiff_side, one_in, early_a, early_b, sent, one, two, delta, halo_stiff,
    halo_two,
):
    del one_in, sent
    masks = lane_masks()
    up1 = ways()[0] == 1
    for high, base, near, far, n_in, n_next, zi in SIDES:
        use_a = up1 if high else jnp.logical_not(up1)

        def tile(t, carry, use_a=use_a, base=base, near=near, far=far, n_in=n_in, n_next=n_next, zi=zi):
            own, rows = pl.ds(pl.multiple_of(8 * t, 8), 8), pl.ds(pl.multiple_of(CORE + 8 * t, 8), 8)
            for i in range(T):
                zero_h = [jnp.where(use_a, early_a[k, i, own, :], early_b[k, i, own, :]) for k in range(2)]
                st_h = [jnp.where(use_a, early_a[2 + k, i, own, :], early_b[2 + k, i, own, :]) for k in range(2)]
                one[n_in + 2, i, rows, :] += stiff[n_in, i, own, :] * (16.0 * zero_h[near] - zero_h[far])
                one[n_next + 2, i, rows, :] -= stiff[n_next, i, own, :] * zero_h[near]
                d_near = st_h[near] * (16.0 * now[n_in + 2, i, rows, :] - now[n_next + 2, i, rows, :])
                d_far = -st_h[far] * now[n_in + 2, i, rows, :]
                for place, d, st in ((near, d_near, st_h[near]), (far, d_far, st_h[far])):
                    one[zi + place, i, rows, :] = d
                    delta[base + place, i, rows, :] = d
                    halo_stiff[base + place, i, own, :] = st
            return carry

        lax.fori_loop(0, X // 8, tile, 0)

    def second(k, carry):
        for row, i, c, lap in full_rows(one, k + 2, *INNER, bands[...]):
            rows, own = slice(row, row + 8), slice(row - CORE, row - CORE + 8)
            two[k + 2, i, rows, :] = 2.0 * c - now[k + 2, i, rows, :] + stiff[k, i, own, :] * lap
        return carry

    lax.fori_loop(0, Z, second, 0, unroll=2)

    def middle(n, carry):
        outer_second(n + 2, bands, now, stiff, stiff_side, one, two)
        return carry

    lax.fori_loop(0, 4, middle, 0, unroll=2)
    place = source_place(cell)
    strike(two, 2, place, amplitudes[1:2, :], (0, Z), [(CORE + 8, CORE + X - 8)])
    strike(two, 2, place, amplitudes[1:2, :], (2, Z - 2), [(CORE - 8, CORE + 8), (CORE + X - 8, CORE + X + 8)])
    for high, base, near, far, n_in, n_next, zi in SIDES:

        def beyond(t, carry, base=base, near=near, far=far, n_in=n_in, n_next=n_next):
            row = pl.multiple_of(CORE + 8 * t, 8)
            for k, i, v in halo_step(delta, one, halo_stiff, base, near, far, n_in, n_next, row, masks):
                halo_two[base + k, i, pl.ds(pl.multiple_of(8 * t, 8), 8), :] = v
            return carry

        lax.fori_loop(1, X // 8 - 1, beyond, 0)


def complete(
    second_half, cell, amplitudes, bands, stiff, now, now_side, stiff_side, one, two, delta, halo_stiff, halo_two, late, three
):
    masks = lane_masks()
    place = source_place(cell)
    high = 1 - ways()[0] if second_half else ways()[0]
    base, near, far, n_in, n_next, zi = 2 * high, 1 - high, high, (Z - 1) * high, 1 + (Z - 3) * high, (Z + 2) * high

    extra = slice(X, X + 8)
    n_third, n_fourth = 2 + (Z - 5) * high, 3 + (Z - 7) * high
    for row in (CORE - 8, CORE + X):
        rows, half = slice(row, row + 8), slice(0, 8) if row < CORE else slice(8, 16)
        for i in range(T):
            zero_near, zero_far = late[near, i, extra, :], late[far, i, extra, :]
            more_in = stiff_side[n_in, i, half, :] * (16.0 * zero_near - zero_far)
            less_next = stiff_side[n_next, i, half, :] * zero_near
            one[n_in + 2, i, rows, :] += more_in
            one[n_next + 2, i, rows, :] -= less_next
            two[n_third + 2, i, rows, :] -= stiff_side[n_third, i, half, :] * (16.0 * less_next + more_in)
            two[n_fourth + 2, i, rows, :] += stiff_side[n_fourth, i, half, :] * less_next
            first, second = now_side[n_in, i, half, :], now_side[n_next, i, half, :]
            for at, term in ((near, 16.0 * first - second), (far, -first)):
                v = late[2 + at, i, extra, :]
                d = pltpu.roll(v, 4, 0) * term
                one[zi + at, i, rows, :] = v + d
                delta[base + at, i, rows, :] = d

    def inner(t, carry):
        row = pl.multiple_of(CORE + 8 * t, 8)
        rows, own = pl.ds(row, 8), pl.ds(pl.multiple_of(8 * t, 8), 8)
        for i in range(T):
            one_near, one_far = late[near, i, own, :], late[far, i, own, :]
            one[zi + near, i, rows, :] += one_near
            one[zi + far, i, rows, :] += one_far
            for k in range(2):
                two[zi + k, i, rows, :] = late[2 + k, i, own, :] + halo_two[base + k, i, own, :]
            two[n_in + 2, i, rows, :] += stiff[n_in, i, own, :] * (16.0 * one_near - one_far)
            two[n_next + 2, i, rows, :] -= stiff[n_next, i, own, :] * one_near
        return carry

    lax.fori_loop(0, X // 8, inner, 0)
    for row in (CORE, CORE + X - 8):
        for k, i, v in halo_step(delta, one, halo_stiff, base, near, far, n_in, n_next, row, masks):
            two[zi + k, i, row : row + 8, :] = late[2 + k, i, row - CORE : row - CORE + 8, :] + v

    lowest = (Z - 2) * high

    def second(n, carry):
        outer_second(lowest + n, bands, now, stiff, stiff_side, one, two)
        return carry

    lax.fori_loop(0, 2, second, 0, unroll=2)
    outer = [(CORE - 8, CORE + 8), (CORE + X - 8, CORE + X + 8)]
    strike(two, 2, place, amplitudes[1:2, :], (lowest, lowest + 2), outer)

    def third(n, carry):
        k = 4 * high + n
        for row, i, c, lap in full_rows(two, k + 2, CORE, X, bands[...]):
            own = slice(row - CORE, row - CORE + 8)
            before = one[k + 2, i, row : row + 8, :]
            three[n, own, 128 * i : 128 * i + 128] = 2.0 * c - before + stiff[k, i, own, :] * lap
        return carry

    lax.fori_loop(0, 4, third, 0, unroll=2)
    z, x, y = place
    n = z - 4 * high

    @pl.when((n >= 0) & (n < 4) & (x >= 0) & (x < X))
    def _():
        ids = lax.broadcasted_iota(jnp.int32, (1, 512), 1)
        amplitude = jnp.concatenate([amplitudes[2:3, :]] * T, axis=1)
        three[n, pl.ds(x, 1), :] = three[n, pl.ds(x, 1), :] + jnp.where(ids == y, amplitude, 0.0)


def weigh(n_dep, transfer, weights):
    for n in range(4):
        for j in range(BUMPS):
            centre = (-3.0 + 6.0 * j / (BUMPS - 1)) / 0.8
            weights[n, j] = transfer[n, j] * (math.exp(-centre * centre) * (-LOG2E * 1.5 / (Z * n_dep) if n == 3 else 1.0))


def look(weights, three, i, own):
    half = BUMPS // 2
    rate = 6.0 / (BUMPS - 1) / (0.8 * 0.8) * LOG2E
    zero = jnp.zeros((8, 128), jnp.float32)
    seen = [zero] * BUMPS
    through = jnp.ones((8, 128), jnp.float32)
    depth = zero
    for n in range(4):
        p = clamp_for_bumps(three[n, own, 128 * i : 128 * i + 128])
        gauss = jnp.exp2(p * p * (-LOG2E / 0.64))
        rise = jnp.exp2(p * rate)
        fall = jnp.exp2(p * -rate)
        up, down = rise * rise, fall * fall
        above, below = gauss * rise, gauss * fall
        a = weights[3, BUMPS - 1] * up + weights[3, BUMPS - 2]
        b = weights[3, 0] * down + weights[3, 1]
        for j in range(2, half):
            a = a * up + weights[3, BUMPS - 1 - j]
            b = b * down + weights[3, j]
        power = a * above + b * below
        stay = jnp.exp2(power)
        weight = through * (1.0 - stay)
        through = through * stay
        depth = depth + power
        above, below = weight * above, weight * below
        for j in range(half):
            seen[half + j] = seen[half + j] + above
            seen[half - 1 - j] = seen[half - 1 - j] + below
            if j < half - 1:
                above, below = above * up, below * down
    return seen, through, depth


def finish_first(
    n_dep, cell, amplitudes, transfer, bands, now, stiff, now_side, stiff_side, one_in, two_in, delta_in, halo_stiff, halo_two,
    late, three, looked, one, two, delta, weights,
):
    del one_in, two_in, delta_in
    weigh(n_dep, transfer, weights)
    complete(False, cell, amplitudes, bands, stiff, now, now_side, stiff_side, one, two, delta, halo_stiff, halo_two, late, three)

    def render(t, carry):
        own = pl.ds(pl.multiple_of(8 * t, 8), 8)
        for i in range(T):
            seen, through, depth = look(weights, three, i, own)
            for j, v in enumerate(seen + [through, depth]):
                looked[j, i, own, :] = v
        return carry

    lax.fori_loop(0, X // 8, render, 0)


def finish_second(
    n_dep, cell, amplitudes, transfer, bands, now, stiff, now_side, stiff_side, one_in, two_in, delta_in, halo_stiff, halo_two,
    late, other, looked, pressure, partial, one, two, delta, weights, three, sems,
):
    del one_in, two_in, delta_in
    high = 1 - ways()[0]
    copies = [
        pltpu.make_async_copy(other, pressure.at[pl.ds(4 - 4 * high, 4)], sems.at[0]),
        pltpu.make_async_copy(three, pressure.at[pl.ds(4 * high, 4)], sems.at[1]),
    ]
    copies[0].start()
    weigh(n_dep, transfer, weights)
    complete(True, cell, amplitudes, bands, stiff, now, now_side, stiff_side, one, two, delta, halo_stiff, halo_two, late, three)
    copies[1].start()
    group = lax.broadcasted_iota(jnp.int32, (8, 128), 1) // 32
    behind = high == 1

    def render(t, carry):
        own = pl.ds(pl.multiple_of(8 * t, 8), 8)
        for i in range(T):
            seen, through, depth = look(weights, three, i, own)
            mine = jnp.where(behind, looked[BUMPS, i, own, :], 1.0)
            others = jnp.where(behind, 1.0, through)
            seen = [mine * seen[j] + others * looked[j, i, own, :] for j in range(BUMPS)]
            depth = depth + looked[BUMPS + 1, i, own, :]
            parts = []
            for n in range(3):
                colour = weights[n, 0] * seen[0]
                for j in range(1, BUMPS):
                    colour = colour + weights[n, j] * seen[j]
                parts.append(colour)
            parts.append(depth * (-1.0 / LOG2E))
            turned = [parts[0]] + [pltpu.roll(parts[n], 32 * n, 1) for n in range(1, 4)]
            for q in range(4):
                packed = turned[0]
                for n in range(1, 4):
                    packed = jnp.where(group == (n + q) % 4, turned[n], packed)
                partial[4 * i + q, own, :] = packed
        return carry

    lax.fori_loop(0, X // 8, render, 0)
    for copy in copies:
        copy.wait()


def composite(parts, image):
    q = lax.axis_index("dep") % 4
    group = lax.broadcasted_iota(jnp.int32, (X, 128), 1) // 32
    last = group == (q + 3) % 4
    others = [group == (q + n) % 4 for n in range(3)]
    before = jnp.zeros((X, 128), jnp.float32)
    total = jnp.zeros((X, 128), jnp.float32)
    for d in range(parts.shape[0]):
        v = parts[d]
        total = total + jnp.exp(-before) * v
        depth = v
        for n in range(3):
            depth = jnp.where(others[n], pltpu.roll(v, 32 * (n + 1), 1), depth)
        before = before + depth
    view = jnp.where(last, 1.0 - jnp.exp(-before), total).T
    for g in range(4):
        image[pl.ds(pl.multiple_of(32 * ((g + 4 - q) % 4), 32), 32), :] = view[32 * g : 32 * g + 32, :]


def swaps(n_lat, n_dep, kind):
    out = []
    for lat in range(n_lat):
        for dep in range(n_dep):
            other_lat, other_dep = lat, dep
            if kind in ("d1", "d2"):
                up = (dep % 2 == 1) == (kind == "d1")
                other_dep = dep + 1 if up else dep - 1
            else:
                right = (lat % 2 == 0) == (kind == "l1")
                other_lat = lat + 1 if right else lat - 1
            if 0 <= other_lat < n_lat and 0 <= other_dep < n_dep:
                out.append((lat * n_dep + dep, other_lat * n_dep + other_dep))
    return out


def on_device(n_lat, n_dep, pressure_prev, pressure_now, materials, courant_table, tf_weights, source_cell, start_step):
    f32 = jnp.float32

    def swap(v, kind):
        return lax.ppermute(v, ("lat", "dep"), swaps(n_lat, n_dep, kind))

    def busy(microseconds):
        return pl.CostEstimate(
            flops=int(microseconds * 1.0e9), bytes_accessed=int(microseconds * 3.0e6), transcendentals=0
        )

    def shape(*dims):
        return jax.ShapeDtypeStruct(dims, f32)

    def kept(*dims):
        return pltpu.VMEM(dims, f32)

    def in_hbm(v):
        return pltpu.with_memory_space_constraint(v, pltpu.HBM)

    params = pltpu.CompilerParams(vmem_limit_bytes=24 * 1024 * 1024)
    i32 = jnp.int32
    blocks = [pltpu.VMEM((Z, X, 512), d) for d in (f32, f32, i32)]
    early_1, early_2, side_1, side_2, *inputs = pl.pallas_call(
        pack,
        in_specs=[HBM] * 4,
        out_specs=[VMEM] * 7,
        out_shape=[kept(4, T, X, 128)] * 2 + [kept(Z, T, 16, 128)] * 2 + blocks,
        scratch_shapes=[pltpu.SMEM((16,), f32), pltpu.SemaphoreType.DMA((13,))],
        compiler_params=params,
        name="pack",
    )(*(in_hbm(v) for v in (courant_table, pressure_now, pressure_prev, materials)))
    side_a = swap(side_1, "l1")
    side_b = swap(side_2, "l2")
    early_a = swap(early_1, "d1")
    early_b = swap(early_2, "d2")

    padded = (Z + 4, T, ROWS, 128)
    bands = pltpu.VMEM((512, 256), jnp.bfloat16)
    block, side = (Z, T, X, 128), (Z, T, 16, 128)
    now, stiff, one, prev, bands_made, amplitudes = pl.pallas_call(
        advance_inner,
        in_specs=[SMEM] * 2 + [HBM] + [VMEM] * 3,
        out_specs=[VMEM] * 6,
        out_shape=[kept(*padded), kept(*block), kept(*padded), kept(*side), bands, kept(8, 128)],
        scratch_shapes=[pltpu.SemaphoreType.DMA(())],
        compiler_params=params,
        cost_estimate=busy(3.0),
        name="advance_inner",
    )(courant_table, start_step, in_hbm(jnp.asarray(band(), jnp.bfloat16)), *inputs)
    now, one, now_side, stiff_side, two = pl.pallas_call(
        advance_outer,
        in_specs=[SMEM] + [VMEM] * 8,
        out_specs=[VMEM] * 5,
        out_shape=[kept(*padded)] * 2 + [kept(*side)] * 2 + [kept(4, T, ROWS, 128)],
        scratch_shapes=[pltpu.VMEM(side, f32)],
        input_output_aliases={3: 0, 5: 1},
        compiler_params=params,
        cost_estimate=busy(5.0),
        name="advance_outer",
    )(source_cell, amplitudes, bands_made, now, stiff, one, prev, side_a, side_b)
    late_1, late_2 = pl.pallas_call(
        pack_late,
        in_specs=[VMEM] * 4,
        out_specs=[VMEM] * 2,
        out_shape=[kept(4, T, X + 8, 128)] * 2,
        compiler_params=params,
        name="pack_late",
    )(now_side, stiff_side, one, two)
    late_a = swap(late_1, "d1")
    late_b = swap(late_2, "d2")
    one, two, delta, halo_stiff, halo_two = pl.pallas_call(
        couple,
        in_specs=[SMEM] + [VMEM] * 9 + [pl.BlockSpec(memory_space=pl.ANY)],
        out_specs=[VMEM] * 5,
        out_shape=[kept(*padded)] * 2 + [kept(4, T, ROWS, 128)] + [kept(4, T, X, 128)] * 2,
        input_output_aliases={7: 0},
        compiler_params=params,
        cost_estimate=busy(4.0),
        name="couple",
    )(source_cell, amplitudes, bands_made, now, stiff, now_side, stiff_side, one, early_a, early_b, late_1)
    changed = [kept(*padded)] * 2 + [kept(4, T, ROWS, 128)]
    scalars, held = (source_cell, amplitudes, tf_weights), (bands_made, now, stiff, now_side, stiff_side)
    three, looked, one, two, delta = pl.pallas_call(
        functools.partial(finish_first, n_dep),
        in_specs=[SMEM, VMEM, SMEM] + [VMEM] * 11,
        out_specs=[VMEM] * 5,
        out_shape=[kept(4, X, 512), kept(BUMPS + 2, T, X, 128)] + changed,
        scratch_shapes=[pltpu.SMEM((4, BUMPS), f32)],
        input_output_aliases={8: 2, 9: 3, 10: 4},
        compiler_params=params,
        cost_estimate=busy(4.0),
        name="finish_first",
    )(*scalars, *held, one, two, delta, halo_stiff, halo_two, late_a)
    pressure, partial, _, _, _ = pl.pallas_call(
        functools.partial(finish_second, n_dep),
        in_specs=[SMEM, VMEM, SMEM] + [VMEM] * 13,
        out_specs=[HBM] + [VMEM] * 4,
        out_shape=[pltpu.HBM((Z, X, 512), f32), kept(n_dep, X, 128)] + changed,
        scratch_shapes=[pltpu.SMEM((4, BUMPS), f32), pltpu.VMEM((4, X, 512), f32), pltpu.SemaphoreType.DMA((2,))],
        input_output_aliases={8: 2, 9: 3, 10: 4},
        compiler_params=params,
        cost_estimate=busy(4.0),
        name="finish_second",
    )(*scalars, *held, one, two, delta, halo_stiff, halo_two, late_b, three, looked)
    parts = lax.all_to_all(partial, "dep", 0, 0, tiled=True)
    image = pl.pallas_call(
        composite,
        in_specs=[VMEM],
        out_specs=VMEM,
        out_shape=shape(128, X),
        compiler_params=params,
        name="composite",
    )(parts)
    return pressure, jnp.swapaxes(image.reshape(4, 512 // n_dep, X), 1, 2)


def solution(mesh):
    block = P("dep", "lat", None)
    return jax.shard_map(
        functools.partial(on_device, mesh.shape["lat"], mesh.shape["dep"]),
        mesh=mesh,
        in_specs=(block, block, block, P(), P(), P(), P()),
        out_specs=(block, P(None, "lat", "dep")),
        check_vma=False,
    )
```

```python
import functools
import math

import jax
import jax.numpy as jnp
from jax import lax
from jax.experimental import pallas as pl
from jax.experimental.pallas import tpu as pltpu
from jax.sharding import PartitionSpec as P

BUMPS = 8
LOG2E = math.log2(math.e)
Z, X, T = 8, 64, 4
ROWS = X + 32
CORE = 16
VMEM = pl.BlockSpec(memory_space=pltpu.VMEM)
SMEM = pl.BlockSpec(memory_space=pltpu.SMEM)
HBM = pl.BlockSpec(memory_space=pltpu.HBM)


def lane_masks():
    lane = lax.broadcasted_iota(jnp.int32, (8, 128), 1)
    return lane < 1, lane < 2, lane >= 127, lane >= 126


def columns_sum(c, masks):
    zero = jnp.zeros((8, 128), jnp.float32)
    low1, low2, high1, high2 = masks
    a1 = [pltpu.roll(v, 1, 1) for v in c]
    a2 = [pltpu.roll(v, 2, 1) for v in c]
    b1 = [pltpu.roll(v, 127, 1) for v in c]
    b2 = [pltpu.roll(v, 126, 1) for v in c]
    out = []
    for i in range(T):
        first, last = i == 0, i == T - 1
        near = jnp.where(low1, zero if first else a1[i - 1], a1[i]) + jnp.where(
            high1, zero if last else b1[i + 1], b1[i]
        )
        far = jnp.where(low2, zero if first else a2[i - 1], a2[i]) + jnp.where(
            high2, zero if last else b2[i + 1], b2[i]
        )
        out.append((near, far))
    return out


def plane_terms(ref, k, row, masks):
    c = [ref[k, i, pl.ds(row, 8), :] for i in range(T)]
    sums = columns_sum(c, masks)
    out = []
    for i in range(T):
        near = sums[i][0] + (ref[k, i, pl.ds(row - 1, 8), :] + ref[k, i, pl.ds(row + 1, 8), :])
        far = sums[i][1] + (ref[k, i, pl.ds(row - 2, 8), :] + ref[k, i, pl.ds(row + 2, 8), :])
        out.append((c[i], near, far))
    return out


def band():
    shape = (256, 256)
    d = jnp.abs(lax.broadcasted_iota(jnp.int32, shape, 0) - lax.broadcasted_iota(jnp.int32, shape, 1))
    half = jnp.where(d == 0, -90.0, jnp.where(d == 1, 16.0, jnp.where(d == 2, -1.0, 0.0))).astype(jnp.bfloat16)
    return jnp.concatenate([half, half], axis=0)


def full_rows(ref, layers, ranges, bands):
    factors, places = [], []
    for k in layers:
        for first, count in ranges:
            rows = slice(first, first + count)
            places.append((k, first, count))
            for h in range(2):
                v = jnp.concatenate([ref[k, 2 * h, rows, :], ref[k, 2 * h + 1, rows, :]], axis=1)
                high = v.astype(jnp.bfloat16)
                low = (v - high.astype(jnp.float32)).astype(jnp.bfloat16)
                factors.append(jnp.concatenate([high, low], axis=1))
    product = jnp.dot(jnp.concatenate(factors, axis=0), bands, preferred_element_type=jnp.float32)
    low1, low2, high1, high2 = lane_masks()
    start = 0
    for k, first, count in places:
        for r in range(0, count, 8):
            row = first + r
            here = slice(row, row + 8)
            for i in range(T):
                c = ref[k, i, here, :]
                at = start + count * (i // 2) + r
                inside = product[at : at + 8, 128 * (i % 2) : 128 * (i % 2) + 128]
                near = ref[k, i, row - 1 : row + 7, :] + ref[k, i, row + 1 : row + 9, :]
                far = ref[k, i, row - 2 : row + 6, :] + ref[k, i, row + 2 : row + 10, :]
                near = near + (ref[k - 1, i, here, :] + ref[k + 1, i, here, :])
                far = far + (ref[k - 2, i, here, :] + ref[k + 2, i, here, :])
                if i == 1:
                    v = ref[k, 2, here, :]
                    near = near + jnp.where(high1, pltpu.roll(v, 127, 1), 0.0)
                    far = far + jnp.where(high2, pltpu.roll(v, 126, 1), 0.0)
                if i == 2:
                    v = ref[k, 1, here, :]
                    near = near + jnp.where(low1, pltpu.roll(v, 1, 1), 0.0)
                    far = far + jnp.where(low2, pltpu.roll(v, 2, 1), 0.0)
                yield k, row, i, c, inside + (16.0 * near - far)
        start += 2 * count


def strike(ref, outer, place, amplitude, layers, rows):
    z, x, y = place
    row = x + CORE
    inside = functools.reduce(jnp.logical_or, [(row >= first) & (row < end) for first, end in rows])

    @pl.when((z >= layers[0]) & (z < layers[1]) & inside)
    def _():
        tile, lane = y // 128, y % 128
        old = ref[z + outer, tile, pl.ds(row, 1), :]
        ids = lax.broadcasted_iota(jnp.int32, (1, 128), 1)
        ref[z + outer, tile, pl.ds(row, 1), :] = old + jnp.where(ids == lane, amplitude, 0.0)


def stiffness(table, materials):
    return jnp.take_along_axis(table, materials, axis=1, mode="promise_in_bounds")


def ways():
    return lax.axis_index("dep") % 2, (lax.axis_index("lat") + 1) % 2


def source_place(cell):
    return cell[0] - lax.axis_index("dep") * Z, cell[1] - lax.axis_index("lat") * X, cell[2]


def wavelets(start):
    level = (lax.broadcasted_iota(jnp.int32, (8, 128), 0) + start[0]).astype(jnp.float32)
    shifted = 0.3 * (level - 10.0)
    return 4.0 * (1.0 - 2.0 * shifted * shifted) * jnp.exp(-shifted * shifted)


def stiffness_table(courant):
    lane = lax.broadcasted_iota(jnp.int32, (8, 128), 1)
    table = jnp.zeros((8, 128), jnp.float32)
    for m in range(16):
        table = jnp.where(lane == m, courant[m], table)
    return table * table * (1.0 / 12.0)


def pack(
    courant_in, now_in, prev_in, mat_in, early_1, early_2, side_1, side_2, now, prev, mat, courant, sems,
):
    up1, right1 = ways()
    scalars = pltpu.make_async_copy(courant_in, courant, sems.at[0])
    scalars.start()
    copies = {}
    for n, pair in enumerate((0, 3, 1, 2)):
        for m, (src, dst) in enumerate(((mat_in, mat), (now_in, now), (prev_in, prev))):
            layers = pl.ds(2 * pair, 2)
            copies[n, m] = pltpu.make_async_copy(src.at[layers], dst.at[layers], sems.at[1 + 3 * n + m])
    order = [(0, 0), (1, 0), (0, 1), (1, 1), (2, 0), (3, 0), (2, 1), (3, 1), (0, 2), (1, 2), (2, 2), (3, 2)]
    for key in order:
        copies[key].start()
    upper_half = (lax.broadcasted_iota(jnp.int32, (8, 128), 0) >= 4).astype(jnp.int32)
    scalars.wait()
    table = stiffness_table(courant)
    for key in order[:4]:
        copies[key].wait()
    for slot, out in enumerate((early_1, early_2)):
        first = 6 * up1 if slot == 0 else 6 - 6 * up1
        for k in range(2):
            for i in range(T):
                lanes = slice(128 * i, 128 * i + 128)
                out[k, i] = now[first + k, :, lanes]
                for t in range(X // 8):
                    rows = slice(8 * t, 8 * t + 8)
                    out[2 + k, i, rows, :] = stiffness(table, mat[first + k, rows, lanes])
    for key in order[4:]:
        copies[key].wait()
    for slot, out in enumerate((side_1, side_2)):
        right = right1 if slot == 0 else 1 - right1
        rows = pl.ds(pl.multiple_of((X - 8) * right, 8), 8)
        keep = upper_half == right
        for k in range(Z):
            for i in range(T):
                lanes = slice(128 * i, 128 * i + 128)
                out[k, i, 0:8, :] = now[k, rows, lanes]
                moved = pltpu.roll(stiffness(table, mat[k, rows, lanes]), 4, 0)
                out[k, i, 8:16, :] = jnp.where(keep, prev[k, rows, lanes], moved)


INNER = ((CORE + 8, X - 16),)
INSIDE = ((CORE, X),)
OUTER = ((CORE - 8, 16), (CORE + X - 8, 16))


def advance_inner(courant, start, now, prev, mat, now_out, stiff_out, one_out, prev_out, bands, amplitudes):
    table = stiffness_table(courant)
    bands[...] = band()
    amplitudes[...] = wavelets(start)
    zeros = jnp.zeros((T, ROWS, 128), jnp.float32)
    for k in (0, 1, Z + 2, Z + 3):
        now_out[k] = zeros
        one_out[k] = zeros

    def fill(k, carry):
        for i in range(T):
            now_out[k + 2, i, CORE : CORE + X, :] = now[k, :, 128 * i : 128 * i + 128]
        return carry

    lax.fori_loop(0, Z, fill, 0)

    def first(n, carry):
        for k in (2 * n, 2 * n + 1):
            for i in range(T):
                lanes = slice(128 * i, 128 * i + 128)
                prev_out[k, i, 0:8, :] = prev[k, 0:8, lanes]
                prev_out[k, i, 8:16, :] = prev[k, X - 8 : X, lanes]
                for t in range(X // 8):
                    rows = slice(8 * t, 8 * t + 8)
                    stiff_out[k, i, rows, :] = stiffness(table, mat[k, rows, lanes])
        for k, row, i, c, lap in full_rows(now_out, (2 * n + 2, 2 * n + 3), INNER, bands[...]):
            own = slice(row - CORE, row - CORE + 8)
            before = prev[k - 2, own, 128 * i : 128 * i + 128]
            one_out[k, i, row : row + 8, :] = 2.0 * c - before + stiff_out[k - 2, i, own, :] * lap
        return carry

    lax.fori_loop(0, Z // 2, first, 0)


def advance_outer(
    cell, amplitudes, bands, now_in, stiff_in, one_in, prev_in, lat_a, lat_b, now, one, now_side, stiff_side, two_out,
    prev_side,
):
    del now_in, one_in
    right1 = ways()[1] == 1

    def fill(k, carry):
        for i in range(T):
            for left in (False, True):
                wanted = jnp.logical_not(right1) if left else right1
                got = jnp.where(wanted, lat_a[k, i], lat_b[k, i])
                row = CORE - 8 if left else CORE + X
                half = slice(0, 8) if left else slice(8, 16)
                now[k + 2, i, row : row + 8, :] = got[0:8]
                now_side[k, i, half, :] = got[0:8]
                prev_side[k, i, half, :] = got[8:16]
                stiff_side[k, i, half, :] = pltpu.roll(got[8:16], 4, 0)
        return carry

    lax.fori_loop(0, Z, fill, 0)

    def first(n, carry):
        for k, row, i, c, lap in full_rows(now, (2 * n + 2, 2 * n + 3), OUTER, bands[...]):
            if row < CORE or row == CORE + X:
                half = slice(0, 8) if row < CORE else slice(8, 16)
                before, stiff = prev_side[k - 2, i, half, :], stiff_side[k - 2, i, half, :]
            else:
                half = slice(0, 8) if row == CORE else slice(8, 16)
                before, stiff = prev_in[k - 2, i, half, :], stiff_in[k - 2, i, row - CORE : row - CORE + 8, :]
            one[k, i, row : row + 8, :] = 2.0 * c - before + stiff * lap
        return carry

    lax.fori_loop(0, Z // 2, first, 0)
    place = source_place(cell)
    strike(one, 2, place, amplitudes[0:1, :], (0, Z), [(CORE - 8, CORE + X + 8)])

    def second(n, carry):
        base = 6 * n
        for k, row, i, c, lap in full_rows(one, (base + 2, base + 3), INSIDE, bands[...]):
            rows = slice(row, row + 8)
            stiff = stiff_in[k - 2, i, row - CORE : row - CORE + 8, :]
            two_out[k - 2 - 4 * n, i, rows, :] = 2.0 * c - now[k, i, rows, :] + stiff * lap
        return carry

    lax.fori_loop(0, 2, second, 0)
    z = place[0]
    inner = (z >= 2) & (z < Z - 2)
    place = (jnp.where(inner, -1, jnp.where(z < 2, z, z - 4)),) + place[1:]
    strike(two_out, 0, place, amplitudes[1:2, :], (0, 4), [(CORE, CORE + X)])


def pack_late(now_side, stiff_side, one, two, out_a, out_b):
    sub = lax.broadcasted_iota(jnp.int32, (8, 128), 0)
    left, right = slice(CORE - 8, CORE), slice(CORE + X, CORE + X + 8)
    up1 = ways()[0]
    for slot, out in ((0, out_a), (1, out_b)):
        high = up1 if slot == 0 else 1 - up1
        for k in range(2):
            z = (Z - 2) * high + k
            for i in range(T):
                out[k, i, 0:X, :] = one[z + 2, i, CORE : CORE + X, :]
                out[2 + k, i, 0:X, :] = two[2 * high + k, i, CORE : CORE + X, :]
                out[k, i, X : X + 8, :] = jnp.where(sub >= 4, now_side[z, i, 0:8, :], now_side[z, i, 8:16, :])
                ones = jnp.where(sub >= 4, one[z + 2, i, left, :], one[z + 2, i, right, :])
                side = jnp.where(sub >= 4, stiff_side[z, i, 0:8, :], stiff_side[z, i, 8:16, :])
                outer = (sub < 2) | (sub >= 6)
                out[2 + k, i, X : X + 8, :] = jnp.where(outer, ones, pltpu.roll(side, 4, 0))


def clamp_for_bumps(p):
    return jnp.minimum(jnp.maximum(p, -7.4), 7.4)


SIDES = ((False, 0, 1, 0, 0, 1, 0), (True, 2, 0, 1, Z - 1, Z - 2, Z + 2))


def halo_step(delta, one, halo_stiff, base, near, far, n_in, n_next, row, masks):
    rows, own = pl.ds(row, 8), pl.ds(row - CORE, 8)
    close, distant = plane_terms(delta, base + near, row, masks), plane_terms(delta, base + far, row, masks)
    for i in range(T):
        inner, following = one[n_in + 2, i, rows, :], one[n_next + 2, i, rows, :]
        for place, (c, near_sum, far_sum), (other, _, _), first, second in (
            (near, close[i], distant[i], inner, following),
            (far, distant[i], close[i], None, inner),
        ):
            near_sum = near_sum + other
            if first is not None:
                near_sum = near_sum + first
            lap = 16.0 * near_sum - (far_sum + second) - 90.0 * c
            yield place, i, 2.0 * c + halo_stiff[base + place, i, own, :] * lap


def outer_second(first, bands, now, stiff, stiff_side, one, two):
    for k, row, i, c, lap in full_rows(one, (first + 2, first + 3), OUTER, bands[...]):
        if CORE <= row < CORE + X:
            st = stiff[k - 2, i, row - CORE : row - CORE + 8, :]
        else:
            st = stiff_side[k - 2, i, 0:8, :] if row < CORE else stiff_side[k - 2, i, 8:16, :]
        rows = slice(row, row + 8)
        two[k, i, rows, :] = 2.0 * c - now[k, i, rows, :] + st * lap


def couple(
    cell, amplitudes, bands, now, stiff, now_side, stiff_side, one_in, early_a, early_b, sent, one, two, delta, halo_stiff,
    halo_two,
):
    del one_in, sent
    masks = lane_masks()
    up1 = ways()[0] == 1
    for high, base, near, far, n_in, n_next, zi in SIDES:
        use_a = up1 if high else jnp.logical_not(up1)

        def tile(t, carry, use_a=use_a, base=base, near=near, far=far, n_in=n_in, n_next=n_next, zi=zi):
            own, rows = pl.ds(pl.multiple_of(8 * t, 8), 8), pl.ds(pl.multiple_of(CORE + 8 * t, 8), 8)
            for i in range(T):
                zero_h = [jnp.where(use_a, early_a[k, i, own, :], early_b[k, i, own, :]) for k in range(2)]
                st_h = [jnp.where(use_a, early_a[2 + k, i, own, :], early_b[2 + k, i, own, :]) for k in range(2)]
                one[n_in + 2, i, rows, :] += stiff[n_in, i, own, :] * (16.0 * zero_h[near] - zero_h[far])
                one[n_next + 2, i, rows, :] -= stiff[n_next, i, own, :] * zero_h[near]
                d_near = st_h[near] * (16.0 * now[n_in + 2, i, rows, :] - now[n_next + 2, i, rows, :])
                d_far = -st_h[far] * now[n_in + 2, i, rows, :]
                for place, d, st in ((near, d_near, st_h[near]), (far, d_far, st_h[far])):
                    one[zi + place, i, rows, :] = d
                    delta[base + place, i, rows, :] = d
                    halo_stiff[base + place, i, own, :] = st
            return carry

        lax.fori_loop(0, X // 8, tile, 0)

    def second(n, carry):
        for k, row, i, c, lap in full_rows(one, (2 * n + 2, 2 * n + 3), INNER, bands[...]):
            rows, own = slice(row, row + 8), slice(row - CORE, row - CORE + 8)
            two[k, i, rows, :] = 2.0 * c - now[k, i, rows, :] + stiff[k - 2, i, own, :] * lap
        return carry

    lax.fori_loop(0, Z // 2, second, 0)

    def middle(n, carry):
        outer_second(2 * n + 2, bands, now, stiff, stiff_side, one, two)
        return carry

    lax.fori_loop(0, 2, middle, 0)
    place = source_place(cell)
    strike(two, 2, place, amplitudes[1:2, :], (0, Z), [(CORE + 8, CORE + X - 8)])
    strike(two, 2, place, amplitudes[1:2, :], (2, Z - 2), [(CORE - 8, CORE + 8), (CORE + X - 8, CORE + X + 8)])
    for high, base, near, far, n_in, n_next, zi in SIDES:

        def beyond(t, carry, base=base, near=near, far=far, n_in=n_in, n_next=n_next):
            row = pl.multiple_of(CORE + 8 * t, 8)
            for k, i, v in halo_step(delta, one, halo_stiff, base, near, far, n_in, n_next, row, masks):
                halo_two[base + k, i, pl.ds(pl.multiple_of(8 * t, 8), 8), :] = v
            return carry

        lax.fori_loop(1, X // 8 - 1, beyond, 0)


def complete(
    second_half, cell, amplitudes, bands, stiff, now, now_side, stiff_side, one, two, delta, halo_stiff, halo_two, late, three
):
    masks = lane_masks()
    place = source_place(cell)
    high = 1 - ways()[0] if second_half else ways()[0]
    base, near, far, n_in, n_next, zi = 2 * high, 1 - high, high, (Z - 1) * high, 1 + (Z - 3) * high, (Z + 2) * high

    extra = slice(X, X + 8)
    n_third, n_fourth = 2 + (Z - 5) * high, 3 + (Z - 7) * high
    for row in (CORE - 8, CORE + X):
        rows, half = slice(row, row + 8), slice(0, 8) if row < CORE else slice(8, 16)
        for i in range(T):
            zero_near, zero_far = late[near, i, extra, :], late[far, i, extra, :]
            more_in = stiff_side[n_in, i, half, :] * (16.0 * zero_near - zero_far)
            less_next = stiff_side[n_next, i, half, :] * zero_near
            one[n_in + 2, i, rows, :] += more_in
            one[n_next + 2, i, rows, :] -= less_next
            two[n_third + 2, i, rows, :] -= stiff_side[n_third, i, half, :] * (16.0 * less_next + more_in)
            two[n_fourth + 2, i, rows, :] += stiff_side[n_fourth, i, half, :] * less_next
            first, second = now_side[n_in, i, half, :], now_side[n_next, i, half, :]
            for at, term in ((near, 16.0 * first - second), (far, -first)):
                v = late[2 + at, i, extra, :]
                d = pltpu.roll(v, 4, 0) * term
                one[zi + at, i, rows, :] = v + d
                delta[base + at, i, rows, :] = d

    def inner(t, carry):
        row = pl.multiple_of(CORE + 8 * t, 8)
        rows, own = pl.ds(row, 8), pl.ds(pl.multiple_of(8 * t, 8), 8)
        for i in range(T):
            one_near, one_far = late[near, i, own, :], late[far, i, own, :]
            one[zi + near, i, rows, :] += one_near
            one[zi + far, i, rows, :] += one_far
            for k in range(2):
                two[zi + k, i, rows, :] = late[2 + k, i, own, :] + halo_two[base + k, i, own, :]
            two[n_in + 2, i, rows, :] += stiff[n_in, i, own, :] * (16.0 * one_near - one_far)
            two[n_next + 2, i, rows, :] -= stiff[n_next, i, own, :] * one_near
        return carry

    lax.fori_loop(0, X // 8, inner, 0)
    for row in (CORE, CORE + X - 8):
        for k, i, v in halo_step(delta, one, halo_stiff, base, near, far, n_in, n_next, row, masks):
            two[zi + k, i, row : row + 8, :] = late[2 + k, i, row - CORE : row - CORE + 8, :] + v

    lowest = (Z - 2) * high

    outer_second(lowest, bands, now, stiff, stiff_side, one, two)
    outer = [(CORE - 8, CORE + 8), (CORE + X - 8, CORE + X + 8)]
    strike(two, 2, place, amplitudes[1:2, :], (lowest, lowest + 2), outer)

    def third(n, carry):
        base = 4 * high + 2 * n
        for k, row, i, c, lap in full_rows(two, (base + 2, base + 3), INSIDE, bands[...]):
            own = slice(row - CORE, row - CORE + 8)
            before = one[k, i, row : row + 8, :]
            three[k - 2 - 4 * high, own, 128 * i : 128 * i + 128] = 2.0 * c - before + stiff[k - 2, i, own, :] * lap
        return carry

    lax.fori_loop(0, 2, third, 0)
    z, x, y = place
    n = z - 4 * high

    @pl.when((n >= 0) & (n < 4) & (x >= 0) & (x < X))
    def _():
        ids = lax.broadcasted_iota(jnp.int32, (1, 512), 1)
        amplitude = jnp.concatenate([amplitudes[2:3, :]] * T, axis=1)
        three[n, pl.ds(x, 1), :] = three[n, pl.ds(x, 1), :] + jnp.where(ids == y, amplitude, 0.0)


def weigh(n_dep, transfer, weights):
    for n in range(4):
        for j in range(BUMPS):
            centre = (-3.0 + 6.0 * j / (BUMPS - 1)) / 0.8
            weights[n, j] = transfer[n, j] * (math.exp(-centre * centre) * (-LOG2E * 1.5 / (Z * n_dep) if n == 3 else 1.0))


def look(weights, three, i, own):
    half = BUMPS // 2
    rate = 6.0 / (BUMPS - 1) / (0.8 * 0.8) * LOG2E
    zero = jnp.zeros((8, 128), jnp.float32)
    seen = [zero] * BUMPS
    through = jnp.ones((8, 128), jnp.float32)
    depth = zero
    for n in range(4):
        p = clamp_for_bumps(three[n, own, 128 * i : 128 * i + 128])
        gauss = jnp.exp2(p * p * (-LOG2E / 0.64))
        rise = jnp.exp2(p * rate)
        fall = jnp.exp2(p * -rate)
        up, down = rise * rise, fall * fall
        above, below = gauss * rise, gauss * fall
        a = weights[3, BUMPS - 1] * up + weights[3, BUMPS - 2]
        b = weights[3, 0] * down + weights[3, 1]
        for j in range(2, half):
            a = a * up + weights[3, BUMPS - 1 - j]
            b = b * down + weights[3, j]
        power = a * above + b * below
        stay = jnp.exp2(power)
        weight = through * (1.0 - stay)
        through = through * stay
        depth = depth + power
        above, below = weight * above, weight * below
        for j in range(half):
            seen[half + j] = seen[half + j] + above
            seen[half - 1 - j] = seen[half - 1 - j] + below
            if j < half - 1:
                above, below = above * up, below * down
    return seen, through, depth


def finish_first(
    n_dep, cell, amplitudes, transfer, bands, now, stiff, now_side, stiff_side, one_in, two_in, delta_in, halo_stiff, halo_two,
    late, three, looked, one, two, delta, weights,
):
    del one_in, two_in, delta_in
    weigh(n_dep, transfer, weights)
    complete(False, cell, amplitudes, bands, stiff, now, now_side, stiff_side, one, two, delta, halo_stiff, halo_two, late, three)

    def render(t, carry):
        own = pl.ds(pl.multiple_of(8 * t, 8), 8)
        for i in range(T):
            seen, through, depth = look(weights, three, i, own)
            for j, v in enumerate(seen + [through, depth]):
                looked[j, i, own, :] = v
        return carry

    lax.fori_loop(0, X // 8, render, 0)


def finish_second(
    n_dep, cell, amplitudes, transfer, bands, now, stiff, now_side, stiff_side, one_in, two_in, delta_in, halo_stiff, halo_two,
    late, other, looked, pressure, partial, one, two, delta, weights, three, sems,
):
    del one_in, two_in, delta_in
    high = 1 - ways()[0]
    copies = [
        pltpu.make_async_copy(other, pressure.at[pl.ds(4 - 4 * high, 4)], sems.at[0]),
        pltpu.make_async_copy(three, pressure.at[pl.ds(4 * high, 4)], sems.at[1]),
    ]
    copies[0].start()
    weigh(n_dep, transfer, weights)
    complete(True, cell, amplitudes, bands, stiff, now, now_side, stiff_side, one, two, delta, halo_stiff, halo_two, late, three)
    copies[1].start()
    group = lax.broadcasted_iota(jnp.int32, (8, 128), 1) // 32
    behind = high == 1

    def render(t, carry):
        own = pl.ds(pl.multiple_of(8 * t, 8), 8)
        for i in range(T):
            seen, through, depth = look(weights, three, i, own)
            mine = jnp.where(behind, looked[BUMPS, i, own, :], 1.0)
            others = jnp.where(behind, 1.0, through)
            seen = [mine * seen[j] + others * looked[j, i, own, :] for j in range(BUMPS)]
            depth = depth + looked[BUMPS + 1, i, own, :]
            parts = []
            for n in range(3):
                colour = weights[n, 0] * seen[0]
                for j in range(1, BUMPS):
                    colour = colour + weights[n, j] * seen[j]
                parts.append(colour)
            parts.append(depth * (-1.0 / LOG2E))
            turned = [parts[0]] + [pltpu.roll(parts[n], 32 * n, 1) for n in range(1, 4)]
            for q in range(4):
                packed = turned[0]
                for n in range(1, 4):
                    packed = jnp.where(group == (n + q) % 4, turned[n], packed)
                partial[4 * i + q, own, :] = packed
        return carry

    lax.fori_loop(0, X // 8, render, 0)
    for copy in copies:
        copy.wait()


def composite(parts, image):
    q = lax.axis_index("dep") % 4
    group = lax.broadcasted_iota(jnp.int32, (X, 128), 1) // 32
    last = group == (q + 3) % 4
    others = [group == (q + n) % 4 for n in range(3)]
    before = jnp.zeros((X, 128), jnp.float32)
    total = jnp.zeros((X, 128), jnp.float32)
    for d in range(parts.shape[0]):
        v = parts[d]
        total = total + jnp.exp(-before) * v
        depth = v
        for n in range(3):
            depth = jnp.where(others[n], pltpu.roll(v, 32 * (n + 1), 1), depth)
        before = before + depth
    view = jnp.where(last, 1.0 - jnp.exp(-before), total).T
    for g in range(4):
        image[pl.ds(pl.multiple_of(32 * ((g + 4 - q) % 4), 32), 32), :] = view[32 * g : 32 * g + 32, :]


def swaps(n_lat, n_dep, kind):
    out = []
    for lat in range(n_lat):
        for dep in range(n_dep):
            other_lat, other_dep = lat, dep
            if kind in ("d1", "d2"):
                up = (dep % 2 == 1) == (kind == "d1")
                other_dep = dep + 1 if up else dep - 1
            else:
                right = (lat % 2 == 0) == (kind == "l1")
                other_lat = lat + 1 if right else lat - 1
            if 0 <= other_lat < n_lat and 0 <= other_dep < n_dep:
                out.append((lat * n_dep + dep, other_lat * n_dep + other_dep))
    return out


def on_device(n_lat, n_dep, pressure_prev, pressure_now, materials, courant_table, tf_weights, source_cell, start_step):
    f32 = jnp.float32

    def swap(v, kind):
        return lax.ppermute(v, ("lat", "dep"), swaps(n_lat, n_dep, kind))

    def busy(microseconds):
        return pl.CostEstimate(
            flops=int(microseconds * 1.0e9), bytes_accessed=int(microseconds * 3.0e6), transcendentals=0
        )

    def shape(*dims):
        return jax.ShapeDtypeStruct(dims, f32)

    def kept(*dims):
        return pltpu.VMEM(dims, f32)

    def in_hbm(v):
        return pltpu.with_memory_space_constraint(v, pltpu.HBM)

    params = pltpu.CompilerParams(vmem_limit_bytes=24 * 1024 * 1024)
    i32 = jnp.int32
    blocks = [pltpu.VMEM((Z, X, 512), d) for d in (f32, f32, i32)]
    early_1, early_2, side_1, side_2, *inputs = pl.pallas_call(
        pack,
        in_specs=[HBM] * 4,
        out_specs=[VMEM] * 7,
        out_shape=[kept(4, T, X, 128)] * 2 + [kept(Z, T, 16, 128)] * 2 + blocks,
        scratch_shapes=[pltpu.SMEM((16,), f32), pltpu.SemaphoreType.DMA((13,))],
        compiler_params=params,
        name="pack",
    )(*(in_hbm(v) for v in (courant_table, pressure_now, pressure_prev, materials)))
    side_a = swap(side_1, "l1")
    side_b = swap(side_2, "l2")
    early_a = swap(early_1, "d1")
    early_b = swap(early_2, "d2")

    padded = (Z + 4, T, ROWS, 128)
    bands = pltpu.VMEM((512, 256), jnp.bfloat16)
    block, side = (Z, T, X, 128), (Z, T, 16, 128)
    now, stiff, one, prev, bands_made, amplitudes = pl.pallas_call(
        advance_inner,
        in_specs=[SMEM] * 2 + [VMEM] * 3,
        out_specs=[VMEM] * 6,
        out_shape=[kept(*padded), kept(*block), kept(*padded), kept(*side), bands, kept(8, 128)],
        compiler_params=params,
        cost_estimate=busy(3.0),
        name="advance_inner",
    )(courant_table, start_step, *inputs)
    now, one, now_side, stiff_side, two = pl.pallas_call(
        advance_outer,
        in_specs=[SMEM] + [VMEM] * 8,
        out_specs=[VMEM] * 5,
        out_shape=[kept(*padded)] * 2 + [kept(*side)] * 2 + [kept(4, T, ROWS, 128)],
        scratch_shapes=[pltpu.VMEM(side, f32)],
        input_output_aliases={3: 0, 5: 1},
        compiler_params=params,
        cost_estimate=busy(5.0),
        name="advance_outer",
    )(source_cell, amplitudes, bands_made, now, stiff, one, prev, side_a, side_b)
    late_1, late_2 = pl.pallas_call(
        pack_late,
        in_specs=[VMEM] * 4,
        out_specs=[VMEM] * 2,
        out_shape=[kept(4, T, X + 8, 128)] * 2,
        compiler_params=params,
        name="pack_late",
    )(now_side, stiff_side, one, two)
    late_a = swap(late_1, "d1")
    late_b = swap(late_2, "d2")
    one, two, delta, halo_stiff, halo_two = pl.pallas_call(
        couple,
        in_specs=[SMEM] + [VMEM] * 9 + [pl.BlockSpec(memory_space=pl.ANY)],
        out_specs=[VMEM] * 5,
        out_shape=[kept(*padded)] * 2 + [kept(4, T, ROWS, 128)] + [kept(4, T, X, 128)] * 2,
        input_output_aliases={7: 0},
        compiler_params=params,
        cost_estimate=busy(4.0),
        name="couple",
    )(source_cell, amplitudes, bands_made, now, stiff, now_side, stiff_side, one, early_a, early_b, late_1)
    changed = [kept(*padded)] * 2 + [kept(4, T, ROWS, 128)]
    scalars, held = (source_cell, amplitudes, tf_weights), (bands_made, now, stiff, now_side, stiff_side)
    three, looked, one, two, delta = pl.pallas_call(
        functools.partial(finish_first, n_dep),
        in_specs=[SMEM, VMEM, SMEM] + [VMEM] * 11,
        out_specs=[VMEM] * 5,
        out_shape=[kept(4, X, 512), kept(BUMPS + 2, T, X, 128)] + changed,
        scratch_shapes=[pltpu.SMEM((4, BUMPS), f32)],
        input_output_aliases={8: 2, 9: 3, 10: 4},
        compiler_params=params,
        cost_estimate=busy(4.0),
        name="finish_first",
    )(*scalars, *held, one, two, delta, halo_stiff, halo_two, late_a)
    pressure, partial, _, _, _ = pl.pallas_call(
        functools.partial(finish_second, n_dep),
        in_specs=[SMEM, VMEM, SMEM] + [VMEM] * 13,
        out_specs=[HBM] + [VMEM] * 4,
        out_shape=[pltpu.HBM((Z, X, 512), f32), kept(n_dep, X, 128)] + changed,
        scratch_shapes=[pltpu.SMEM((4, BUMPS), f32), pltpu.VMEM((4, X, 512), f32), pltpu.SemaphoreType.DMA((2,))],
        input_output_aliases={8: 2, 9: 3, 10: 4},
        compiler_params=params,
        cost_estimate=busy(4.0),
        name="finish_second",
    )(*scalars, *held, one, two, delta, halo_stiff, halo_two, late_b, three, looked)
    parts = lax.all_to_all(partial, "dep", 0, 0, tiled=True)
    image = pl.pallas_call(
        composite,
        in_specs=[VMEM],
        out_specs=VMEM,
        out_shape=shape(128, X),
        compiler_params=params,
        name="composite",
    )(parts)
    return pressure, jnp.swapaxes(image.reshape(4, 512 // n_dep, X), 1, 2)


def solution(mesh):
    block = P("dep", "lat", None)
    return jax.shard_map(
        functools.partial(on_device, mesh.shape["lat"], mesh.shape["dep"]),
        mesh=mesh,
        in_specs=(block, block, block, P(), P(), P(), P()),
        out_specs=(block, P(None, "lat", "dep")),
        check_vma=False,
    )
```

```python
import functools
import math

import jax
import jax.numpy as jnp
from jax import lax
from jax.experimental import pallas as pl
from jax.experimental.pallas import tpu as pltpu
from jax.sharding import PartitionSpec as P

BUMPS = 8
LOG2E = math.log2(math.e)
Z, X, T = 8, 64, 4
ROWS = X + 32
CORE = 16
VMEM = pl.BlockSpec(memory_space=pltpu.VMEM)
SMEM = pl.BlockSpec(memory_space=pltpu.SMEM)
HBM = pl.BlockSpec(memory_space=pltpu.HBM)


def lane_masks():
    lane = lax.broadcasted_iota(jnp.int32, (8, 128), 1)
    return lane < 1, lane < 2, lane >= 127, lane >= 126


def columns_sum(c, masks):
    zero = jnp.zeros((8, 128), jnp.float32)
    low1, low2, high1, high2 = masks
    a1 = [pltpu.roll(v, 1, 1) for v in c]
    a2 = [pltpu.roll(v, 2, 1) for v in c]
    b1 = [pltpu.roll(v, 127, 1) for v in c]
    b2 = [pltpu.roll(v, 126, 1) for v in c]
    out = []
    for i in range(T):
        first, last = i == 0, i == T - 1
        near = jnp.where(low1, zero if first else a1[i - 1], a1[i]) + jnp.where(
            high1, zero if last else b1[i + 1], b1[i]
        )
        far = jnp.where(low2, zero if first else a2[i - 1], a2[i]) + jnp.where(
            high2, zero if last else b2[i + 1], b2[i]
        )
        out.append((near, far))
    return out


def plane_terms(ref, k, row, masks):
    c = [ref[k, i, pl.ds(row, 8), :] for i in range(T)]
    sums = columns_sum(c, masks)
    out = []
    for i in range(T):
        near = sums[i][0] + (ref[k, i, pl.ds(row - 1, 8), :] + ref[k, i, pl.ds(row + 1, 8), :])
        far = sums[i][1] + (ref[k, i, pl.ds(row - 2, 8), :] + ref[k, i, pl.ds(row + 2, 8), :])
        out.append((c[i], near, far))
    return out


def band():
    shape = (256, 256)
    d = jnp.abs(lax.broadcasted_iota(jnp.int32, shape, 0) - lax.broadcasted_iota(jnp.int32, shape, 1))
    half = jnp.where(d == 0, -90.0, jnp.where(d == 1, 16.0, jnp.where(d == 2, -1.0, 0.0))).astype(jnp.bfloat16)
    return jnp.concatenate([half, half], axis=0)


def full_rows(ref, layers, ranges, bands):
    factors, places = [], []
    for k in layers:
        for first, count in ranges:
            rows = slice(first, first + count)
            places.append((k, first, count))
            for h in range(2):
                v = jnp.concatenate([ref[k, 2 * h, rows, :], ref[k, 2 * h + 1, rows, :]], axis=1)
                high = v.astype(jnp.bfloat16)
                low = (v - high.astype(jnp.float32)).astype(jnp.bfloat16)
                factors.append(jnp.concatenate([high, low], axis=1))
    product = jnp.dot(jnp.concatenate(factors, axis=0), bands, preferred_element_type=jnp.float32)
    low1, low2, high1, high2 = lane_masks()
    start = 0
    for k, first, count in places:
        for r in range(0, count, 8):
            row = first + r
            here = slice(row, row + 8)
            for i in range(T):
                c = ref[k, i, here, :]
                at = start + count * (i // 2) + r
                inside = product[at : at + 8, 128 * (i % 2) : 128 * (i % 2) + 128]
                near = ref[k, i, row - 1 : row + 7, :] + ref[k, i, row + 1 : row + 9, :]
                far = ref[k, i, row - 2 : row + 6, :] + ref[k, i, row + 2 : row + 10, :]
                near = near + (ref[k - 1, i, here, :] + ref[k + 1, i, here, :])
                far = far + (ref[k - 2, i, here, :] + ref[k + 2, i, here, :])
                if i == 1:
                    v = ref[k, 2, here, :]
                    near = near + jnp.where(high1, pltpu.roll(v, 127, 1), 0.0)
                    far = far + jnp.where(high2, pltpu.roll(v, 126, 1), 0.0)
                if i == 2:
                    v = ref[k, 1, here, :]
                    near = near + jnp.where(low1, pltpu.roll(v, 1, 1), 0.0)
                    far = far + jnp.where(low2, pltpu.roll(v, 2, 1), 0.0)
                yield k, row, i, c, inside + (16.0 * near - far)
        start += 2 * count


def strike(ref, outer, place, amplitude, layers, rows):
    z, x, y = place
    row = x + CORE
    inside = functools.reduce(jnp.logical_or, [(row >= first) & (row < end) for first, end in rows])

    @pl.when((z >= layers[0]) & (z < layers[1]) & inside)
    def _():
        tile, lane = y // 128, y % 128
        old = ref[z + outer, tile, pl.ds(row, 1), :]
        ids = lax.broadcasted_iota(jnp.int32, (1, 128), 1)
        ref[z + outer, tile, pl.ds(row, 1), :] = old + jnp.where(ids == lane, amplitude, 0.0)


def stiffness(table, materials):
    return jnp.take_along_axis(table, materials, axis=1, mode="promise_in_bounds")


def ways():
    return lax.axis_index("dep") % 2, (lax.axis_index("lat") + 1) % 2


def source_place(cell):
    return cell[0] - lax.axis_index("dep") * Z, cell[1] - lax.axis_index("lat") * X, cell[2]


def wavelets(start):
    level = (lax.broadcasted_iota(jnp.int32, (8, 128), 0) + start[0]).astype(jnp.float32)
    shifted = 0.3 * (level - 10.0)
    return 4.0 * (1.0 - 2.0 * shifted * shifted) * jnp.exp(-shifted * shifted)


def stiffness_table(courant):
    lane = lax.broadcasted_iota(jnp.int32, (8, 128), 1)
    table = jnp.zeros((8, 128), jnp.float32)
    for m in range(16):
        table = jnp.where(lane == m, courant[m], table)
    return table * table * (1.0 / 12.0)


def pack(
    courant_in, now_in, prev_in, mat_in, early_1, early_2, side_1, side_2, now, prev, mat, courant, sems,
):
    up1, right1 = ways()
    scalars = pltpu.make_async_copy(courant_in, courant, sems.at[0])
    scalars.start()
    copies = {}
    for n, pair in enumerate((0, 3, 1, 2)):
        for m, (src, dst) in enumerate(((mat_in, mat), (now_in, now), (prev_in, prev))):
            layers = pl.ds(2 * pair, 2)
            copies[n, m] = pltpu.make_async_copy(src.at[layers], dst.at[layers], sems.at[1 + 3 * n + m])
    order = [(0, 0), (1, 0), (0, 1), (1, 1), (2, 0), (3, 0), (2, 1), (3, 1), (0, 2), (1, 2), (2, 2), (3, 2)]
    for key in order:
        copies[key].start()
    upper_half = (lax.broadcasted_iota(jnp.int32, (8, 128), 0) >= 4).astype(jnp.int32)
    scalars.wait()
    table = stiffness_table(courant)
    for key in order[:4]:
        copies[key].wait()
    for slot, out in enumerate((early_1, early_2)):
        first = 6 * up1 if slot == 0 else 6 - 6 * up1
        for k in range(2):
            for i in range(T):
                lanes = slice(128 * i, 128 * i + 128)
                out[k, i] = now[first + k, :, lanes]
                for t in range(X // 8):
                    rows = slice(8 * t, 8 * t + 8)
                    out[2 + k, i, rows, :] = stiffness(table, mat[first + k, rows, lanes])
    for key in order[4:]:
        copies[key].wait()
    for slot, out in enumerate((side_1, side_2)):
        right = right1 if slot == 0 else 1 - right1
        rows = pl.ds(pl.multiple_of((X - 8) * right, 8), 8)
        keep = upper_half == right
        for k in range(Z):
            for i in range(T):
                lanes = slice(128 * i, 128 * i + 128)
                out[k, i, 0:8, :] = now[k, rows, lanes]
                moved = pltpu.roll(stiffness(table, mat[k, rows, lanes]), 4, 0)
                out[k, i, 8:16, :] = jnp.where(keep, prev[k, rows, lanes], moved)


INNER = ((CORE + 8, X - 16),)
INSIDE = ((CORE, X),)
OUTER = ((CORE - 8, 16), (CORE + X - 8, 16))


def advance_inner(courant, start, now, prev, mat, now_out, stiff_out, one_out, prev_out, bands, amplitudes):
    table = stiffness_table(courant)
    bands[...] = band()
    amplitudes[...] = wavelets(start)
    zeros = jnp.zeros((T, ROWS, 128), jnp.float32)
    for k in (0, 1, Z + 2, Z + 3):
        now_out[k] = zeros
        one_out[k] = zeros

    def fill(k, carry):
        for i in range(T):
            now_out[k + 2, i, CORE : CORE + X, :] = now[k, :, 128 * i : 128 * i + 128]
        return carry

    lax.fori_loop(0, Z, fill, 0)

    def first(n, carry):
        for k in (2 * n, 2 * n + 1):
            for i in range(T):
                lanes = slice(128 * i, 128 * i + 128)
                prev_out[k, i, 0:8, :] = prev[k, 0:8, lanes]
                prev_out[k, i, 8:16, :] = prev[k, X - 8 : X, lanes]
                for t in range(X // 8):
                    rows = slice(8 * t, 8 * t + 8)
                    stiff_out[k, i, rows, :] = stiffness(table, mat[k, rows, lanes])
        for k, row, i, c, lap in full_rows(now_out, (2 * n + 2, 2 * n + 3), INNER, bands[...]):
            own = slice(row - CORE, row - CORE + 8)
            before = prev[k - 2, own, 128 * i : 128 * i + 128]
            one_out[k, i, row : row + 8, :] = 2.0 * c - before + stiff_out[k - 2, i, own, :] * lap
        return carry

    lax.fori_loop(0, Z // 2, first, 0)


def advance_outer(
    cell, amplitudes, bands, now_in, stiff_in, one_in, prev_in, lat_a, lat_b, now, one, now_side, stiff_side, two_out,
    prev_side,
):
    del now_in, one_in
    right1 = ways()[1] == 1

    def fill(k, carry):
        for i in range(T):
            for left in (False, True):
                wanted = jnp.logical_not(right1) if left else right1
                got = jnp.where(wanted, lat_a[k, i], lat_b[k, i])
                row = CORE - 8 if left else CORE + X
                half = slice(0, 8) if left else slice(8, 16)
                now[k + 2, i, row : row + 8, :] = got[0:8]
                now_side[k, i, half, :] = got[0:8]
                prev_side[k, i, half, :] = got[8:16]
                stiff_side[k, i, half, :] = pltpu.roll(got[8:16], 4, 0)
        return carry

    lax.fori_loop(0, Z, fill, 0)

    def first(n, carry):
        for k, row, i, c, lap in full_rows(now, (2 * n + 2, 2 * n + 3), OUTER, bands[...]):
            if row < CORE or row == CORE + X:
                half = slice(0, 8) if row < CORE else slice(8, 16)
                before, stiff = prev_side[k - 2, i, half, :], stiff_side[k - 2, i, half, :]
            else:
                half = slice(0, 8) if row == CORE else slice(8, 16)
                before, stiff = prev_in[k - 2, i, half, :], stiff_in[k - 2, i, row - CORE : row - CORE + 8, :]
            one[k, i, row : row + 8, :] = 2.0 * c - before + stiff * lap
        return carry

    lax.fori_loop(0, Z // 2, first, 0)
    place = source_place(cell)
    strike(one, 2, place, amplitudes[0:1, :], (0, Z), [(CORE - 8, CORE + X + 8)])

    def second(n, carry):
        base = 6 * n
        for k, row, i, c, lap in full_rows(one, (base + 2, base + 3), INSIDE, bands[...]):
            rows = slice(row, row + 8)
            stiff = stiff_in[k - 2, i, row - CORE : row - CORE + 8, :]
            two_out[k - 2 - 4 * n, i, rows, :] = 2.0 * c - now[k, i, rows, :] + stiff * lap
        return carry

    lax.fori_loop(0, 2, second, 0)
    z = place[0]
    inner = (z >= 2) & (z < Z - 2)
    place = (jnp.where(inner, -1, jnp.where(z < 2, z, z - 4)),) + place[1:]
    strike(two_out, 0, place, amplitudes[1:2, :], (0, 4), [(CORE, CORE + X)])


def pack_late(now_side, stiff_side, one, two, out_a, out_b):
    sub = lax.broadcasted_iota(jnp.int32, (8, 128), 0)
    left, right = slice(CORE - 8, CORE), slice(CORE + X, CORE + X + 8)
    up1 = ways()[0]
    for slot, out in ((0, out_a), (1, out_b)):
        high = up1 if slot == 0 else 1 - up1
        for k in range(2):
            z = (Z - 2) * high + k
            for i in range(T):
                out[k, i, 0:X, :] = one[z + 2, i, CORE : CORE + X, :]
                out[2 + k, i, 0:X, :] = two[2 * high + k, i, CORE : CORE + X, :]
                out[k, i, X : X + 8, :] = jnp.where(sub >= 4, now_side[z, i, 0:8, :], now_side[z, i, 8:16, :])
                ones = jnp.where(sub >= 4, one[z + 2, i, left, :], one[z + 2, i, right, :])
                side = jnp.where(sub >= 4, stiff_side[z, i, 0:8, :], stiff_side[z, i, 8:16, :])
                outer = (sub < 2) | (sub >= 6)
                out[2 + k, i, X : X + 8, :] = jnp.where(outer, ones, pltpu.roll(side, 4, 0))


def clamp_for_bumps(p):
    return jnp.minimum(jnp.maximum(p, -7.4), 7.4)


ORDERS = (
    (4, 9, 7, 10, 1, 5, 15, 13, 12, 3, 2, 14, 11, 8, 0, 6),
    (14, 8, 0, 9, 2, 1, 15, 3, 12, 13, 6, 4, 5, 11, 7, 10),
)


def rank(dep):
    even, odd = (order.index(dep) for order in ORDERS)
    return even + (odd - even) * (lax.axis_index("lat") % 2)


SIDES = ((False, 0, 1, 0, 0, 1, 0), (True, 2, 0, 1, Z - 1, Z - 2, Z + 2))


def halo_step(delta, one, halo_stiff, base, near, far, n_in, n_next, row, masks):
    rows, own = pl.ds(row, 8), pl.ds(row - CORE, 8)
    close, distant = plane_terms(delta, base + near, row, masks), plane_terms(delta, base + far, row, masks)
    for i in range(T):
        inner, following = one[n_in + 2, i, rows, :], one[n_next + 2, i, rows, :]
        for place, (c, near_sum, far_sum), (other, _, _), first, second in (
            (near, close[i], distant[i], inner, following),
            (far, distant[i], close[i], None, inner),
        ):
            near_sum = near_sum + other
            if first is not None:
                near_sum = near_sum + first
            lap = 16.0 * near_sum - (far_sum + second) - 90.0 * c
            yield place, i, 2.0 * c + halo_stiff[base + place, i, own, :] * lap


def outer_second(first, bands, now, stiff, stiff_side, one, two):
    for k, row, i, c, lap in full_rows(one, (first + 2, first + 3), OUTER, bands[...]):
        if CORE <= row < CORE + X:
            st = stiff[k - 2, i, row - CORE : row - CORE + 8, :]
        else:
            st = stiff_side[k - 2, i, 0:8, :] if row < CORE else stiff_side[k - 2, i, 8:16, :]
        rows = slice(row, row + 8)
        two[k, i, rows, :] = 2.0 * c - now[k, i, rows, :] + st * lap


def couple(
    cell, amplitudes, bands, now, stiff, now_side, stiff_side, one_in, early_a, early_b, sent, one, two, delta, halo_stiff,
    halo_two,
):
    del one_in, sent
    masks = lane_masks()
    up1 = ways()[0] == 1
    for high, base, near, far, n_in, n_next, zi in SIDES:
        use_a = up1 if high else jnp.logical_not(up1)

        def tile(t, carry, use_a=use_a, base=base, near=near, far=far, n_in=n_in, n_next=n_next, zi=zi):
            own, rows = pl.ds(pl.multiple_of(8 * t, 8), 8), pl.ds(pl.multiple_of(CORE + 8 * t, 8), 8)
            for i in range(T):
                zero_h = [jnp.where(use_a, early_a[k, i, own, :], early_b[k, i, own, :]) for k in range(2)]
                st_h = [jnp.where(use_a, early_a[2 + k, i, own, :], early_b[2 + k, i, own, :]) for k in range(2)]
                one[n_in + 2, i, rows, :] += stiff[n_in, i, own, :] * (16.0 * zero_h[near] - zero_h[far])
                one[n_next + 2, i, rows, :] -= stiff[n_next, i, own, :] * zero_h[near]
                d_near = st_h[near] * (16.0 * now[n_in + 2, i, rows, :] - now[n_next + 2, i, rows, :])
                d_far = -st_h[far] * now[n_in + 2, i, rows, :]
                for place, d, st in ((near, d_near, st_h[near]), (far, d_far, st_h[far])):
                    one[zi + place, i, rows, :] = d
                    delta[base + place, i, rows, :] = d
                    halo_stiff[base + place, i, own, :] = st
            return carry

        lax.fori_loop(0, X // 8, tile, 0)

    def second(n, carry):
        for k, row, i, c, lap in full_rows(one, (2 * n + 2, 2 * n + 3), INNER, bands[...]):
            rows, own = slice(row, row + 8), slice(row - CORE, row - CORE + 8)
            two[k, i, rows, :] = 2.0 * c - now[k, i, rows, :] + stiff[k - 2, i, own, :] * lap
        return carry

    lax.fori_loop(0, Z // 2, second, 0)

    def middle(n, carry):
        outer_second(2 * n + 2, bands, now, stiff, stiff_side, one, two)
        return carry

    lax.fori_loop(0, 2, middle, 0)
    place = source_place(cell)
    strike(two, 2, place, amplitudes[1:2, :], (0, Z), [(CORE + 8, CORE + X - 8)])
    strike(two, 2, place, amplitudes[1:2, :], (2, Z - 2), [(CORE - 8, CORE + 8), (CORE + X - 8, CORE + X + 8)])
    for high, base, near, far, n_in, n_next, zi in SIDES:

        def beyond(t, carry, base=base, near=near, far=far, n_in=n_in, n_next=n_next):
            row = pl.multiple_of(CORE + 8 * t, 8)
            for k, i, v in halo_step(delta, one, halo_stiff, base, near, far, n_in, n_next, row, masks):
                halo_two[base + k, i, pl.ds(pl.multiple_of(8 * t, 8), 8), :] = v
            return carry

        lax.fori_loop(1, X // 8 - 1, beyond, 0)


def complete(
    second_half, cell, amplitudes, bands, stiff, now, now_side, stiff_side, one, two, delta, halo_stiff, halo_two, late, three
):
    masks = lane_masks()
    place = source_place(cell)
    high = 1 - ways()[0] if second_half else ways()[0]
    base, near, far, n_in, n_next, zi = 2 * high, 1 - high, high, (Z - 1) * high, 1 + (Z - 3) * high, (Z + 2) * high

    extra = slice(X, X + 8)
    n_third, n_fourth = 2 + (Z - 5) * high, 3 + (Z - 7) * high
    for row in (CORE - 8, CORE + X):
        rows, half = slice(row, row + 8), slice(0, 8) if row < CORE else slice(8, 16)
        for i in range(T):
            zero_near, zero_far = late[near, i, extra, :], late[far, i, extra, :]
            more_in = stiff_side[n_in, i, half, :] * (16.0 * zero_near - zero_far)
            less_next = stiff_side[n_next, i, half, :] * zero_near
            one[n_in + 2, i, rows, :] += more_in
            one[n_next + 2, i, rows, :] -= less_next
            two[n_third + 2, i, rows, :] -= stiff_side[n_third, i, half, :] * (16.0 * less_next + more_in)
            two[n_fourth + 2, i, rows, :] += stiff_side[n_fourth, i, half, :] * less_next
            first, second = now_side[n_in, i, half, :], now_side[n_next, i, half, :]
            for at, term in ((near, 16.0 * first - second), (far, -first)):
                v = late[2 + at, i, extra, :]
                d = pltpu.roll(v, 4, 0) * term
                one[zi + at, i, rows, :] = v + d
                delta[base + at, i, rows, :] = d

    def inner(t, carry):
        row = pl.multiple_of(CORE + 8 * t, 8)
        rows, own = pl.ds(row, 8), pl.ds(pl.multiple_of(8 * t, 8), 8)
        for i in range(T):
            one_near, one_far = late[near, i, own, :], late[far, i, own, :]
            one[zi + near, i, rows, :] += one_near
            one[zi + far, i, rows, :] += one_far
            for k in range(2):
                two[zi + k, i, rows, :] = late[2 + k, i, own, :] + halo_two[base + k, i, own, :]
            two[n_in + 2, i, rows, :] += stiff[n_in, i, own, :] * (16.0 * one_near - one_far)
            two[n_next + 2, i, rows, :] -= stiff[n_next, i, own, :] * one_near
        return carry

    lax.fori_loop(0, X // 8, inner, 0)
    for row in (CORE, CORE + X - 8):
        for k, i, v in halo_step(delta, one, halo_stiff, base, near, far, n_in, n_next, row, masks):
            two[zi + k, i, row : row + 8, :] = late[2 + k, i, row - CORE : row - CORE + 8, :] + v

    lowest = (Z - 2) * high

    outer_second(lowest, bands, now, stiff, stiff_side, one, two)
    outer = [(CORE - 8, CORE + 8), (CORE + X - 8, CORE + X + 8)]
    strike(two, 2, place, amplitudes[1:2, :], (lowest, lowest + 2), outer)

    def third(n, carry):
        base = 4 * high + 2 * n
        for k, row, i, c, lap in full_rows(two, (base + 2, base + 3), INSIDE, bands[...]):
            own = slice(row - CORE, row - CORE + 8)
            before = one[k, i, row : row + 8, :]
            three[k - 2 - 4 * high, own, 128 * i : 128 * i + 128] = 2.0 * c - before + stiff[k - 2, i, own, :] * lap
        return carry

    lax.fori_loop(0, 2, third, 0)
    z, x, y = place
    n = z - 4 * high

    @pl.when((n >= 0) & (n < 4) & (x >= 0) & (x < X))
    def _():
        ids = lax.broadcasted_iota(jnp.int32, (1, 512), 1)
        amplitude = jnp.concatenate([amplitudes[2:3, :]] * T, axis=1)
        three[n, pl.ds(x, 1), :] = three[n, pl.ds(x, 1), :] + jnp.where(ids == y, amplitude, 0.0)


def weigh(n_dep, transfer, weights):
    for n in range(4):
        for j in range(BUMPS):
            centre = (-3.0 + 6.0 * j / (BUMPS - 1)) / 0.8
            weights[n, j] = transfer[n, j] * (math.exp(-centre * centre) * (-LOG2E * 1.5 / (Z * n_dep) if n == 3 else 1.0))


def look(weights, three, i, own):
    half = BUMPS // 2
    rate = 6.0 / (BUMPS - 1) / (0.8 * 0.8) * LOG2E
    zero = jnp.zeros((8, 128), jnp.float32)
    seen = [zero] * BUMPS
    through = jnp.ones((8, 128), jnp.float32)
    depth = zero
    for n in range(4):
        p = clamp_for_bumps(three[n, own, 128 * i : 128 * i + 128])
        gauss = jnp.exp2(p * p * (-LOG2E / 0.64))
        rise = jnp.exp2(p * rate)
        fall = jnp.exp2(p * -rate)
        up, down = rise * rise, fall * fall
        above, below = gauss * rise, gauss * fall
        a = weights[3, BUMPS - 1] * up + weights[3, BUMPS - 2]
        b = weights[3, 0] * down + weights[3, 1]
        for j in range(2, half):
            a = a * up + weights[3, BUMPS - 1 - j]
            b = b * down + weights[3, j]
        power = a * above + b * below
        stay = jnp.exp2(power)
        weight = through * (1.0 - stay)
        through = through * stay
        depth = depth + power
        above, below = weight * above, weight * below
        for j in range(half):
            seen[half + j] = seen[half + j] + above
            seen[half - 1 - j] = seen[half - 1 - j] + below
            if j < half - 1:
                above, below = above * up, below * down
    return seen, through, depth


def finish_first(
    n_dep, cell, amplitudes, transfer, bands, now, stiff, now_side, stiff_side, one_in, two_in, delta_in, halo_stiff, halo_two,
    late, three, looked, one, two, delta, weights,
):
    del one_in, two_in, delta_in
    weigh(n_dep, transfer, weights)
    complete(False, cell, amplitudes, bands, stiff, now, now_side, stiff_side, one, two, delta, halo_stiff, halo_two, late, three)

    def render(t, carry):
        own = pl.ds(pl.multiple_of(8 * t, 8), 8)
        for i in range(T):
            seen, through, depth = look(weights, three, i, own)
            for j, v in enumerate(seen + [through, depth]):
                looked[j, i, own, :] = v
        return carry

    lax.fori_loop(0, X // 8, render, 0)


def finish_second(
    n_dep, cell, amplitudes, transfer, bands, now, stiff, now_side, stiff_side, one_in, two_in, delta_in, halo_stiff, halo_two,
    late, other, looked, pressure, partial, one, two, delta, weights, three, sems,
):
    del one_in, two_in, delta_in
    high = 1 - ways()[0]
    copies = [
        pltpu.make_async_copy(other, pressure.at[pl.ds(4 - 4 * high, 4)], sems.at[0]),
        pltpu.make_async_copy(three, pressure.at[pl.ds(4 * high, 4)], sems.at[1]),
    ]
    copies[0].start()
    weigh(n_dep, transfer, weights)
    complete(True, cell, amplitudes, bands, stiff, now, now_side, stiff_side, one, two, delta, halo_stiff, halo_two, late, three)
    copies[1].start()
    group = lax.broadcasted_iota(jnp.int32, (8, 128), 1) // 32
    behind = high == 1

    def render(t, carry):
        own = pl.ds(pl.multiple_of(8 * t, 8), 8)
        for i in range(T):
            seen, through, depth = look(weights, three, i, own)
            mine = jnp.where(behind, looked[BUMPS, i, own, :], 1.0)
            others = jnp.where(behind, 1.0, through)
            seen = [mine * seen[j] + others * looked[j, i, own, :] for j in range(BUMPS)]
            depth = depth + looked[BUMPS + 1, i, own, :]
            parts = []
            for n in range(3):
                colour = weights[n, 0] * seen[0]
                for j in range(1, BUMPS):
                    colour = colour + weights[n, j] * seen[j]
                parts.append(colour)
            parts.append(depth * (-1.0 / LOG2E))
            turned = [parts[0]] + [pltpu.roll(parts[n], 32 * n, 1) for n in range(1, 4)]
            for q in range(4):
                packed = turned[0]
                for n in range(1, 4):
                    packed = jnp.where(group == (n + q) % 4, turned[n], packed)
                partial[rank(4 * i + q), own, :] = packed
        return carry

    lax.fori_loop(0, X // 8, render, 0)
    for copy in copies:
        copy.wait()


def composite(parts, image):
    q = lax.axis_index("dep") % 4
    group = lax.broadcasted_iota(jnp.int32, (X, 128), 1) // 32
    last = group == (q + 3) % 4
    others = [group == (q + n) % 4 for n in range(3)]
    before = jnp.zeros((X, 128), jnp.float32)
    total = jnp.zeros((X, 128), jnp.float32)
    for d in range(parts.shape[0]):
        v = parts[rank(d)]
        total = total + jnp.exp(-before) * v
        depth = v
        for n in range(3):
            depth = jnp.where(others[n], pltpu.roll(v, 32 * (n + 1), 1), depth)
        before = before + depth
    view = jnp.where(last, 1.0 - jnp.exp(-before), total).T
    for g in range(4):
        image[pl.ds(pl.multiple_of(32 * ((g + 4 - q) % 4), 32), 32), :] = view[32 * g : 32 * g + 32, :]


def swaps(n_lat, n_dep, kind):
    out = []
    for lat in range(n_lat):
        for dep in range(n_dep):
            other_lat, other_dep = lat, dep
            if kind in ("d1", "d2"):
                up = (dep % 2 == 1) == (kind == "d1")
                other_dep = dep + 1 if up else dep - 1
            else:
                right = (lat % 2 == 0) == (kind == "l1")
                other_lat = lat + 1 if right else lat - 1
            if 0 <= other_lat < n_lat and 0 <= other_dep < n_dep:
                out.append((lat * n_dep + dep, other_lat * n_dep + other_dep))
    return out


def on_device(n_lat, n_dep, pressure_prev, pressure_now, materials, courant_table, tf_weights, source_cell, start_step):
    f32 = jnp.float32

    def swap(v, kind):
        return lax.ppermute(v, ("lat", "dep"), swaps(n_lat, n_dep, kind))

    def busy(microseconds):
        return pl.CostEstimate(
            flops=int(microseconds * 1.0e9), bytes_accessed=int(microseconds * 3.0e6), transcendentals=0
        )

    def shape(*dims):
        return jax.ShapeDtypeStruct(dims, f32)

    def kept(*dims):
        return pltpu.VMEM(dims, f32)

    def in_hbm(v):
        return pltpu.with_memory_space_constraint(v, pltpu.HBM)

    params = pltpu.CompilerParams(vmem_limit_bytes=24 * 1024 * 1024)
    i32 = jnp.int32
    blocks = [pltpu.VMEM((Z, X, 512), d) for d in (f32, f32, i32)]
    early_1, early_2, side_1, side_2, *inputs = pl.pallas_call(
        pack,
        in_specs=[HBM] * 4,
        out_specs=[VMEM] * 7,
        out_shape=[kept(4, T, X, 128)] * 2 + [kept(Z, T, 16, 128)] * 2 + blocks,
        scratch_shapes=[pltpu.SMEM((16,), f32), pltpu.SemaphoreType.DMA((13,))],
        compiler_params=params,
        name="pack",
    )(*(in_hbm(v) for v in (courant_table, pressure_now, pressure_prev, materials)))
    side_a = swap(side_1, "l1")
    side_b = swap(side_2, "l2")
    early_a = swap(early_1, "d1")
    early_b = swap(early_2, "d2")

    padded = (Z + 4, T, ROWS, 128)
    bands = pltpu.VMEM((512, 256), jnp.bfloat16)
    block, side = (Z, T, X, 128), (Z, T, 16, 128)
    now, stiff, one, prev, bands_made, amplitudes = pl.pallas_call(
        advance_inner,
        in_specs=[SMEM] * 2 + [VMEM] * 3,
        out_specs=[VMEM] * 6,
        out_shape=[kept(*padded), kept(*block), kept(*padded), kept(*side), bands, kept(8, 128)],
        compiler_params=params,
        cost_estimate=busy(3.0),
        name="advance_inner",
    )(courant_table, start_step, *inputs)
    now, one, now_side, stiff_side, two = pl.pallas_call(
        advance_outer,
        in_specs=[SMEM] + [VMEM] * 8,
        out_specs=[VMEM] * 5,
        out_shape=[kept(*padded)] * 2 + [kept(*side)] * 2 + [kept(4, T, ROWS, 128)],
        scratch_shapes=[pltpu.VMEM(side, f32)],
        input_output_aliases={3: 0, 5: 1},
        compiler_params=params,
        cost_estimate=busy(5.0),
        name="advance_outer",
    )(source_cell, amplitudes, bands_made, now, stiff, one, prev, side_a, side_b)
    late_1, late_2 = pl.pallas_call(
        pack_late,
        in_specs=[VMEM] * 4,
        out_specs=[VMEM] * 2,
        out_shape=[kept(4, T, X + 8, 128)] * 2,
        compiler_params=params,
        name="pack_late",
    )(now_side, stiff_side, one, two)
    late_a = swap(late_1, "d1")
    late_b = swap(late_2, "d2")
    one, two, delta, halo_stiff, halo_two = pl.pallas_call(
        couple,
        in_specs=[SMEM] + [VMEM] * 9 + [pl.BlockSpec(memory_space=pl.ANY)],
        out_specs=[VMEM] * 5,
        out_shape=[kept(*padded)] * 2 + [kept(4, T, ROWS, 128)] + [kept(4, T, X, 128)] * 2,
        input_output_aliases={7: 0},
        compiler_params=params,
        cost_estimate=busy(4.0),
        name="couple",
    )(source_cell, amplitudes, bands_made, now, stiff, now_side, stiff_side, one, early_a, early_b, late_1)
    changed = [kept(*padded)] * 2 + [kept(4, T, ROWS, 128)]
    scalars, held = (source_cell, amplitudes, tf_weights), (bands_made, now, stiff, now_side, stiff_side)
    three, looked, one, two, delta = pl.pallas_call(
        functools.partial(finish_first, n_dep),
        in_specs=[SMEM, VMEM, SMEM] + [VMEM] * 11,
        out_specs=[VMEM] * 5,
        out_shape=[kept(4, X, 512), kept(BUMPS + 2, T, X, 128)] + changed,
        scratch_shapes=[pltpu.SMEM((4, BUMPS), f32)],
        input_output_aliases={8: 2, 9: 3, 10: 4},
        compiler_params=params,
        cost_estimate=busy(4.0),
        name="finish_first",
    )(*scalars, *held, one, two, delta, halo_stiff, halo_two, late_a)
    pressure, partial, _, _, _ = pl.pallas_call(
        functools.partial(finish_second, n_dep),
        in_specs=[SMEM, VMEM, SMEM] + [VMEM] * 13,
        out_specs=[HBM] + [VMEM] * 4,
        out_shape=[pltpu.HBM((Z, X, 512), f32), kept(n_dep, X, 128)] + changed,
        scratch_shapes=[pltpu.SMEM((4, BUMPS), f32), pltpu.VMEM((4, X, 512), f32), pltpu.SemaphoreType.DMA((2,))],
        input_output_aliases={8: 2, 9: 3, 10: 4},
        compiler_params=params,
        cost_estimate=busy(4.0),
        name="finish_second",
    )(*scalars, *held, one, two, delta, halo_stiff, halo_two, late_b, three, looked)
    groups = [[lat * n_dep + dep for dep in ORDERS[lat % 2]] for lat in range(n_lat)]
    parts = lax.all_to_all(partial, ("lat", "dep"), 0, 0, axis_index_groups=groups, tiled=True)
    image = pl.pallas_call(
        composite,
        in_specs=[VMEM],
        out_specs=VMEM,
        out_shape=shape(128, X),
        compiler_params=params,
        name="composite",
    )(parts)
    return pressure, jnp.swapaxes(image.reshape(4, 512 // n_dep, X), 1, 2)


def solution(mesh):
    block = P("dep", "lat", None)
    return jax.shard_map(
        functools.partial(on_device, mesh.shape["lat"], mesh.shape["dep"]),
        mesh=mesh,
        in_specs=(block, block, block, P(), P(), P(), P()),
        out_specs=(block, P(None, "lat", "dep")),
        check_vma=False,
    )
```

```python
import functools
import math

import jax
import jax.numpy as jnp
from jax import lax
from jax.experimental import pallas as pl
from jax.experimental.pallas import tpu as pltpu
from jax.sharding import PartitionSpec as P

BUMPS = 8
LOG2E = math.log2(math.e)
Z, X, T = 8, 64, 4
ROWS = X + 32
CORE = 16
VMEM = pl.BlockSpec(memory_space=pltpu.VMEM)
SMEM = pl.BlockSpec(memory_space=pltpu.SMEM)
HBM = pl.BlockSpec(memory_space=pltpu.HBM)


def lane_masks():
    lane = lax.broadcasted_iota(jnp.int32, (8, 128), 1)
    return lane < 1, lane < 2, lane >= 127, lane >= 126


def columns_sum(c, masks):
    zero = jnp.zeros((8, 128), jnp.float32)
    low1, low2, high1, high2 = masks
    a1 = [pltpu.roll(v, 1, 1) for v in c]
    a2 = [pltpu.roll(v, 2, 1) for v in c]
    b1 = [pltpu.roll(v, 127, 1) for v in c]
    b2 = [pltpu.roll(v, 126, 1) for v in c]
    out = []
    for i in range(T):
        first, last = i == 0, i == T - 1
        near = jnp.where(low1, zero if first else a1[i - 1], a1[i]) + jnp.where(
            high1, zero if last else b1[i + 1], b1[i]
        )
        far = jnp.where(low2, zero if first else a2[i - 1], a2[i]) + jnp.where(
            high2, zero if last else b2[i + 1], b2[i]
        )
        out.append((near, far))
    return out


def plane_terms(ref, k, row, masks):
    c = [ref[k, i, pl.ds(row, 8), :] for i in range(T)]
    sums = columns_sum(c, masks)
    out = []
    for i in range(T):
        near = sums[i][0] + (ref[k, i, pl.ds(row - 1, 8), :] + ref[k, i, pl.ds(row + 1, 8), :])
        far = sums[i][1] + (ref[k, i, pl.ds(row - 2, 8), :] + ref[k, i, pl.ds(row + 2, 8), :])
        out.append((c[i], near, far))
    return out


def band():
    shape = (256, 256)
    d = jnp.abs(lax.broadcasted_iota(jnp.int32, shape, 0) - lax.broadcasted_iota(jnp.int32, shape, 1))
    half = jnp.where(d == 0, -90.0, jnp.where(d == 1, 16.0, jnp.where(d == 2, -1.0, 0.0))).astype(jnp.bfloat16)
    return jnp.concatenate([half, half], axis=0)


def full_rows(ref, layers, ranges, bands):
    factors, places = [], []
    for k in layers:
        for first, count in ranges:
            rows = slice(first, first + count)
            places.append((k, first, count))
            for h in range(2):
                v = jnp.concatenate([ref[k, 2 * h, rows, :], ref[k, 2 * h + 1, rows, :]], axis=1)
                high = v.astype(jnp.bfloat16)
                low = (v - high.astype(jnp.float32)).astype(jnp.bfloat16)
                factors.append(jnp.concatenate([high, low], axis=1))
    product = jnp.dot(jnp.concatenate(factors, axis=0), bands, preferred_element_type=jnp.float32)
    low1, low2, high1, high2 = lane_masks()
    start = 0
    for k, first, count in places:
        for r in range(0, count, 8):
            row = first + r
            here = slice(row, row + 8)
            for i in range(T):
                c = ref[k, i, here, :]
                at = start + count * (i // 2) + r
                inside = product[at : at + 8, 128 * (i % 2) : 128 * (i % 2) + 128]
                near = ref[k, i, row - 1 : row + 7, :] + ref[k, i, row + 1 : row + 9, :]
                far = ref[k, i, row - 2 : row + 6, :] + ref[k, i, row + 2 : row + 10, :]
                near = near + (ref[k - 1, i, here, :] + ref[k + 1, i, here, :])
                far = far + (ref[k - 2, i, here, :] + ref[k + 2, i, here, :])
                if i == 1:
                    v = ref[k, 2, here, :]
                    near = near + jnp.where(high1, pltpu.roll(v, 127, 1), 0.0)
                    far = far + jnp.where(high2, pltpu.roll(v, 126, 1), 0.0)
                if i == 2:
                    v = ref[k, 1, here, :]
                    near = near + jnp.where(low1, pltpu.roll(v, 1, 1), 0.0)
                    far = far + jnp.where(low2, pltpu.roll(v, 2, 1), 0.0)
                yield k, row, i, c, inside + (16.0 * near - far)
        start += 2 * count


def strike(ref, outer, place, amplitude, layers, rows):
    z, x, y = place
    row = x + CORE
    inside = functools.reduce(jnp.logical_or, [(row >= first) & (row < end) for first, end in rows])

    @pl.when((z >= layers[0]) & (z < layers[1]) & inside)
    def _():
        tile, lane = y // 128, y % 128
        old = ref[z + outer, tile, pl.ds(row, 1), :]
        ids = lax.broadcasted_iota(jnp.int32, (1, 128), 1)
        ref[z + outer, tile, pl.ds(row, 1), :] = old + jnp.where(ids == lane, amplitude, 0.0)


def stiffness(table, materials):
    return jnp.take_along_axis(table, materials, axis=1, mode="promise_in_bounds")


def ways():
    return lax.axis_index("dep") % 2, (lax.axis_index("lat") + 1) % 2


def source_place(cell):
    return cell[0] - lax.axis_index("dep") * Z, cell[1] - lax.axis_index("lat") * X, cell[2]


def wavelets(start):
    level = (lax.broadcasted_iota(jnp.int32, (8, 128), 0) + start[0]).astype(jnp.float32)
    shifted = 0.3 * (level - 10.0)
    return 4.0 * (1.0 - 2.0 * shifted * shifted) * jnp.exp(-shifted * shifted)


def stiffness_table(courant):
    lane = lax.broadcasted_iota(jnp.int32, (8, 128), 1)
    table = jnp.zeros((8, 128), jnp.float32)
    for m in range(16):
        table = jnp.where(lane == m, courant[m], table)
    return table * table * (1.0 / 12.0)


def pack(
    courant_in, now_in, prev_in, mat_in, early_1, early_2, side_1, side_2, now, prev, mat, courant, sems,
):
    up1, right1 = ways()
    scalars = pltpu.make_async_copy(courant_in, courant, sems.at[0])
    scalars.start()
    copies = {}
    for n, pair in enumerate((0, 3, 1, 2)):
        for m, (src, dst) in enumerate(((mat_in, mat), (now_in, now), (prev_in, prev))):
            layers = pl.ds(2 * pair, 2)
            copies[n, m] = pltpu.make_async_copy(src.at[layers], dst.at[layers], sems.at[1 + 3 * n + m])
    order = [(0, 0), (1, 0), (0, 1), (1, 1), (2, 0), (3, 0), (2, 1), (3, 1), (0, 2), (1, 2), (2, 2), (3, 2)]
    for key in order:
        copies[key].start()
    upper_half = (lax.broadcasted_iota(jnp.int32, (8, 128), 0) >= 4).astype(jnp.int32)
    scalars.wait()
    table = stiffness_table(courant)
    for key in order[:4]:
        copies[key].wait()
    for slot, out in enumerate((early_1, early_2)):
        first = 6 * up1 if slot == 0 else 6 - 6 * up1
        for k in range(2):
            for i in range(T):
                lanes = slice(128 * i, 128 * i + 128)
                out[k, i] = now[first + k, :, lanes]
                for t in range(X // 8):
                    rows = slice(8 * t, 8 * t + 8)
                    out[2 + k, i, rows, :] = stiffness(table, mat[first + k, rows, lanes])
    for key in order[4:]:
        copies[key].wait()
    for slot, out in enumerate((side_1, side_2)):
        right = right1 if slot == 0 else 1 - right1
        rows = pl.ds(pl.multiple_of((X - 8) * right, 8), 8)
        keep = upper_half == right
        for k in range(Z):
            for i in range(T):
                lanes = slice(128 * i, 128 * i + 128)
                out[k, i, 0:8, :] = now[k, rows, lanes]
                moved = pltpu.roll(stiffness(table, mat[k, rows, lanes]), 4, 0)
                out[k, i, 8:16, :] = jnp.where(keep, prev[k, rows, lanes], moved)


INNER = ((CORE + 8, X - 16),)
INSIDE = ((CORE, X),)
OUTER = ((CORE - 8, 16), (CORE + X - 8, 16))


def advance_inner(courant, start, now, prev, mat, now_out, stiff_out, one_out, prev_out, bands, amplitudes):
    table = stiffness_table(courant)
    bands[...] = band()
    amplitudes[...] = wavelets(start)
    zeros = jnp.zeros((T, ROWS, 128), jnp.float32)
    for k in (0, 1, Z + 2, Z + 3):
        now_out[k] = zeros
        one_out[k] = zeros

    def fill(k, carry):
        for i in range(T):
            now_out[k + 2, i, CORE : CORE + X, :] = now[k, :, 128 * i : 128 * i + 128]
        return carry

    lax.fori_loop(0, Z, fill, 0)

    def first(n, carry):
        for k in (2 * n, 2 * n + 1):
            for i in range(T):
                lanes = slice(128 * i, 128 * i + 128)
                prev_out[k, i, 0:8, :] = prev[k, 0:8, lanes]
                prev_out[k, i, 8:16, :] = prev[k, X - 8 : X, lanes]
                for t in range(X // 8):
                    rows = slice(8 * t, 8 * t + 8)
                    stiff_out[k, i, rows, :] = stiffness(table, mat[k, rows, lanes])
        for k, row, i, c, lap in full_rows(now_out, (2 * n + 2, 2 * n + 3), INNER, bands[...]):
            own = slice(row - CORE, row - CORE + 8)
            before = prev[k - 2, own, 128 * i : 128 * i + 128]
            one_out[k, i, row : row + 8, :] = 2.0 * c - before + stiff_out[k - 2, i, own, :] * lap
        return carry

    lax.fori_loop(0, Z // 2, first, 0)


def advance_outer(
    cell, amplitudes, bands, now_in, stiff_in, one_in, prev_in, lat_a, lat_b, now, one, now_side, stiff_side, two_out,
    prev_side,
):
    del now_in, one_in
    right1 = ways()[1] == 1

    def fill(k, carry):
        for i in range(T):
            for left in (False, True):
                wanted = jnp.logical_not(right1) if left else right1
                got = jnp.where(wanted, lat_a[k, i], lat_b[k, i])
                row = CORE - 8 if left else CORE + X
                half = slice(0, 8) if left else slice(8, 16)
                now[k + 2, i, row : row + 8, :] = got[0:8]
                now_side[k, i, half, :] = got[0:8]
                prev_side[k, i, half, :] = got[8:16]
                stiff_side[k, i, half, :] = pltpu.roll(got[8:16], 4, 0)
        return carry

    lax.fori_loop(0, Z, fill, 0)

    def first(n, carry):
        for k, row, i, c, lap in full_rows(now, (2 * n + 2, 2 * n + 3), OUTER, bands[...]):
            if row < CORE or row == CORE + X:
                half = slice(0, 8) if row < CORE else slice(8, 16)
                before, stiff = prev_side[k - 2, i, half, :], stiff_side[k - 2, i, half, :]
            else:
                half = slice(0, 8) if row == CORE else slice(8, 16)
                before, stiff = prev_in[k - 2, i, half, :], stiff_in[k - 2, i, row - CORE : row - CORE + 8, :]
            one[k, i, row : row + 8, :] = 2.0 * c - before + stiff * lap
        return carry

    lax.fori_loop(0, Z // 2, first, 0)
    place = source_place(cell)
    strike(one, 2, place, amplitudes[0:1, :], (0, Z), [(CORE - 8, CORE + X + 8)])

    def second(n, carry):
        base = 6 * n
        for k, row, i, c, lap in full_rows(one, (base + 2, base + 3), INSIDE, bands[...]):
            rows = slice(row, row + 8)
            stiff = stiff_in[k - 2, i, row - CORE : row - CORE + 8, :]
            two_out[k - 2 - 4 * n, i, rows, :] = 2.0 * c - now[k, i, rows, :] + stiff * lap
        return carry

    lax.fori_loop(0, 2, second, 0)
    z = place[0]
    inner = (z >= 2) & (z < Z - 2)
    place = (jnp.where(inner, -1, jnp.where(z < 2, z, z - 4)),) + place[1:]
    strike(two_out, 0, place, amplitudes[1:2, :], (0, 4), [(CORE, CORE + X)])


def pack_late(now_side, stiff_side, one, two, out_a, out_b):
    sub = lax.broadcasted_iota(jnp.int32, (8, 128), 0)
    left, right = slice(CORE - 8, CORE), slice(CORE + X, CORE + X + 8)
    up1 = ways()[0]
    for slot, out in ((0, out_a), (1, out_b)):
        high = up1 if slot == 0 else 1 - up1
        for k in range(2):
            z = (Z - 2) * high + k
            for i in range(T):
                out[k, i, 0:X, :] = one[z + 2, i, CORE : CORE + X, :]
                out[2 + k, i, 0:X, :] = two[2 * high + k, i, CORE : CORE + X, :]
                out[k, i, X : X + 8, :] = jnp.where(sub >= 4, now_side[z, i, 0:8, :], now_side[z, i, 8:16, :])
                ones = jnp.where(sub >= 4, one[z + 2, i, left, :], one[z + 2, i, right, :])
                side = jnp.where(sub >= 4, stiff_side[z, i, 0:8, :], stiff_side[z, i, 8:16, :])
                outer = (sub < 2) | (sub >= 6)
                out[2 + k, i, X : X + 8, :] = jnp.where(outer, ones, pltpu.roll(side, 4, 0))


def clamp_for_bumps(p):
    return jnp.minimum(jnp.maximum(p, -7.4), 7.4)


ORDERS = (
    (8, 2, 0, 15, 1, 13, 12, 9, 3, 7, 4, 10, 14, 11, 6, 5),
    (10, 15, 7, 4, 12, 5, 8, 0, 13, 3, 2, 1, 6, 9, 14, 11),
)


def rank(dep):
    even, odd = (order.index(dep) for order in ORDERS)
    return even + (odd - even) * (lax.axis_index("lat") % 2)


SIDES = ((False, 0, 1, 0, 0, 1, 0), (True, 2, 0, 1, Z - 1, Z - 2, Z + 2))


def halo_step(delta, one, halo_stiff, base, near, far, n_in, n_next, row, masks):
    rows, own = pl.ds(row, 8), pl.ds(row - CORE, 8)
    close, distant = plane_terms(delta, base + near, row, masks), plane_terms(delta, base + far, row, masks)
    for i in range(T):
        inner, following = one[n_in + 2, i, rows, :], one[n_next + 2, i, rows, :]
        for place, (c, near_sum, far_sum), (other, _, _), first, second in (
            (near, close[i], distant[i], inner, following),
            (far, distant[i], close[i], None, inner),
        ):
            near_sum = near_sum + other
            if first is not None:
                near_sum = near_sum + first
            lap = 16.0 * near_sum - (far_sum + second) - 90.0 * c
            yield place, i, 2.0 * c + halo_stiff[base + place, i, own, :] * lap


def outer_second(first, bands, now, stiff, stiff_side, one, two):
    for k, row, i, c, lap in full_rows(one, (first + 2, first + 3), OUTER, bands[...]):
        if CORE <= row < CORE + X:
            st = stiff[k - 2, i, row - CORE : row - CORE + 8, :]
        else:
            st = stiff_side[k - 2, i, 0:8, :] if row < CORE else stiff_side[k - 2, i, 8:16, :]
        rows = slice(row, row + 8)
        two[k, i, rows, :] = 2.0 * c - now[k, i, rows, :] + st * lap


def couple(
    cell, amplitudes, bands, now, stiff, now_side, stiff_side, one_in, early_a, early_b, sent, one, two, delta, halo_stiff,
    halo_two,
):
    del one_in, sent
    masks = lane_masks()
    up1 = ways()[0] == 1
    for high, base, near, far, n_in, n_next, zi in SIDES:
        use_a = up1 if high else jnp.logical_not(up1)

        def tile(t, carry, use_a=use_a, base=base, near=near, far=far, n_in=n_in, n_next=n_next, zi=zi):
            own, rows = pl.ds(pl.multiple_of(8 * t, 8), 8), pl.ds(pl.multiple_of(CORE + 8 * t, 8), 8)
            for i in range(T):
                zero_h = [jnp.where(use_a, early_a[k, i, own, :], early_b[k, i, own, :]) for k in range(2)]
                st_h = [jnp.where(use_a, early_a[2 + k, i, own, :], early_b[2 + k, i, own, :]) for k in range(2)]
                one[n_in + 2, i, rows, :] += stiff[n_in, i, own, :] * (16.0 * zero_h[near] - zero_h[far])
                one[n_next + 2, i, rows, :] -= stiff[n_next, i, own, :] * zero_h[near]
                d_near = st_h[near] * (16.0 * now[n_in + 2, i, rows, :] - now[n_next + 2, i, rows, :])
                d_far = -st_h[far] * now[n_in + 2, i, rows, :]
                for place, d, st in ((near, d_near, st_h[near]), (far, d_far, st_h[far])):
                    one[zi + place, i, rows, :] = d
                    delta[base + place, i, rows, :] = d
                    halo_stiff[base + place, i, own, :] = st
            return carry

        lax.fori_loop(0, X // 8, tile, 0)

    def second(n, carry):
        for k, row, i, c, lap in full_rows(one, (2 * n + 2, 2 * n + 3), INNER, bands[...]):
            rows, own = slice(row, row + 8), slice(row - CORE, row - CORE + 8)
            two[k, i, rows, :] = 2.0 * c - now[k, i, rows, :] + stiff[k - 2, i, own, :] * lap
        return carry

    lax.fori_loop(0, Z // 2, second, 0)

    def middle(n, carry):
        outer_second(2 * n + 2, bands, now, stiff, stiff_side, one, two)
        return carry

    lax.fori_loop(0, 2, middle, 0)
    place = source_place(cell)
    strike(two, 2, place, amplitudes[1:2, :], (0, Z), [(CORE + 8, CORE + X - 8)])
    strike(two, 2, place, amplitudes[1:2, :], (2, Z - 2), [(CORE - 8, CORE + 8), (CORE + X - 8, CORE + X + 8)])
    for high, base, near, far, n_in, n_next, zi in SIDES:

        def beyond(t, carry, base=base, near=near, far=far, n_in=n_in, n_next=n_next):
            row = pl.multiple_of(CORE + 8 * t, 8)
            for k, i, v in halo_step(delta, one, halo_stiff, base, near, far, n_in, n_next, row, masks):
                halo_two[base + k, i, pl.ds(pl.multiple_of(8 * t, 8), 8), :] = v
            return carry

        lax.fori_loop(1, X // 8 - 1, beyond, 0)


def complete(
    second_half, cell, amplitudes, bands, stiff, now, now_side, stiff_side, one, two, delta, halo_stiff, halo_two, late, three
):
    masks = lane_masks()
    place = source_place(cell)
    high = 1 - ways()[0] if second_half else ways()[0]
    base, near, far, n_in, n_next, zi = 2 * high, 1 - high, high, (Z - 1) * high, 1 + (Z - 3) * high, (Z + 2) * high

    extra = slice(X, X + 8)
    n_third, n_fourth = 2 + (Z - 5) * high, 3 + (Z - 7) * high
    for row in (CORE - 8, CORE + X):
        rows, half = slice(row, row + 8), slice(0, 8) if row < CORE else slice(8, 16)
        for i in range(T):
            zero_near, zero_far = late[near, i, extra, :], late[far, i, extra, :]
            more_in = stiff_side[n_in, i, half, :] * (16.0 * zero_near - zero_far)
            less_next = stiff_side[n_next, i, half, :] * zero_near
            one[n_in + 2, i, rows, :] += more_in
            one[n_next + 2, i, rows, :] -= less_next
            two[n_third + 2, i, rows, :] -= stiff_side[n_third, i, half, :] * (16.0 * less_next + more_in)
            two[n_fourth + 2, i, rows, :] += stiff_side[n_fourth, i, half, :] * less_next
            first, second = now_side[n_in, i, half, :], now_side[n_next, i, half, :]
            for at, term in ((near, 16.0 * first - second), (far, -first)):
                v = late[2 + at, i, extra, :]
                d = pltpu.roll(v, 4, 0) * term
                one[zi + at, i, rows, :] = v + d
                delta[base + at, i, rows, :] = d

    def inner(t, carry):
        row = pl.multiple_of(CORE + 8 * t, 8)
        rows, own = pl.ds(row, 8), pl.ds(pl.multiple_of(8 * t, 8), 8)
        for i in range(T):
            one_near, one_far = late[near, i, own, :], late[far, i, own, :]
            one[zi + near, i, rows, :] += one_near
            one[zi + far, i, rows, :] += one_far
            for k in range(2):
                two[zi + k, i, rows, :] = late[2 + k, i, own, :] + halo_two[base + k, i, own, :]
            two[n_in + 2, i, rows, :] += stiff[n_in, i, own, :] * (16.0 * one_near - one_far)
            two[n_next + 2, i, rows, :] -= stiff[n_next, i, own, :] * one_near
        return carry

    lax.fori_loop(0, X // 8, inner, 0)
    for row in (CORE, CORE + X - 8):
        for k, i, v in halo_step(delta, one, halo_stiff, base, near, far, n_in, n_next, row, masks):
            two[zi + k, i, row : row + 8, :] = late[2 + k, i, row - CORE : row - CORE + 8, :] + v

    lowest = (Z - 2) * high

    outer_second(lowest, bands, now, stiff, stiff_side, one, two)
    outer = [(CORE - 8, CORE + 8), (CORE + X - 8, CORE + X + 8)]
    strike(two, 2, place, amplitudes[1:2, :], (lowest, lowest + 2), outer)

    def third(n, carry):
        base = 4 * high + 2 * n
        for k, row, i, c, lap in full_rows(two, (base + 2, base + 3), INSIDE, bands[...]):
            own = slice(row - CORE, row - CORE + 8)
            before = one[k, i, row : row + 8, :]
            three[k - 2 - 4 * high, own, 128 * i : 128 * i + 128] = 2.0 * c - before + stiff[k - 2, i, own, :] * lap
        return carry

    lax.fori_loop(0, 2, third, 0)
    z, x, y = place
    n = z - 4 * high

    @pl.when((n >= 0) & (n < 4) & (x >= 0) & (x < X))
    def _():
        ids = lax.broadcasted_iota(jnp.int32, (1, 512), 1)
        amplitude = jnp.concatenate([amplitudes[2:3, :]] * T, axis=1)
        three[n, pl.ds(x, 1), :] = three[n, pl.ds(x, 1), :] + jnp.where(ids == y, amplitude, 0.0)


def weigh(n_dep, transfer, weights):
    for n in range(4):
        for j in range(BUMPS):
            centre = (-3.0 + 6.0 * j / (BUMPS - 1)) / 0.8
            weights[n, j] = transfer[n, j] * (math.exp(-centre * centre) * (-LOG2E * 1.5 / (Z * n_dep) if n == 3 else 1.0))


def look(weights, three, i, own):
    half = BUMPS // 2
    rate = 6.0 / (BUMPS - 1) / (0.8 * 0.8) * LOG2E
    zero = jnp.zeros((8, 128), jnp.float32)
    seen = [zero] * BUMPS
    through = jnp.ones((8, 128), jnp.float32)
    depth = zero
    for n in range(4):
        p = clamp_for_bumps(three[n, own, 128 * i : 128 * i + 128])
        gauss = jnp.exp2(p * p * (-LOG2E / 0.64))
        rise = jnp.exp2(p * rate)
        fall = jnp.exp2(p * -rate)
        up, down = rise * rise, fall * fall
        above, below = gauss * rise, gauss * fall
        a = weights[3, BUMPS - 1] * up + weights[3, BUMPS - 2]
        b = weights[3, 0] * down + weights[3, 1]
        for j in range(2, half):
            a = a * up + weights[3, BUMPS - 1 - j]
            b = b * down + weights[3, j]
        power = a * above + b * below
        stay = jnp.exp2(power)
        weight = through * (1.0 - stay)
        through = through * stay
        depth = depth + power
        above, below = weight * above, weight * below
        for j in range(half):
            seen[half + j] = seen[half + j] + above
            seen[half - 1 - j] = seen[half - 1 - j] + below
            if j < half - 1:
                above, below = above * up, below * down
    return seen, through, depth


def finish_first(
    n_dep, cell, amplitudes, transfer, bands, now, stiff, now_side, stiff_side, one_in, two_in, delta_in, halo_stiff, halo_two,
    late, three, looked, one, two, delta, weights,
):
    del one_in, two_in, delta_in
    weigh(n_dep, transfer, weights)
    complete(False, cell, amplitudes, bands, stiff, now, now_side, stiff_side, one, two, delta, halo_stiff, halo_two, late, three)

    def render(t, carry):
        own = pl.ds(pl.multiple_of(8 * t, 8), 8)
        for i in range(T):
            seen, through, depth = look(weights, three, i, own)
            for j, v in enumerate(seen + [through, depth]):
                looked[j, i, own, :] = v
        return carry

    lax.fori_loop(0, X // 8, render, 0)


def finish_second(
    n_dep, cell, amplitudes, transfer, bands, now, stiff, now_side, stiff_side, one_in, two_in, delta_in, halo_stiff, halo_two,
    late, other, looked, pressure, partial, one, two, delta, weights, three, sems,
):
    del one_in, two_in, delta_in
    high = 1 - ways()[0]
    copies = [
        pltpu.make_async_copy(other, pressure.at[pl.ds(4 - 4 * high, 4)], sems.at[0]),
        pltpu.make_async_copy(three, pressure.at[pl.ds(4 * high, 4)], sems.at[1]),
    ]
    copies[0].start()
    weigh(n_dep, transfer, weights)
    complete(True, cell, amplitudes, bands, stiff, now, now_side, stiff_side, one, two, delta, halo_stiff, halo_two, late, three)
    copies[1].start()
    group = lax.broadcasted_iota(jnp.int32, (8, 128), 1) // 32
    behind = high == 1

    def render(t, carry):
        own = pl.ds(pl.multiple_of(8 * t, 8), 8)
        for i in range(T):
            seen, through, depth = look(weights, three, i, own)
            mine = jnp.where(behind, looked[BUMPS, i, own, :], 1.0)
            others = jnp.where(behind, 1.0, through)
            seen = [mine * seen[j] + others * looked[j, i, own, :] for j in range(BUMPS)]
            depth = depth + looked[BUMPS + 1, i, own, :]
            parts = []
            for n in range(3):
                colour = weights[n, 0] * seen[0]
                for j in range(1, BUMPS):
                    colour = colour + weights[n, j] * seen[j]
                parts.append(colour)
            parts.append(depth * (-1.0 / LOG2E))
            turned = [parts[0]] + [pltpu.roll(parts[n], 32 * n, 1) for n in range(1, 4)]
            for q in range(4):
                packed = turned[0]
                for n in range(1, 4):
                    packed = jnp.where(group == (n + q) % 4, turned[n], packed)
                partial[rank(4 * i + q), own, :] = packed
        return carry

    lax.fori_loop(0, X // 8, render, 0)
    for copy in copies:
        copy.wait()


def composite(parts, image):
    q = lax.axis_index("dep") % 4
    group = lax.broadcasted_iota(jnp.int32, (X, 128), 1) // 32
    last = group == (q + 3) % 4
    others = [group == (q + n) % 4 for n in range(3)]
    before = jnp.zeros((X, 128), jnp.float32)
    total = jnp.zeros((X, 128), jnp.float32)
    for d in range(parts.shape[0]):
        v = parts[rank(d)]
        total = total + jnp.exp(-before) * v
        depth = v
        for n in range(3):
            depth = jnp.where(others[n], pltpu.roll(v, 32 * (n + 1), 1), depth)
        before = before + depth
    view = jnp.where(last, 1.0 - jnp.exp(-before), total).T
    for g in range(4):
        image[pl.ds(pl.multiple_of(32 * ((g + 4 - q) % 4), 32), 32), :] = view[32 * g : 32 * g + 32, :]


def swaps(n_lat, n_dep, kind):
    out = []
    for lat in range(n_lat):
        for dep in range(n_dep):
            other_lat, other_dep = lat, dep
            if kind in ("d1", "d2"):
                up = (dep % 2 == 1) == (kind == "d1")
                other_dep = dep + 1 if up else dep - 1
            else:
                right = (lat % 2 == 0) == (kind == "l1")
                other_lat = lat + 1 if right else lat - 1
            if 0 <= other_lat < n_lat and 0 <= other_dep < n_dep:
                out.append((lat * n_dep + dep, other_lat * n_dep + other_dep))
    return out


def on_device(n_lat, n_dep, pressure_prev, pressure_now, materials, courant_table, tf_weights, source_cell, start_step):
    f32 = jnp.float32

    def swap(v, kind):
        return lax.ppermute(v, ("lat", "dep"), swaps(n_lat, n_dep, kind))

    def busy(microseconds):
        return pl.CostEstimate(
            flops=int(microseconds * 1.0e9), bytes_accessed=int(microseconds * 3.0e6), transcendentals=0
        )

    def shape(*dims):
        return jax.ShapeDtypeStruct(dims, f32)

    def kept(*dims):
        return pltpu.VMEM(dims, f32)

    def in_hbm(v):
        return pltpu.with_memory_space_constraint(v, pltpu.HBM)

    params = pltpu.CompilerParams(vmem_limit_bytes=24 * 1024 * 1024)
    i32 = jnp.int32
    blocks = [pltpu.VMEM((Z, X, 512), d) for d in (f32, f32, i32)]
    early_1, early_2, side_1, side_2, *inputs = pl.pallas_call(
        pack,
        in_specs=[HBM] * 4,
        out_specs=[VMEM] * 7,
        out_shape=[kept(4, T, X, 128)] * 2 + [kept(Z, T, 16, 128)] * 2 + blocks,
        scratch_shapes=[pltpu.SMEM((16,), f32), pltpu.SemaphoreType.DMA((13,))],
        compiler_params=params,
        name="pack",
    )(*(in_hbm(v) for v in (courant_table, pressure_now, pressure_prev, materials)))
    side_a = swap(side_1, "l1")
    side_b = swap(side_2, "l2")
    early_a = swap(early_1, "d1")
    early_b = swap(early_2, "d2")

    padded = (Z + 4, T, ROWS, 128)
    bands = pltpu.VMEM((512, 256), jnp.bfloat16)
    block, side = (Z, T, X, 128), (Z, T, 16, 128)
    now, stiff, one, prev, bands_made, amplitudes = pl.pallas_call(
        advance_inner,
        in_specs=[SMEM] * 2 + [VMEM] * 3,
        out_specs=[VMEM] * 6,
        out_shape=[kept(*padded), kept(*block), kept(*padded), kept(*side), bands, kept(8, 128)],
        compiler_params=params,
        cost_estimate=busy(3.0),
        name="advance_inner",
    )(courant_table, start_step, *inputs)
    now, one, now_side, stiff_side, two = pl.pallas_call(
        advance_outer,
        in_specs=[SMEM] + [VMEM] * 8,
        out_specs=[VMEM] * 5,
        out_shape=[kept(*padded)] * 2 + [kept(*side)] * 2 + [kept(4, T, ROWS, 128)],
        scratch_shapes=[pltpu.VMEM(side, f32)],
        input_output_aliases={3: 0, 5: 1},
        compiler_params=params,
        cost_estimate=busy(5.0),
        name="advance_outer",
    )(source_cell, amplitudes, bands_made, now, stiff, one, prev, side_a, side_b)
    late_1, late_2 = pl.pallas_call(
        pack_late,
        in_specs=[VMEM] * 4,
        out_specs=[VMEM] * 2,
        out_shape=[kept(4, T, X + 8, 128)] * 2,
        compiler_params=params,
        name="pack_late",
    )(now_side, stiff_side, one, two)
    late_a = swap(late_1, "d1")
    late_b = swap(late_2, "d2")
    one, two, delta, halo_stiff, halo_two = pl.pallas_call(
        couple,
        in_specs=[SMEM] + [VMEM] * 9 + [pl.BlockSpec(memory_space=pl.ANY)],
        out_specs=[VMEM] * 5,
        out_shape=[kept(*padded)] * 2 + [kept(4, T, ROWS, 128)] + [kept(4, T, X, 128)] * 2,
        input_output_aliases={7: 0},
        compiler_params=params,
        cost_estimate=busy(4.0),
        name="couple",
    )(source_cell, amplitudes, bands_made, now, stiff, now_side, stiff_side, one, early_a, early_b, late_1)
    changed = [kept(*padded)] * 2 + [kept(4, T, ROWS, 128)]
    scalars, held = (source_cell, amplitudes, tf_weights), (bands_made, now, stiff, now_side, stiff_side)
    three, looked, one, two, delta = pl.pallas_call(
        functools.partial(finish_first, n_dep),
        in_specs=[SMEM, VMEM, SMEM] + [VMEM] * 11,
        out_specs=[VMEM] * 5,
        out_shape=[kept(4, X, 512), kept(BUMPS + 2, T, X, 128)] + changed,
        scratch_shapes=[pltpu.SMEM((4, BUMPS), f32)],
        input_output_aliases={8: 2, 9: 3, 10: 4},
        compiler_params=params,
        cost_estimate=busy(4.0),
        name="finish_first",
    )(*scalars, *held, one, two, delta, halo_stiff, halo_two, late_a)
    pressure, partial, _, _, _ = pl.pallas_call(
        functools.partial(finish_second, n_dep),
        in_specs=[SMEM, VMEM, SMEM] + [VMEM] * 13,
        out_specs=[HBM] + [VMEM] * 4,
        out_shape=[pltpu.HBM((Z, X, 512), f32), kept(n_dep, X, 128)] + changed,
        scratch_shapes=[pltpu.SMEM((4, BUMPS), f32), pltpu.VMEM((4, X, 512), f32), pltpu.SemaphoreType.DMA((2,))],
        input_output_aliases={8: 2, 9: 3, 10: 4},
        compiler_params=params,
        cost_estimate=busy(4.0),
        name="finish_second",
    )(*scalars, *held, one, two, delta, halo_stiff, halo_two, late_b, three, looked)
    groups = [[lat * n_dep + dep for dep in ORDERS[lat % 2]] for lat in range(n_lat)]
    parts = lax.all_to_all(partial, ("lat", "dep"), 0, 0, axis_index_groups=groups, tiled=True)
    image = pl.pallas_call(
        composite,
        in_specs=[VMEM],
        out_specs=VMEM,
        out_shape=shape(128, X),
        compiler_params=params,
        name="composite",
    )(parts)
    return pressure, jnp.swapaxes(image.reshape(4, 512 // n_dep, X), 1, 2)


def solution(mesh):
    block = P("dep", "lat", None)
    return jax.shard_map(
        functools.partial(on_device, mesh.shape["lat"], mesh.shape["dep"]),
        mesh=mesh,
        in_specs=(block, block, block, P(), P(), P(), P()),
        out_specs=(block, P(None, "lat", "dep")),
        check_vma=False,
    )
```

```python
import functools
import math

import jax
import jax.numpy as jnp
from jax import lax
from jax.experimental import pallas as pl
from jax.experimental.pallas import tpu as pltpu
from jax.sharding import PartitionSpec as P

BUMPS = 8
LOG2E = math.log2(math.e)
Z, X, T = 8, 64, 4
ROWS = X + 32
CORE = 16
VMEM = pl.BlockSpec(memory_space=pltpu.VMEM)
SMEM = pl.BlockSpec(memory_space=pltpu.SMEM)
HBM = pl.BlockSpec(memory_space=pltpu.HBM)


def lane_masks():
    lane = lax.broadcasted_iota(jnp.int32, (8, 128), 1)
    return lane < 1, lane < 2, lane >= 127, lane >= 126


def columns_sum(c, masks):
    zero = jnp.zeros((8, 128), jnp.float32)
    low1, low2, high1, high2 = masks
    a1 = [pltpu.roll(v, 1, 1) for v in c]
    a2 = [pltpu.roll(v, 2, 1) for v in c]
    b1 = [pltpu.roll(v, 127, 1) for v in c]
    b2 = [pltpu.roll(v, 126, 1) for v in c]
    out = []
    for i in range(T):
        first, last = i == 0, i == T - 1
        near = jnp.where(low1, zero if first else a1[i - 1], a1[i]) + jnp.where(
            high1, zero if last else b1[i + 1], b1[i]
        )
        far = jnp.where(low2, zero if first else a2[i - 1], a2[i]) + jnp.where(
            high2, zero if last else b2[i + 1], b2[i]
        )
        out.append((near, far))
    return out


def plane_terms(ref, k, row, masks):
    c = [ref[k, i, pl.ds(row, 8), :] for i in range(T)]
    sums = columns_sum(c, masks)
    out = []
    for i in range(T):
        near = sums[i][0] + (ref[k, i, pl.ds(row - 1, 8), :] + ref[k, i, pl.ds(row + 1, 8), :])
        far = sums[i][1] + (ref[k, i, pl.ds(row - 2, 8), :] + ref[k, i, pl.ds(row + 2, 8), :])
        out.append((c[i], near, far))
    return out


def band():
    shape = (256, 256)
    d = jnp.abs(lax.broadcasted_iota(jnp.int32, shape, 0) - lax.broadcasted_iota(jnp.int32, shape, 1))
    half = jnp.where(d == 0, -90.0, jnp.where(d == 1, 16.0, jnp.where(d == 2, -1.0, 0.0))).astype(jnp.bfloat16)
    return jnp.concatenate([half, half], axis=0)


def full_rows(ref, layers, ranges, bands):
    factors, places = [], []
    for k in layers:
        for first, count in ranges:
            rows = slice(first, first + count)
            places.append((k, first, count))
            for h in range(2):
                v = jnp.concatenate([ref[k, 2 * h, rows, :], ref[k, 2 * h + 1, rows, :]], axis=1)
                high = v.astype(jnp.bfloat16)
                low = (v - high.astype(jnp.float32)).astype(jnp.bfloat16)
                factors.append(jnp.concatenate([high, low], axis=1))
    product = jnp.dot(jnp.concatenate(factors, axis=0), bands, preferred_element_type=jnp.float32)
    low1, low2, high1, high2 = lane_masks()
    start = 0
    for k, first, count in places:
        for r in range(0, count, 8):
            row = first + r
            here = slice(row, row + 8)
            for i in range(T):
                c = ref[k, i, here, :]
                at = start + count * (i // 2) + r
                inside = product[at : at + 8, 128 * (i % 2) : 128 * (i % 2) + 128]
                near = ref[k, i, row - 1 : row + 7, :] + ref[k, i, row + 1 : row + 9, :]
                far = ref[k, i, row - 2 : row + 6, :] + ref[k, i, row + 2 : row + 10, :]
                near = near + (ref[k - 1, i, here, :] + ref[k + 1, i, here, :])
                far = far + (ref[k - 2, i, here, :] + ref[k + 2, i, here, :])
                if i == 1:
                    v = ref[k, 2, here, :]
                    near = near + jnp.where(high1, pltpu.roll(v, 127, 1), 0.0)
                    far = far + jnp.where(high2, pltpu.roll(v, 126, 1), 0.0)
                if i == 2:
                    v = ref[k, 1, here, :]
                    near = near + jnp.where(low1, pltpu.roll(v, 1, 1), 0.0)
                    far = far + jnp.where(low2, pltpu.roll(v, 2, 1), 0.0)
                yield k, row, i, c, inside + (16.0 * near - far)
        start += 2 * count


def strike(ref, outer, place, amplitude, layers, rows):
    z, x, y = place
    row = x + CORE
    inside = functools.reduce(jnp.logical_or, [(row >= first) & (row < end) for first, end in rows])

    @pl.when((z >= layers[0]) & (z < layers[1]) & inside)
    def _():
        tile, lane = y // 128, y % 128
        old = ref[z + outer, tile, pl.ds(row, 1), :]
        ids = lax.broadcasted_iota(jnp.int32, (1, 128), 1)
        ref[z + outer, tile, pl.ds(row, 1), :] = old + jnp.where(ids == lane, amplitude, 0.0)


def stiffness(table, materials):
    return jnp.take_along_axis(table, materials, axis=1, mode="promise_in_bounds")


def ways():
    return lax.axis_index("dep") % 2, (lax.axis_index("lat") + 1) % 2


def source_place(cell):
    return cell[0] - lax.axis_index("dep") * Z, cell[1] - lax.axis_index("lat") * X, cell[2]


def wavelets(start):
    level = (lax.broadcasted_iota(jnp.int32, (8, 128), 0) + start[0]).astype(jnp.float32)
    shifted = 0.3 * (level - 10.0)
    return 4.0 * (1.0 - 2.0 * shifted * shifted) * jnp.exp(-shifted * shifted)


def stiffness_table(courant):
    lane = lax.broadcasted_iota(jnp.int32, (8, 128), 1)
    table = jnp.zeros((8, 128), jnp.float32)
    for m in range(16):
        table = jnp.where(lane == m, courant[m], table)
    return table * table * (1.0 / 12.0)


def pack(
    courant_in, now_in, prev_in, mat_in, early_1, early_2, side_1, side_2, now, prev, mat, courant, sems,
):
    up1, right1 = ways()
    scalars = pltpu.make_async_copy(courant_in, courant, sems.at[0])
    scalars.start()
    copies = {}
    for n, pair in enumerate((0, 3, 1, 2)):
        for m, (src, dst) in enumerate(((mat_in, mat), (now_in, now), (prev_in, prev))):
            layers = pl.ds(2 * pair, 2)
            copies[n, m] = pltpu.make_async_copy(src.at[layers], dst.at[layers], sems.at[1 + 3 * n + m])
    order = [(0, 0), (1, 0), (0, 1), (1, 1), (2, 0), (3, 0), (2, 1), (3, 1), (0, 2), (1, 2), (2, 2), (3, 2)]
    for key in order:
        copies[key].start()
    upper_half = (lax.broadcasted_iota(jnp.int32, (8, 128), 0) >= 4).astype(jnp.int32)
    scalars.wait()
    table = stiffness_table(courant)
    for key in order[:4]:
        copies[key].wait()
    for slot, out in enumerate((early_1, early_2)):
        first = 6 * up1 if slot == 0 else 6 - 6 * up1
        for k in range(2):
            for i in range(T):
                lanes = slice(128 * i, 128 * i + 128)
                out[k, i] = now[first + k, :, lanes]
                for t in range(X // 8):
                    rows = slice(8 * t, 8 * t + 8)
                    out[2 + k, i, rows, :] = stiffness(table, mat[first + k, rows, lanes])
    for key in order[4:]:
        copies[key].wait()
    for slot, out in enumerate((side_1, side_2)):
        right = right1 if slot == 0 else 1 - right1
        rows = pl.ds(pl.multiple_of((X - 8) * right, 8), 8)
        keep = upper_half == right
        for k in range(Z):
            for i in range(T):
                lanes = slice(128 * i, 128 * i + 128)
                out[k, i, 0:8, :] = now[k, rows, lanes]
                moved = pltpu.roll(stiffness(table, mat[k, rows, lanes]), 4, 0)
                out[k, i, 8:16, :] = jnp.where(keep, prev[k, rows, lanes], moved)


INNER = ((CORE + 8, X - 16),)
INSIDE = ((CORE, X),)
OUTER = ((CORE - 8, 16), (CORE + X - 8, 16))


def advance_inner(courant, start, now, prev, mat, now_out, stiff_out, one_out, prev_out, bands, amplitudes):
    table = stiffness_table(courant)
    bands[...] = band()
    amplitudes[...] = wavelets(start)
    zeros = jnp.zeros((T, ROWS, 128), jnp.float32)
    for k in (0, 1, Z + 2, Z + 3):
        now_out[k] = zeros
        one_out[k] = zeros

    def fill(k, carry):
        for i in range(T):
            now_out[k + 2, i, CORE : CORE + X, :] = now[k, :, 128 * i : 128 * i + 128]
        return carry

    lax.fori_loop(0, Z, fill, 0)

    def first(n, carry):
        for k in (2 * n, 2 * n + 1):
            for i in range(T):
                lanes = slice(128 * i, 128 * i + 128)
                prev_out[k, i, 0:8, :] = prev[k, 0:8, lanes]
                prev_out[k, i, 8:16, :] = prev[k, X - 8 : X, lanes]
                for t in range(X // 8):
                    rows = slice(8 * t, 8 * t + 8)
                    stiff_out[k, i, rows, :] = stiffness(table, mat[k, rows, lanes])
        for k, row, i, c, lap in full_rows(now_out, (2 * n + 2, 2 * n + 3), INNER, bands[...]):
            own = slice(row - CORE, row - CORE + 8)
            before = prev[k - 2, own, 128 * i : 128 * i + 128]
            one_out[k, i, row : row + 8, :] = 2.0 * c - before + stiff_out[k - 2, i, own, :] * lap
        return carry

    lax.fori_loop(0, Z // 2, first, 0)


def advance_outer(
    cell, amplitudes, bands, now_in, stiff_in, one_in, prev_in, lat_a, lat_b, now, one, now_side, stiff_side, two_out,
    prev_side,
):
    del now_in, one_in
    right1 = ways()[1] == 1

    def fill(k, carry):
        for i in range(T):
            for left in (False, True):
                wanted = jnp.logical_not(right1) if left else right1
                got = jnp.where(wanted, lat_a[k, i], lat_b[k, i])
                row = CORE - 8 if left else CORE + X
                half = slice(0, 8) if left else slice(8, 16)
                now[k + 2, i, row : row + 8, :] = got[0:8]
                now_side[k, i, half, :] = got[0:8]
                prev_side[k, i, half, :] = got[8:16]
                stiff_side[k, i, half, :] = pltpu.roll(got[8:16], 4, 0)
        return carry

    lax.fori_loop(0, Z, fill, 0)

    def first(n, carry):
        for k, row, i, c, lap in full_rows(now, (2 * n + 2, 2 * n + 3), OUTER, bands[...]):
            if row < CORE or row == CORE + X:
                half = slice(0, 8) if row < CORE else slice(8, 16)
                before, stiff = prev_side[k - 2, i, half, :], stiff_side[k - 2, i, half, :]
            else:
                half = slice(0, 8) if row == CORE else slice(8, 16)
                before, stiff = prev_in[k - 2, i, half, :], stiff_in[k - 2, i, row - CORE : row - CORE + 8, :]
            one[k, i, row : row + 8, :] = 2.0 * c - before + stiff * lap
        return carry

    lax.fori_loop(0, Z // 2, first, 0)
    place = source_place(cell)
    strike(one, 2, place, amplitudes[0:1, :], (0, Z), [(CORE - 8, CORE + X + 8)])

    def second(n, carry):
        base = 6 * n
        for k, row, i, c, lap in full_rows(one, (base + 2, base + 3), INSIDE, bands[...]):
            rows = slice(row, row + 8)
            stiff = stiff_in[k - 2, i, row - CORE : row - CORE + 8, :]
            two_out[k - 2 - 4 * n, i, rows, :] = 2.0 * c - now[k, i, rows, :] + stiff * lap
        return carry

    lax.fori_loop(0, 2, second, 0)
    z = place[0]
    inner = (z >= 2) & (z < Z - 2)
    place = (jnp.where(inner, -1, jnp.where(z < 2, z, z - 4)),) + place[1:]
    strike(two_out, 0, place, amplitudes[1:2, :], (0, 4), [(CORE, CORE + X)])


def pack_late(now_side, stiff_side, one, two, out_a, out_b):
    sub = lax.broadcasted_iota(jnp.int32, (8, 128), 0)
    left, right = slice(CORE - 8, CORE), slice(CORE + X, CORE + X + 8)
    up1 = ways()[0]
    for slot, out in ((0, out_a), (1, out_b)):
        high = up1 if slot == 0 else 1 - up1
        for k in range(2):
            z = (Z - 2) * high + k
            for i in range(T):
                out[k, i, 0:X, :] = one[z + 2, i, CORE : CORE + X, :]
                out[2 + k, i, 0:X, :] = two[2 * high + k, i, CORE : CORE + X, :]
                out[k, i, X : X + 8, :] = jnp.where(sub >= 4, now_side[z, i, 0:8, :], now_side[z, i, 8:16, :])
                ones = jnp.where(sub >= 4, one[z + 2, i, left, :], one[z + 2, i, right, :])
                side = jnp.where(sub >= 4, stiff_side[z, i, 0:8, :], stiff_side[z, i, 8:16, :])
                outer = (sub < 2) | (sub >= 6)
                out[2 + k, i, X : X + 8, :] = jnp.where(outer, ones, pltpu.roll(side, 4, 0))


def clamp_for_bumps(p):
    return jnp.minimum(jnp.maximum(p, -7.4), 7.4)


ORDERS = (
    (8, 2, 0, 15, 1, 13, 12, 9, 3, 7, 4, 10, 14, 11, 6, 5),
    (10, 15, 7, 4, 12, 5, 8, 0, 13, 3, 2, 1, 6, 9, 14, 11),
)


def rank(dep):
    even, odd = (order.index(dep) for order in ORDERS)
    return even + (odd - even) * (lax.axis_index("lat") % 2)


SIDES = ((False, 0, 1, 0, 0, 1, 0), (True, 2, 0, 1, Z - 1, Z - 2, Z + 2))


def halo_step(delta, one, halo_stiff, base, near, far, n_in, n_next, row, masks):
    rows, own = pl.ds(row, 8), pl.ds(row - CORE, 8)
    close, distant = plane_terms(delta, base + near, row, masks), plane_terms(delta, base + far, row, masks)
    for i in range(T):
        inner, following = one[n_in + 2, i, rows, :], one[n_next + 2, i, rows, :]
        for place, (c, near_sum, far_sum), (other, _, _), first, second in (
            (near, close[i], distant[i], inner, following),
            (far, distant[i], close[i], None, inner),
        ):
            near_sum = near_sum + other
            if first is not None:
                near_sum = near_sum + first
            lap = 16.0 * near_sum - (far_sum + second) - 90.0 * c
            yield place, i, 2.0 * c + halo_stiff[base + place, i, own, :] * lap


def outer_second(first, bands, now, stiff, stiff_side, one, two):
    for k, row, i, c, lap in full_rows(one, (first + 2, first + 3), OUTER, bands[...]):
        if CORE <= row < CORE + X:
            st = stiff[k - 2, i, row - CORE : row - CORE + 8, :]
        else:
            st = stiff_side[k - 2, i, 0:8, :] if row < CORE else stiff_side[k - 2, i, 8:16, :]
        rows = slice(row, row + 8)
        two[k, i, rows, :] = 2.0 * c - now[k, i, rows, :] + st * lap


def couple(
    cell, amplitudes, bands, now, stiff, now_side, stiff_side, one_in, early_a, early_b, sent, one, two, delta, halo_stiff,
    halo_two,
):
    del one_in, sent
    masks = lane_masks()
    up1 = ways()[0] == 1
    for high, base, near, far, n_in, n_next, zi in SIDES:
        use_a = up1 if high else jnp.logical_not(up1)

        def tile(t, carry, use_a=use_a, base=base, near=near, far=far, n_in=n_in, n_next=n_next, zi=zi):
            own, rows = pl.ds(pl.multiple_of(8 * t, 8), 8), pl.ds(pl.multiple_of(CORE + 8 * t, 8), 8)
            for i in range(T):
                zero_h = [jnp.where(use_a, early_a[k, i, own, :], early_b[k, i, own, :]) for k in range(2)]
                st_h = [jnp.where(use_a, early_a[2 + k, i, own, :], early_b[2 + k, i, own, :]) for k in range(2)]
                one[n_in + 2, i, rows, :] += stiff[n_in, i, own, :] * (16.0 * zero_h[near] - zero_h[far])
                one[n_next + 2, i, rows, :] -= stiff[n_next, i, own, :] * zero_h[near]
                d_near = st_h[near] * (16.0 * now[n_in + 2, i, rows, :] - now[n_next + 2, i, rows, :])
                d_far = -st_h[far] * now[n_in + 2, i, rows, :]
                for place, d, st in ((near, d_near, st_h[near]), (far, d_far, st_h[far])):
                    one[zi + place, i, rows, :] = d
                    delta[base + place, i, rows, :] = d
                    halo_stiff[base + place, i, own, :] = st
            return carry

        lax.fori_loop(0, X // 8, tile, 0)

    def second(n, carry):
        for k, row, i, c, lap in full_rows(one, (2 * n + 2, 2 * n + 3), INNER, bands[...]):
            rows, own = slice(row, row + 8), slice(row - CORE, row - CORE + 8)
            two[k, i, rows, :] = 2.0 * c - now[k, i, rows, :] + stiff[k - 2, i, own, :] * lap
        return carry

    lax.fori_loop(0, Z // 2, second, 0)

    def middle(n, carry):
        outer_second(2 * n + 2, bands, now, stiff, stiff_side, one, two)
        return carry

    lax.fori_loop(0, 2, middle, 0)
    place = source_place(cell)
    strike(two, 2, place, amplitudes[1:2, :], (0, Z), [(CORE + 8, CORE + X - 8)])
    strike(two, 2, place, amplitudes[1:2, :], (2, Z - 2), [(CORE - 8, CORE + 8), (CORE + X - 8, CORE + X + 8)])
    for high, base, near, far, n_in, n_next, zi in SIDES:

        def beyond(t, carry, base=base, near=near, far=far, n_in=n_in, n_next=n_next):
            row = pl.multiple_of(CORE + 8 * t, 8)
            for k, i, v in halo_step(delta, one, halo_stiff, base, near, far, n_in, n_next, row, masks):
                halo_two[base + k, i, pl.ds(pl.multiple_of(8 * t, 8), 8), :] = v
            return carry

        lax.fori_loop(1, X // 8 - 1, beyond, 0)


def complete(
    second_half, cell, amplitudes, bands, stiff, now, now_side, stiff_side, one, two, delta, halo_stiff, halo_two, late, three
):
    masks = lane_masks()
    place = source_place(cell)
    high = 1 - ways()[0] if second_half else ways()[0]
    base, near, far, n_in, n_next, zi = 2 * high, 1 - high, high, (Z - 1) * high, 1 + (Z - 3) * high, (Z + 2) * high

    extra = slice(X, X + 8)
    n_third, n_fourth = 2 + (Z - 5) * high, 3 + (Z - 7) * high
    for row in (CORE - 8, CORE + X):
        rows, half = slice(row, row + 8), slice(0, 8) if row < CORE else slice(8, 16)
        for i in range(T):
            zero_near, zero_far = late[near, i, extra, :], late[far, i, extra, :]
            more_in = stiff_side[n_in, i, half, :] * (16.0 * zero_near - zero_far)
            less_next = stiff_side[n_next, i, half, :] * zero_near
            one[n_in + 2, i, rows, :] += more_in
            one[n_next + 2, i, rows, :] -= less_next
            two[n_third + 2, i, rows, :] -= stiff_side[n_third, i, half, :] * (16.0 * less_next + more_in)
            two[n_fourth + 2, i, rows, :] += stiff_side[n_fourth, i, half, :] * less_next
            first, second = now_side[n_in, i, half, :], now_side[n_next, i, half, :]
            for at, term in ((near, 16.0 * first - second), (far, -first)):
                v = late[2 + at, i, extra, :]
                d = pltpu.roll(v, 4, 0) * term
                one[zi + at, i, rows, :] = v + d
                delta[base + at, i, rows, :] = d

    def inner(t, carry):
        row = pl.multiple_of(CORE + 8 * t, 8)
        rows, own = pl.ds(row, 8), pl.ds(pl.multiple_of(8 * t, 8), 8)
        for i in range(T):
            one_near, one_far = late[near, i, own, :], late[far, i, own, :]
            one[zi + near, i, rows, :] += one_near
            one[zi + far, i, rows, :] += one_far
            for k in range(2):
                two[zi + k, i, rows, :] = late[2 + k, i, own, :] + halo_two[base + k, i, own, :]
            two[n_in + 2, i, rows, :] += stiff[n_in, i, own, :] * (16.0 * one_near - one_far)
            two[n_next + 2, i, rows, :] -= stiff[n_next, i, own, :] * one_near
        return carry

    lax.fori_loop(0, X // 8, inner, 0, unroll=2)
    for row in (CORE, CORE + X - 8):
        for k, i, v in halo_step(delta, one, halo_stiff, base, near, far, n_in, n_next, row, masks):
            two[zi + k, i, row : row + 8, :] = late[2 + k, i, row - CORE : row - CORE + 8, :] + v

    lowest = (Z - 2) * high

    outer_second(lowest, bands, now, stiff, stiff_side, one, two)
    outer = [(CORE - 8, CORE + 8), (CORE + X - 8, CORE + X + 8)]
    strike(two, 2, place, amplitudes[1:2, :], (lowest, lowest + 2), outer)

    def third(n, carry):
        base = 4 * high + 2 * n
        for k, row, i, c, lap in full_rows(two, (base + 2, base + 3), INSIDE, bands[...]):
            own = slice(row - CORE, row - CORE + 8)
            before = one[k, i, row : row + 8, :]
            three[k - 2 - 4 * high, own, 128 * i : 128 * i + 128] = 2.0 * c - before + stiff[k - 2, i, own, :] * lap
        return carry

    lax.fori_loop(0, 2, third, 0)
    z, x, y = place
    n = z - 4 * high

    @pl.when((n >= 0) & (n < 4) & (x >= 0) & (x < X))
    def _():
        ids = lax.broadcasted_iota(jnp.int32, (1, 512), 1)
        amplitude = jnp.concatenate([amplitudes[2:3, :]] * T, axis=1)
        three[n, pl.ds(x, 1), :] = three[n, pl.ds(x, 1), :] + jnp.where(ids == y, amplitude, 0.0)


def weigh(n_dep, transfer, weights):
    for n in range(4):
        for j in range(BUMPS):
            centre = (-3.0 + 6.0 * j / (BUMPS - 1)) / 0.8
            weights[n, j] = transfer[n, j] * (math.exp(-centre * centre) * (-LOG2E * 1.5 / (Z * n_dep) if n == 3 else 1.0))


def look(weights, three, i, own):
    half = BUMPS // 2
    rate = 6.0 / (BUMPS - 1) / (0.8 * 0.8) * LOG2E
    zero = jnp.zeros((8, 128), jnp.float32)
    seen = [zero] * BUMPS
    through = jnp.ones((8, 128), jnp.float32)
    depth = zero
    for n in range(4):
        p = clamp_for_bumps(three[n, own, 128 * i : 128 * i + 128])
        gauss = jnp.exp2(p * p * (-LOG2E / 0.64))
        rise = jnp.exp2(p * rate)
        fall = jnp.exp2(p * -rate)
        up, down = rise * rise, fall * fall
        above, below = gauss * rise, gauss * fall
        a = weights[3, BUMPS - 1] * up + weights[3, BUMPS - 2]
        b = weights[3, 0] * down + weights[3, 1]
        for j in range(2, half):
            a = a * up + weights[3, BUMPS - 1 - j]
            b = b * down + weights[3, j]
        power = a * above + b * below
        stay = jnp.exp2(power)
        weight = through * (1.0 - stay)
        through = through * stay
        depth = depth + power
        above, below = weight * above, weight * below
        for j in range(half):
            seen[half + j] = seen[half + j] + above
            seen[half - 1 - j] = seen[half - 1 - j] + below
            if j < half - 1:
                above, below = above * up, below * down
    return seen, through, depth


def finish_first(
    n_dep, cell, amplitudes, transfer, bands, now, stiff, now_side, stiff_side, one_in, two_in, delta_in, halo_stiff, halo_two,
    late, three, looked, one, two, delta, weights,
):
    del one_in, two_in, delta_in
    weigh(n_dep, transfer, weights)
    complete(False, cell, amplitudes, bands, stiff, now, now_side, stiff_side, one, two, delta, halo_stiff, halo_two, late, three)

    def render(t, carry):
        own = pl.ds(pl.multiple_of(8 * t, 8), 8)
        for i in range(T):
            seen, through, depth = look(weights, three, i, own)
            for j, v in enumerate(seen + [through, depth]):
                looked[j, i, own, :] = v
        return carry

    lax.fori_loop(0, X // 8, render, 0, unroll=2)


def finish_second(
    n_dep, cell, amplitudes, transfer, bands, now, stiff, now_side, stiff_side, one_in, two_in, delta_in, halo_stiff, halo_two,
    late, other, looked, pressure, partial, one, two, delta, weights, three, sems,
):
    del one_in, two_in, delta_in
    high = 1 - ways()[0]
    copies = [
        pltpu.make_async_copy(other, pressure.at[pl.ds(4 - 4 * high, 4)], sems.at[0]),
        pltpu.make_async_copy(three, pressure.at[pl.ds(4 * high, 4)], sems.at[1]),
    ]
    copies[0].start()
    weigh(n_dep, transfer, weights)
    complete(True, cell, amplitudes, bands, stiff, now, now_side, stiff_side, one, two, delta, halo_stiff, halo_two, late, three)
    copies[1].start()
    group = lax.broadcasted_iota(jnp.int32, (8, 128), 1) // 32
    behind = high == 1

    def render(t, carry):
        own = pl.ds(pl.multiple_of(8 * t, 8), 8)
        for i in range(T):
            seen, through, depth = look(weights, three, i, own)
            mine = jnp.where(behind, looked[BUMPS, i, own, :], 1.0)
            others = jnp.where(behind, 1.0, through)
            seen = [mine * seen[j] + others * looked[j, i, own, :] for j in range(BUMPS)]
            depth = depth + looked[BUMPS + 1, i, own, :]
            parts = []
            for n in range(3):
                colour = weights[n, 0] * seen[0]
                for j in range(1, BUMPS):
                    colour = colour + weights[n, j] * seen[j]
                parts.append(colour)
            parts.append(depth * (-1.0 / LOG2E))
            turned = [parts[0]] + [pltpu.roll(parts[n], 32 * n, 1) for n in range(1, 4)]
            for q in range(4):
                packed = turned[0]
                for n in range(1, 4):
                    packed = jnp.where(group == (n + q) % 4, turned[n], packed)
                partial[rank(4 * i + q), own, :] = packed
        return carry

    lax.fori_loop(0, X // 8, render, 0, unroll=2)
    for copy in copies:
        copy.wait()


def composite(parts, image):
    q = lax.axis_index("dep") % 4
    group = lax.broadcasted_iota(jnp.int32, (X, 128), 1) // 32
    last = group == (q + 3) % 4
    others = [group == (q + n) % 4 for n in range(3)]
    before = jnp.zeros((X, 128), jnp.float32)
    total = jnp.zeros((X, 128), jnp.float32)
    for d in range(parts.shape[0]):
        v = parts[rank(d)]
        total = total + jnp.exp(-before) * v
        depth = v
        for n in range(3):
            depth = jnp.where(others[n], pltpu.roll(v, 32 * (n + 1), 1), depth)
        before = before + depth
    view = jnp.where(last, 1.0 - jnp.exp(-before), total).T
    for g in range(4):
        image[pl.ds(pl.multiple_of(32 * ((g + 4 - q) % 4), 32), 32), :] = view[32 * g : 32 * g + 32, :]


def swaps(n_lat, n_dep, kind):
    out = []
    for lat in range(n_lat):
        for dep in range(n_dep):
            other_lat, other_dep = lat, dep
            if kind in ("d1", "d2"):
                up = (dep % 2 == 1) == (kind == "d1")
                other_dep = dep + 1 if up else dep - 1
            else:
                right = (lat % 2 == 0) == (kind == "l1")
                other_lat = lat + 1 if right else lat - 1
            if 0 <= other_lat < n_lat and 0 <= other_dep < n_dep:
                out.append((lat * n_dep + dep, other_lat * n_dep + other_dep))
    return out


def on_device(n_lat, n_dep, pressure_prev, pressure_now, materials, courant_table, tf_weights, source_cell, start_step):
    f32 = jnp.float32

    def swap(v, kind):
        return lax.ppermute(v, ("lat", "dep"), swaps(n_lat, n_dep, kind))

    def busy(microseconds):
        return pl.CostEstimate(
            flops=int(microseconds * 1.0e9), bytes_accessed=int(microseconds * 3.0e6), transcendentals=0
        )

    def shape(*dims):
        return jax.ShapeDtypeStruct(dims, f32)

    def kept(*dims):
        return pltpu.VMEM(dims, f32)

    def in_hbm(v):
        return pltpu.with_memory_space_constraint(v, pltpu.HBM)

    params = pltpu.CompilerParams(vmem_limit_bytes=24 * 1024 * 1024)
    i32 = jnp.int32
    blocks = [pltpu.VMEM((Z, X, 512), d) for d in (f32, f32, i32)]
    early_1, early_2, side_1, side_2, *inputs = pl.pallas_call(
        pack,
        in_specs=[HBM] * 4,
        out_specs=[VMEM] * 7,
        out_shape=[kept(4, T, X, 128)] * 2 + [kept(Z, T, 16, 128)] * 2 + blocks,
        scratch_shapes=[pltpu.SMEM((16,), f32), pltpu.SemaphoreType.DMA((13,))],
        compiler_params=params,
        name="pack",
    )(*(in_hbm(v) for v in (courant_table, pressure_now, pressure_prev, materials)))
    side_a = swap(side_1, "l1")
    side_b = swap(side_2, "l2")
    early_a = swap(early_1, "d1")
    early_b = swap(early_2, "d2")

    padded = (Z + 4, T, ROWS, 128)
    bands = pltpu.VMEM((512, 256), jnp.bfloat16)
    block, side = (Z, T, X, 128), (Z, T, 16, 128)
    now, stiff, one, prev, bands_made, amplitudes = pl.pallas_call(
        advance_inner,
        in_specs=[SMEM] * 2 + [VMEM] * 3,
        out_specs=[VMEM] * 6,
        out_shape=[kept(*padded), kept(*block), kept(*padded), kept(*side), bands, kept(8, 128)],
        compiler_params=params,
        cost_estimate=busy(3.0),
        name="advance_inner",
    )(courant_table, start_step, *inputs)
    now, one, now_side, stiff_side, two = pl.pallas_call(
        advance_outer,
        in_specs=[SMEM] + [VMEM] * 8,
        out_specs=[VMEM] * 5,
        out_shape=[kept(*padded)] * 2 + [kept(*side)] * 2 + [kept(4, T, ROWS, 128)],
        scratch_shapes=[pltpu.VMEM(side, f32)],
        input_output_aliases={3: 0, 5: 1},
        compiler_params=params,
        cost_estimate=busy(5.0),
        name="advance_outer",
    )(source_cell, amplitudes, bands_made, now, stiff, one, prev, side_a, side_b)
    late_1, late_2 = pl.pallas_call(
        pack_late,
        in_specs=[VMEM] * 4,
        out_specs=[VMEM] * 2,
        out_shape=[kept(4, T, X + 8, 128)] * 2,
        compiler_params=params,
        name="pack_late",
    )(now_side, stiff_side, one, two)
    late_a = swap(late_1, "d1")
    late_b = swap(late_2, "d2")
    one, two, delta, halo_stiff, halo_two = pl.pallas_call(
        couple,
        in_specs=[SMEM] + [VMEM] * 9 + [pl.BlockSpec(memory_space=pl.ANY)],
        out_specs=[VMEM] * 5,
        out_shape=[kept(*padded)] * 2 + [kept(4, T, ROWS, 128)] + [kept(4, T, X, 128)] * 2,
        input_output_aliases={7: 0},
        compiler_params=params,
        cost_estimate=busy(4.0),
        name="couple",
    )(source_cell, amplitudes, bands_made, now, stiff, now_side, stiff_side, one, early_a, early_b, late_1)
    changed = [kept(*padded)] * 2 + [kept(4, T, ROWS, 128)]
    scalars, held = (source_cell, amplitudes, tf_weights), (bands_made, now, stiff, now_side, stiff_side)
    three, looked, one, two, delta = pl.pallas_call(
        functools.partial(finish_first, n_dep),
        in_specs=[SMEM, VMEM, SMEM] + [VMEM] * 11,
        out_specs=[VMEM] * 5,
        out_shape=[kept(4, X, 512), kept(BUMPS + 2, T, X, 128)] + changed,
        scratch_shapes=[pltpu.SMEM((4, BUMPS), f32)],
        input_output_aliases={8: 2, 9: 3, 10: 4},
        compiler_params=params,
        cost_estimate=busy(4.0),
        name="finish_first",
    )(*scalars, *held, one, two, delta, halo_stiff, halo_two, late_a)
    pressure, partial, _, _, _ = pl.pallas_call(
        functools.partial(finish_second, n_dep),
        in_specs=[SMEM, VMEM, SMEM] + [VMEM] * 13,
        out_specs=[HBM] + [VMEM] * 4,
        out_shape=[pltpu.HBM((Z, X, 512), f32), kept(n_dep, X, 128)] + changed,
        scratch_shapes=[pltpu.SMEM((4, BUMPS), f32), pltpu.VMEM((4, X, 512), f32), pltpu.SemaphoreType.DMA((2,))],
        input_output_aliases={8: 2, 9: 3, 10: 4},
        compiler_params=params,
        cost_estimate=busy(4.0),
        name="finish_second",
    )(*scalars, *held, one, two, delta, halo_stiff, halo_two, late_b, three, looked)
    groups = [[lat * n_dep + dep for dep in ORDERS[lat % 2]] for lat in range(n_lat)]
    parts = lax.all_to_all(partial, ("lat", "dep"), 0, 0, axis_index_groups=groups, tiled=True)
    image = pl.pallas_call(
        composite,
        in_specs=[VMEM],
        out_specs=VMEM,
        out_shape=shape(128, X),
        compiler_params=params,
        name="composite",
    )(parts)
    return pressure, jnp.swapaxes(image.reshape(4, 512 // n_dep, X), 1, 2)


def solution(mesh):
    block = P("dep", "lat", None)
    return jax.shard_map(
        functools.partial(on_device, mesh.shape["lat"], mesh.shape["dep"]),
        mesh=mesh,
        in_specs=(block, block, block, P(), P(), P(), P()),
        out_specs=(block, P(None, "lat", "dep")),
        check_vma=False,
    )
```
